32 devices in a mesh: section: 2 (over core), dp: 16 (over z, y, x).
Axes of the slice: x: 2, y: 2, z: 4, core: 2. Of those that a mesh axis runs over, the one named last changes fastest.
Arguments:
- tokens: bfloat16 [18432, 768], P('dp', 'section'), may hold values from -6 to 6
- image_ids: int32 [32, 576], P('dp'), may hold values from -1 to 4, as said below
- routes: int32 [18432, 2], P('dp'), may hold values from 0 to 3, all different within a row; in each aligned block of 576 rows (0 to 575, 576 to 1151, ...) at most 304 rows name the same one
- norm1_gain: bfloat16 [768], P('section'), may hold values from 0.5 to 1.5
- norm1_bias: bfloat16 [768], P('section'), may hold values from -3 to 3
- qkv_weight: bfloat16 [768, 2304], P('section'), may hold values from -0.21875 to 0.21875
- attn_out_weight: bfloat16 [768, 768], P('section'), may hold values from -0.625 to 0.625
- norm2_gain: bfloat16 [768], P('section'), may hold values from 0.5 to 1.5
- norm2_bias: bfloat16 [768], P('section'), may hold values from -3 to 3
- fc1_weight: bfloat16 [768, 3072], P('section'), may hold values from -0.21875 to 0.21875
- fc2_weight: bfloat16 [3072, 768], P('section'), may hold values from -0.109375 to 0.109375
- norm3_gain: bfloat16 [768], P('section'), may hold values from 0.5 to 1.5
- norm3_bias: bfloat16 [768], P('section'), may hold values from -3 to 3
- router_weight: bfloat16 [768, 4], P('section'), may hold values from -0.15625 to 0.15625
- expert_up: bfloat16 [768, 12288], P('section', 'dp'), may hold values from -0.21875 to 0.21875
- expert_down: bfloat16 [768, 12288], P('section', 'dp'), may hold values from -0.109375 to 0.109375
- cotangent: bfloat16 [18432, 768], P('dp', 'section'), may hold values from -6 to 6
Outputs:
- block_out: bfloat16 [18432, 768], P('dp', 'section')
- input_grad: float32 [18432, 768], P('dp', 'section')
- grad_norm1_gain: float32 [768], P('section')
- grad_norm1_bias: float32 [768], P('section')
- grad_qkv: float32 [768, 2304], P('section')
- grad_attn_out: float32 [768, 768], P('section')
- grad_norm2_gain: float32 [768], P('section')
- grad_norm2_bias: float32 [768], P('section')
- grad_fc1: float32 [768, 3072], P('section')
- grad_fc2: float32 [3072, 768], P('section')
- grad_norm3_gain: float32 [768], P('section')
- grad_norm3_bias: float32 [768], P('section')
- grad_router: float32 [768, 4], P('section')
- grad_expert_up: float32 [768, 12288], P('section', 'dp')
- grad_expert_down: float32 [768, 12288], P('section', 'dp')
The draws below stay inside these ranges and needn't reach their ends.
Inputs may be any that keep to these rules, and one draw needn't show every extreme that they name: `image_ids`: in each row, padding (-1) stands only at the end and covers at most 144 slots; live slots carry image numbers that never fall along the row and that take every value 0 to 4; some row has no padding and some row has 144 padded slots. The routes of padding slots are not used.
All inputs are finite; a program needn't handle non-finite values.
Results may differ from the reference program's by a relative error of at most 0.014.
Values may be sent and summed in bfloat16 or wider, within the bound.
No kernel may reach another device: no remote copies, remote signals or barrier semaphores. Data moves between devices by JAX's collectives and lax.ppermute only.
A program may use at most 384 MiB of HBM per device.

```python
import math
import jax
import jax.numpy as jnp
import numpy as np
from jax import lax

D = 768
HEADS = 12
HEAD = 64
FF = 3072
TOP = 2
SLOTS = 576
IMAGES = 5
MICRO = 2
GROUP = 4
ROWS_MB = 1
EXPERTS = 4
FFQ = 768
TOK_MB = 576
ROWS = 32
TOKENS = 18432
CAP = 304
N_DP = 16


def draw_image_ids(key, part):
    key = jax.random.fold_in(key, 7)
    pad_key, cut_key = jax.random.split(key)
    padding = jax.random.randint(pad_key, (ROWS,), 0, SLOTS // 4 + 1)
    padding = padding.at[0].set(0).at[1].set(SLOTS // 4)
    live_count = SLOTS - padding
    steps_up = jnp.arange(1, IMAGES, dtype=jnp.int32)
    jitter_top = jnp.maximum(live_count // (2 * IMAGES), 1)
    jitter = jax.random.randint(cut_key, (ROWS, IMAGES - 1), 0, jitter_top[:, None])
    boundaries = steps_up[None, :] * live_count[:, None] // IMAGES + jitter
    position = jnp.arange(SLOTS, dtype=jnp.int32)
    numbers = jnp.sum((position[None, :, None] >= boundaries[:, None, :]).astype(jnp.int32), axis=-1)
    return jnp.where(position[None, :] < live_count[:, None], numbers, -1).astype(jnp.int32)


def level_of(rng, shape, cuts, smallest, top_value):
    gain, own = 1.0, jax.random.fold_in(rng, 6)
    for dim, blocks in cuts:
        draws = jnp.exp(jax.random.uniform(jax.random.fold_in(own, dim), (blocks,), jnp.float32, smallest / len(cuts), top_value / len(cuts)))
        gain = gain * jnp.repeat(draws, shape[dim] // blocks).reshape([-1 if axis == dim else 1 for axis in range(len(shape))])
    return gain


def assign_block(own_key, own, number, rows, count, top, reach, skew):
    order = jax.random.permutation(own_key, count)
    heavy_load, usual = load_shares(count, rows * top, reach, skew, True), load_shares(count, rows * top, reach, skew, False)
    places = jnp.arange(count)

    def named(sizes, turn):
        used = int((sizes > 0).sum())
        fixed = max(1, used // 4)
        moved = fixed + (places - fixed + turn * (used - fixed)) % max(1, count - fixed)
        return jnp.zeros((count,), jnp.int32).at[order[jnp.where(places < fixed, places, moved)]].set(jnp.asarray(sizes, jnp.int32))

    sizes = jnp.where(number % 4 == 0, named(heavy_load, number // 4), named(usual, number - number // 4 - 1))
    mixed = jax.random.permutation(jax.random.fold_in(own, 3), count)
    giver, receiver = mixed[0:count // 2 * 2:2], mixed[1:count // 2 * 2:2]
    margin = jnp.minimum(sizes[giver] - 1, reach - sizes[receiver]) // 2
    margin = jnp.where((giver == order[0]) | (receiver == order[0]) | (sizes[receiver] == 0), 0, jnp.maximum(margin, 0))
    moved = jax.random.randint(jax.random.fold_in(own, 4), (count // 2,), 0, 1 << 20) % (margin + 1)
    sizes = sizes.at[giver].add(-moved).at[receiver].add(moved)
    labels = jnp.searchsorted(jnp.cumsum(sizes), jnp.arange(rows * top), side="right").astype(jnp.int32)
    grid = labels.reshape(top, rows).T
    grid = grid[jax.random.permutation(jax.random.fold_in(own, 1), rows)]
    turn = jax.random.randint(jax.random.fold_in(own, 2), (rows, 1), 0, top)
    return jnp.take_along_axis(grid, (jnp.arange(top)[None, :] + turn) % top, axis=1)


def load_shares(count, total, bound, slope, full):
    portions = [(1 << 20) // math.isqrt(standing ** slope) + 1 for standing in range(1, count + 1)]
    largest = bound if full else min(bound, max(-(-total // count), total * portions[0] // sum(portions)))
    least = 1 if total - largest >= count - 1 else 0
    holding, surplus = [largest] + [least] * (count - 1), total - largest - least * (count - 1)
    while surplus > 0:
        movable = [i for i in range(1, count) if holding[i] < largest] or [i for i in range(1, count) if holding[i] < bound]
        whole, left = sum([portions[i] for i in movable]), surplus
        for i in movable:
            more = min(bound - holding[i], max(1, left * portions[i] // whole), surplus)
            holding[i] = holding[i] + more
            surplus = surplus - more
    return np.array(holding)


def noise(rng, extent, width, bound, shards=(), kind=jnp.bfloat16):
    array = width * jax.random.normal(rng, extent, jnp.float32)
    if shards:
        array = array * level_of(rng, extent, shards, -0.22, 0.18)
    return jnp.clip(array, -bound, bound).astype(kind)


def setup_inputs(seed: int = 0) -> dict:
    seeds = jax.random.split(jax.random.key(seed), 18)
    tokens = noise(seeds[0], (TOKENS, D), 1.0, 6.0, ((0, 16), (1, 2)))
    image_ids = draw_image_ids(jax.random.fold_in(seeds[17], 71), 0)
    routes_keys = jax.random.split(jax.random.fold_in(seeds[2], 1), TOKENS // TOK_MB)
    routes_turns = jax.random.permutation(jax.random.fold_in(seeds[2], 3), TOKENS // TOK_MB)
    routes = jax.vmap(lambda own, number: assign_block(jax.random.fold_in(seeds[2], 2), own, number, TOK_MB, EXPERTS, TOP, CAP, 2))(routes_keys, routes_turns).reshape((TOKENS, TOP))
    norm1_gain = jnp.clip(1.0 + 0.1 * jax.random.normal(seeds[3], (D,), jnp.float32), 0.5, 1.5).astype(jnp.bfloat16)
    norm1_bias = noise(seeds[4], (D,), 0.2, 3.0, ((0, 2),))
    qkv_weight = noise(seeds[5], (D, 3 * D), D ** -0.5, 0.21875, ((0, 2),))
    attn_out_weight = noise(seeds[6], (D, D), (D // 8) ** -0.5, 0.625, ((0, 2),))
    norm2_gain = jnp.clip(1.0 + 0.1 * jax.random.normal(seeds[7], (D,), jnp.float32), 0.5, 1.5).astype(jnp.bfloat16)
    norm2_bias = noise(seeds[8], (D,), 0.2, 3.0, ((0, 2),))
    fc1_weight = noise(seeds[9], (D, FF), D ** -0.5, 0.21875, ((0, 2),))
    fc2_weight = noise(seeds[10], (FF, D), FF ** -0.5, 0.109375, ((0, 2),))
    norm3_gain = jnp.clip(1.0 + 0.1 * jax.random.normal(seeds[11], (D,), jnp.float32), 0.5, 1.5).astype(jnp.bfloat16)
    norm3_bias = noise(seeds[12], (D,), 0.2, 3.0, ((0, 2),))
    router_weight = noise(seeds[13], (D, EXPERTS), (2 * D) ** -0.5, 0.15625, ((0, 2),))
    expert_up = noise(seeds[14], (D, EXPERTS * FF), D ** -0.5, 0.21875, ((0, 2), (1, 16)))
    expert_down = noise(seeds[15], (D, EXPERTS * FF), FF ** -0.5, 0.109375, ((0, 2), (1, 16)))
    cotangent = noise(seeds[16], (TOKENS, D), 1.0, 6.0, ((0, 16), (1, 2)))
    return dict(tokens=tokens, image_ids=image_ids, routes=routes, norm1_gain=norm1_gain, norm1_bias=norm1_bias, qkv_weight=qkv_weight, attn_out_weight=attn_out_weight, norm2_gain=norm2_gain, norm2_bias=norm2_bias, fc1_weight=fc1_weight, fc2_weight=fc2_weight, norm3_gain=norm3_gain, norm3_bias=norm3_bias, router_weight=router_weight, expert_up=expert_up, expert_down=expert_down, cotangent=cotangent)


@jax.custom_vjp
def low(v):
    return lax.optimization_barrier(v.astype(jnp.bfloat16)).astype(jnp.float32)

@jax.custom_vjp
def low_back(v):
    return v

def low_keep(v):
    return (low(v), None)

def low_pass(kept, grad):
    return (grad,)

def back_keep(v):
    return (v, None)

def back_low(kept, grad):
    return (low(grad),)
low.defvjp(low_keep, low_pass)
low_back.defvjp(back_keep, back_low)
EPSILON = 1e-06
MASKED = -1e+30
HIGH = lax.Precision.HIGHEST

def layer_norm(values, gain_row, bias_row):
    center = values - lax.optimization_barrier(jnp.mean(values, axis=-1, keepdims=True))
    variance = lax.optimization_barrier(jnp.mean(center * center, axis=-1, keepdims=True))
    return center * lax.rsqrt(variance + EPSILON) * gain_row + bias_row

def matmul(left_side, right_side):
    return jnp.dot(left_side, right_side, precision=HIGH)

def attend_row(operands):
    packed, row_ids = operands
    queries = packed[:, :D].reshape(SLOTS, HEADS, HEAD)
    key_rows = packed[:, D:2 * D].reshape(SLOTS, HEADS, HEAD)
    values = packed[:, 2 * D:].reshape(SLOTS, HEADS, HEAD)
    scores = low_back(jnp.einsum('qhd,khd->hqk', queries, key_rows, precision=HIGH) * HEAD ** (-0.5))
    same_image = row_ids[:, None] == row_ids[None, :]
    scores = jnp.where(same_image[None], scores, MASKED)
    attn_probs = low(jax.nn.softmax(scores, axis=-1))
    context = jnp.einsum('hqk,khd->qhd', attn_probs, values, precision=HIGH)
    return low_back(low(context.reshape(SLOTS, D)))

def place_routes(route_rows, live_mask):
    flat_routes = jnp.transpose(route_rows).reshape(-1)
    live_pairs = jnp.concatenate([live_mask, live_mask])
    expert_ids = jnp.arange(EXPERTS, dtype=jnp.int32)
    matches = (flat_routes[:, None] == expert_ids[None, :]) & live_pairs[:, None]
    counts = jnp.cumsum(matches.astype(jnp.int32), axis=0) - 1
    within = lax.optimization_barrier(jnp.sum(jnp.where(matches, counts, 0), axis=1)).astype(jnp.int32)
    places = jnp.where(live_pairs, flat_routes * CAP + within, EXPERTS * CAP).astype(jnp.int32)
    sources = jnp.full((EXPERTS * CAP,), TOP * TOK_MB, jnp.int32)
    sources = sources.at[places].set(jnp.arange(TOP * TOK_MB, dtype=jnp.int32), mode='drop')
    return (places, sources)

def block_forward(block_tokens, row_ids, route_rows, params):
    norm1_gain, norm1_bias, qkv_weight, attn_out_weight, norm2_gain, norm2_bias, fc1_weight, fc2_weight, norm3_gain, norm3_bias, router_weight, expert_up, expert_down = params
    normed1 = low(layer_norm(block_tokens, norm1_gain, norm1_bias))
    packed = low_back(low(matmul(normed1, qkv_weight)))
    context = lax.map(jax.checkpoint(attend_row), (packed.reshape(ROWS_MB, SLOTS, 3 * D), row_ids))
    context = context.reshape(TOK_MB, D)
    hidden = block_tokens + low_back(matmul(context, attn_out_weight))
    normed2 = low(layer_norm(hidden, norm2_gain, norm2_bias))
    preact = low_back(matmul(normed2, fc1_weight))
    activated = low(jax.nn.gelu(preact, approximate=False))
    dense_out = hidden + low_back(matmul(activated, fc2_weight))
    normed3 = low(layer_norm(dense_out, norm3_gain, norm3_bias))
    logits = low_back(matmul(normed3, router_weight))
    live_mask = row_ids.reshape(-1) >= 0
    expert_ids = jnp.arange(EXPERTS, dtype=jnp.int32)
    picked = (route_rows[:, :, None] == expert_ids[None, None, :]).astype(jnp.float32)
    chosen = lax.optimization_barrier(jnp.sum(logits[:, None, :] * picked, axis=-1))
    gate_values = jax.nn.softmax(chosen, axis=-1) * live_mask[:, None].astype(jnp.float32)
    places, sources = place_routes(route_rows, live_mask)
    pair_rows = jnp.concatenate([normed3, normed3, jnp.zeros((1, D), jnp.float32)])
    buffer = pair_rows[sources].reshape(EXPERTS, CAP, D)
    up_parts = expert_up.reshape(D, EXPERTS, GROUP, FFQ)
    down_parts = expert_down.reshape(D, EXPERTS, GROUP, FFQ)
    expert_sum = jnp.zeros((EXPERTS, CAP, D), jnp.float32)
    for quarter in range(GROUP):
        rows_in = low_back(buffer)
        inner_part = low_back(jnp.einsum('ecd,def->ecf', rows_in, up_parts[:, :, quarter], precision=HIGH))
        act_part = low(jax.nn.gelu(inner_part, approximate=False))
        part_out = jnp.einsum('ecf,def->ecd', act_part, down_parts[:, :, quarter], precision=HIGH)
        expert_sum = expert_sum + low_back(low(part_out))
    padded = jnp.concatenate([expert_sum.reshape(EXPERTS * CAP, D), jnp.zeros((1, D), jnp.float32)])
    gathered = padded[places].reshape(TOP, TOK_MB, D)
    branch_out = lax.optimization_barrier(jnp.sum(jnp.transpose(gate_values)[:, :, None] * gathered, axis=0))
    return dense_out + branch_out

def reference(tokens, image_ids, routes, norm1_gain, norm1_bias, qkv_weight, attn_out_weight, norm2_gain, norm2_bias, fc1_weight, fc2_weight, norm3_gain, norm3_bias, router_weight, expert_up, expert_down, cotangent):
    blocks = N_DP * MICRO
    params = (norm1_gain.astype(jnp.float32), norm1_bias.astype(jnp.float32), qkv_weight.astype(jnp.float32), attn_out_weight.astype(jnp.float32), norm2_gain.astype(jnp.float32), norm2_bias.astype(jnp.float32), fc1_weight.astype(jnp.float32), fc2_weight.astype(jnp.float32), norm3_gain.astype(jnp.float32), norm3_bias.astype(jnp.float32), router_weight.astype(jnp.float32), expert_up.astype(jnp.float32), expert_down.astype(jnp.float32))
    inputs = tokens.astype(jnp.float32).reshape(blocks, TOK_MB, D)
    id_blocks = image_ids.reshape(blocks, ROWS_MB, SLOTS)
    route_blocks = routes.reshape(blocks, TOK_MB, TOP)

    def forward(block_inputs, weights):

        def run_block(operands):
            return block_forward(operands[0], operands[1], operands[2], weights)
        return lax.map(jax.checkpoint(run_block), (block_inputs, id_blocks, route_blocks))
    outputs, pullback = jax.vjp(forward, inputs, params)
    input_grad, grads = pullback(cotangent.astype(jnp.float32).reshape(blocks, TOK_MB, D))
    return (outputs.reshape(TOKENS, D).astype(jnp.bfloat16), input_grad.reshape(TOKENS, D), grads[0], grads[1], grads[2], grads[3], grads[4], grads[5], grads[6], grads[7], grads[8], grads[9], grads[10], grads[11], grads[12])
```

```python
import jax
import jax.numpy as jnp
from jax import lax
from jax.sharding import PartitionSpec as P

HEAD = 64
TOP = 2
GROUP = 4
SLOTS = 576

EPSILON = 1e-06
MASKED = -1e30
BF = jnp.bfloat16
F32 = jnp.float32


def product(left_side, right_side):
    return jnp.dot(left_side, right_side, preferred_element_type=F32)


def inner_rows(left_side, right_side):
    return lax.dot_general(
        left_side, right_side, (((0,), (0,)), ((), ())), preferred_element_type=F32
    )


def times_transposed(left_side, right_side):
    return lax.dot_general(
        left_side, right_side, (((1,), (1,)), ((), ())), preferred_element_type=F32
    )


def normalize(values):
    center = values - jnp.mean(values, axis=-1, keepdims=True)
    variance = jnp.mean(center * center, axis=-1, keepdims=True)
    scale = lax.rsqrt(variance + EPSILON)
    return center * scale, scale


def norm_back(values, gain, upstream):
    n, scale = normalize(values)
    ug = upstream * gain
    dv = scale * (
        ug - jnp.mean(ug, axis=-1, keepdims=True) - n * jnp.mean(ug * n, axis=-1, keepdims=True)
    )
    return dv, jnp.sum(upstream * n, axis=0), jnp.sum(upstream, axis=0)


def normal_cdf(values):
    return 0.5 * (1.0 + lax.erf(values * (0.5**0.5)))


def gelu_slope(values):
    density = jnp.exp(-0.5 * values * values) * 0.3989422804014327
    return normal_cdf(values) + values * density


def split_heads(packed):
    feature_count = packed.shape[1] // 3
    head_count = feature_count // HEAD
    return tuple(
        packed[:, i * feature_count : (i + 1) * feature_count].reshape(-1, head_count, HEAD)
        for i in range(3)
    )


def row_scores(queries, key_rows, row_ids):
    scores = jnp.einsum("qhd,khd->hqk", queries, key_rows, preferred_element_type=F32)
    same_image = row_ids[:, None] == row_ids[None, :]
    return jnp.where(same_image[None], scores * HEAD ** (-0.5), MASKED)


def attend_forward(packed, row_ids):
    queries, key_rows, values = split_heads(packed)
    scores = row_scores(queries, key_rows, row_ids)
    top_score = jnp.max(scores, axis=-1, keepdims=True)
    exp_scores = jnp.exp(scores - top_score)
    totals = jnp.sum(exp_scores, axis=-1, keepdims=True)
    attn_probs = (exp_scores / totals).astype(BF)
    context = jnp.einsum("hqk,khd->qhd", attn_probs, values, preferred_element_type=F32)
    return context.reshape(packed.shape[0], -1).astype(BF), top_score + jnp.log(totals)


def attend_backward(packed, row_ids, log_total, grad_context):
    queries, key_rows, values = split_heads(packed)
    scores = row_scores(queries, key_rows, row_ids)
    attn_probs = jnp.exp(scores - log_total)
    rounded = attn_probs.astype(BF)
    grad_heads = grad_context.reshape(values.shape)
    grad_probs = jnp.einsum("qhd,khd->hqk", grad_heads, values, preferred_element_type=F32)
    grad_values = jnp.einsum("hqk,qhd->khd", rounded, grad_heads, preferred_element_type=F32)
    inner_sum = jnp.sum(attn_probs * grad_probs, axis=-1, keepdims=True)
    grad_scores = (attn_probs * (grad_probs - inner_sum)).astype(BF)
    grad_queries = jnp.einsum("hqk,khd->qhd", grad_scores, key_rows, preferred_element_type=F32)
    grad_keys = jnp.einsum("hqk,qhd->khd", grad_scores, queries, preferred_element_type=F32)
    rows = packed.shape[0]
    return jnp.concatenate(
        [
            (grad_queries * HEAD ** (-0.5)).reshape(rows, -1),
            (grad_keys * HEAD ** (-0.5)).reshape(rows, -1),
            grad_values.reshape(rows, -1),
        ],
        axis=1,
    ).astype(BF)


def dense_front(x, row_ids, gain1, bias1, qkv, attn):
    n1, _ = normalize(x)
    normed1 = (n1 * gain1 + bias1).astype(BF)
    packed = product(normed1, qkv).astype(BF)
    context, log_total = attend_forward(packed, row_ids)
    hidden = x + product(context, attn)
    return normed1, packed, context, log_total, hidden


def dense_mlp(hidden, gain2, bias2, fc1, fc2):
    n2, _ = normalize(hidden)
    normed2 = (n2 * gain2 + bias2).astype(BF)
    preact = product(normed2, fc1)
    activated = (preact * normal_cdf(preact)).astype(BF)
    return normed2, preact, activated, hidden + product(activated, fc2)


def places_of(routes, live, experts, capacity):
    tokens = routes.shape[0]
    ids = jnp.arange(experts, dtype=jnp.int32)
    match = [
        ((routes[:, k : k + 1] == ids[None, :]) & live[:, None]).astype(F32) for k in range(TOP)
    ]
    order = jnp.arange(tokens, dtype=jnp.int32)
    below = (order[:, None] > order[None, :]).astype(BF)
    before = jnp.zeros((1, experts), F32)
    out = []
    for k in range(TOP):
        counts = product(below, match[k].astype(BF)) + before
        before = before + jnp.sum(match[k], axis=0, keepdims=True)
        within = jnp.sum(counts * match[k], axis=1).astype(jnp.int32)
        out.append(jnp.where(live, routes[:, k] * capacity + within, experts * capacity))
    return out


def local(
    tokens,
    image_ids,
    routes,
    norm1_gain,
    norm1_bias,
    qkv_weight,
    attn_out_weight,
    norm2_gain,
    norm2_bias,
    fc1_weight,
    fc2_weight,
    norm3_gain,
    norm3_bias,
    router_weight,
    expert_up,
    expert_down,
    cotangent,
):
    s = lax.axis_index("section")
    d = lax.axis_index("dp")
    dp_count = lax.axis_size("dp")
    experts = dp_count // GROUP
    e, q = d // GROUP, d % GROUP
    capacity = GROUP * ((21 * SLOTS + 10 * experts * GROUP - 1) // (10 * experts * GROUP))
    half = tokens.shape[1]
    D = 2 * half

    def swap(v):
        return lax.ppermute(v, "section", [(0, 1), (1, 0)])

    def join(own, other, axis):
        return jnp.where(
            s == 0,
            jnp.concatenate([own, other], axis=axis),
            jnp.concatenate([other, own], axis=axis),
        )

    def part(v, index, size, axis=0):
        return lax.dynamic_slice_in_dim(v, index * size, size, axis)

    def gathered(v, axis=0):
        return join(v, swap(v), axis)

    def over_q(v, bit):
        return lax.ppermute(v, "dp", [(i, i ^ bit) for i in range(dp_count)])

    def over_e(v, r):
        return lax.ppermute(
            v,
            "dp",
            [(i, ((i // GROUP + r) % experts) * GROUP + i % GROUP) for i in range(dp_count)],
        )

    x = join(part(tokens, s, SLOTS), swap(part(tokens, 1 - s, SLOTS)), 1).astype(F32)
    dy_low = join(part(cotangent, s, SLOTS), swap(part(cotangent, 1 - s, SLOTS)), 1)
    dy = dy_low.astype(F32)
    row_ids = part(image_ids, s, 1).reshape(-1)
    route = part(routes, s, SLOTS)
    live = row_ids >= 0
    live_f = live.astype(F32)

    small = jnp.stack(
        [norm1_gain, norm1_bias, norm2_gain, norm2_bias, norm3_gain, norm3_bias]
        + [router_weight[:, i] for i in range(experts)]
    )
    small = gathered(small, 1)
    gain1, bias1, gain2, bias2, gain3, bias3 = [small[i].astype(F32) for i in range(6)]
    router_t = small[6:]
    qkv, attn = gathered(qkv_weight), gathered(attn_out_weight)
    fc1, fc2 = gathered(fc1_weight), gathered(fc2_weight)

    places = places_of(route, live, experts, capacity)
    spots = jnp.arange(experts * capacity, dtype=jnp.int32)
    hot = [(places[k][:, None] == spots[None, :]) for k in range(TOP)]
    hot_any = (hot[0] | hot[1]).astype(BF)

    planes = [[p * GROUP + i for p in range(experts)] for i in range(GROUP)]
    few = experts <= 8

    def exchange(buffer):
        if not few:
            return [
                lax.all_to_all(
                    buffer, "dp", 0, 0, axis_index_groups=planes, tiled=True
                )
            ]
        own = part(buffer, e, capacity)
        return [own] + [
            over_e(part(buffer, (e + r) % experts, capacity), r) for r in range(1, experts)
        ]

    def give_back(chunks):
        if not few:
            return exchange(jnp.concatenate(chunks))[0]
        got = [chunks[0]] + [over_e(chunks[r], experts - r) for r in range(1, experts)]
        out = jnp.zeros((experts * capacity,) + chunks[0].shape[1:], chunks[0].dtype)
        for r in range(experts):
            out = lax.dynamic_update_slice_in_dim(out, got[r], ((e + r) % experts) * capacity, 0)
        return out

    dy_rows = jnp.concatenate(exchange(inner_rows(hot_any, dy_low).astype(BF)))

    def quarters(v):
        got = [v] + [over_q(v, bit) for bit in (1, 2, 3)]
        out = jnp.zeros((GROUP,) + v.shape, v.dtype)
        for bit in range(GROUP):
            out = lax.dynamic_update_slice_in_dim(out, got[bit][None], q ^ bit, 0)
        return out

    up = gathered(quarters(expert_up), 1)
    down = gathered(quarters(expert_down), 1)
    up = jnp.transpose(up, (1, 0, 2)).reshape(D, -1)
    down = jnp.transpose(down, (1, 0, 2)).reshape(D, -1)

    normed1, packed, context, log_total, hidden = dense_front(x, row_ids, gain1, bias1, qkv, attn)
    normed2, preact, activated, dense_out = dense_mlp(hidden, gain2, bias2, fc1, fc2)

    n3, _ = normalize(dense_out)
    normed3 = (n3 * gain3 + bias3).astype(BF)
    logits = times_transposed(normed3, router_t)
    ids = jnp.arange(experts, dtype=jnp.int32)
    picked = [(route[:, k : k + 1] == ids[None, :]) for k in range(TOP)]
    chosen = jnp.stack([jnp.sum(jnp.where(p, logits, 0.0), axis=1) for p in picked], axis=1)
    soft = jax.nn.softmax(chosen, axis=-1)
    gates = soft * live_f[:, None]
    gate_at = sum(
        jnp.sum(jnp.where(hot[k], gates[:, k : k + 1], 0.0), axis=0) for k in range(TOP)
    )

    rows_in = jnp.concatenate(exchange(inner_rows(hot_any, normed3).astype(BF)))
    gate_rows = jnp.concatenate(exchange(gate_at))

    inner = product(rows_in, up)
    act = (inner * normal_cdf(inner)).astype(BF)
    expert_out = times_transposed(act, down)
    out_back = (gate_rows[:, None] * expert_out).astype(BF)
    dgate_back = jnp.sum(dy_rows.astype(F32) * expert_out, axis=1)
    grad_place = (gate_rows[:, None] * dy_rows.astype(F32)).astype(BF)
    dact = product(grad_place, down)
    dinner = (dact * gelu_slope(inner)).astype(BF)
    dpart = times_transposed(dinner, up).astype(BF)

    def chunked(v):
        return [v[r * capacity : (r + 1) * capacity] for r in range(experts)]

    dpart_home = give_back(chunked(dpart))
    dgate_home = give_back(chunked(dgate_back))
    out_home = give_back(chunked(out_back))

    grad_up = inner_rows(rows_in, dinner).astype(BF)
    grad_down = inner_rows(grad_place, act).astype(BF)

    branch = product(hot_any, out_home)
    block_out = (dense_out + branch).astype(BF)

    dgate = (
        jnp.stack(
            [jnp.sum(jnp.where(hot[k], dgate_home[None, :], 0.0), axis=1) for k in range(TOP)],
            axis=1,
        )
        * live_f[:, None]
    )
    dsoft = soft * (dgate - jnp.sum(soft * dgate, axis=1, keepdims=True))
    dlogits = sum(
        jnp.where(picked[k], dsoft[:, k : k + 1], 0.0) for k in range(TOP)
    ).astype(BF)
    grad_router = inner_rows(dlogits, normed3)
    dnormed3 = product(dlogits, router_t) + product(hot_any, dpart_home)
    dv3, grad_g3, grad_b3 = norm_back(dense_out, gain3, dnormed3)
    ddense = dy + dv3

    dmlp = ddense.astype(BF)
    grad_fc2 = inner_rows(activated, dmlp).astype(BF)
    dpre2 = (times_transposed(dmlp, fc2) * gelu_slope(preact)).astype(BF)
    grad_fc1 = inner_rows(normed2, dpre2).astype(BF)
    dv2, grad_g2, grad_b2 = norm_back(hidden, gain2, times_transposed(dpre2, fc1))
    dhidden = ddense + dv2

    dattn = dhidden.astype(BF)
    grad_attn = inner_rows(context, dattn).astype(BF)
    dcontext = times_transposed(dattn, attn).astype(BF)
    dpacked = attend_backward(packed, row_ids, log_total, dcontext)
    grad_qkv = inner_rows(normed1, dpacked).astype(BF)
    dv1, grad_g1, grad_b1 = norm_back(x, gain1, times_transposed(dpacked, qkv))
    input_grad = dhidden + dv1

    def rejoin(v):
        own, other = part(v, s, half, 1), swap(part(v, 1 - s, half, 1))
        return join(own, other, 0)

    def add(a, b):
        return (a.astype(F32) + b.astype(F32)).astype(BF)

    def fold_section(v, rows):
        return add(part(v, s, rows), swap(part(v, 1 - s, rows)))

    def by_quarter(v):
        v = jnp.transpose(v.reshape(D, GROUP, -1), (1, 0, 2))
        v = add(part(v, s, half, 1), swap(part(v, 1 - s, half, 1)))
        return v.reshape(2, 2, half, -1)

    def keep(v, bit, axis, low):
        mine = (q // bit) % 2
        got = over_q(part(v, 1 - mine, 1, axis), bit)
        total = part(v, mine, 1, axis).astype(F32) + got.astype(F32)
        return total.astype(BF) if low else total

    half_up = keep(keep(by_quarter(grad_up), 1, 1, True), 2, 0, False)[0, 0]
    half_down = keep(keep(by_quarter(grad_down), 2, 0, True), 1, 1, False)[0, 0]

    def fold_q(v, bit):
        mine, rows = (q // bit) % 2, v.shape[0] // 2
        return add(part(v, mine, rows), over_q(part(v, 1 - mine, rows), bit))

    def spread_q(v, bit):
        mine, other = (q // bit) % 2, over_q(v, bit)
        return jnp.where(
            mine == 0, jnp.concatenate([v, other]), jnp.concatenate([other, v])
        )

    def sum_e(v):
        if not few:
            return lax.psum(v, "dp", axis_index_groups=planes)
        rows = v.shape[0] // experts
        total = part(v, e, rows).astype(F32)
        for r in range(1, experts):
            total = total + over_e(part(v, (e + r) % experts, rows), r).astype(F32)
        total = total.astype(BF)
        out = jnp.zeros_like(v)
        for r in range(experts):
            got = total if r == 0 else over_e(total, r)
            out = lax.dynamic_update_slice_in_dim(out, got, ((e - r) % experts) * rows, 0)
        return out

    def sum_dp(v):
        rows = v.shape[0] // 2
        a, b = v[:rows], v[rows:]
        a, b = fold_q(a, 1), fold_q(b, 2)
        a, b = fold_q(a, 2), fold_q(b, 1)
        a, b = sum_e(a), sum_e(b)
        a, b = spread_q(a, 2), spread_q(b, 1)
        a, b = spread_q(a, 1), spread_q(b, 2)
        return jnp.concatenate([a, b]).astype(F32)

    def pack(v):
        return jnp.transpose(v.reshape(half, -1, D), (1, 0, 2)).reshape(-1, D)

    def unpack(v):
        return jnp.transpose(v.reshape(-1, half, D), (1, 0, 2)).reshape(half, -1)

    sum_fc2 = sum_dp(fold_section(grad_fc2, fc2_weight.shape[0]))
    sum_fc1 = unpack(sum_dp(pack(fold_section(grad_fc1, half))))
    sum_attn = sum_dp(fold_section(grad_attn, half))
    sum_qkv = unpack(sum_dp(pack(fold_section(grad_qkv, half))))

    tiny = jnp.concatenate(
        [jnp.stack([grad_g1, grad_b1, grad_g2, grad_b2, grad_g3, grad_b3]), grad_router]
    )
    tiny = part(tiny, s, half, 1) + swap(part(tiny, 1 - s, half, 1))
    tiny = tiny + over_q(tiny, 1)
    tiny = tiny + over_q(tiny, 2)
    total = tiny
    if few:
        for r in range(1, experts):
            total = total + over_e(tiny, r)
    else:
        total = lax.psum(tiny, "dp", axis_index_groups=planes)
    return (
        rejoin(block_out),
        rejoin(input_grad),
        total[0],
        total[1],
        sum_qkv,
        sum_attn,
        total[2],
        total[3],
        sum_fc1,
        sum_fc2,
        total[4],
        total[5],
        jnp.transpose(total[6:]),
        half_up,
        half_down,
    )


def solution(mesh):
    placed = (
        P("dp", "section"),
        P("dp", None),
        P("dp", None),
        P("section"),
        P("section"),
        P("section", None),
        P("section", None),
        P("section"),
        P("section"),
        P("section", None),
        P("section", None),
        P("section"),
        P("section"),
        P("section", None),
        P("section", "dp"),
        P("section", "dp"),
        P("dp", "section"),
    )
    return jax.shard_map(
        local,
        mesh=mesh,
        in_specs=placed,
        out_specs=(
            P("dp", "section"),
            P("dp", "section"),
            P("section"),
            P("section"),
            P("section", None),
            P("section", None),
            P("section"),
            P("section"),
            P("section", None),
            P("section", None),
            P("section"),
            P("section"),
            P("section", None),
            P("section", "dp"),
            P("section", "dp"),
        ),
        check_vma=False,
    )
```

```python
import functools

import jax
import jax.numpy as jnp
from jax import lax
from jax.experimental import pallas as pl
from jax.experimental.pallas import tpu as pltpu
from jax.sharding import PartitionSpec as P

HEAD = 64
TOP = 2
GROUP = 4
SLOTS = 576
WIDE = 128

EPSILON = 1e-06
MASKED = -1e30
BF = jnp.bfloat16
F32 = jnp.float32
LIMIT = 60 * 1024 * 1024


def dot(a, b):
    return jnp.dot(a, b, preferred_element_type=F32)


def dot_nt(a, b):
    return lax.dot_general(a, b, (((1,), (1,)), ((), ())), preferred_element_type=F32)


def dot_tn(a, b):
    return lax.dot_general(a, b, (((0,), (0,)), ((), ())), preferred_element_type=F32)


def normalize(v):
    center = v - jnp.mean(v, axis=-1, keepdims=True)
    scale = lax.rsqrt(jnp.mean(center * center, axis=-1, keepdims=True) + EPSILON)
    return center * scale, scale


def gelu_pair(x):
    bell = jnp.exp(x * x * -0.5)
    t = 1.0 / (1.0 + jnp.abs(x) * (0.3275911 * 0.5**0.5))
    tail = (
        t
        * (
            0.127414796
            + t * (-0.142248368 + t * (0.7107068705 + t * (-0.7265760135 + t * 0.5307027145)))
        )
        * bell
    )
    cdf = jnp.where(x >= 0.0, 1.0 - tail, tail)
    return x * cdf, cdf + x * (bell * 0.3989422804014327)


def iota(shape, axis):
    return lax.broadcasted_iota(jnp.int32, shape, axis)


def halves_into(s, own, other, dest, sems, first):
    rows = own.shape[0]
    return [
        pltpu.make_async_copy(own, dest.at[pl.ds(pl.multiple_of(s * rows, rows), rows)], sems.at[first]),
        pltpu.make_async_copy(
            other, dest.at[pl.ds(pl.multiple_of((1 - s) * rows, rows), rows)], sems.at[first + 1]
        ),
    ]


def split3(v):
    hi = v.astype(BF)
    rest = v - hi.astype(F32)
    mid = rest.astype(BF)
    low = (rest - mid.astype(F32)).astype(BF)
    return hi, mid, low


VM = pl.BlockSpec(memory_space=pltpu.VMEM)
SM = pl.BlockSpec(memory_space=pltpu.SMEM)
HB = pl.BlockSpec(memory_space=pl.ANY)


def call(kernel, in_specs, out_shape, scratch, flops, moved, name):
    return pl.pallas_call(
        kernel,
        in_specs=in_specs,
        out_specs=jax.tree.map(lambda _: VM, out_shape),
        out_shape=out_shape,
        scratch_shapes=scratch,
        compiler_params=pltpu.CompilerParams(vmem_limit_bytes=LIMIT),
        cost_estimate=pl.CostEstimate(flops=flops, bytes_accessed=moved, transcendentals=0),
        name=name,
    )


def shape(dims, kind):
    return jax.ShapeDtypeStruct(dims, kind)


def front_kernel(
    s_ref, x_ref, id_row, id_col, gb_ref, qkv_a, qkv_b, wo_a, wo_b,
    normed, packed, context, lse, hidden,
    wq, wo, bias, lse_col, sems,
):
    s = s_ref[0]
    rows, width = x_ref.shape
    copies = halves_into(s, qkv_a, qkv_b, wq, sems, 0) + halves_into(s, wo_a, wo_b, wo, sems, 2)
    for c in copies:
        c.start()
    tile = rows // 6

    @pl.loop(0, 6)
    def _(i):
        at = pl.ds(pl.multiple_of(i * tile, 16), tile)
        n, _ = normalize(x_ref[at, :].astype(F32))
        normed[at, :] = (n * gb_ref[0:1, :] + gb_ref[1:2, :]).astype(BF)
        bias[at, :] = jnp.where(id_col[at, :] == id_row[...], 0.0, MASKED)

    copies[0].wait()
    copies[1].wait()

    @pl.loop(0, wq.shape[1] // 256)
    def _(j):
        at = pl.ds(pl.multiple_of(j * 256, 256), 256)
        packed[:, at] = dot(normed[...], wq[:, at]).astype(BF)

    lane = iota((1, WIDE), 1)
    lse_col[...] = jnp.zeros_like(lse_col)
    third = rows // 3

    @pl.loop(0, width // WIDE)
    def _(pair):
        col = pl.multiple_of(pair * WIDE, WIDE)
        keys = packed[:, pl.ds(width + col, WIDE)]
        values = packed[:, pl.ds(2 * width + col, WIDE)]
        for r in range(3):
            at = slice(r * third, (r + 1) * third)
            q = packed[at, pl.ds(col, WIDE)] * jnp.asarray(HEAD**-0.5, BF)
            outs = []
            sums = lse_col[at, :]
            for h in range(2):
                mine = (lane >= h * HEAD) & (lane < (h + 1) * HEAD)
                scores = dot_nt(jnp.where(mine, q, jnp.zeros_like(q)), keys) + bias[at, :]
                top = jnp.max(scores, axis=1, keepdims=True)
                p = jnp.exp(scores - top)
                total = jnp.sum(p, axis=1, keepdims=True)
                outs.append(dot(p.astype(BF), values) * (1.0 / total))
                sums = jnp.where(lane == 2 * pair + h, top + jnp.log(total), sums)
            lse_col[at, :] = sums
            context[at, pl.ds(col, WIDE)] = jnp.where(lane < HEAD, outs[0], outs[1]).astype(BF)

    lse[...] = jnp.transpose(lse_col[...])[0 : lse.shape[0], :]
    copies[2].wait()
    copies[3].wait()

    @pl.loop(0, width // 256)
    def _(j):
        at = pl.ds(pl.multiple_of(j * 256, 256), 256)
        hidden[:, at] = x_ref[:, at].astype(F32) + dot(context[...], wo[:, at])


def front(s, x, ids, gb, qkv, wo):
    rows, width = x.shape
    n3 = qkv[0].shape[1]
    return call(
        front_kernel,
        [SM, VM, VM, VM, VM, HB, HB, HB, HB],
        [
            shape((rows, width), BF),
            shape((rows, n3), BF),
            shape((rows, width), BF),
            shape((16, rows), F32),
            shape((rows, width), F32),
        ],
        [
            pltpu.VMEM((width, n3), BF),
            pltpu.VMEM((width, width), BF),
            pltpu.VMEM((rows, rows), F32),
            pltpu.VMEM((rows, WIDE), F32),
            pltpu.SemaphoreType.DMA((4,)),
        ],
        2 * rows * width * (n3 + width) + 4 * rows * rows * width,
        2 * (width * (n3 + width) + rows * (3 * width + n3)) + 4 * rows * width,
        "attention_forward",
    )(s, x, ids[None, :], ids[:, None], gb, *qkv, *wo)


def mlp_kernel(experts, cap, s_ref, hid, gb_ref, router, place, route, live, fc1_a, fc1_b, fc2_a, fc2_b, *refs):
    normed2, act, slope, dense, normed3, soft = refs[:6]
    chunks = refs[6 : 6 + experts]
    w1, w2, sems = refs[6 + experts :]
    s = s_ref[0]
    rows, width = hid.shape
    copies = halves_into(s, fc1_a, fc1_b, w1, sems, 0) + halves_into(s, fc2_a, fc2_b, w2, sems, 2)
    for c in copies:
        c.start()
    tile = rows // 6

    @pl.loop(0, 6)
    def _(i):
        at = pl.ds(pl.multiple_of(i * tile, 16), tile)
        n, _ = normalize(hid[at, :])
        normed2[at, :] = (n * gb_ref[2:3, :] + gb_ref[3:4, :]).astype(BF)
        dense[at, :] = hid[at, :]

    for c in copies:
        c.wait()

    @pl.loop(0, w1.shape[1] // 512)
    def _(j):
        at = pl.ds(pl.multiple_of(j * 512, 512), 512)
        a, sl = gelu_pair(dot(normed2[...], w1[:, at]))
        act[:, at] = a.astype(BF)
        slope[:, at] = sl.astype(BF)
        dense[...] += dot(act[:, at], w2[at, :])

    @pl.loop(0, 6)
    def _(i):
        at = pl.ds(pl.multiple_of(i * tile, 16), tile)
        n, _ = normalize(dense[at, :])
        normed3[at, :] = (n * gb_ref[4:5, :] + gb_ref[5:6, :]).astype(BF)

    logits = dot_nt(router[...], normed3[...])
    expert = iota(logits.shape, 0)
    chosen = [
        jnp.sum(jnp.where(expert == route[k : k + 1, :], logits, 0.0), axis=0, keepdims=True)
        for k in range(TOP)
    ]
    top = jnp.maximum(chosen[0], chosen[1])
    raised = [jnp.exp(c - top) for c in chosen]
    total = raised[0] + raised[1]
    pieces = []
    for k in range(TOP):
        share = raised[k] / total
        soft[k : k + 1, :] = share
        three = split3(share * live[...])
        row = iota((16, rows), 0)
        pieces.append(
            jnp.where(row == 0, three[0].astype(F32), 0.0)
            + jnp.where(row == 1, three[1].astype(F32), 0.0)
            + jnp.where(row == 2, three[2].astype(F32), 0.0)
        )
    pieces = [p.astype(BF) for p in pieces]
    lanes = -(-cap // WIDE) * WIDE
    spot = iota((lanes, rows), 0)
    spot = jnp.where(spot < cap, spot, -2 * experts * cap)
    for r in range(experts):
        hot = [jnp.where(spot + r * cap == place[k : k + 1, :], 1.0, 0.0).astype(BF) for k in range(TOP)]
        both = (hot[0] + hot[1])[0:cap, :]
        chunks[r][0:cap, :] = dot(both, normed3[...]).astype(BF)
        chunks[r][cap : cap + 16, :] = jnp.zeros((16, width), BF)
        chunks[r][cap : cap + 16, 0:lanes] = (
            dot_nt(pieces[0], hot[0]) + dot_nt(pieces[1], hot[1])
        ).astype(BF)


def mlp(s, hid, gb, router, place, route, live, fc1, fc2, experts, cap):
    rows, width = hid.shape
    ff = fc1[0].shape[1]
    return call(
        functools.partial(mlp_kernel, experts, cap),
        [SM, VM, VM, VM, VM, VM, VM, HB, HB, HB, HB],
        [
            shape((rows, width), BF),
            shape((rows, ff), BF),
            shape((rows, ff), BF),
            shape((rows, width), F32),
            shape((rows, width), BF),
            shape((8, rows), F32),
        ]
        + [shape((cap + 16, width), BF)] * experts,
        [
            pltpu.VMEM((width, ff), BF),
            pltpu.VMEM((ff, width), BF),
            pltpu.SemaphoreType.DMA((4,)),
        ],
        4 * rows * width * ff + 2 * rows * width * experts * cap,
        4 * width * ff + rows * (4 * ff + 12 * width),
        "dense_forward",
    )(s, hid, gb, router, place, route, live, *fc1, *fc2)


def expert_kernel(cap, n, s_ref, *refs):
    rows_in, dys = refs[:n], refs[n : 2 * n]
    own, other = refs[2 * n : 2 * n + 6], refs[2 * n + 6 : 2 * n + 12]
    outs = refs[2 * n + 12 : -3]
    wu, wd, sems = refs[-3:]
    s = s_ref[0]
    width = wu.shape[1]
    half = width // 2
    copies = [[] for _ in range(GROUP)]
    k = 0
    for part, src in ((s, own), (1 - s, other)):
        at = pl.ds(pl.multiple_of(part * half, half), half)
        ud, xs, ys, dg_up, dg_down = src[0:2], src[2], src[3], src[4], src[5]
        lists = [(ud[0], ud[1]), (xs.at[0], xs.at[1]), (ys.at[0], ys.at[1]), (dg_up, dg_down)]
        for b in range(GROUP):
            for w, one in zip((wu, wd), lists[b]):
                copies[b].append(pltpu.make_async_copy(one, w.at[b, at], sems.at[k]))
                k += 1
    for b in range(GROUP):
        for c in copies[b]:
            c.start()
    lanes = -(-cap // WIDE) * WIDE
    eye = iota((lanes, lanes), 0) == iota((lanes, lanes), 1)
    gates = []
    for i in range(n):
        back, out, act, dinner, gp = outs[5 * i : 5 * i + 5]
        g = jnp.sum(rows_in[i][cap : cap + 16, 0:lanes].astype(F32), axis=0, keepdims=True)
        gate = jnp.sum(jnp.where(eye, g, 0.0), axis=1, keepdims=True)[0:cap, :]
        gp[...] = (gate * dys[i][...].astype(F32)).astype(BF)
        gates.append(gate)
    sums = [None] * n
    backs = [None] * n
    for b in range(GROUP):
        for c in copies[b]:
            c.wait()
        at = slice(b * width, (b + 1) * width)
        for i in range(n):
            back, out, act, dinner, gp = outs[5 * i : 5 * i + 5]
            a, slope = gelu_pair(dot(rows_in[i][0:cap, :], wu[b]))
            act[:, at] = a.astype(BF)
            dinner[:, at] = (dot(gp[...], wd[b]) * slope).astype(BF)
            o = dot_nt(act[:, at], wd[b])
            d = dot_nt(dinner[:, at], wu[b])
            sums[i] = o if b == 0 else sums[i] + o
            backs[i] = d if b == 0 else backs[i] + d
    for i in range(n):
        back, out, act, dinner, gp = outs[5 * i : 5 * i + 5]
        out[...] = (gates[i] * sums[i]).astype(BF)
        back[0:cap, :] = backs[i].astype(BF)
        dg = jnp.sum(dys[i][...].astype(F32) * sums[i], axis=1, keepdims=True)
        pad = jnp.where(eye[0:cap, :], dg, 0.0)
        dg_row = jnp.sum(pad, axis=0, keepdims=True)
        three = split3(dg_row)
        row = iota((16, lanes), 0)
        back[cap : cap + 16, :] = jnp.zeros((16, width), BF)
        back[cap : cap + 16, 0:lanes] = (
            jnp.where(row == 0, three[0].astype(F32), 0.0)
            + jnp.where(row == 1, three[1].astype(F32), 0.0)
            + jnp.where(row == 2, three[2].astype(F32), 0.0)
        ).astype(BF)


def expert(s, rows_in, dys, own, other, cap):
    n = len(rows_in)
    width = rows_in[0].shape[1]
    ff = GROUP * width
    res = call(
        functools.partial(expert_kernel, cap, n),
        [SM] + [VM] * (2 * n) + [HB] * 12,
        [
            shape((cap + 16, width), BF),
            shape((cap, width), BF),
            shape((cap, ff), BF),
            shape((cap, ff), BF),
            shape((cap, width), BF),
        ]
        * n,
        [
            pltpu.VMEM((GROUP, width, width), BF),
            pltpu.VMEM((GROUP, width, width), BF),
            pltpu.SemaphoreType.DMA((16,)),
        ],
        8 * n * cap * width * ff,
        4 * width * ff + n * cap * (4 * ff + 10 * width),
        "expert",
    )(s, *rows_in, *dys, *own, *other)
    return [res[5 * i : 5 * i + 5] for i in range(n)]


def grad_kernel(n, m, part_ref, *refs):
    lefts, rights, out = refs[:n], refs[n : 2 * n], refs[2 * n]
    if n == 1:
        out[0] = dot_tn(lefts[0][...], rights[0][...]).astype(BF)
        return
    whole_left, whole_right = refs[2 * n + 1 :]
    rows = lefts[0].shape[0]
    for i in range(n):
        whole_left[i * rows : (i + 1) * rows, :] = lefts[i][...]
        whole_right[i * rows : (i + 1) * rows, :] = rights[i][...]
    out[0] = dot_tn(whole_left[...], whole_right[...]).astype(BF)


def weight_grad(part, lefts, rights, rows=None):
    n = len(lefts)
    t = rows or lefts[0].shape[0]
    half = lefts[0].shape[1] // 2
    width = 768 if rights[0].shape[1] % 768 == 0 else rights[0].shape[1]
    m, nb = half // 384, rights[0].shape[1] // width
    scratch = []
    if n > 1:
        scratch = [pltpu.VMEM((n * t, 384), BF), pltpu.VMEM((n * t, width), BF)]
    return pl.pallas_call(
        functools.partial(grad_kernel, n, m),
        grid_spec=pltpu.PrefetchScalarGridSpec(
            num_scalar_prefetch=1,
            grid=(m, nb),
            in_specs=[pl.BlockSpec((t, 384), lambda i, j, p: (0, p[0] * m + i))] * n
            + [pl.BlockSpec((t, width), lambda i, j, p: (0, j))] * n,
            out_specs=pl.BlockSpec((1, 384, width), lambda i, j, p: (i * nb + j, 0, 0)),
            scratch_shapes=scratch,
        ),
        out_shape=shape((m * nb, 384, width), BF),
        compiler_params=pltpu.CompilerParams(vmem_limit_bytes=LIMIT),
        cost_estimate=pl.CostEstimate(
            flops=2 * n * t * half * width * nb,
            bytes_accessed=2 * (n * t * (half + width * nb) + half * width * nb),
            transcendentals=0,
        ),
        name="weight_grad",
    )(part, *lefts, *rights)


def back_kernel(experts, cap, s_ref, dy, dense, hid, gb_ref, router, place, route, live, soft, normed3, slope, fc1_a, fc1_b, fc2_a, fc2_b, *refs):
    homes = refs[:experts]
    dmlp, dpre, dhidden, tiny, drouter = refs[experts : experts + 5]
    w1, w2, spots, ups, sems = refs[experts + 5 :]
    s = s_ref[0]
    rows, width = hid.shape
    copies = halves_into(s, fc1_a, fc1_b, w1, sems, 0) + halves_into(s, fc2_a, fc2_b, w2, sems, 2)
    for c in copies:
        c.start()
    lanes = -(-cap // WIDE) * WIDE
    spot = iota((lanes, rows), 0)
    spot = jnp.where(spot < cap, spot, -2 * experts * cap)
    dgate = [jnp.zeros((16, rows), F32) for _ in range(TOP)]
    for r in range(experts):
        tail = homes[r][cap : cap + 16, 0:lanes]
        hot = [jnp.where(spot + r * cap == place[k : k + 1, :], 1.0, 0.0).astype(BF) for k in range(TOP)]
        for k in range(TOP):
            dgate[k] = dgate[k] + dot(tail, hot[k])
        term = dot_tn((hot[0] + hot[1])[0:cap, :], homes[r][0:cap, :])
        ups[...] = term if r == 0 else ups[...] + term
    dgate = [jnp.sum(d, axis=0, keepdims=True) * live[...] for d in dgate]
    mix = soft[0:1, :] * dgate[0] + soft[1:2, :] * dgate[1]
    dsoft = [soft[k : k + 1, :] * (dgate[k] - mix) for k in range(TOP)]
    index = iota((router.shape[0], rows), 0)
    dlogits = sum(jnp.where(index == route[k : k + 1, :], dsoft[k], 0.0) for k in range(TOP))
    dlogits = dlogits.astype(BF)
    drouter[...] = dot(dlogits, normed3[...])
    ups[...] += dot_tn(dlogits, router[...])
    tile = rows // 6
    tiny[...] = jnp.zeros_like(tiny)

    def norm_back(at, values, gain, bias_row, base):
        n, scale = normalize(values)
        u = ups[at, :]
        tiny[bias_row - 1 : bias_row, :] += jnp.sum(u * n, axis=0, keepdims=True)
        tiny[bias_row : bias_row + 1, :] += jnp.sum(u, axis=0, keepdims=True)
        ug = u * gain
        dv = scale * (
            ug
            - jnp.mean(ug, axis=-1, keepdims=True)
            - n * jnp.mean(ug * n, axis=-1, keepdims=True)
        )
        return base + dv

    @pl.loop(0, 6)
    def _(i):
        at = pl.ds(pl.multiple_of(i * tile, 16), tile)
        dd = norm_back(at, dense[at, :], gb_ref[4:5, :], 5, dy[at, :].astype(F32))
        dhidden[at, :] = dd
        dmlp[at, :] = dd.astype(BF)

    for c in copies:
        c.wait()
    ups[...] = jnp.zeros_like(ups)

    @pl.loop(0, w1.shape[1] // 512)
    def _(j):
        at = pl.ds(pl.multiple_of(j * 512, 512), 512)
        dpre[:, at] = (dot_nt(dmlp[...], w2[at, :]) * slope[:, at].astype(F32)).astype(BF)
        ups[...] += dot_nt(dpre[:, at], w1[:, at])

    @pl.loop(0, 6)
    def _(i):
        at = pl.ds(pl.multiple_of(i * tile, 16), tile)
        dhidden[at, :] = norm_back(at, hid[at, :], gb_ref[2:3, :], 3, dhidden[at, :])


def back(s, dy, dense, hid, gb, router, place, route, live, soft, normed3, slope, fc1, fc2, homes, experts, cap):
    rows, width = hid.shape
    ff = fc1[0].shape[1]
    return call(
        functools.partial(back_kernel, experts, cap),
        [SM] + [VM] * 11 + [HB] * 4 + [VM] * experts,
        [
            shape((rows, width), BF),
            shape((rows, ff), BF),
            shape((rows, width), F32),
            shape((8, width), F32),
            shape(router.shape, F32),
        ],
        [
            pltpu.VMEM((width, ff), BF),
            pltpu.VMEM((ff, width), BF),
            pltpu.VMEM((8, WIDE), F32),
            pltpu.VMEM((rows, width), F32),
            pltpu.SemaphoreType.DMA((4,)),
        ],
        4 * rows * width * ff + 2 * rows * width * experts * cap,
        4 * width * ff + rows * (4 * ff + 18 * width),
        "dense_backward",
    )(s, dy, dense, hid, gb, router, place, route, live, soft, normed3, slope, *fc1, *fc2, *homes)


def attend_back_kernel(
    s_ref, x_ref, dhid, id_row, id_col, gb_ref, packed, lse, qkv_a, qkv_b, wo_a, wo_b,
    dattn, dpacked, grad_in, tiny,
    wq, wo, bias, dctx, ups, sems,
):
    s = s_ref[0]
    rows, width = x_ref.shape
    copies = halves_into(s, wo_a, wo_b, wo, sems, 0) + halves_into(s, qkv_a, qkv_b, wq, sems, 2)
    for c in copies:
        c.start()
    tile = rows // 6

    @pl.loop(0, 6)
    def _(i):
        at = pl.ds(pl.multiple_of(i * tile, 16), tile)
        dattn[at, :] = dhid[at, :].astype(BF)
        bias[at, :] = jnp.where(id_col[at, :] == id_row[...], 0.0, MASKED)

    copies[0].wait()
    copies[1].wait()

    @pl.loop(0, width // 256)
    def _(j):
        at = pl.ds(pl.multiple_of(j * 256, 256), 256)
        dctx[:, at] = dot_nt(dattn[...], wo[at, :]).astype(BF)

    lane = iota((1, WIDE), 1)

    @pl.loop(0, width // WIDE)
    def _(pair):
        col = pl.multiple_of(pair * WIDE, WIDE)
        q = packed[:, pl.ds(col, WIDE)] * jnp.asarray(HEAD**-0.5, BF)
        keys = packed[:, pl.ds(width + col, WIDE)]
        values = packed[:, pl.ds(2 * width + col, WIDE)]
        dc = dctx[:, pl.ds(col, WIDE)]
        dq, dk, dv = [], [], []
        for h in range(2):
            mine = (lane >= h * HEAD) & (lane < (h + 1) * HEAD)
            scores = dot_nt(jnp.where(mine, keys, jnp.zeros_like(keys)), q) + bias[...]
            p = jnp.exp(scores - lse[pl.ds(2 * pair + h, 1), :])
            dp = dot_nt(jnp.where(mine, values, jnp.zeros_like(values)), dc)
            inner = jnp.sum(p * dp, axis=0, keepdims=True)
            ds = (p * (dp - inner)).astype(BF)
            dv.append(dot(p.astype(BF), dc))
            dk.append(dot(ds, q))
            dq.append(dot_tn(ds, keys) * HEAD**-0.5)
        low = lane < HEAD
        dpacked[:, pl.ds(col, WIDE)] = jnp.where(low, dq[0], dq[1]).astype(BF)
        dpacked[:, pl.ds(width + col, WIDE)] = jnp.where(low, dk[0], dk[1]).astype(BF)
        dpacked[:, pl.ds(2 * width + col, WIDE)] = jnp.where(low, dv[0], dv[1]).astype(BF)

    copies[2].wait()
    copies[3].wait()

    @pl.loop(0, width // 256)
    def _(j):
        at = pl.ds(pl.multiple_of(j * 256, 256), 256)
        ups[:, at] = dot_nt(dpacked[...], wq[at, :])

    tiny[...] = jnp.zeros_like(tiny)

    @pl.loop(0, 6)
    def _(i):
        at = pl.ds(pl.multiple_of(i * tile, 16), tile)
        n, scale = normalize(x_ref[at, :].astype(F32))
        u = ups[at, :]
        tiny[0:1, :] += jnp.sum(u * n, axis=0, keepdims=True)
        tiny[1:2, :] += jnp.sum(u, axis=0, keepdims=True)
        ug = u * gb_ref[0:1, :]
        grad_in[at, :] = dhid[at, :] + scale * (
            ug
            - jnp.mean(ug, axis=-1, keepdims=True)
            - n * jnp.mean(ug * n, axis=-1, keepdims=True)
        )


def attend_back(s, x, dhid, ids, gb, packed, lse, qkv, wo):
    rows, width = x.shape
    n3 = packed.shape[1]
    return call(
        attend_back_kernel,
        [SM] + [VM] * 7 + [HB] * 4,
        [
            shape((rows, width), BF),
            shape((rows, n3), BF),
            shape((rows, width), F32),
            shape((8, width), F32),
        ],
        [
            pltpu.VMEM((width, n3), BF),
            pltpu.VMEM((width, width), BF),
            pltpu.VMEM((rows, rows), F32),
            pltpu.VMEM((rows, width), BF),
            pltpu.VMEM((rows, width), F32),
            pltpu.SemaphoreType.DMA((4,)),
        ],
        2 * rows * width * (n3 + width) + 10 * rows * rows * width,
        2 * (width * (n3 + width) + rows * (3 * width + 2 * n3)) + 8 * rows * width,
        "attention_backward",
    )(s, x, dhid, ids[None, :], ids[:, None], gb, packed, lse, *qkv, *wo)


def merge_kernel(experts, cap, dense, place, *refs):
    outs, result = refs[:experts], refs[experts]
    rows = dense.shape[0]
    total = dense[...]
    spot = iota((cap, rows), 0)
    for r in range(experts):
        hot = sum(jnp.where(spot + r * cap == place[k : k + 1, :], 1.0, 0.0) for k in range(TOP))
        total = total + dot_tn(hot.astype(BF), outs[r][...])
    result[...] = total.astype(BF)


def merge(dense, place, outs, experts, cap):
    rows, width = dense.shape
    return call(
        functools.partial(merge_kernel, experts, cap),
        [VM] * (2 + experts),
        shape((rows, width), BF),
        [],
        2 * rows * width * experts * cap,
        rows * width * 6 + 2 * experts * cap * width,
        "merge",
    )(dense, place, *outs)


def spread_kernel(experts, cap, rows_in, place, *chunks):
    spot = iota((cap, rows_in.shape[0]), 0)
    for r in range(experts):
        hot = sum(jnp.where(spot + r * cap == place[k : k + 1, :], 1.0, 0.0) for k in range(TOP))
        chunks[r][...] = dot(hot.astype(BF), rows_in[...]).astype(BF)


def spread(rows_in, place, experts, cap):
    rows, width = rows_in.shape
    return call(
        functools.partial(spread_kernel, experts, cap),
        [VM, VM],
        [shape((cap, width), BF)] * experts,
        [],
        2 * rows * width * experts * cap,
        2 * (rows + experts * cap) * width,
        "spread",
    )(rows_in, place)


def places_of(routes, live, experts, capacity):
    tokens = routes.shape[0]
    ids = jnp.arange(experts, dtype=jnp.int32)
    match = [
        ((routes[:, k : k + 1] == ids[None, :]) & live[:, None]).astype(F32) for k in range(TOP)
    ]
    order = jnp.arange(tokens, dtype=jnp.int32)
    below = (order[:, None] > order[None, :]).astype(BF)
    before = jnp.zeros((1, experts), F32)
    out = []
    for k in range(TOP):
        counts = dot(below, match[k].astype(BF)) + before
        before = before + jnp.sum(match[k], axis=0, keepdims=True)
        within = jnp.sum(counts * match[k], axis=1).astype(jnp.int32)
        out.append(jnp.where(live, routes[:, k] * capacity + within, experts * capacity))
    return out

def local(
    tokens,
    image_ids,
    routes,
    norm1_gain,
    norm1_bias,
    qkv_weight,
    attn_out_weight,
    norm2_gain,
    norm2_bias,
    fc1_weight,
    fc2_weight,
    norm3_gain,
    norm3_bias,
    router_weight,
    expert_up,
    expert_down,
    cotangent,
):
    s = lax.axis_index("section")
    e = lax.axis_index("dp") // GROUP
    q = lax.axis_index("dp") % GROUP
    dp_count = lax.axis_size("dp")
    experts = dp_count // GROUP
    cap = GROUP * ((21 * SLOTS + 10 * experts * GROUP - 1) // (10 * experts * GROUP))
    cap = -(-cap // 16) * 16
    half = tokens.shape[1]
    width = 2 * half
    few = experts <= 8
    planes = [[p * GROUP + i for p in range(experts)] for i in range(GROUP)]
    here, there = jnp.reshape(s, (1,)), jnp.reshape(1 - s, (1,))

    def swap(v):
        return lax.ppermute(v, "section", [(0, 1), (1, 0)])

    def over_q(v, bit):
        return lax.ppermute(v, "dp", [(i, i ^ bit) for i in range(dp_count)])

    def over_e(v, r):
        return lax.ppermute(
            v,
            "dp",
            [(i, ((i // GROUP + r) % experts) * GROUP + i % GROUP) for i in range(dp_count)],
        )

    def part(v, index, size, axis=0):
        return lax.dynamic_slice_in_dim(v, index * size, size, axis)

    def join(own, other, axis):
        return jnp.where(
            s == 0,
            jnp.concatenate([own, other], axis=axis),
            jnp.concatenate([other, own], axis=axis),
        )

    def add(a, b):
        return (a.astype(F32) + b.astype(F32)).astype(BF)

    def out_chunks(chunks):
        if not few:
            return list(lax.all_to_all(jnp.stack(chunks), "dp", 0, 0, axis_index_groups=planes))
        return [chunks[0]] + [over_e(chunks[r], r) for r in range(1, experts)]

    def home_chunks(chunks):
        if not few:
            return list(lax.all_to_all(jnp.stack(chunks), "dp", 0, 0, axis_index_groups=planes))
        return [chunks[0]] + [over_e(chunks[r], experts - r) for r in range(1, experts)]

    x = join(part(tokens, s, SLOTS), swap(part(tokens, 1 - s, SLOTS)), 1)
    ids = part(image_ids, s, 1).reshape(-1)
    route = part(routes, s, SLOTS)
    live = ids >= 0
    small = jnp.stack([norm1_gain, norm1_bias, norm2_gain, norm2_bias, norm3_gain, norm3_bias])
    small = jnp.concatenate([small, jnp.transpose(router_weight)])
    small = join(small, swap(small), 1)
    gb = jnp.concatenate([small[:6], jnp.zeros((2, width), BF)]).astype(F32)
    router_rows = -(-experts // 16) * 16
    router = jnp.concatenate([small[6:], jnp.zeros((router_rows - experts, width), BF)])

    def both(w):
        return (w, swap(w))

    qkv, wo = both(qkv_weight), both(attn_out_weight)
    fc1, fc2 = both(fc1_weight), both(fc2_weight)
    dy = join(part(cotangent, s, SLOTS), swap(part(cotangent, 1 - s, SLOTS)), 1)

    pair = jnp.stack([expert_up, expert_down])
    from_x, from_y = over_q(pair, 1), over_q(pair, 2)
    far_up, far_down = over_q(from_x[0], 2), over_q(from_y[1], 1)
    own = [expert_up, expert_down, from_x, from_y, far_up, far_down]
    other = [swap(v) for v in own]

    if few:
        distance = (route - e) % experts
    else:
        distance = route
    spots = places_of(distance, live, experts, cap)
    place = jnp.stack(spots + [jnp.full_like(spots[0], -1)] * 6)
    route_rows = jnp.concatenate([jnp.transpose(route), jnp.full((6, SLOTS), -1, jnp.int32)])
    live_row = live.astype(F32)[None, :]
    dy_out = out_chunks(spread(dy, place, experts, cap))

    normed1, packed, context, lse, hidden = front(here, x, ids, gb, qkv, wo)
    normed2, act, slope, dense, normed3, soft, *sent = mlp(
        here, hidden, gb, router, place, route_rows, live_row, fc1, fc2, experts, cap
    )
    got = out_chunks(sent)

    step = max(1, experts // 4)
    results = []
    for i in range(0, experts, step):
        results += expert(here, got[i : i + step], dy_out[i : i + step], own, other, cap)
    homes = home_chunks([r[0] for r in results])
    outs = home_chunks([r[1] for r in results])
    acts, dinners, scaled = ([r[i] for r in results] for i in (2, 3, 4))

    def grad_sum(lefts, rights, rows=None):
        away = weight_grad(there, lefts, rights, rows)
        kept = weight_grad(here, lefts, rights, rows)
        return add(kept, swap(away))

    sum_up = grad_sum(got, dinners, cap)
    sum_down = grad_sum(scaled, acts)
    moved = over_q(jnp.stack([sum_up[1], sum_up[3]]), 1)
    near, far = add(sum_up[0], moved[0]), add(sum_up[2], moved[1])
    half_up = near.astype(F32) + over_q(far, 2).astype(F32)
    moved = over_q(sum_down[2:], 2)
    near, far = add(sum_down[0], moved[0]), add(sum_down[1], moved[1])
    half_down = near.astype(F32) + over_q(far, 1).astype(F32)

    dmlp, dpre, dhidden, tiny23, drouter = back(
        here, dy, dense, hidden, gb, router, place, route_rows, live_row, soft, normed3, slope,
        fc1, fc2, homes, experts, cap,
    )
    grad_fc2 = grad_sum([act], [dmlp])
    grad_fc1 = grad_sum([normed2], [dpre])
    dattn, dpacked, grad_in, tiny1 = attend_back(
        here, x, dhidden, ids, gb, packed, lse, qkv, wo
    )
    grad_attn = add(
        jnp.concatenate(
            [weight_grad(here, [normed1], [dpacked]), weight_grad(here, [context], [dattn])]
        ),
        swap(
            jnp.concatenate(
                [weight_grad(there, [normed1], [dpacked]), weight_grad(there, [context], [dattn])]
            )
        ),
    )
    block_out = merge(dense, place, outs, experts, cap)

    def rejoin(v):
        return join(part(v, s, half, 1), swap(part(v, 1 - s, half, 1)), 0)

    def fold(v, bit):
        mine, rows = (q // bit) % 2, v.shape[0] // 2
        return add(part(v, mine, rows), over_q(part(v, 1 - mine, rows), bit))

    def unfold(v, bit):
        mine, got_v = (q // bit) % 2, over_q(v, bit)
        return jnp.where(
            mine == 0, jnp.concatenate([v, got_v]), jnp.concatenate([got_v, v])
        )

    def fold_planes(a, b):
        both_ab = jnp.stack([a, b])
        if not few:
            return lax.psum(both_ab, "dp", axis_index_groups=planes)
        rows = a.shape[0] // experts
        total = part(both_ab, e, rows, 1).astype(F32)
        for r in range(1, experts):
            total = total + over_e(part(both_ab, (e + r) % experts, rows, 1), r).astype(F32)
        total = total.astype(BF)
        whole = jnp.zeros_like(both_ab)
        for r in range(experts):
            piece = total if r == 0 else over_e(total, r)
            whole = lax.dynamic_update_slice_in_dim(whole, piece, ((e - r) % experts) * rows, 1)
        return whole

    def sum_dp(a, b):
        a, b = fold(a, 1), fold(b, 2)
        a, b = fold(a, 2), fold(b, 1)
        ab = fold_planes(a, b)
        a, b = unfold(ab[0], 2), unfold(ab[1], 1)
        a, b = unfold(a, 1), unfold(b, 2)
        return a.astype(F32), b.astype(F32)

    sum_fc2, sum_fc1 = sum_dp(grad_fc2.reshape(-1, width), grad_fc1.reshape(-1, width))
    flat = grad_attn.reshape(-1, width)
    sum_a, sum_b = sum_dp(flat[:width], flat[width:])
    sum_qkv = jnp.concatenate([sum_a, sum_b[:half]]).reshape(3, half, width)

    def columns(v):
        return jnp.transpose(v, (1, 0, 2)).reshape(half, -1)

    tiny = jnp.concatenate([tiny1[:2], tiny23[2:6], drouter[:experts]])
    tiny = part(tiny, s, half, 1) + swap(part(tiny, 1 - s, half, 1))
    tiny = tiny + over_q(tiny, 1)
    tiny = tiny + over_q(tiny, 2)
    total = tiny
    if few:
        for r in range(1, experts):
            total = total + over_e(tiny, r)
    else:
        total = lax.psum(tiny, "dp", axis_index_groups=planes)
    return (
        rejoin(block_out),
        rejoin(grad_in),
        total[0],
        total[1],
        columns(sum_qkv),
        sum_b[half:],
        total[2],
        total[3],
        columns(sum_fc1.reshape(-1, half, width)),
        sum_fc2,
        total[4],
        total[5],
        jnp.transpose(total[6:]),
        half_up,
        half_down,
    )


def solution(mesh):
    placed = (
        P("dp", "section"),
        P("dp", None),
        P("dp", None),
        P("section"),
        P("section"),
        P("section", None),
        P("section", None),
        P("section"),
        P("section"),
        P("section", None),
        P("section", None),
        P("section"),
        P("section"),
        P("section", None),
        P("section", "dp"),
        P("section", "dp"),
        P("dp", "section"),
    )
    return jax.shard_map(
        local,
        mesh=mesh,
        in_specs=placed,
        out_specs=(
            P("dp", "section"),
            P("dp", "section"),
            P("section"),
            P("section"),
            P("section", None),
            P("section", None),
            P("section"),
            P("section"),
            P("section", None),
            P("section", None),
            P("section"),
            P("section"),
            P("section", None),
            P("section", "dp"),
            P("section", "dp"),
        ),
        check_vma=False,
    )
```

```python
import functools

import jax
import jax.numpy as jnp
from jax import lax
from jax.experimental import pallas as pl
from jax.experimental.pallas import tpu as pltpu
from jax.sharding import PartitionSpec as P

HEAD = 64
TOP = 2
GROUP = 4
SLOTS = 576
WIDE = 128

EPSILON = 1e-06
MASKED = -1e30
BF = jnp.bfloat16
F32 = jnp.float32
LIMIT = 60 * 1024 * 1024


def dot(a, b):
    return jnp.dot(a, b, preferred_element_type=F32)


def dot_nt(a, b):
    return lax.dot_general(a, b, (((1,), (1,)), ((), ())), preferred_element_type=F32)


def dot_tn(a, b):
    return lax.dot_general(a, b, (((0,), (0,)), ((), ())), preferred_element_type=F32)


def normalize(v):
    center = v - jnp.mean(v, axis=-1, keepdims=True)
    scale = lax.rsqrt(jnp.mean(center * center, axis=-1, keepdims=True) + EPSILON)
    return center * scale, scale


def gelu_pair(x):
    bell = jnp.exp(x * x * -0.5)
    t = 1.0 / (1.0 + jnp.abs(x) * (0.3275911 * 0.5**0.5))
    tail = (
        t
        * (
            0.127414796
            + t * (-0.142248368 + t * (0.7107068705 + t * (-0.7265760135 + t * 0.5307027145)))
        )
        * bell
    )
    cdf = jnp.where(x >= 0.0, 1.0 - tail, tail)
    return x * cdf, cdf + x * (bell * 0.3989422804014327)


def iota(shape, axis):
    return lax.broadcasted_iota(jnp.int32, shape, axis)


def halves_into(s, own, other, dest, sems, first):
    rows = own.shape[0]
    return [
        pltpu.make_async_copy(own, dest.at[pl.ds(pl.multiple_of(s * rows, rows), rows)], sems.at[first]),
        pltpu.make_async_copy(
            other, dest.at[pl.ds(pl.multiple_of((1 - s) * rows, rows), rows)], sems.at[first + 1]
        ),
    ]


def split3(v):
    hi = v.astype(BF)
    rest = v - hi.astype(F32)
    mid = rest.astype(BF)
    low = (rest - mid.astype(F32)).astype(BF)
    return hi, mid, low


VM = pl.BlockSpec(memory_space=pltpu.VMEM)
SM = pl.BlockSpec(memory_space=pltpu.SMEM)
HB = pl.BlockSpec(memory_space=pl.ANY)


def call(kernel, in_specs, out_shape, scratch, flops, moved, name, after=(), weight=16):
    count, extra = len(in_specs), len(after)

    def body(*refs):
        kernel(*refs[:count], *refs[count + extra :])

    made = pl.pallas_call(
        body,
        in_specs=in_specs + [HB] * extra,
        out_specs=jax.tree.map(lambda _: VM, out_shape),
        out_shape=out_shape,
        scratch_shapes=scratch,
        compiler_params=pltpu.CompilerParams(vmem_limit_bytes=LIMIT),
        cost_estimate=pl.CostEstimate(
            flops=int(weight * flops), bytes_accessed=int(weight * moved), transcendentals=0
        ),
        name=name,
    )
    return lambda *operands: made(*operands, *after)


def shape(dims, kind):
    return jax.ShapeDtypeStruct(dims, kind)


def front_kernel(
    s_ref, x_ref, id_row, id_col, gb_ref, qkv_a, qkv_b, wo_a, wo_b,
    normed, packed, context, lse, hidden,
    wq, wo, bias, lse_col, sems,
):
    s = s_ref[0]
    rows, width = x_ref.shape
    copies = halves_into(s, qkv_a, qkv_b, wq, sems, 0) + halves_into(s, wo_a, wo_b, wo, sems, 2)
    for c in copies:
        c.start()
    tile = rows // 6

    @pl.loop(0, 6)
    def _(i):
        at = pl.ds(pl.multiple_of(i * tile, 16), tile)
        n, _ = normalize(x_ref[at, :].astype(F32))
        normed[at, :] = (n * gb_ref[0:1, :] + gb_ref[1:2, :]).astype(BF)
        bias[at, :] = jnp.where(id_col[at, :] == id_row[...], 0.0, MASKED)

    copies[0].wait()
    copies[1].wait()

    @pl.loop(0, wq.shape[1] // 256)
    def _(j):
        at = pl.ds(pl.multiple_of(j * 256, 256), 256)
        packed[:, at] = dot(normed[...], wq[:, at]).astype(BF)

    lane = iota((1, WIDE), 1)
    lse_col[...] = jnp.zeros_like(lse_col)
    third = rows // 3

    @pl.loop(0, width // WIDE)
    def _(pair):
        col = pl.multiple_of(pair * WIDE, WIDE)
        keys = packed[:, pl.ds(width + col, WIDE)]
        values = packed[:, pl.ds(2 * width + col, WIDE)]
        for r in range(3):
            at = slice(r * third, (r + 1) * third)
            q = packed[at, pl.ds(col, WIDE)] * jnp.asarray(HEAD**-0.5, BF)
            outs = []
            sums = lse_col[at, :]
            for h in range(2):
                mine = (lane >= h * HEAD) & (lane < (h + 1) * HEAD)
                scores = dot_nt(jnp.where(mine, q, jnp.zeros_like(q)), keys) + bias[at, :]
                top = jnp.max(scores, axis=1, keepdims=True)
                p = jnp.exp(scores - top)
                total = jnp.sum(p, axis=1, keepdims=True)
                outs.append(dot(p.astype(BF), values) * (1.0 / total))
                sums = jnp.where(lane == 2 * pair + h, top + jnp.log(total), sums)
            lse_col[at, :] = sums
            context[at, pl.ds(col, WIDE)] = jnp.where(lane < HEAD, outs[0], outs[1]).astype(BF)

    lse[...] = jnp.transpose(lse_col[...])[0 : lse.shape[0], :]
    copies[2].wait()
    copies[3].wait()

    @pl.loop(0, width // 256)
    def _(j):
        at = pl.ds(pl.multiple_of(j * 256, 256), 256)
        hidden[:, at] = x_ref[:, at].astype(F32) + dot(context[...], wo[:, at])


def front(s, x, ids, gb, qkv, wo, after):
    rows, width = x.shape
    n3 = qkv[0].shape[1]
    return call(
        front_kernel,
        [SM, VM, VM, VM, VM, HB, HB, HB, HB],
        [
            shape((rows, width), BF),
            shape((rows, n3), BF),
            shape((rows, width), BF),
            shape((16, rows), F32),
            shape((rows, width), F32),
        ],
        [
            pltpu.VMEM((width, n3), BF),
            pltpu.VMEM((width, width), BF),
            pltpu.VMEM((rows, rows), F32),
            pltpu.VMEM((rows, WIDE), F32),
            pltpu.SemaphoreType.DMA((4,)),
        ],
        2 * rows * width * (n3 + width) + 4 * rows * rows * width,
        2 * (width * (n3 + width) + rows * (3 * width + n3)) + 4 * rows * width,
        "attention_forward",
        after,
    )(s, x, ids[None, :], ids[:, None], gb, *qkv, *wo)


def mlp_kernel(experts, cap, hid, gb_ref, router, place, route, live, fc1, fc2, *refs):
    normed2, act, slope, dense, normed3, soft = refs[:6]
    chunks = refs[6 : 6 + experts]
    w1, w2, sems = refs[6 + experts :]
    rows, width = hid.shape
    copies = [
        pltpu.make_async_copy(fc1, w1, sems.at[0]),
        pltpu.make_async_copy(fc2, w2, sems.at[1]),
    ]
    for c in copies:
        c.start()
    tile = rows // 6

    @pl.loop(0, 6)
    def _(i):
        at = pl.ds(pl.multiple_of(i * tile, 16), tile)
        n, _ = normalize(hid[at, :])
        normed2[at, :] = (n * gb_ref[2:3, :] + gb_ref[3:4, :]).astype(BF)
        dense[at, :] = hid[at, :]

    for c in copies:
        c.wait()

    @pl.loop(0, w1.shape[1] // 512)
    def _(j):
        at = pl.ds(pl.multiple_of(j * 512, 512), 512)
        a, sl = gelu_pair(dot(normed2[...], w1[:, at]))
        act[:, at] = a.astype(BF)
        slope[:, at] = sl.astype(BF)
        dense[...] += dot(act[:, at], w2[at, :])

    @pl.loop(0, 6)
    def _(i):
        at = pl.ds(pl.multiple_of(i * tile, 16), tile)
        n, _ = normalize(dense[at, :])
        normed3[at, :] = (n * gb_ref[4:5, :] + gb_ref[5:6, :]).astype(BF)

    logits = dot_nt(router[...], normed3[...])
    expert = iota(logits.shape, 0)
    chosen = [
        jnp.sum(jnp.where(expert == route[k : k + 1, :], logits, 0.0), axis=0, keepdims=True)
        for k in range(TOP)
    ]
    top = jnp.maximum(chosen[0], chosen[1])
    raised = [jnp.exp(c - top) for c in chosen]
    total = raised[0] + raised[1]
    pieces = []
    for k in range(TOP):
        share = raised[k] / total
        soft[k : k + 1, :] = share
        three = split3(share * live[...])
        row = iota((16, rows), 0)
        pieces.append(
            jnp.where(row == 0, three[0].astype(F32), 0.0)
            + jnp.where(row == 1, three[1].astype(F32), 0.0)
            + jnp.where(row == 2, three[2].astype(F32), 0.0)
        )
    pieces = [p.astype(BF) for p in pieces]
    lanes = -(-cap // WIDE) * WIDE
    spot = iota((lanes, rows), 0)
    spot = jnp.where(spot < cap, spot, -2 * experts * cap)
    for r in range(experts):
        hot = [jnp.where(spot + r * cap == place[k : k + 1, :], 1.0, 0.0).astype(BF) for k in range(TOP)]
        both = (hot[0] + hot[1])[0:cap, :]
        chunks[r][0:cap, :] = dot(both, normed3[...]).astype(BF)
        chunks[r][cap : cap + 16, :] = jnp.zeros((16, width), BF)
        chunks[r][cap : cap + 16, 0:lanes] = (
            dot_nt(pieces[0], hot[0]) + dot_nt(pieces[1], hot[1])
        ).astype(BF)


def mlp(hid, gb, router, place, route, live, fc1, fc2, experts, cap, after):
    rows, width = hid.shape
    ff = fc1.shape[1]
    return call(
        functools.partial(mlp_kernel, experts, cap),
        [VM, VM, VM, VM, VM, VM, HB, HB],
        [
            shape((rows, width), BF),
            shape((rows, ff), BF),
            shape((rows, ff), BF),
            shape((rows, width), F32),
            shape((rows, width), BF),
            shape((8, rows), F32),
        ]
        + [shape((cap + 16, width), BF)] * experts,
        [
            pltpu.VMEM((width, ff), BF),
            pltpu.VMEM((ff, width), BF),
            pltpu.SemaphoreType.DMA((2,)),
        ],
        4 * rows * width * ff + 2 * rows * width * experts * cap,
        4 * width * ff + rows * (4 * ff + 12 * width),
        "dense_forward",
        after,
    )(hid, gb, router, place, route, live, fc1, fc2)


def expert_kernel(cap, n, *refs):
    rows_in, dys, weights = refs[:n], refs[n : 2 * n], refs[2 * n : 2 * n + GROUP]
    outs = refs[2 * n + GROUP : -3]
    wu, wd, sems = refs[-3:]
    width = wu.shape[1]
    half = width // 2
    copies = [
        [
            pltpu.make_async_copy(
                weights[b].at[h, u], w.at[b, h * half : (h + 1) * half], sems.at[4 * b + 2 * h + u]
            )
            for h in range(2)
            for u, w in enumerate((wu, wd))
        ]
        for b in range(GROUP)
    ]
    for b in range(GROUP):
        for c in copies[b]:
            c.start()
    lanes = -(-cap // WIDE) * WIDE
    eye = iota((lanes, lanes), 0) == iota((lanes, lanes), 1)
    gates = []
    for i in range(n):
        back, out, act, dinner, gp = outs[5 * i : 5 * i + 5]
        g = jnp.sum(rows_in[i][cap : cap + 16, 0:lanes].astype(F32), axis=0, keepdims=True)
        gate = jnp.sum(jnp.where(eye, g, 0.0), axis=1, keepdims=True)[0:cap, :]
        gp[...] = (gate * dys[i][...].astype(F32)).astype(BF)
        gates.append(gate)
    sums = [None] * n
    backs = [None] * n
    for b in range(GROUP):
        for c in copies[b]:
            c.wait()
        at = slice(b * width, (b + 1) * width)
        for i in range(n):
            back, out, act, dinner, gp = outs[5 * i : 5 * i + 5]
            a, slope = gelu_pair(dot(rows_in[i][0:cap, :], wu[b]))
            act[:, at] = a.astype(BF)
            dinner[:, at] = (dot(gp[...], wd[b]) * slope).astype(BF)
            o = dot_nt(act[:, at], wd[b])
            d = dot_nt(dinner[:, at], wu[b])
            sums[i] = o if b == 0 else sums[i] + o
            backs[i] = d if b == 0 else backs[i] + d
    for i in range(n):
        back, out, act, dinner, gp = outs[5 * i : 5 * i + 5]
        out[...] = (gates[i] * sums[i]).astype(BF)
        back[0:cap, :] = backs[i].astype(BF)
        dg = jnp.sum(dys[i][...].astype(F32) * sums[i], axis=1, keepdims=True)
        pad = jnp.where(eye[0:cap, :], dg, 0.0)
        dg_row = jnp.sum(pad, axis=0, keepdims=True)
        three = split3(dg_row)
        row = iota((16, lanes), 0)
        back[cap : cap + 16, :] = jnp.zeros((16, width), BF)
        back[cap : cap + 16, 0:lanes] = (
            jnp.where(row == 0, three[0].astype(F32), 0.0)
            + jnp.where(row == 1, three[1].astype(F32), 0.0)
            + jnp.where(row == 2, three[2].astype(F32), 0.0)
        ).astype(BF)


def expert(rows_in, dys, weights, cap):
    n = len(rows_in)
    width = rows_in[0].shape[1]
    ff = GROUP * width
    res = call(
        functools.partial(expert_kernel, cap, n),
        [VM] * (2 * n) + [HB] * GROUP,
        [
            shape((cap + 16, width), BF),
            shape((cap, width), BF),
            shape((cap, ff), BF),
            shape((cap, ff), BF),
            shape((cap, width), BF),
        ]
        * n,
        [
            pltpu.VMEM((GROUP, width, width), BF),
            pltpu.VMEM((GROUP, width, width), BF),
            pltpu.SemaphoreType.DMA((16,)),
        ],
        8 * n * cap * width * ff,
        4 * width * ff + n * cap * (4 * ff + 10 * width),
        "expert",
    )(*rows_in, *dys, *weights)
    return [res[5 * i : 5 * i + 5] for i in range(n)]


def grad_kernel(n, s_ref, *refs):
    lefts, rights, (give, keep) = refs[:n], refs[n : 2 * n], refs[2 * n : 2 * n + 2]
    if n == 1:
        left, right = lefts[0], rights[0]
    else:
        left, right = refs[2 * n + 2 :]
        rows = lefts[0].shape[0]
        for i in range(n):
            left[i * rows : (i + 1) * rows, :] = lefts[i][...]
            right[i * rows : (i + 1) * rows, :] = rights[i][...]
    value = dot_tn(left[...], right[...]).astype(BF)

    @pl.when(pl.program_id(0) == 0)
    def _():
        give[0] = value

    @pl.when(pl.program_id(0) == 1)
    def _():
        keep[0] = value


def weight_grad(s, lefts, rights, rows=None, weight=16):
    n = len(lefts)
    t = rows or lefts[0].shape[0]
    width = min(lefts[0].shape[1], rights[0].shape[1])
    high = width // 2
    m, nb = lefts[0].shape[1] // width, rights[0].shape[1] // width
    scratch = []
    if n > 1:
        scratch = [pltpu.VMEM((n * t, high), BF), pltpu.VMEM((n * t, width), BF)]
    left_at = lambda h, i, j, c: (0, jnp.where(h == 0, 1 - c[0], c[0]) * m + i)
    give_at = lambda h, i, j, c: (jnp.where(h == 0, i * nb + j, m * nb - 1), 0, 0)
    keep_at = lambda h, i, j, c: (jnp.where(h == 0, 0, i * nb + j), 0, 0)
    return pl.pallas_call(
        functools.partial(grad_kernel, n),
        grid_spec=pltpu.PrefetchScalarGridSpec(
            num_scalar_prefetch=1,
            grid=(2, m, nb),
            in_specs=[pl.BlockSpec((t, high), left_at)] * n
            + [pl.BlockSpec((t, width), lambda h, i, j, c: (0, j))] * n,
            out_specs=[pl.BlockSpec((1, high, width), at) for at in (give_at, keep_at)],
            scratch_shapes=scratch,
        ),
        out_shape=[shape((m * nb, high, width), BF)] * 2,
        compiler_params=pltpu.CompilerParams(vmem_limit_bytes=LIMIT),
        cost_estimate=pl.CostEstimate(
            flops=int(weight * 4) * n * t * m * high * width * nb,
            bytes_accessed=int(weight * 2) * (n * t * (2 * m * high + width * nb) + 2 * m * high * width * nb),
            transcendentals=0,
        ),
        name="weight_grad",
    )(s, *lefts, *rights)


def back_kernel(
    experts, cap, dy, dense, hid, gb_ref, router, place, route, live, soft, normed3, slope, fc1, fc2, *refs
):
    homes = refs[:experts]
    dmlp, dpre, dhidden, tiny, drouter = refs[experts : experts + 5]
    w1, w2, ups, sems = refs[experts + 5 :]
    rows, width = hid.shape
    copies = [
        pltpu.make_async_copy(fc1, w1, sems.at[0]),
        pltpu.make_async_copy(fc2, w2, sems.at[1]),
    ]
    for c in copies:
        c.start()
    lanes = -(-cap // WIDE) * WIDE
    spot = iota((lanes, rows), 0)
    spot = jnp.where(spot < cap, spot, -2 * experts * cap)
    dgate = [jnp.zeros((16, rows), F32) for _ in range(TOP)]
    for r in range(experts):
        tail = homes[r][cap : cap + 16, 0:lanes]
        hot = [jnp.where(spot + r * cap == place[k : k + 1, :], 1.0, 0.0).astype(BF) for k in range(TOP)]
        for k in range(TOP):
            dgate[k] = dgate[k] + dot(tail, hot[k])
        term = dot_tn((hot[0] + hot[1])[0:cap, :], homes[r][0:cap, :])
        ups[...] = term if r == 0 else ups[...] + term
    dgate = [jnp.sum(d, axis=0, keepdims=True) * live[...] for d in dgate]
    mix = soft[0:1, :] * dgate[0] + soft[1:2, :] * dgate[1]
    dsoft = [soft[k : k + 1, :] * (dgate[k] - mix) for k in range(TOP)]
    index = iota((router.shape[0], rows), 0)
    dlogits = sum(jnp.where(index == route[k : k + 1, :], dsoft[k], 0.0) for k in range(TOP))
    dlogits = dlogits.astype(BF)
    drouter[...] = dot(dlogits, normed3[...])
    ups[...] += dot_tn(dlogits, router[...])
    tile = rows // 6
    tiny[...] = jnp.zeros_like(tiny)

    def norm_back(at, values, gain, bias_row, base):
        n, scale = normalize(values)
        u = ups[at, :]
        tiny[bias_row - 1 : bias_row, :] += jnp.sum(u * n, axis=0, keepdims=True)
        tiny[bias_row : bias_row + 1, :] += jnp.sum(u, axis=0, keepdims=True)
        ug = u * gain
        dv = scale * (
            ug
            - jnp.mean(ug, axis=-1, keepdims=True)
            - n * jnp.mean(ug * n, axis=-1, keepdims=True)
        )
        return base + dv

    @pl.loop(0, 6)
    def _(i):
        at = pl.ds(pl.multiple_of(i * tile, 16), tile)
        dd = norm_back(at, dense[at, :], gb_ref[4:5, :], 5, dy[at, :].astype(F32))
        dhidden[at, :] = dd
        dmlp[at, :] = dd.astype(BF)

    for c in copies:
        c.wait()
    ups[...] = jnp.zeros_like(ups)

    @pl.loop(0, w1.shape[1] // 512)
    def _(j):
        at = pl.ds(pl.multiple_of(j * 512, 512), 512)
        dpre[:, at] = (dot_nt(dmlp[...], w2[at, :]) * slope[:, at].astype(F32)).astype(BF)
        ups[...] += dot_nt(dpre[:, at], w1[:, at])

    @pl.loop(0, 6)
    def _(i):
        at = pl.ds(pl.multiple_of(i * tile, 16), tile)
        dhidden[at, :] = norm_back(at, hid[at, :], gb_ref[2:3, :], 3, dhidden[at, :])


def back(
    dy, dense, hid, gb, router, place, route, live, soft, normed3, slope, fc1, fc2, homes, experts, cap, after
):
    rows, width = hid.shape
    ff = fc1.shape[1]
    return call(
        functools.partial(back_kernel, experts, cap),
        [VM] * 11 + [HB] * 2 + [VM] * experts,
        [
            shape((rows, width), BF),
            shape((rows, ff), BF),
            shape((rows, width), F32),
            shape((8, width), F32),
            shape(router.shape, F32),
        ],
        [
            pltpu.VMEM((width, ff), BF),
            pltpu.VMEM((ff, width), BF),
            pltpu.VMEM((rows, width), F32),
            pltpu.SemaphoreType.DMA((2,)),
        ],
        4 * rows * width * ff + 2 * rows * width * experts * cap,
        4 * width * ff + rows * (4 * ff + 18 * width),
        "dense_backward",
        after,
    )(dy, dense, hid, gb, router, place, route, live, soft, normed3, slope, fc1, fc2, *homes)


def attend_back_kernel(
    s_ref, dhid, id_row, id_col, packed, lse, wo_a, wo_b, dattn, dpacked, wo, bias, dctx, sems
):
    s = s_ref[0]
    rows, width = dhid.shape
    copies = halves_into(s, wo_a, wo_b, wo, sems, 0)
    for c in copies:
        c.start()
    tile = rows // 6

    @pl.loop(0, 6)
    def _(i):
        at = pl.ds(pl.multiple_of(i * tile, 16), tile)
        dattn[at, :] = dhid[at, :].astype(BF)
        bias[at, :] = jnp.where(id_col[at, :] == id_row[...], 0.0, MASKED)

    copies[0].wait()
    copies[1].wait()

    @pl.loop(0, width // 256)
    def _(j):
        at = pl.ds(pl.multiple_of(j * 256, 256), 256)
        dctx[:, at] = dot_nt(dattn[...], wo[at, :]).astype(BF)

    lane = iota((1, WIDE), 1)

    @pl.loop(0, width // WIDE)
    def _(pair):
        col = pl.multiple_of(pair * WIDE, WIDE)
        q = packed[:, pl.ds(col, WIDE)] * jnp.asarray(HEAD**-0.5, BF)
        keys = packed[:, pl.ds(width + col, WIDE)]
        values = packed[:, pl.ds(2 * width + col, WIDE)]
        dc = dctx[:, pl.ds(col, WIDE)]
        dq, dk, dv = [], [], []
        for h in range(2):
            mine = (lane >= h * HEAD) & (lane < (h + 1) * HEAD)
            scores = dot_nt(jnp.where(mine, keys, jnp.zeros_like(keys)), q) + bias[...]
            p = jnp.exp(scores - lse[pl.ds(2 * pair + h, 1), :])
            dp = dot_nt(jnp.where(mine, values, jnp.zeros_like(values)), dc)
            inner = jnp.sum(p * dp, axis=0, keepdims=True)
            ds = (p * (dp - inner)).astype(BF)
            dv.append(dot(p.astype(BF), dc))
            dk.append(dot(ds, q))
            dq.append(dot_tn(ds, keys) * HEAD**-0.5)
        low = lane < HEAD
        dpacked[:, pl.ds(col, WIDE)] = jnp.where(low, dq[0], dq[1]).astype(BF)
        dpacked[:, pl.ds(width + col, WIDE)] = jnp.where(low, dk[0], dk[1]).astype(BF)
        dpacked[:, pl.ds(2 * width + col, WIDE)] = jnp.where(low, dv[0], dv[1]).astype(BF)


def input_kernel(s_ref, x_ref, dhid, gb_ref, dpacked, qkv_a, qkv_b, grad_in, tiny, wq, ups, sems):
    s = s_ref[0]
    rows, width = x_ref.shape
    tile = rows // 6
    copies = halves_into(s, qkv_a, qkv_b, wq, sems, 0)
    for c in copies:
        c.start()
    copies[0].wait()
    copies[1].wait()

    @pl.loop(0, width // 256)
    def _(j):
        at = pl.ds(pl.multiple_of(j * 256, 256), 256)
        ups[:, at] = dot_nt(dpacked[...], wq[at, :])

    tiny[...] = jnp.zeros_like(tiny)

    @pl.loop(0, 6)
    def _(i):
        at = pl.ds(pl.multiple_of(i * tile, 16), tile)
        n, scale = normalize(x_ref[at, :].astype(F32))
        u = ups[at, :]
        tiny[0:1, :] += jnp.sum(u * n, axis=0, keepdims=True)
        tiny[1:2, :] += jnp.sum(u, axis=0, keepdims=True)
        ug = u * gb_ref[0:1, :]
        grad_in[at, :] = dhid[at, :] + scale * (
            ug
            - jnp.mean(ug, axis=-1, keepdims=True)
            - n * jnp.mean(ug * n, axis=-1, keepdims=True)
        )


def attend_back(s, dhid, ids, packed, lse, wo, after):
    rows, width = dhid.shape
    n3 = packed.shape[1]
    return call(
        attend_back_kernel,
        [SM] + [VM] * 5 + [HB] * 2,
        [shape((rows, width), BF), shape((rows, n3), BF)],
        [
            pltpu.VMEM((width, width), BF),
            pltpu.VMEM((rows, rows), F32),
            pltpu.VMEM((rows, width), BF),
            pltpu.SemaphoreType.DMA((2,)),
        ],
        2 * rows * width * width + 20 * rows * rows * width,
        2 * (width * width + rows * (3 * width + 2 * n3)),
        "attention_backward",
        after,
    )(s, dhid, ids[None, :], ids[:, None], packed, lse, *wo)


def input_back(s, x, dhid, gb, dpacked, qkv, after):
    rows, width = x.shape
    n3 = dpacked.shape[1]
    return call(
        input_kernel,
        [SM] + [VM] * 4 + [HB] * 2,
        [shape((rows, width), F32), shape((8, width), F32)],
        [
            pltpu.VMEM((width, n3), BF),
            pltpu.VMEM((rows, width), F32),
            pltpu.SemaphoreType.DMA((2,)),
        ],
        2 * rows * width * n3,
        2 * (width * n3 + rows * n3) + 10 * rows * width,
        "input_backward",
        after,
        0.5,
    )(s, x, dhid, gb, dpacked, *qkv)


def merge_kernel(experts, cap, dense, place, *refs):
    outs, result = refs[:experts], refs[experts]
    rows = dense.shape[0]
    total = dense[...]
    spot = iota((cap, rows), 0)
    for r in range(experts):
        hot = sum(jnp.where(spot + r * cap == place[k : k + 1, :], 1.0, 0.0) for k in range(TOP))
        total = total + dot_tn(hot.astype(BF), outs[r][...])
    result[...] = total.astype(BF)


def merge(dense, place, outs, experts, cap):
    rows, width = dense.shape
    return call(
        functools.partial(merge_kernel, experts, cap),
        [VM] * (2 + experts),
        shape((rows, width), BF),
        [],
        2 * rows * width * experts * cap,
        rows * width * 6 + 2 * experts * cap * width,
        "merge",
        (),
        0.25,
    )(dense, place, *outs)


def hold_kernel(n, *refs):
    for i in range(n):
        refs[n + i][...] = refs[i][...]


def hold(chunks, after):
    n = len(chunks)
    dims = chunks[0].shape
    return call(
        functools.partial(hold_kernel, n),
        [VM] * n,
        [shape(dims, BF)] * n,
        [],
        0,
        4 * n * dims[0] * dims[1],
        "hold",
        after,
    )(*chunks)


def finish_kernel(columns, blocks, out):
    n, high, width = blocks.shape
    for i in range(n):
        value = blocks[i].astype(F32)
        if columns:
            out[:, i * width : (i + 1) * width] = value
        else:
            out[i * high : (i + 1) * high, :] = value


def finish(blocks, columns):
    n, high, width = blocks.shape
    dims = (high, n * width) if columns else (n * high, width)
    return call(
        functools.partial(finish_kernel, columns),
        [VM],
        shape(dims, F32),
        [],
        0,
        6 * n * high * width,
        "finish",
    )(blocks)


def spread_kernel(experts, cap, rows_in, place, *chunks):
    spot = iota((cap, rows_in.shape[0]), 0)
    for r in range(experts):
        hot = sum(jnp.where(spot + r * cap == place[k : k + 1, :], 1.0, 0.0) for k in range(TOP))
        chunks[r][...] = dot(hot.astype(BF), rows_in[...]).astype(BF)


def spread(rows_in, place, experts, cap):
    rows, width = rows_in.shape
    return call(
        functools.partial(spread_kernel, experts, cap),
        [VM, VM],
        [shape((cap, width), BF)] * experts,
        [],
        2 * rows * width * experts * cap,
        2 * (rows + experts * cap) * width,
        "spread",
    )(rows_in, place)


def places_of(routes, live, experts, capacity):
    tokens = routes.shape[0]
    ids = jnp.arange(experts, dtype=jnp.int32)
    match = [
        ((routes[:, k : k + 1] == ids[None, :]) & live[:, None]).astype(F32) for k in range(TOP)
    ]
    order = jnp.arange(tokens, dtype=jnp.int32)
    below = (order[:, None] > order[None, :]).astype(BF)
    before = jnp.zeros((1, experts), F32)
    out = []
    for k in range(TOP):
        counts = dot(below, match[k].astype(BF)) + before
        before = before + jnp.sum(match[k], axis=0, keepdims=True)
        within = jnp.sum(counts * match[k], axis=1).astype(jnp.int32)
        out.append(jnp.where(live, routes[:, k] * capacity + within, experts * capacity))
    return out

def local(
    tokens,
    image_ids,
    routes,
    norm1_gain,
    norm1_bias,
    qkv_weight,
    attn_out_weight,
    norm2_gain,
    norm2_bias,
    fc1_weight,
    fc2_weight,
    norm3_gain,
    norm3_bias,
    router_weight,
    expert_up,
    expert_down,
    cotangent,
):
    s = lax.axis_index("section")
    e = lax.axis_index("dp") // GROUP
    q = lax.axis_index("dp") % GROUP
    dp_count = lax.axis_size("dp")
    experts = dp_count // GROUP
    cap = GROUP * ((21 * SLOTS + 10 * experts * GROUP - 1) // (10 * experts * GROUP))
    cap = -(-cap // 16) * 16
    half = tokens.shape[1]
    width = 2 * half
    few = experts <= 8
    planes = [[p * GROUP + i for p in range(experts)] for i in range(GROUP)]
    here = jnp.reshape(s, (1,))

    def swap(v):
        return lax.ppermute(v, "section", [(0, 1), (1, 0)])

    def over_q(v, bit):
        return lax.ppermute(v, "dp", [(i, i ^ bit) for i in range(dp_count)])

    def over_e(v, r):
        return lax.ppermute(
            v,
            "dp",
            [(i, ((i // GROUP + r) % experts) * GROUP + i % GROUP) for i in range(dp_count)],
        )

    def part(v, index, size, axis=0):
        return lax.dynamic_slice_in_dim(v, index * size, size, axis)

    def join(own, other, axis):
        return jnp.where(
            s == 0,
            jnp.concatenate([own, other], axis=axis),
            jnp.concatenate([other, own], axis=axis),
        )

    def add(a, b):
        return (a.astype(F32) + b.astype(F32)).astype(BF)

    def out_chunks(chunks):
        if not few:
            return list(lax.all_to_all(jnp.stack(chunks), "dp", 0, 0, axis_index_groups=planes))
        return [chunks[0]] + [over_e(chunks[r], r) for r in range(1, experts)]

    def home_chunks(chunks):
        if not few:
            return list(lax.all_to_all(jnp.stack(chunks), "dp", 0, 0, axis_index_groups=planes))
        return [chunks[0]] + [over_e(chunks[r], experts - r) for r in range(1, experts)]

    small = jnp.stack([norm1_gain, norm1_bias, norm2_gain, norm2_bias, norm3_gain, norm3_bias])
    small = jnp.concatenate([small, jnp.transpose(router_weight)])
    small = join(small, swap(small), 1)
    x = join(part(tokens, s, SLOTS), swap(part(tokens, 1 - s, SLOTS)), 1)
    dy = join(part(cotangent, s, SLOTS), swap(part(cotangent, 1 - s, SLOTS)), 1)
    ids = part(image_ids, s, 1).reshape(-1)
    route = part(routes, s, SLOTS)
    live = ids >= 0
    gb = jnp.concatenate([small[:6], jnp.zeros((2, width), BF)]).astype(F32)
    router_rows = -(-experts // 16) * 16
    router = jnp.concatenate([small[6 : 6 + experts], jnp.zeros((router_rows - experts, width), BF)])
    qkv, wo = (qkv_weight, swap(qkv_weight)), (attn_out_weight, swap(attn_out_weight))

    pair = jnp.stack([expert_up, expert_down])
    from_x, from_y = over_q(pair, 1), over_q(pair, 2)

    def gather(v, tiled):
        return lax.all_gather(v, "section", axis=0, tiled=tiled)

    tie = lax.optimization_barrier
    (x, qkv, wo, fc2_weight, pair_late) = tie((x, qkv, wo, fc2_weight, pair))
    fc1, fc2 = gather(fc1_weight, True), gather(fc2_weight, True)
    weights = [gather(pair_late, False)]

    if few:
        distance = (route - e) % experts
    else:
        distance = route
    spots = places_of(distance, live, experts, cap)
    place = jnp.stack(spots + [jnp.full_like(spots[0], -1)] * 6)
    route_rows = jnp.concatenate([jnp.transpose(route), jnp.full((6, SLOTS), -1, jnp.int32)])
    live_row = live.astype(F32)[None, :]
    dy_sent = spread(dy, place, experts, cap)
    dy_out = out_chunks(dy_sent)

    normed1, packed, context, lse, hidden = front(here, x, ids, gb, qkv, wo, dy_sent[:1])
    hidden, from_x, from_y, *dy_out[:-1] = tie((hidden, from_x, from_y, *dy_out[:-1]))
    weights += [gather(from_x, False), gather(from_y, False)]
    far = [over_q(from_x[0], 2), over_q(from_y[1], 1)]
    normed2, act, slope, dense, normed3, soft, *sent = mlp(
        hidden, gb, router, place, route_rows, live_row, fc1, fc2, experts, cap, []
    )
    sent, far, dy_out[-1] = tie((sent, far, dy_out[-1]))
    weights.append(gather(jnp.stack(far), False))
    got = out_chunks(sent)

    step = max(1, experts // 4)
    results = [None] * experts
    previous = None
    for i in [0] + list(range(experts - step, 0, -step)):
        if i:
            got[i], results[previous] = tie((got[i], results[previous]))
        results[i : i + step] = expert(got[i : i + step], dy_out[i : i + step], weights, cap)
        previous = i
    homes = home_chunks([r[0] for r in results])
    acts, dinners, scaled = ([r[i] for r in results] for i in (2, 3, 4))

    def grad_sum(*operands, weight=16):
        give, keep = weight_grad(here, *operands, weight=weight)
        return add(keep, swap(give))

    if few:
        dinners, homes[-1] = tie((dinners, homes[-1]))
        acts, homes[-2] = tie((acts, homes[-2]))
    sum_up, sum_down = grad_sum(got, dinners, cap), grad_sum(scaled, acts)
    dmlp, dpre, dhidden, tiny23, drouter = back(
        dy, dense, hidden, gb, router, place, route_rows, live_row, soft, normed3, slope,
        fc1, fc2, homes, experts, cap, [],
    )
    moved_up = over_q(jnp.stack([sum_up[1], sum_up[3]]), 1)
    moved_down = over_q(sum_down[2:], 2)
    outs = home_chunks(hold([r[1] for r in results], [dmlp]))
    grads1, grads2 = weight_grad(here, [normed2], [dpre]), weight_grad(here, [act], [dmlp])
    dhidden, grads1, grads2, moved_up, moved_down = tie(
        (dhidden, grads1, grads2, moved_up, moved_down)
    )
    mlp_sums = tuple(add(keep, swap(give)) for give, keep in (grads1, grads2))
    near_up, far_up = add(sum_up[0], moved_up[0]), add(sum_up[2], moved_up[1])
    near_down, far_down = add(sum_down[0], moved_down[0]), add(sum_down[1], moved_down[1])
    dattn, dpacked = attend_back(here, dhidden, ids, packed, lse, wo, [])
    far_up, far_down = over_q(far_up, 2), over_q(far_down, 1)
    dpacked, dattn, mlp_sums = tie((dpacked, dattn, mlp_sums))
    grad_fc1, grad_fc2 = lax.psum(mlp_sums, "dp")
    dpacked, dattn, outs = tie((dpacked, dattn, outs))
    grad_qkv, grad_wo = (
        grad_sum([normed1], [dpacked], weight=0.5),
        grad_sum([context], [dattn], weight=0.5),
    )
    outs, far_up, far_down = tie((outs, far_up, far_down))
    half_up = near_up.astype(F32) + far_up.astype(F32)
    half_down = near_down.astype(F32) + far_down.astype(F32)
    grad_in, tiny1 = input_back(here, x, dhidden, gb, dpacked, qkv, [])
    block_out = merge(dense, place, outs, experts, cap)
    grad_qkv, grad_wo, grad_fc1, grad_fc2 = tie((grad_qkv, grad_wo, grad_fc1, grad_fc2))
    grad_qkv, grad_wo = lax.psum((grad_qkv, grad_wo), "dp")

    def rejoin(v):
        return join(part(v, s, half, 1), swap(part(v, 1 - s, half, 1)), 0)

    sum_fc1, sum_fc2 = finish(grad_fc1, True), finish(grad_fc2, False)
    sum_qkv, sum_attn = finish(grad_qkv, True), finish(grad_wo, False)

    tiny = jnp.concatenate([tiny1[:2], tiny23[2:6], drouter[:experts]])
    tiny = part(tiny, s, half, 1) + swap(part(tiny, 1 - s, half, 1))
    tiny = tiny + over_q(tiny, 1)
    tiny = tiny + over_q(tiny, 2)
    total = tiny
    if few:
        for r in range(1, experts):
            total = total + over_e(tiny, r)
    else:
        total = lax.psum(tiny, "dp", axis_index_groups=planes)
    return (
        rejoin(block_out),
        rejoin(grad_in),
        total[0],
        total[1],
        sum_qkv,
        sum_attn,
        total[2],
        total[3],
        sum_fc1,
        sum_fc2,
        total[4],
        total[5],
        jnp.transpose(total[6:]),
        half_up,
        half_down,
    )


def solution(mesh):
    placed = (
        P("dp", "section"),
        P("dp", None),
        P("dp", None),
        P("section"),
        P("section"),
        P("section", None),
        P("section", None),
        P("section"),
        P("section"),
        P("section", None),
        P("section", None),
        P("section"),
        P("section"),
        P("section", None),
        P("section", "dp"),
        P("section", "dp"),
        P("dp", "section"),
    )
    return jax.shard_map(
        local,
        mesh=mesh,
        in_specs=placed,
        out_specs=(
            P("dp", "section"),
            P("dp", "section"),
            P("section"),
            P("section"),
            P("section", None),
            P("section", None),
            P("section"),
            P("section"),
            P("section", None),
            P("section", None),
            P("section"),
            P("section"),
            P("section", None),
            P("section", "dp"),
            P("section", "dp"),
        ),
        check_vma=False,
    )
```

```python
import functools

import jax
import jax.numpy as jnp
from jax import lax
from jax.experimental import pallas as pl
from jax.experimental.pallas import tpu as pltpu
from jax.sharding import PartitionSpec as P

HEAD = 64
TOP = 2
GROUP = 4
SLOTS = 576
WIDE = 128

EPSILON = 1e-06
MASKED = -1e30
BF = jnp.bfloat16
F32 = jnp.float32
LIMIT = 60 * 1024 * 1024


def dot(a, b):
    return jnp.dot(a, b, preferred_element_type=F32)


def dot_nt(a, b):
    return lax.dot_general(a, b, (((1,), (1,)), ((), ())), preferred_element_type=F32)


def dot_tn(a, b):
    return lax.dot_general(a, b, (((0,), (0,)), ((), ())), preferred_element_type=F32)


def normalize(v):
    center = v - jnp.mean(v, axis=-1, keepdims=True)
    scale = lax.rsqrt(jnp.mean(center * center, axis=-1, keepdims=True) + EPSILON)
    return center * scale, scale


def gelu_pair(x):
    bell = jnp.exp(x * x * -0.5)
    t = 1.0 / (1.0 + jnp.abs(x) * (0.3275911 * 0.5**0.5))
    tail = (
        t
        * (
            0.127414796
            + t * (-0.142248368 + t * (0.7107068705 + t * (-0.7265760135 + t * 0.5307027145)))
        )
        * bell
    )
    cdf = jnp.where(x >= 0.0, 1.0 - tail, tail)
    return x * cdf, cdf + x * (bell * 0.3989422804014327)


def iota(shape, axis):
    return lax.broadcasted_iota(jnp.int32, shape, axis)


def halves_into(s, own, other, dest, sems, first):
    rows = own.shape[0]
    return [
        pltpu.make_async_copy(own, dest.at[pl.ds(pl.multiple_of(s * rows, rows), rows)], sems.at[first]),
        pltpu.make_async_copy(
            other, dest.at[pl.ds(pl.multiple_of((1 - s) * rows, rows), rows)], sems.at[first + 1]
        ),
    ]


def split3(v):
    hi = v.astype(BF)
    rest = v - hi.astype(F32)
    mid = rest.astype(BF)
    low = (rest - mid.astype(F32)).astype(BF)
    return hi, mid, low


VM = pl.BlockSpec(memory_space=pltpu.VMEM)
SM = pl.BlockSpec(memory_space=pltpu.SMEM)
HB = pl.BlockSpec(memory_space=pl.ANY)


def call(kernel, in_specs, out_shape, scratch, flops, moved, name, after=(), weight=16):
    count, extra = len(in_specs), len(after)

    def body(*refs):
        kernel(*refs[:count], *refs[count + extra :])

    made = pl.pallas_call(
        body,
        in_specs=in_specs + [HB] * extra,
        out_specs=jax.tree.map(lambda _: VM, out_shape),
        out_shape=out_shape,
        scratch_shapes=scratch,
        compiler_params=pltpu.CompilerParams(vmem_limit_bytes=LIMIT),
        cost_estimate=pl.CostEstimate(
            flops=int(weight * flops), bytes_accessed=int(weight * moved), transcendentals=0
        ),
        name=name,
    )
    return lambda *operands: made(*operands, *after)


def shape(dims, kind):
    return jax.ShapeDtypeStruct(dims, kind)


def front_kernel(
    s_ref, x_ref, id_row, id_col, gb_ref, qkv_a, qkv_b, wo_a, wo_b,
    normed, packed, context, lse, hidden,
    wq, wo, bias, lse_col, sems,
):
    s = s_ref[0]
    rows, width = x_ref.shape
    copies = halves_into(s, qkv_a, qkv_b, wq, sems, 0) + halves_into(s, wo_a, wo_b, wo, sems, 2)
    for c in copies:
        c.start()
    tile = rows // 6

    @pl.loop(0, 6)
    def _(i):
        at = pl.ds(pl.multiple_of(i * tile, 16), tile)
        n, _ = normalize(x_ref[at, :].astype(F32))
        normed[at, :] = (n * gb_ref[0:1, :] + gb_ref[1:2, :]).astype(BF)
        bias[at, :] = jnp.where(id_col[at, :] == id_row[...], 0.0, MASKED)

    copies[0].wait()
    copies[1].wait()

    @pl.loop(0, wq.shape[1] // 256)
    def _(j):
        at = pl.ds(pl.multiple_of(j * 256, 256), 256)
        packed[:, at] = dot(normed[...], wq[:, at]).astype(BF)

    lane = iota((1, WIDE), 1)
    lse_col[...] = jnp.zeros_like(lse_col)
    third = rows // 3

    @pl.loop(0, width // WIDE)
    def _(pair):
        col = pl.multiple_of(pair * WIDE, WIDE)
        keys = packed[:, pl.ds(width + col, WIDE)]
        values = packed[:, pl.ds(2 * width + col, WIDE)]
        for r in range(3):
            at = slice(r * third, (r + 1) * third)
            q = packed[at, pl.ds(col, WIDE)] * jnp.asarray(HEAD**-0.5, BF)
            outs = []
            sums = lse_col[at, :]
            for h in range(2):
                mine = (lane >= h * HEAD) & (lane < (h + 1) * HEAD)
                scores = dot_nt(jnp.where(mine, q, jnp.zeros_like(q)), keys) + bias[at, :]
                top = jnp.max(scores, axis=1, keepdims=True)
                p = jnp.exp(scores - top)
                total = jnp.sum(p, axis=1, keepdims=True)
                outs.append(dot(p.astype(BF), values) * (1.0 / total))
                sums = jnp.where(lane == 2 * pair + h, top + jnp.log(total), sums)
            lse_col[at, :] = sums
            context[at, pl.ds(col, WIDE)] = jnp.where(lane < HEAD, outs[0], outs[1]).astype(BF)

    lse[...] = jnp.transpose(lse_col[...])[0 : lse.shape[0], :]
    copies[2].wait()
    copies[3].wait()

    @pl.loop(0, width // 256)
    def _(j):
        at = pl.ds(pl.multiple_of(j * 256, 256), 256)
        hidden[:, at] = x_ref[:, at].astype(F32) + dot(context[...], wo[:, at])


def front(s, x, ids, gb, qkv, wo, after):
    rows, width = x.shape
    n3 = qkv[0].shape[1]
    return call(
        front_kernel,
        [SM, VM, VM, VM, VM, HB, HB, HB, HB],
        [
            shape((rows, width), BF),
            shape((rows, n3), BF),
            shape((rows, width), BF),
            shape((16, rows), F32),
            shape((rows, width), F32),
        ],
        [
            pltpu.VMEM((width, n3), BF),
            pltpu.VMEM((width, width), BF),
            pltpu.VMEM((rows, rows), F32),
            pltpu.VMEM((rows, WIDE), F32),
            pltpu.SemaphoreType.DMA((4,)),
        ],
        2 * rows * width * (n3 + width) + 4 * rows * rows * width,
        2 * (width * (n3 + width) + rows * (3 * width + n3)) + 4 * rows * width,
        "attention_forward",
        after,
    )(s, x, ids[None, :], ids[:, None], gb, *qkv, *wo)


def mlp_kernel(experts, cap, hid, gb_ref, router, place, route, live, fc1, fc2, *refs):
    normed2, act, slope, dense, normed3, soft = refs[:6]
    chunks = refs[6 : 6 + experts]
    w1, w2, sems = refs[6 + experts :]
    rows, width = hid.shape
    copies = [
        pltpu.make_async_copy(fc1, w1, sems.at[0]),
        pltpu.make_async_copy(fc2, w2, sems.at[1]),
    ]
    for c in copies:
        c.start()
    tile = rows // 6

    @pl.loop(0, 6)
    def _(i):
        at = pl.ds(pl.multiple_of(i * tile, 16), tile)
        n, _ = normalize(hid[at, :])
        normed2[at, :] = (n * gb_ref[2:3, :] + gb_ref[3:4, :]).astype(BF)
        dense[at, :] = hid[at, :]

    for c in copies:
        c.wait()

    @pl.loop(0, w1.shape[1] // 512)
    def _(j):
        at = pl.ds(pl.multiple_of(j * 512, 512), 512)
        a, sl = gelu_pair(dot(normed2[...], w1[:, at]))
        act[:, at] = a.astype(BF)
        slope[:, at] = sl.astype(BF)
        dense[...] += dot(act[:, at], w2[at, :])

    @pl.loop(0, 6)
    def _(i):
        at = pl.ds(pl.multiple_of(i * tile, 16), tile)
        n, _ = normalize(dense[at, :])
        normed3[at, :] = (n * gb_ref[4:5, :] + gb_ref[5:6, :]).astype(BF)

    logits = dot_nt(router[...], normed3[...])
    expert = iota(logits.shape, 0)
    chosen = [
        jnp.sum(jnp.where(expert == route[k : k + 1, :], logits, 0.0), axis=0, keepdims=True)
        for k in range(TOP)
    ]
    top = jnp.maximum(chosen[0], chosen[1])
    raised = [jnp.exp(c - top) for c in chosen]
    total = raised[0] + raised[1]
    pieces = []
    for k in range(TOP):
        share = raised[k] / total
        soft[k : k + 1, :] = share
        three = split3(share * live[...])
        row = iota((16, rows), 0)
        pieces.append(
            jnp.where(row == 0, three[0].astype(F32), 0.0)
            + jnp.where(row == 1, three[1].astype(F32), 0.0)
            + jnp.where(row == 2, three[2].astype(F32), 0.0)
        )
    pieces = [p.astype(BF) for p in pieces]
    lanes = -(-cap // WIDE) * WIDE
    spot = iota((lanes, rows), 0)
    spot = jnp.where(spot < cap, spot, -2 * experts * cap)
    for r in range(experts):
        hot = [jnp.where(spot + r * cap == place[k : k + 1, :], 1.0, 0.0).astype(BF) for k in range(TOP)]
        both = (hot[0] + hot[1])[0:cap, :]
        chunks[r][0:cap, :] = dot(both, normed3[...]).astype(BF)
        chunks[r][cap : cap + 16, :] = jnp.zeros((16, width), BF)
        chunks[r][cap : cap + 16, 0:lanes] = (
            dot_nt(pieces[0], hot[0]) + dot_nt(pieces[1], hot[1])
        ).astype(BF)


def mlp(hid, gb, router, place, route, live, fc1, fc2, experts, cap, after):
    rows, width = hid.shape
    ff = fc1.shape[1]
    return call(
        functools.partial(mlp_kernel, experts, cap),
        [VM, VM, VM, VM, VM, VM, HB, HB],
        [
            shape((rows, width), BF),
            shape((rows, ff), BF),
            shape((rows, ff), BF),
            shape((rows, width), F32),
            shape((rows, width), BF),
            shape((8, rows), F32),
        ]
        + [shape((cap + 16, width), BF)] * experts,
        [
            pltpu.VMEM((width, ff), BF),
            pltpu.VMEM((ff, width), BF),
            pltpu.SemaphoreType.DMA((2,)),
        ],
        4 * rows * width * ff + 2 * rows * width * experts * cap,
        4 * width * ff + rows * (4 * ff + 12 * width),
        "dense_forward",
        after,
    )(hid, gb, router, place, route, live, fc1, fc2)


def expert_kernel(cap, n, *refs):
    rows_in, dys, weights = refs[:n], refs[n : 2 * n], refs[2 * n : 2 * n + GROUP]
    outs = refs[2 * n + GROUP : -3]
    wu, wd, sems = refs[-3:]
    width = wu.shape[1]
    half = width // 2
    copies = [
        [
            pltpu.make_async_copy(
                weights[b].at[h, u], w.at[b, h * half : (h + 1) * half], sems.at[4 * b + 2 * h + u]
            )
            for h in range(2)
            for u, w in enumerate((wu, wd))
        ]
        for b in range(GROUP)
    ]
    for b in range(GROUP):
        for c in copies[b]:
            c.start()
    lanes = -(-cap // WIDE) * WIDE
    eye = iota((lanes, lanes), 0) == iota((lanes, lanes), 1)
    gates = []
    for i in range(n):
        back, out, act, dinner, gp = outs[5 * i : 5 * i + 5]
        g = jnp.sum(rows_in[i][cap : cap + 16, 0:lanes].astype(F32), axis=0, keepdims=True)
        gate = jnp.sum(jnp.where(eye, g, 0.0), axis=1, keepdims=True)[0:cap, :]
        gp[...] = (gate * dys[i][...].astype(F32)).astype(BF)
        gates.append(gate)
    sums = [None] * n
    backs = [None] * n
    for b in range(GROUP):
        for c in copies[b]:
            c.wait()
        at = slice(b * width, (b + 1) * width)
        for i in range(n):
            back, out, act, dinner, gp = outs[5 * i : 5 * i + 5]
            a, slope = gelu_pair(dot(rows_in[i][0:cap, :], wu[b]))
            act[:, at] = a.astype(BF)
            dinner[:, at] = (dot(gp[...], wd[b]) * slope).astype(BF)
            o = dot_nt(act[:, at], wd[b])
            d = dot_nt(dinner[:, at], wu[b])
            sums[i] = o if b == 0 else sums[i] + o
            backs[i] = d if b == 0 else backs[i] + d
    for i in range(n):
        back, out, act, dinner, gp = outs[5 * i : 5 * i + 5]
        out[...] = (gates[i] * sums[i]).astype(BF)
        back[0:cap, :] = backs[i].astype(BF)
        dg = jnp.sum(dys[i][...].astype(F32) * sums[i], axis=1, keepdims=True)
        pad = jnp.where(eye[0:cap, :], dg, 0.0)
        dg_row = jnp.sum(pad, axis=0, keepdims=True)
        three = split3(dg_row)
        row = iota((16, lanes), 0)
        back[cap : cap + 16, :] = jnp.zeros((16, width), BF)
        back[cap : cap + 16, 0:lanes] = (
            jnp.where(row == 0, three[0].astype(F32), 0.0)
            + jnp.where(row == 1, three[1].astype(F32), 0.0)
            + jnp.where(row == 2, three[2].astype(F32), 0.0)
        ).astype(BF)


def expert(rows_in, dys, weights, cap):
    n = len(rows_in)
    width = rows_in[0].shape[1]
    ff = GROUP * width
    res = call(
        functools.partial(expert_kernel, cap, n),
        [VM] * (2 * n) + [HB] * GROUP,
        [
            shape((cap + 16, width), BF),
            shape((cap, width), BF),
            shape((cap, ff), BF),
            shape((cap, ff), BF),
            shape((cap, width), BF),
        ]
        * n,
        [
            pltpu.VMEM((GROUP, width, width), BF),
            pltpu.VMEM((GROUP, width, width), BF),
            pltpu.SemaphoreType.DMA((16,)),
        ],
        8 * n * cap * width * ff,
        4 * width * ff + n * cap * (4 * ff + 10 * width),
        "expert",
    )(*rows_in, *dys, *weights)
    return [res[5 * i : 5 * i + 5] for i in range(n)]


def grad_kernel(n, s_ref, *refs):
    lefts, rights, (give, keep) = refs[:n], refs[n : 2 * n], refs[2 * n : 2 * n + 2]
    if n == 1:
        left, right = lefts[0], rights[0]
    else:
        left, right = refs[2 * n + 2 :]
        rows = lefts[0].shape[0]
        for i in range(n):
            left[i * rows : (i + 1) * rows, :] = lefts[i][...]
            right[i * rows : (i + 1) * rows, :] = rights[i][...]
    value = dot_tn(left[...], right[...]).astype(BF)

    @pl.when(pl.program_id(0) == 0)
    def _():
        give[0] = value

    @pl.when(pl.program_id(0) == 1)
    def _():
        keep[0] = value


def weight_grad(s, lefts, rights, rows=None, weight=16):
    n = len(lefts)
    t = rows or lefts[0].shape[0]
    width = min(lefts[0].shape[1], rights[0].shape[1])
    high = width // 2
    m, nb = lefts[0].shape[1] // width, rights[0].shape[1] // width
    scratch = []
    if n > 1:
        scratch = [pltpu.VMEM((n * t, high), BF), pltpu.VMEM((n * t, width), BF)]
    left_at = lambda h, i, j, c: (0, jnp.where(h == 0, 1 - c[0], c[0]) * m + i)
    give_at = lambda h, i, j, c: (jnp.where(h == 0, i * nb + j, m * nb - 1), 0, 0)
    keep_at = lambda h, i, j, c: (jnp.where(h == 0, 0, i * nb + j), 0, 0)
    return pl.pallas_call(
        functools.partial(grad_kernel, n),
        grid_spec=pltpu.PrefetchScalarGridSpec(
            num_scalar_prefetch=1,
            grid=(2, m, nb),
            in_specs=[pl.BlockSpec((t, high), left_at)] * n
            + [pl.BlockSpec((t, width), lambda h, i, j, c: (0, j))] * n,
            out_specs=[pl.BlockSpec((1, high, width), at) for at in (give_at, keep_at)],
            scratch_shapes=scratch,
        ),
        out_shape=[shape((m * nb, high, width), BF)] * 2,
        compiler_params=pltpu.CompilerParams(vmem_limit_bytes=LIMIT),
        cost_estimate=pl.CostEstimate(
            flops=int(weight * 4) * n * t * m * high * width * nb,
            bytes_accessed=int(weight * 2) * (n * t * (2 * m * high + width * nb) + 2 * m * high * width * nb),
            transcendentals=0,
        ),
        name="weight_grad",
    )(s, *lefts, *rights)


def attention_grad_kernel(s_ref, normed, context, dpacked, dattn, give, keep):
    j = pl.program_id(1)

    def write(value):
        @pl.when(pl.program_id(0) == 0)
        def _():
            give[0] = value

        @pl.when(pl.program_id(0) == 1)
        def _():
            keep[0] = value

    @pl.when(j < 3)
    def _():
        write(dot_tn(normed[...], dpacked[...]).astype(BF))

    @pl.when(j == 3)
    def _():
        write(dot_tn(context[...], dattn[...]).astype(BF))


def attention_grad(s, normed, context, dpacked, dattn):
    t, width = normed.shape
    high = width // 2
    half_at = lambda h, j, c: (0, jnp.where(h == 0, 1 - c[0], c[0]))
    return pl.pallas_call(
        attention_grad_kernel,
        grid_spec=pltpu.PrefetchScalarGridSpec(
            num_scalar_prefetch=1,
            grid=(2, 4),
            in_specs=[
                pl.BlockSpec((t, high), half_at),
                pl.BlockSpec((t, high), half_at),
                pl.BlockSpec((t, width), lambda h, j, c: (0, jnp.minimum(j, 2))),
                pl.BlockSpec((t, width), lambda h, j, c: (0, 0)),
            ],
            out_specs=[
                pl.BlockSpec((1, high, width), lambda h, j, c: (jnp.where(h == 0, j, 3), 0, 0)),
                pl.BlockSpec((1, high, width), lambda h, j, c: (jnp.where(h == 0, 0, j), 0, 0)),
            ],
        ),
        out_shape=[shape((4, high, width), BF)] * 2,
        compiler_params=pltpu.CompilerParams(vmem_limit_bytes=LIMIT),
        cost_estimate=pl.CostEstimate(
            flops=128 * t * width * width, bytes_accessed=64 * t * width, transcendentals=0
        ),
        name="attention_grad",
    )(s, normed, context, dpacked, dattn)


def back_kernel(
    experts, cap, dy, dense, hid, gb_ref, router, place, route, live, soft, normed3, slope, fc1, fc2, *refs
):
    homes = refs[:experts]
    dmlp, dpre, dhidden, tiny, drouter = refs[experts : experts + 5]
    w1, w2, ups, sems = refs[experts + 5 :]
    rows, width = hid.shape
    copies = [
        pltpu.make_async_copy(fc1, w1, sems.at[0]),
        pltpu.make_async_copy(fc2, w2, sems.at[1]),
    ]
    for c in copies:
        c.start()
    lanes = -(-cap // WIDE) * WIDE
    spot = iota((lanes, rows), 0)
    spot = jnp.where(spot < cap, spot, -2 * experts * cap)
    dgate = [jnp.zeros((16, rows), F32) for _ in range(TOP)]
    for r in range(experts):
        tail = homes[r][cap : cap + 16, 0:lanes]
        hot = [jnp.where(spot + r * cap == place[k : k + 1, :], 1.0, 0.0).astype(BF) for k in range(TOP)]
        for k in range(TOP):
            dgate[k] = dgate[k] + dot(tail, hot[k])
        term = dot_tn((hot[0] + hot[1])[0:cap, :], homes[r][0:cap, :])
        ups[...] = term if r == 0 else ups[...] + term
    dgate = [jnp.sum(d, axis=0, keepdims=True) * live[...] for d in dgate]
    mix = soft[0:1, :] * dgate[0] + soft[1:2, :] * dgate[1]
    dsoft = [soft[k : k + 1, :] * (dgate[k] - mix) for k in range(TOP)]
    index = iota((router.shape[0], rows), 0)
    dlogits = sum(jnp.where(index == route[k : k + 1, :], dsoft[k], 0.0) for k in range(TOP))
    dlogits = dlogits.astype(BF)
    drouter[...] = dot(dlogits, normed3[...])
    ups[...] += dot_tn(dlogits, router[...])
    tile = rows // 6
    tiny[...] = jnp.zeros_like(tiny)

    def norm_back(at, values, gain, bias_row, base):
        n, scale = normalize(values)
        u = ups[at, :]
        tiny[bias_row - 1 : bias_row, :] += jnp.sum(u * n, axis=0, keepdims=True)
        tiny[bias_row : bias_row + 1, :] += jnp.sum(u, axis=0, keepdims=True)
        ug = u * gain
        dv = scale * (
            ug
            - jnp.mean(ug, axis=-1, keepdims=True)
            - n * jnp.mean(ug * n, axis=-1, keepdims=True)
        )
        return base + dv

    @pl.loop(0, 6)
    def _(i):
        at = pl.ds(pl.multiple_of(i * tile, 16), tile)
        dd = norm_back(at, dense[at, :], gb_ref[4:5, :], 5, dy[at, :].astype(F32))
        dhidden[at, :] = dd
        dmlp[at, :] = dd.astype(BF)

    for c in copies:
        c.wait()
    ups[...] = jnp.zeros_like(ups)

    @pl.loop(0, w1.shape[1] // 512)
    def _(j):
        at = pl.ds(pl.multiple_of(j * 512, 512), 512)
        dpre[:, at] = (dot_nt(dmlp[...], w2[at, :]) * slope[:, at].astype(F32)).astype(BF)
        ups[...] += dot_nt(dpre[:, at], w1[:, at])

    @pl.loop(0, 6)
    def _(i):
        at = pl.ds(pl.multiple_of(i * tile, 16), tile)
        dhidden[at, :] = norm_back(at, hid[at, :], gb_ref[2:3, :], 3, dhidden[at, :])


def back(
    dy, dense, hid, gb, router, place, route, live, soft, normed3, slope, fc1, fc2, homes, experts, cap, after
):
    rows, width = hid.shape
    ff = fc1.shape[1]
    return call(
        functools.partial(back_kernel, experts, cap),
        [VM] * 11 + [HB] * 2 + [VM] * experts,
        [
            shape((rows, width), BF),
            shape((rows, ff), BF),
            shape((rows, width), F32),
            shape((8, width), F32),
            shape(router.shape, F32),
        ],
        [
            pltpu.VMEM((width, ff), BF),
            pltpu.VMEM((ff, width), BF),
            pltpu.VMEM((rows, width), F32),
            pltpu.SemaphoreType.DMA((2,)),
        ],
        4 * rows * width * ff + 2 * rows * width * experts * cap,
        4 * width * ff + rows * (4 * ff + 18 * width),
        "dense_backward",
        after,
    )(dy, dense, hid, gb, router, place, route, live, soft, normed3, slope, fc1, fc2, *homes)


def attend_back_kernel(
    s_ref, dhid, id_row, id_col, packed, lse, wo_a, wo_b, dattn, dpacked, wo, bias, dctx, sems
):
    s = s_ref[0]
    rows, width = dhid.shape
    copies = halves_into(s, wo_a, wo_b, wo, sems, 0)
    for c in copies:
        c.start()
    tile = rows // 6

    @pl.loop(0, 6)
    def _(i):
        at = pl.ds(pl.multiple_of(i * tile, 16), tile)
        dattn[at, :] = dhid[at, :].astype(BF)
        bias[at, :] = jnp.where(id_col[at, :] == id_row[...], 0.0, MASKED)

    copies[0].wait()
    copies[1].wait()

    @pl.loop(0, width // 256)
    def _(j):
        at = pl.ds(pl.multiple_of(j * 256, 256), 256)
        dctx[:, at] = dot_nt(dattn[...], wo[at, :]).astype(BF)

    lane = iota((1, WIDE), 1)

    @pl.loop(0, width // WIDE)
    def _(pair):
        col = pl.multiple_of(pair * WIDE, WIDE)
        q = packed[:, pl.ds(col, WIDE)] * jnp.asarray(HEAD**-0.5, BF)
        keys = packed[:, pl.ds(width + col, WIDE)]
        values = packed[:, pl.ds(2 * width + col, WIDE)]
        dc = dctx[:, pl.ds(col, WIDE)]
        dq, dk, dv = [], [], []
        for h in range(2):
            mine = (lane >= h * HEAD) & (lane < (h + 1) * HEAD)
            scores = dot_nt(jnp.where(mine, keys, jnp.zeros_like(keys)), q) + bias[...]
            p = jnp.exp(scores - lse[pl.ds(2 * pair + h, 1), :])
            dp = dot_nt(jnp.where(mine, values, jnp.zeros_like(values)), dc)
            inner = jnp.sum(p * dp, axis=0, keepdims=True)
            ds = (p * (dp - inner)).astype(BF)
            dv.append(dot(p.astype(BF), dc))
            dk.append(dot(ds, q))
            dq.append(dot_tn(ds, keys) * HEAD**-0.5)
        low = lane < HEAD
        dpacked[:, pl.ds(col, WIDE)] = jnp.where(low, dq[0], dq[1]).astype(BF)
        dpacked[:, pl.ds(width + col, WIDE)] = jnp.where(low, dk[0], dk[1]).astype(BF)
        dpacked[:, pl.ds(2 * width + col, WIDE)] = jnp.where(low, dv[0], dv[1]).astype(BF)


def input_kernel(s_ref, x_ref, dhid, gb_ref, dpacked, qkv_a, qkv_b, grad_in, tiny, wq, ups, sems):
    s = s_ref[0]
    rows, width = x_ref.shape
    tile = rows // 6
    copies = halves_into(s, qkv_a, qkv_b, wq, sems, 0)
    for c in copies:
        c.start()
    copies[0].wait()
    copies[1].wait()

    @pl.loop(0, width // 256)
    def _(j):
        at = pl.ds(pl.multiple_of(j * 256, 256), 256)
        ups[:, at] = dot_nt(dpacked[...], wq[at, :])

    tiny[...] = jnp.zeros_like(tiny)

    @pl.loop(0, 6)
    def _(i):
        at = pl.ds(pl.multiple_of(i * tile, 16), tile)
        n, scale = normalize(x_ref[at, :].astype(F32))
        u = ups[at, :]
        tiny[0:1, :] += jnp.sum(u * n, axis=0, keepdims=True)
        tiny[1:2, :] += jnp.sum(u, axis=0, keepdims=True)
        ug = u * gb_ref[0:1, :]
        grad_in[at, :] = dhid[at, :] + scale * (
            ug
            - jnp.mean(ug, axis=-1, keepdims=True)
            - n * jnp.mean(ug * n, axis=-1, keepdims=True)
        )


def attend_back(s, dhid, ids, packed, lse, wo, after):
    rows, width = dhid.shape
    n3 = packed.shape[1]
    return call(
        attend_back_kernel,
        [SM] + [VM] * 5 + [HB] * 2,
        [shape((rows, width), BF), shape((rows, n3), BF)],
        [
            pltpu.VMEM((width, width), BF),
            pltpu.VMEM((rows, rows), F32),
            pltpu.VMEM((rows, width), BF),
            pltpu.SemaphoreType.DMA((2,)),
        ],
        2 * rows * width * width + 20 * rows * rows * width,
        2 * (width * width + rows * (3 * width + 2 * n3)),
        "attention_backward",
        after,
    )(s, dhid, ids[None, :], ids[:, None], packed, lse, *wo)


def input_back(s, x, dhid, gb, dpacked, qkv, after):
    rows, width = x.shape
    n3 = dpacked.shape[1]
    return call(
        input_kernel,
        [SM] + [VM] * 4 + [HB] * 2,
        [shape((rows, width), F32), shape((8, width), F32)],
        [
            pltpu.VMEM((width, n3), BF),
            pltpu.VMEM((rows, width), F32),
            pltpu.SemaphoreType.DMA((2,)),
        ],
        2 * rows * width * n3,
        2 * (width * n3 + rows * n3) + 10 * rows * width,
        "input_backward",
        after,
    )(s, x, dhid, gb, dpacked, *qkv)


def merge_kernel(experts, cap, dense, place, *refs):
    outs, result = refs[:experts], refs[experts]
    rows = dense.shape[0]
    total = dense[...]
    spot = iota((cap, rows), 0)
    for r in range(experts):
        hot = sum(jnp.where(spot + r * cap == place[k : k + 1, :], 1.0, 0.0) for k in range(TOP))
        total = total + dot_tn(hot.astype(BF), outs[r][...])
    result[...] = total.astype(BF)


def merge(dense, place, outs, experts, cap):
    rows, width = dense.shape
    return call(
        functools.partial(merge_kernel, experts, cap),
        [VM] * (2 + experts),
        shape((rows, width), BF),
        [],
        2 * rows * width * experts * cap,
        rows * width * 6 + 2 * experts * cap * width,
        "merge",
        (),
        0.25,
    )(dense, place, *outs)


def hold_kernel(n, *refs):
    for i in range(n):
        refs[n + i][...] = refs[i][...]


def hold(chunks, after):
    n = len(chunks)
    dims = chunks[0].shape
    return call(
        functools.partial(hold_kernel, n),
        [VM] * n,
        [shape(dims, BF)] * n,
        [],
        0,
        4 * n * dims[0] * dims[1],
        "hold",
        after,
    )(*chunks)


def finish_kernel(columns, m_ref, mine, got, out):
    n, high, width = mine.shape
    for which, src in ((m_ref[0], mine), (1 - m_ref[0], got)):
        for i in range(n):
            value = src[i].astype(F32)
            if columns:
                out[:, pl.ds(pl.multiple_of((which * n + i) * width, width), width)] = value
            else:
                out[pl.ds(pl.multiple_of((which * n + i) * high, high), high), :] = value


def finish(m, mine, got, columns):
    n, high, width = mine.shape
    dims = (high, 2 * n * width) if columns else (2 * n * high, width)
    return call(
        functools.partial(finish_kernel, columns),
        [SM, VM, VM],
        shape(dims, F32),
        [],
        0,
        12 * n * high * width,
        "finish",
    )(m, mine, got)


def spread_kernel(experts, cap, rows_in, place, *chunks):
    spot = iota((cap, rows_in.shape[0]), 0)
    for r in range(experts):
        hot = sum(jnp.where(spot + r * cap == place[k : k + 1, :], 1.0, 0.0) for k in range(TOP))
        chunks[r][...] = dot(hot.astype(BF), rows_in[...]).astype(BF)


def spread(rows_in, place, experts, cap):
    rows, width = rows_in.shape
    return call(
        functools.partial(spread_kernel, experts, cap),
        [VM, VM],
        [shape((cap, width), BF)] * experts,
        [],
        2 * rows * width * experts * cap,
        2 * (rows + experts * cap) * width,
        "spread",
    )(rows_in, place)


def places_of(routes, live, experts, capacity):
    tokens = routes.shape[0]
    ids = jnp.arange(experts, dtype=jnp.int32)
    match = [
        ((routes[:, k : k + 1] == ids[None, :]) & live[:, None]).astype(F32) for k in range(TOP)
    ]
    order = jnp.arange(tokens, dtype=jnp.int32)
    below = (order[:, None] > order[None, :]).astype(BF)
    before = jnp.zeros((1, experts), F32)
    out = []
    for k in range(TOP):
        counts = dot(below, match[k].astype(BF)) + before
        before = before + jnp.sum(match[k], axis=0, keepdims=True)
        within = jnp.sum(counts * match[k], axis=1).astype(jnp.int32)
        out.append(jnp.where(live, routes[:, k] * capacity + within, experts * capacity))
    return out

def local(
    tokens,
    image_ids,
    routes,
    norm1_gain,
    norm1_bias,
    qkv_weight,
    attn_out_weight,
    norm2_gain,
    norm2_bias,
    fc1_weight,
    fc2_weight,
    norm3_gain,
    norm3_bias,
    router_weight,
    expert_up,
    expert_down,
    cotangent,
):
    s = lax.axis_index("section")
    e = lax.axis_index("dp") // GROUP
    q = lax.axis_index("dp") % GROUP
    dp_count = lax.axis_size("dp")
    experts = dp_count // GROUP
    cap = GROUP * ((21 * SLOTS + 10 * experts * GROUP - 1) // (10 * experts * GROUP))
    cap = -(-cap // 16) * 16
    half = tokens.shape[1]
    width = 2 * half
    few = experts <= 8
    planes = [[p * GROUP + i for p in range(experts)] for i in range(GROUP)]
    here = jnp.reshape(s, (1,))

    def swap(v):
        return lax.ppermute(v, "section", [(0, 1), (1, 0)])

    def over_q(v, bit):
        return lax.ppermute(v, "dp", [(i, i ^ bit) for i in range(dp_count)])

    def over_e(v, r):
        return lax.ppermute(
            v,
            "dp",
            [(i, ((i // GROUP + r) % experts) * GROUP + i % GROUP) for i in range(dp_count)],
        )

    def part(v, index, size, axis=0):
        return lax.dynamic_slice_in_dim(v, index * size, size, axis)

    def join(own, other, axis):
        return jnp.where(
            s == 0,
            jnp.concatenate([own, other], axis=axis),
            jnp.concatenate([other, own], axis=axis),
        )

    def add(a, b):
        return (a.astype(F32) + b.astype(F32)).astype(BF)

    def out_chunks(chunks):
        if not few:
            return list(lax.all_to_all(jnp.stack(chunks), "dp", 0, 0, axis_index_groups=planes))
        return [chunks[0]] + [over_e(chunks[r], r) for r in range(1, experts)]

    def home_chunks(chunks):
        if not few:
            return list(lax.all_to_all(jnp.stack(chunks), "dp", 0, 0, axis_index_groups=planes))
        return [chunks[0]] + [over_e(chunks[r], experts - r) for r in range(1, experts)]

    small = jnp.stack([norm1_gain, norm1_bias, norm2_gain, norm2_bias, norm3_gain, norm3_bias])
    small = jnp.concatenate([small, jnp.transpose(router_weight)])
    small = join(small, swap(small), 1)
    x = join(part(tokens, s, SLOTS), swap(part(tokens, 1 - s, SLOTS)), 1)
    dy = join(part(cotangent, s, SLOTS), swap(part(cotangent, 1 - s, SLOTS)), 1)
    ids = part(image_ids, s, 1).reshape(-1)
    route = part(routes, s, SLOTS)
    live = ids >= 0
    gb = jnp.concatenate([small[:6], jnp.zeros((2, width), BF)]).astype(F32)
    router_rows = -(-experts // 16) * 16
    router = jnp.concatenate([small[6 : 6 + experts], jnp.zeros((router_rows - experts, width), BF)])
    qkv, wo = (qkv_weight, swap(qkv_weight)), (attn_out_weight, swap(attn_out_weight))

    pair = jnp.stack([expert_up, expert_down])
    from_x, from_y = over_q(pair, 1), over_q(pair, 2)

    def gather(v, tiled):
        return lax.all_gather(v, "section", axis=0, tiled=tiled)

    tie = lax.optimization_barrier
    (x, qkv, wo, fc2_weight, pair_late) = tie((x, qkv, wo, fc2_weight, pair))
    fc1, fc2 = gather(fc1_weight, True), gather(fc2_weight, True)
    weights = [gather(pair_late, False)]

    if few:
        distance = (route - e) % experts
    else:
        distance = route
    spots = places_of(distance, live, experts, cap)
    place = jnp.stack(spots + [jnp.full_like(spots[0], -1)] * 6)
    route_rows = jnp.concatenate([jnp.transpose(route), jnp.full((6, SLOTS), -1, jnp.int32)])
    live_row = live.astype(F32)[None, :]
    dy_sent = spread(dy, place, experts, cap)
    dy_out = out_chunks(dy_sent)

    normed1, packed, context, lse, hidden = front(here, x, ids, gb, qkv, wo, dy_sent[:1])
    hidden, from_x, from_y, *dy_out[:-1] = tie((hidden, from_x, from_y, *dy_out[:-1]))
    weights += [gather(from_x, False), gather(from_y, False)]
    far = [over_q(from_x[0], 2), over_q(from_y[1], 1)]
    normed2, act, slope, dense, normed3, soft, *sent = mlp(
        hidden, gb, router, place, route_rows, live_row, fc1, fc2, experts, cap, []
    )
    sent, far, dy_out[-1] = tie((sent, far, dy_out[-1]))
    weights.append(gather(jnp.stack(far), False))
    got = out_chunks(sent)

    step = max(1, experts // 4)
    results = [None] * experts
    previous = None
    for i in [0] + list(range(experts - step, 0, -step)):
        if i:
            got[i], results[previous] = tie((got[i], results[previous]))
        results[i : i + step] = expert(got[i : i + step], dy_out[i : i + step], weights, cap)
        previous = i
    homes = home_chunks([r[0] for r in results])
    acts, dinners, scaled = ([r[i] for r in results] for i in (2, 3, 4))

    def grad_sum(*operands, weight=16):
        give, keep = weight_grad(here, *operands, weight=weight)
        return add(keep, swap(give))

    if few:
        acts, homes[-1], homes[-2] = tie((acts, homes[-1], homes[-2]))
    sum_up, sum_down = grad_sum(got, dinners, cap), grad_sum(scaled, acts)
    dmlp, dpre, dhidden, tiny23, drouter = back(
        dy, dense, hidden, gb, router, place, route_rows, live_row, soft, normed3, slope,
        fc1, fc2, homes, experts, cap, [],
    )
    outs = hold([r[1] for r in results], [dmlp])
    dpre, sum_up, sum_down = tie((dpre, sum_up, sum_down))

    moved_up = over_q(jnp.stack([sum_up[1], sum_up[3]]), 1)
    moved_down = over_q(sum_down[2:], 2)
    grads1, grads2 = weight_grad(here, [normed2], [dpre]), weight_grad(here, [act], [dmlp])
    dhidden, grads1, grads2, moved_up, moved_down, outs = tie(
        (dhidden, grads1, grads2, moved_up, moved_down, outs)
    )
    near_up, far_up = add(sum_up[0], moved_up[0]), add(sum_up[2], moved_up[1])
    near_down, far_down = add(sum_down[0], moved_down[0]), add(sum_down[1], moved_down[1])
    far_up, far_down = over_q(far_up, 2), over_q(far_down, 1)

    def fold(v, bit):
        mine, rows = (q // bit) % 2, v.shape[0] // 2
        return part(v, mine, rows), over_q(part(v, 1 - mine, rows), bit)

    def unfold(v, got, bit):
        return jnp.where(
            (q // bit) % 2 == 0, jnp.concatenate([v, got]), jnp.concatenate([got, v])
        )

    def plane_out(a, b):
        ab = jnp.stack([a, b])
        rows = a.shape[0] // experts
        if not few:
            return [lax.psum(ab, "dp", axis_index_groups=planes)]
        return [part(ab, (e + r) % experts, rows, 1) for r in range(experts)]

    def plane_sum(pieces):
        if not few:
            return pieces
        total = sum(p.astype(F32) for p in pieces).astype(BF)
        return [total] * experts

    def plane_move(pieces):
        return pieces[:1] + [over_e(p, r) for r, p in enumerate(pieces) if r]

    def plane_join(pieces):
        if not few:
            return pieces[0][0], pieces[0][1]
        rows = pieces[0].shape[1]
        whole = jnp.zeros((2, experts * rows, width), BF)
        for r, piece in enumerate(pieces):
            whole = lax.dynamic_update_slice_in_dim(whole, piece, ((e - r) % experts) * rows, 1)
        return whole[0], whole[1]

    dattn, dpacked = attend_back(here, dhidden, ids, packed, lse, wo, [])
    away1, away2 = swap(grads1[0]), swap(grads2[0])
    out1 = over_e(outs[1], experts - 1) if few else outs[1]
    dpacked, dattn, away1, away2, far_up, far_down, out1 = tie(
        (dpacked, dattn, away1, away2, far_up, far_down, out1)
    )
    half_up = near_up.astype(F32) + far_up.astype(F32)
    half_down = near_down.astype(F32) + far_down.astype(F32)

    a, b = add(grads2[1], away2).reshape(-1, width), add(grads1[1], away1).reshape(-1, width)
    a, b = fold(a, 1), fold(b, 2)
    if few:
        home_outs = [outs[0], out1] + [over_e(outs[r], experts - r) for r in range(2, experts)]
    else:
        home_outs = home_chunks([outs[0], out1, *outs[2:]])
    grad_in, tiny1 = input_back(here, x, dhidden, gb, dpacked, qkv, [])
    give, keep = attention_grad(here, normed1, context, dpacked, dattn)
    give, keep, a, b, home_outs = tie((give, keep, a, b, home_outs))
    tiny = jnp.concatenate([tiny1[:2], tiny23[2:6], drouter[:experts]])

    def swapped(v):
        return part(v, s, half, 1), swap(part(v, 1 - s, half, 1))

    away = swap(give)
    a, b = fold(add(*a), 2), fold(add(*b), 1)
    block_out = merge(dense, place, home_outs, experts, cap)
    grad_in, tiny = swapped(grad_in), swapped(tiny)
    away, a, b, grad_in, tiny = tie((away, a, b, grad_in, tiny))
    tiny = tiny[0] + tiny[1]

    ab = plane_move(plane_out(add(*a), add(*b)))
    t = add(keep, away).reshape(-1, width)
    ta, tb = fold(t[:width], 1), fold(t[width:], 2)
    ab, ta, tb = tie((ab, ta, tb))

    ab = plane_move(plane_sum(ab))
    ta, tb = fold(add(*ta), 2), fold(add(*tb), 1)
    ab, ta, tb, block_out = tie((ab, ta, tb, block_out))

    a, b = plane_join(ab)
    a_got, b_got = over_q(a, 2), over_q(b, 1)
    tab = plane_move(plane_out(add(*ta), add(*tb)))
    a_got, b_got, tab = tie((a_got, b_got, tab))
    a, b = unfold(a, a_got, 2), unfold(b, b_got, 1)
    a_got, b_got = over_q(a, 1), over_q(b, 2)
    tab = plane_move(plane_sum(tab))
    a_got, b_got, tab = tie((a_got, b_got, tab))

    side_x, side_y = jnp.reshape(q % 2, (1,)), jnp.reshape(q // 2, (1,))

    def blocks(v):
        return v.reshape(-1, half, width)

    ta, tb = plane_join(tab)
    ta_got, tb_got = over_q(ta, 2), over_q(tb, 1)
    block_out = swapped(block_out)
    tiny_q = [over_q(tiny, bit) for bit in (1, 2, 3)]
    sum_fc2 = finish(side_x, blocks(a), blocks(a_got), False)
    sum_fc1 = finish(side_y, blocks(b), blocks(b_got), True)
    ta_got, tb_got, block_out, tiny_q, sum_fc2, sum_fc1 = tie(
        (ta_got, tb_got, block_out, tiny_q, sum_fc2, sum_fc1)
    )
    ta, tb = unfold(ta, ta_got, 2), unfold(tb, tb_got, 1)
    ta_got, tb_got = over_q(ta, 1), over_q(tb, 2)
    tiny = tiny + tiny_q[0] + (tiny_q[1] + tiny_q[2])
    if few:
        total = sum(over_e(tiny, r) if r else tiny for r in range(experts))
    else:
        total = lax.psum(tiny, "dp", axis_index_groups=planes)
    q_and_k = finish(side_x, blocks(ta), blocks(ta_got), True)
    first = q // 2 == 0
    v_sum, sum_attn = (
        jnp.where(first, p, r).astype(F32) for p, r in ((tb, tb_got), (tb_got, tb))
    )
    sum_qkv = jnp.concatenate([q_and_k, v_sum], axis=1)
    return (
        join(*block_out, 0),
        join(*grad_in, 0),
        total[0],
        total[1],
        sum_qkv,
        sum_attn,
        total[2],
        total[3],
        sum_fc1,
        sum_fc2,
        total[4],
        total[5],
        jnp.transpose(total[6:]),
        half_up,
        half_down,
    )


def solution(mesh):
    placed = (
        P("dp", "section"),
        P("dp", None),
        P("dp", None),
        P("section"),
        P("section"),
        P("section", None),
        P("section", None),
        P("section"),
        P("section"),
        P("section", None),
        P("section", None),
        P("section"),
        P("section"),
        P("section", None),
        P("section", "dp"),
        P("section", "dp"),
        P("dp", "section"),
    )
    return jax.shard_map(
        local,
        mesh=mesh,
        in_specs=placed,
        out_specs=(
            P("dp", "section"),
            P("dp", "section"),
            P("section"),
            P("section"),
            P("section", None),
            P("section", None),
            P("section"),
            P("section"),
            P("section", None),
            P("section", None),
            P("section"),
            P("section"),
            P("section", None),
            P("section", "dp"),
            P("section", "dp"),
        ),
        check_vma=False,
    )
```

```python
import functools

import jax
import jax.numpy as jnp
from jax import lax
from jax.experimental import pallas as pl
from jax.experimental.pallas import tpu as pltpu
from jax.sharding import PartitionSpec as P

HEAD = 64
TOP = 2
GROUP = 4
SLOTS = 576
WIDE = 128

EPSILON = 1e-06
MASKED = -1e30
BF = jnp.bfloat16
F32 = jnp.float32
LIMIT = 24 * 1024 * 1024
LIMITS = dict(
    attention_forward=28,
    dense_forward=36,
    expert=28,
    dense_backward=40,
    attention_backward=28,
    input_backward=24,
    merge=20,
    hold=12,
    finish=24,
    spread=16,
)


def dot(a, b):
    return jnp.dot(a, b, preferred_element_type=F32)


def dot_nt(a, b):
    return lax.dot_general(a, b, (((1,), (1,)), ((), ())), preferred_element_type=F32)


def dot_tn(a, b):
    return lax.dot_general(a, b, (((0,), (0,)), ((), ())), preferred_element_type=F32)


def normalize(v):
    center = v - jnp.mean(v, axis=-1, keepdims=True)
    scale = lax.rsqrt(jnp.mean(center * center, axis=-1, keepdims=True) + EPSILON)
    return center * scale, scale


def gelu_pair(x):
    bell = jnp.exp(x * x * -0.5)
    t = 1.0 / (1.0 + jnp.abs(x) * (0.3275911 * 0.5**0.5))
    tail = (
        t
        * (
            0.127414796
            + t * (-0.142248368 + t * (0.7107068705 + t * (-0.7265760135 + t * 0.5307027145)))
        )
        * bell
    )
    cdf = jnp.where(x >= 0.0, 1.0 - tail, tail)
    return x * cdf, cdf + x * (bell * 0.3989422804014327)


def iota(shape, axis):
    return lax.broadcasted_iota(jnp.int32, shape, axis)


def halves_into(s, own, other, dest, sems, first):
    rows = own.shape[0]
    return [
        pltpu.make_async_copy(own, dest.at[pl.ds(pl.multiple_of(s * rows, rows), rows)], sems.at[first]),
        pltpu.make_async_copy(
            other, dest.at[pl.ds(pl.multiple_of((1 - s) * rows, rows), rows)], sems.at[first + 1]
        ),
    ]


def split3(v):
    hi = v.astype(BF)
    rest = v - hi.astype(F32)
    mid = rest.astype(BF)
    low = (rest - mid.astype(F32)).astype(BF)
    return hi, mid, low


VM = pl.BlockSpec(memory_space=pltpu.VMEM)
SM = pl.BlockSpec(memory_space=pltpu.SMEM)
HB = pl.BlockSpec(memory_space=pl.ANY)


def call(kernel, in_specs, out_shape, scratch, flops, moved, name, after=(), weight=16):
    limit = LIMITS[name] * 1024 * 1024
    count, extra = len(in_specs), len(after)

    def body(*refs):
        kernel(*refs[:count], *refs[count + extra :])

    made = pl.pallas_call(
        body,
        in_specs=in_specs + [HB] * extra,
        out_specs=jax.tree.map(lambda _: VM, out_shape),
        out_shape=out_shape,
        scratch_shapes=scratch,
        compiler_params=pltpu.CompilerParams(vmem_limit_bytes=limit),
        cost_estimate=pl.CostEstimate(
            flops=int(weight * flops), bytes_accessed=int(weight * moved), transcendentals=0
        ),
        name=name,
    )
    return lambda *operands: made(*operands, *after)


def shape(dims, kind):
    return jax.ShapeDtypeStruct(dims, kind)


def front_kernel(
    s_ref, x_ref, id_row, id_col, gb_ref, qkv_a, qkv_b, wo_a, wo_b,
    normed, packed, context, lse, hidden,
    wq, wo, bias, lse_col, sems,
):
    s = s_ref[0]
    rows, width = x_ref.shape
    copies = halves_into(s, qkv_a, qkv_b, wq, sems, 0) + halves_into(s, wo_a, wo_b, wo, sems, 2)
    for c in copies:
        c.start()
    tile = rows // 6

    @pl.loop(0, 6)
    def _(i):
        at = pl.ds(pl.multiple_of(i * tile, 16), tile)
        n, _ = normalize(x_ref[at, :].astype(F32))
        normed[at, :] = (n * gb_ref[0:1, :] + gb_ref[1:2, :]).astype(BF)
        bias[at, :] = jnp.where(id_col[at, :] == id_row[...], 0.0, MASKED)

    copies[0].wait()
    copies[1].wait()

    @pl.loop(0, wq.shape[1] // 256)
    def _(j):
        at = pl.ds(pl.multiple_of(j * 256, 256), 256)
        packed[:, at] = dot(normed[...], wq[:, at]).astype(BF)

    lane = iota((1, WIDE), 1)
    lse_col[...] = jnp.zeros_like(lse_col)
    third = rows // 3

    @pl.loop(0, width // WIDE)
    def _(pair):
        col = pl.multiple_of(pair * WIDE, WIDE)
        keys = packed[:, pl.ds(width + col, WIDE)]
        values = packed[:, pl.ds(2 * width + col, WIDE)]
        for r in range(3):
            at = slice(r * third, (r + 1) * third)
            q = packed[at, pl.ds(col, WIDE)] * jnp.asarray(HEAD**-0.5, BF)
            outs = []
            sums = lse_col[at, :]
            for h in range(2):
                mine = (lane >= h * HEAD) & (lane < (h + 1) * HEAD)
                scores = dot_nt(jnp.where(mine, q, jnp.zeros_like(q)), keys) + bias[at, :]
                top = jnp.max(scores, axis=1, keepdims=True)
                p = jnp.exp(scores - top)
                total = jnp.sum(p, axis=1, keepdims=True)
                outs.append(dot(p.astype(BF), values) * (1.0 / total))
                sums = jnp.where(lane == 2 * pair + h, top + jnp.log(total), sums)
            lse_col[at, :] = sums
            context[at, pl.ds(col, WIDE)] = jnp.where(lane < HEAD, outs[0], outs[1]).astype(BF)

    lse[...] = jnp.transpose(lse_col[...])[0 : lse.shape[0], :]
    copies[2].wait()
    copies[3].wait()

    @pl.loop(0, width // 256)
    def _(j):
        at = pl.ds(pl.multiple_of(j * 256, 256), 256)
        hidden[:, at] = x_ref[:, at].astype(F32) + dot(context[...], wo[:, at])


def front(s, x, ids, gb, qkv, wo, after):
    rows, width = x.shape
    n3 = qkv[0].shape[1]
    return call(
        front_kernel,
        [SM, VM, VM, VM, VM, HB, HB, HB, HB],
        [
            shape((rows, width), BF),
            shape((rows, n3), BF),
            shape((rows, width), BF),
            shape((16, rows), F32),
            shape((rows, width), F32),
        ],
        [
            pltpu.VMEM((width, n3), BF),
            pltpu.VMEM((width, width), BF),
            pltpu.VMEM((rows, rows), F32),
            pltpu.VMEM((rows, WIDE), F32),
            pltpu.SemaphoreType.DMA((4,)),
        ],
        2 * rows * width * (n3 + width) + 4 * rows * rows * width,
        2 * (width * (n3 + width) + rows * (3 * width + n3)) + 4 * rows * width,
        "attention_forward",
        after,
    )(s, x, ids[None, :], ids[:, None], gb, *qkv, *wo)


def mlp_kernel(experts, cap, hid, gb_ref, router, place, route, live, fc1, fc2, *refs):
    normed2, act, slope, dense, normed3, soft = refs[:6]
    chunks = refs[6 : 6 + experts]
    w1, w2, sems = refs[6 + experts :]
    rows, width = hid.shape
    copies = [
        pltpu.make_async_copy(fc1, w1, sems.at[0]),
        pltpu.make_async_copy(fc2, w2, sems.at[1]),
    ]
    for c in copies:
        c.start()
    tile = rows // 6

    @pl.loop(0, 6)
    def _(i):
        at = pl.ds(pl.multiple_of(i * tile, 16), tile)
        n, _ = normalize(hid[at, :])
        normed2[at, :] = (n * gb_ref[2:3, :] + gb_ref[3:4, :]).astype(BF)
        dense[at, :] = hid[at, :]

    for c in copies:
        c.wait()

    @pl.loop(0, w1.shape[1] // 512)
    def _(j):
        at = pl.ds(pl.multiple_of(j * 512, 512), 512)
        a, sl = gelu_pair(dot(normed2[...], w1[:, at]))
        act[:, at] = a.astype(BF)
        slope[:, at] = sl.astype(BF)
        dense[...] += dot(act[:, at], w2[at, :])

    @pl.loop(0, 6)
    def _(i):
        at = pl.ds(pl.multiple_of(i * tile, 16), tile)
        n, _ = normalize(dense[at, :])
        normed3[at, :] = (n * gb_ref[4:5, :] + gb_ref[5:6, :]).astype(BF)

    logits = dot_nt(router[...], normed3[...])
    expert = iota(logits.shape, 0)
    chosen = [
        jnp.sum(jnp.where(expert == route[k : k + 1, :], logits, 0.0), axis=0, keepdims=True)
        for k in range(TOP)
    ]
    top = jnp.maximum(chosen[0], chosen[1])
    raised = [jnp.exp(c - top) for c in chosen]
    total = raised[0] + raised[1]
    pieces = []
    for k in range(TOP):
        share = raised[k] / total
        soft[k : k + 1, :] = share
        three = split3(share * live[...])
        row = iota((16, rows), 0)
        pieces.append(
            jnp.where(row == 0, three[0].astype(F32), 0.0)
            + jnp.where(row == 1, three[1].astype(F32), 0.0)
            + jnp.where(row == 2, three[2].astype(F32), 0.0)
        )
    pieces = [p.astype(BF) for p in pieces]
    lanes = -(-cap // WIDE) * WIDE
    spot = iota((lanes, rows), 0)
    spot = jnp.where(spot < cap, spot, -2 * experts * cap)
    for r in range(experts):
        hot = [jnp.where(spot + r * cap == place[k : k + 1, :], 1.0, 0.0).astype(BF) for k in range(TOP)]
        both = (hot[0] + hot[1])[0:cap, :]
        chunks[r][0:cap, :] = dot(both, normed3[...]).astype(BF)
        chunks[r][cap : cap + 16, :] = jnp.zeros((16, width), BF)
        chunks[r][cap : cap + 16, 0:lanes] = (
            dot_nt(pieces[0], hot[0]) + dot_nt(pieces[1], hot[1])
        ).astype(BF)


def mlp(hid, gb, router, place, route, live, fc1, fc2, experts, cap, after):
    rows, width = hid.shape
    ff = fc1.shape[1]
    return call(
        functools.partial(mlp_kernel, experts, cap),
        [VM, VM, VM, VM, VM, VM, HB, HB],
        [
            shape((rows, width), BF),
            shape((rows, ff), BF),
            shape((rows, ff), BF),
            shape((rows, width), F32),
            shape((rows, width), BF),
            shape((8, rows), F32),
        ]
        + [shape((cap + 16, width), BF)] * experts,
        [
            pltpu.VMEM((width, ff), BF),
            pltpu.VMEM((ff, width), BF),
            pltpu.SemaphoreType.DMA((2,)),
        ],
        4 * rows * width * ff + 2 * rows * width * experts * cap,
        4 * width * ff + rows * (4 * ff + 12 * width),
        "dense_forward",
        after,
    )(hid, gb, router, place, route, live, fc1, fc2)


def expert_kernel(cap, n, s_ref, *refs):
    rows_in, dys = refs[:n], refs[n : 2 * n]
    own, other = refs[2 * n : 2 * n + GROUP], refs[2 * n + GROUP : 2 * n + 2 * GROUP]
    outs = refs[2 * n + 2 * GROUP : -3]
    wu, wd, sems = refs[-3:]
    s = s_ref[0]
    width = wu.shape[1]
    half = width // 2
    copies = [
        [
            pltpu.make_async_copy(
                src[b].at[u],
                w.at[b, pl.ds(pl.multiple_of(side * half, half), half)],
                sems.at[4 * b + 2 * h + u],
            )
            for h, (side, src) in enumerate(((s, own), (1 - s, other)))
            for u, w in enumerate((wu, wd))
        ]
        for b in range(GROUP)
    ]
    for b in range(GROUP):
        for c in copies[b]:
            c.start()
    lanes = -(-cap // WIDE) * WIDE
    eye = iota((lanes, lanes), 0) == iota((lanes, lanes), 1)
    gates = []
    for i in range(n):
        back, out, act, dinner, gp = outs[5 * i : 5 * i + 5]
        g = jnp.sum(rows_in[i][cap : cap + 16, 0:lanes].astype(F32), axis=0, keepdims=True)
        gate = jnp.sum(jnp.where(eye, g, 0.0), axis=1, keepdims=True)[0:cap, :]
        gp[...] = (gate * dys[i][...].astype(F32)).astype(BF)
        gates.append(gate)
    sums = [None] * n
    backs = [None] * n
    for b in range(GROUP):
        for c in copies[b]:
            c.wait()
        at = slice(b * width, (b + 1) * width)
        for i in range(n):
            back, out, act, dinner, gp = outs[5 * i : 5 * i + 5]
            a, slope = gelu_pair(dot(rows_in[i][0:cap, :], wu[b]))
            act[:, at] = a.astype(BF)
            dinner[:, at] = (dot(gp[...], wd[b]) * slope).astype(BF)
            o = dot_nt(act[:, at], wd[b])
            d = dot_nt(dinner[:, at], wu[b])
            sums[i] = o if b == 0 else sums[i] + o
            backs[i] = d if b == 0 else backs[i] + d
    for i in range(n):
        back, out, act, dinner, gp = outs[5 * i : 5 * i + 5]
        out[...] = (gates[i] * sums[i]).astype(BF)
        back[0:cap, :] = backs[i].astype(BF)
        dg = jnp.sum(dys[i][...].astype(F32) * sums[i], axis=1, keepdims=True)
        pad = jnp.where(eye[0:cap, :], dg, 0.0)
        dg_row = jnp.sum(pad, axis=0, keepdims=True)
        three = split3(dg_row)
        row = iota((16, lanes), 0)
        back[cap : cap + 16, :] = jnp.zeros((16, width), BF)
        back[cap : cap + 16, 0:lanes] = (
            jnp.where(row == 0, three[0].astype(F32), 0.0)
            + jnp.where(row == 1, three[1].astype(F32), 0.0)
            + jnp.where(row == 2, three[2].astype(F32), 0.0)
        ).astype(BF)


def expert(s, rows_in, dys, own, other, cap):
    n = len(rows_in)
    width = rows_in[0].shape[1]
    ff = GROUP * width
    res = call(
        functools.partial(expert_kernel, cap, n),
        [SM] + [VM] * (2 * n) + [HB] * (2 * GROUP),
        [
            shape((cap + 16, width), BF),
            shape((cap, width), BF),
            shape((cap, ff), BF),
            shape((cap, ff), BF),
            shape((cap, width), BF),
        ]
        * n,
        [
            pltpu.VMEM((GROUP, width, width), BF),
            pltpu.VMEM((GROUP, width, width), BF),
            pltpu.SemaphoreType.DMA((16,)),
        ],
        8 * n * cap * width * ff,
        4 * width * ff + n * cap * (4 * ff + 10 * width),
        "expert",
    )(s, *rows_in, *dys, *own, *other)
    return [res[5 * i : 5 * i + 5] for i in range(n)]


def grad_kernel(n, s_ref, *refs):
    lefts, rights, (give, keep) = refs[:n], refs[n : 2 * n], refs[2 * n : 2 * n + 2]
    if n == 1:
        left, right = lefts[0], rights[0]
    else:
        left, right = refs[2 * n + 2 :]
        rows = lefts[0].shape[0]
        for i in range(n):
            left[i * rows : (i + 1) * rows, :] = lefts[i][...]
            right[i * rows : (i + 1) * rows, :] = rights[i][...]
    value = dot_tn(left[...], right[...]).astype(BF)

    @pl.when(pl.program_id(0) == 0)
    def _():
        give[0] = value

    @pl.when(pl.program_id(0) == 1)
    def _():
        keep[0] = value


def weight_grad(s, lefts, rights, rows=None, weight=16):
    n = len(lefts)
    t = rows or lefts[0].shape[0]
    width = min(lefts[0].shape[1], rights[0].shape[1])
    high = width // 2
    m, nb = lefts[0].shape[1] // width, rights[0].shape[1] // width
    scratch = []
    if n > 1:
        scratch = [pltpu.VMEM((n * t, high), BF), pltpu.VMEM((n * t, width), BF)]
    left_at = lambda h, i, j, c: (0, jnp.where(h == 0, 1 - c[0], c[0]) * m + i)
    give_at = lambda h, i, j, c: (jnp.where(h == 0, i * nb + j, m * nb - 1), 0, 0)
    keep_at = lambda h, i, j, c: (jnp.where(h == 0, 0, i * nb + j), 0, 0)
    return pl.pallas_call(
        functools.partial(grad_kernel, n),
        grid_spec=pltpu.PrefetchScalarGridSpec(
            num_scalar_prefetch=1,
            grid=(2, m, nb),
            in_specs=[pl.BlockSpec((t, high), left_at)] * n
            + [pl.BlockSpec((t, width), lambda h, i, j, c: (0, j))] * n,
            out_specs=[pl.BlockSpec((1, high, width), at) for at in (give_at, keep_at)],
            scratch_shapes=scratch,
        ),
        out_shape=[shape((m * nb, high, width), BF)] * 2,
        compiler_params=pltpu.CompilerParams(vmem_limit_bytes=LIMIT),
        cost_estimate=pl.CostEstimate(
            flops=int(weight * 4) * n * t * m * high * width * nb,
            bytes_accessed=int(weight * 2) * (n * t * (2 * m * high + width * nb) + 2 * m * high * width * nb),
            transcendentals=0,
        ),
        name="weight_grad",
    )(s, *lefts, *rights)


def attention_grad_kernel(s_ref, normed, context, dpacked, dattn, give, keep):
    j = pl.program_id(1)

    def write(value):
        @pl.when(pl.program_id(0) == 0)
        def _():
            give[0] = value

        @pl.when(pl.program_id(0) == 1)
        def _():
            keep[0] = value

    @pl.when(j < 3)
    def _():
        write(dot_tn(normed[...], dpacked[...]).astype(BF))

    @pl.when(j == 3)
    def _():
        write(dot_tn(context[...], dattn[...]).astype(BF))


def attention_grad(s, normed, context, dpacked, dattn):
    t, width = normed.shape
    high = width // 2
    half_at = lambda h, j, c: (0, jnp.where(h == 0, 1 - c[0], c[0]))
    return pl.pallas_call(
        attention_grad_kernel,
        grid_spec=pltpu.PrefetchScalarGridSpec(
            num_scalar_prefetch=1,
            grid=(2, 4),
            in_specs=[
                pl.BlockSpec((t, high), half_at),
                pl.BlockSpec((t, high), half_at),
                pl.BlockSpec((t, width), lambda h, j, c: (0, jnp.minimum(j, 2))),
                pl.BlockSpec((t, width), lambda h, j, c: (0, 0)),
            ],
            out_specs=[
                pl.BlockSpec((1, high, width), lambda h, j, c: (jnp.where(h == 0, j, 3), 0, 0)),
                pl.BlockSpec((1, high, width), lambda h, j, c: (jnp.where(h == 0, 0, j), 0, 0)),
            ],
        ),
        out_shape=[shape((4, high, width), BF)] * 2,
        compiler_params=pltpu.CompilerParams(vmem_limit_bytes=LIMIT),
        cost_estimate=pl.CostEstimate(
            flops=128 * t * width * width, bytes_accessed=64 * t * width, transcendentals=0
        ),
        name="attention_grad",
    )(s, normed, context, dpacked, dattn)


def back_kernel(
    experts, cap, dy, dense, hid, gb_ref, router, place, route, live, soft, normed3, slope, fc1, fc2, *refs
):
    homes = refs[:experts]
    dmlp, dpre, dhidden, tiny, drouter = refs[experts : experts + 5]
    w1, w2, ups, sems = refs[experts + 5 :]
    rows, width = hid.shape
    copies = [
        pltpu.make_async_copy(fc1, w1, sems.at[0]),
        pltpu.make_async_copy(fc2, w2, sems.at[1]),
    ]
    for c in copies:
        c.start()
    lanes = -(-cap // WIDE) * WIDE
    spot = iota((lanes, rows), 0)
    spot = jnp.where(spot < cap, spot, -2 * experts * cap)
    dgate = [jnp.zeros((16, rows), F32) for _ in range(TOP)]
    for r in range(experts):
        tail = homes[r][cap : cap + 16, 0:lanes]
        hot = [jnp.where(spot + r * cap == place[k : k + 1, :], 1.0, 0.0).astype(BF) for k in range(TOP)]
        for k in range(TOP):
            dgate[k] = dgate[k] + dot(tail, hot[k])
        term = dot_tn((hot[0] + hot[1])[0:cap, :], homes[r][0:cap, :])
        ups[...] = term if r == 0 else ups[...] + term
    dgate = [jnp.sum(d, axis=0, keepdims=True) * live[...] for d in dgate]
    mix = soft[0:1, :] * dgate[0] + soft[1:2, :] * dgate[1]
    dsoft = [soft[k : k + 1, :] * (dgate[k] - mix) for k in range(TOP)]
    index = iota((router.shape[0], rows), 0)
    dlogits = sum(jnp.where(index == route[k : k + 1, :], dsoft[k], 0.0) for k in range(TOP))
    dlogits = dlogits.astype(BF)
    drouter[...] = dot(dlogits, normed3[...])
    ups[...] += dot_tn(dlogits, router[...])
    tile = rows // 6
    tiny[...] = jnp.zeros_like(tiny)

    def norm_back(at, values, gain, bias_row, base):
        n, scale = normalize(values)
        u = ups[at, :]
        tiny[bias_row - 1 : bias_row, :] += jnp.sum(u * n, axis=0, keepdims=True)
        tiny[bias_row : bias_row + 1, :] += jnp.sum(u, axis=0, keepdims=True)
        ug = u * gain
        dv = scale * (
            ug
            - jnp.mean(ug, axis=-1, keepdims=True)
            - n * jnp.mean(ug * n, axis=-1, keepdims=True)
        )
        return base + dv

    @pl.loop(0, 6)
    def _(i):
        at = pl.ds(pl.multiple_of(i * tile, 16), tile)
        dd = norm_back(at, dense[at, :], gb_ref[4:5, :], 5, dy[at, :].astype(F32))
        dhidden[at, :] = dd
        dmlp[at, :] = dd.astype(BF)

    for c in copies:
        c.wait()
    ups[...] = jnp.zeros_like(ups)

    @pl.loop(0, w1.shape[1] // 512)
    def _(j):
        at = pl.ds(pl.multiple_of(j * 512, 512), 512)
        dpre[:, at] = (dot_nt(dmlp[...], w2[at, :]) * slope[:, at].astype(F32)).astype(BF)
        ups[...] += dot_nt(dpre[:, at], w1[:, at])

    @pl.loop(0, 6)
    def _(i):
        at = pl.ds(pl.multiple_of(i * tile, 16), tile)
        dhidden[at, :] = norm_back(at, hid[at, :], gb_ref[2:3, :], 3, dhidden[at, :])


def back(
    dy, dense, hid, gb, router, place, route, live, soft, normed3, slope, fc1, fc2, homes, experts, cap, after
):
    rows, width = hid.shape
    ff = fc1.shape[1]
    return call(
        functools.partial(back_kernel, experts, cap),
        [VM] * 11 + [HB] * 2 + [VM] * experts,
        [
            shape((rows, width), BF),
            shape((rows, ff), BF),
            shape((rows, width), F32),
            shape((8, width), F32),
            shape(router.shape, F32),
        ],
        [
            pltpu.VMEM((width, ff), BF),
            pltpu.VMEM((ff, width), BF),
            pltpu.VMEM((rows, width), F32),
            pltpu.SemaphoreType.DMA((2,)),
        ],
        4 * rows * width * ff + 2 * rows * width * experts * cap,
        4 * width * ff + rows * (4 * ff + 18 * width),
        "dense_backward",
        after,
    )(dy, dense, hid, gb, router, place, route, live, soft, normed3, slope, fc1, fc2, *homes)


def attend_back_kernel(
    s_ref, dhid, id_row, id_col, packed, lse, wo_a, wo_b, dattn, dpacked, wo, bias, dctx, sems
):
    s = s_ref[0]
    rows, width = dhid.shape
    copies = halves_into(s, wo_a, wo_b, wo, sems, 0)
    for c in copies:
        c.start()
    tile = rows // 6

    @pl.loop(0, 6)
    def _(i):
        at = pl.ds(pl.multiple_of(i * tile, 16), tile)
        dattn[at, :] = dhid[at, :].astype(BF)
        bias[at, :] = jnp.where(id_col[at, :] == id_row[...], 0.0, MASKED)

    copies[0].wait()
    copies[1].wait()

    @pl.loop(0, width // 256)
    def _(j):
        at = pl.ds(pl.multiple_of(j * 256, 256), 256)
        dctx[:, at] = dot_nt(dattn[...], wo[at, :]).astype(BF)

    lane = iota((1, WIDE), 1)

    @pl.loop(0, width // WIDE)
    def _(pair):
        col = pl.multiple_of(pair * WIDE, WIDE)
        q = packed[:, pl.ds(col, WIDE)] * jnp.asarray(HEAD**-0.5, BF)
        keys = packed[:, pl.ds(width + col, WIDE)]
        values = packed[:, pl.ds(2 * width + col, WIDE)]
        dc = dctx[:, pl.ds(col, WIDE)]
        dq, dk, dv = [], [], []
        for h in range(2):
            mine = (lane >= h * HEAD) & (lane < (h + 1) * HEAD)
            scores = dot_nt(jnp.where(mine, keys, jnp.zeros_like(keys)), q) + bias[...]
            p = jnp.exp(scores - lse[pl.ds(2 * pair + h, 1), :])
            dp = dot_nt(jnp.where(mine, values, jnp.zeros_like(values)), dc)
            inner = jnp.sum(p * dp, axis=0, keepdims=True)
            ds = (p * (dp - inner)).astype(BF)
            dv.append(dot(p.astype(BF), dc))
            dk.append(dot(ds, q))
            dq.append(dot_tn(ds, keys) * HEAD**-0.5)
        low = lane < HEAD
        dpacked[:, pl.ds(col, WIDE)] = jnp.where(low, dq[0], dq[1]).astype(BF)
        dpacked[:, pl.ds(width + col, WIDE)] = jnp.where(low, dk[0], dk[1]).astype(BF)
        dpacked[:, pl.ds(2 * width + col, WIDE)] = jnp.where(low, dv[0], dv[1]).astype(BF)


def input_kernel(s_ref, x_ref, dhid, gb_ref, dpacked, qkv_a, qkv_b, grad_in, tiny, wq, ups, sems):
    s = s_ref[0]
    rows, width = x_ref.shape
    tile = rows // 6
    copies = halves_into(s, qkv_a, qkv_b, wq, sems, 0)
    for c in copies:
        c.start()
    copies[0].wait()
    copies[1].wait()

    @pl.loop(0, width // 256)
    def _(j):
        at = pl.ds(pl.multiple_of(j * 256, 256), 256)
        ups[:, at] = dot_nt(dpacked[...], wq[at, :])

    tiny[...] = jnp.zeros_like(tiny)

    @pl.loop(0, 6)
    def _(i):
        at = pl.ds(pl.multiple_of(i * tile, 16), tile)
        n, scale = normalize(x_ref[at, :].astype(F32))
        u = ups[at, :]
        tiny[0:1, :] += jnp.sum(u * n, axis=0, keepdims=True)
        tiny[1:2, :] += jnp.sum(u, axis=0, keepdims=True)
        ug = u * gb_ref[0:1, :]
        grad_in[at, :] = dhid[at, :] + scale * (
            ug
            - jnp.mean(ug, axis=-1, keepdims=True)
            - n * jnp.mean(ug * n, axis=-1, keepdims=True)
        )


def attend_back(s, dhid, ids, packed, lse, wo, after):
    rows, width = dhid.shape
    n3 = packed.shape[1]
    return call(
        attend_back_kernel,
        [SM] + [VM] * 5 + [HB] * 2,
        [shape((rows, width), BF), shape((rows, n3), BF)],
        [
            pltpu.VMEM((width, width), BF),
            pltpu.VMEM((rows, rows), F32),
            pltpu.VMEM((rows, width), BF),
            pltpu.SemaphoreType.DMA((2,)),
        ],
        2 * rows * width * width + 20 * rows * rows * width,
        2 * (width * width + rows * (3 * width + 2 * n3)),
        "attention_backward",
        after,
    )(s, dhid, ids[None, :], ids[:, None], packed, lse, *wo)


def input_back(s, x, dhid, gb, dpacked, qkv, after):
    rows, width = x.shape
    n3 = dpacked.shape[1]
    return call(
        input_kernel,
        [SM] + [VM] * 4 + [HB] * 2,
        [shape((rows, width), F32), shape((8, width), F32)],
        [
            pltpu.VMEM((width, n3), BF),
            pltpu.VMEM((rows, width), F32),
            pltpu.SemaphoreType.DMA((2,)),
        ],
        2 * rows * width * n3,
        2 * (width * n3 + rows * n3) + 10 * rows * width,
        "input_backward",
        after,
    )(s, x, dhid, gb, dpacked, *qkv)


def merge_kernel(experts, cap, dense, place, *refs):
    outs, result = refs[:experts], refs[experts]
    rows = dense.shape[0]
    total = dense[...]
    spot = iota((cap, rows), 0)
    for r in range(experts):
        hot = sum(jnp.where(spot + r * cap == place[k : k + 1, :], 1.0, 0.0) for k in range(TOP))
        total = total + dot_tn(hot.astype(BF), outs[r][...])
    result[...] = total.astype(BF)


def merge(dense, place, outs, experts, cap):
    rows, width = dense.shape
    return call(
        functools.partial(merge_kernel, experts, cap),
        [VM] * (2 + experts),
        shape((rows, width), BF),
        [],
        2 * rows * width * experts * cap,
        rows * width * 6 + 2 * experts * cap * width,
        "merge",
        (),
        0.25,
    )(dense, place, *outs)


def hold_kernel(n, *refs):
    for i in range(n):
        refs[n + i][...] = refs[i][...]


def hold(chunks, after):
    n = len(chunks)
    dims = chunks[0].shape
    return call(
        functools.partial(hold_kernel, n),
        [VM] * n,
        [shape(dims, BF)] * n,
        [],
        0,
        4 * n * dims[0] * dims[1],
        "hold",
        after,
    )(*chunks)


def finish_kernel(columns, m_ref, mine, got, out):
    n, high, width = mine.shape
    for which, src in ((m_ref[0], mine), (1 - m_ref[0], got)):
        for i in range(n):
            value = src[i].astype(F32)
            if columns:
                out[:, pl.ds(pl.multiple_of((which * n + i) * width, width), width)] = value
            else:
                out[pl.ds(pl.multiple_of((which * n + i) * high, high), high), :] = value


def finish(m, mine, got, columns):
    n, high, width = mine.shape
    dims = (high, 2 * n * width) if columns else (2 * n * high, width)
    return call(
        functools.partial(finish_kernel, columns),
        [SM, VM, VM],
        shape(dims, F32),
        [],
        0,
        12 * n * high * width,
        "finish",
    )(m, mine, got)


def spread_kernel(experts, cap, rows_in, place, *chunks):
    spot = iota((cap, rows_in.shape[0]), 0)
    for r in range(experts):
        hot = sum(jnp.where(spot + r * cap == place[k : k + 1, :], 1.0, 0.0) for k in range(TOP))
        chunks[r][...] = dot(hot.astype(BF), rows_in[...]).astype(BF)


def spread(rows_in, place, experts, cap):
    rows, width = rows_in.shape
    return call(
        functools.partial(spread_kernel, experts, cap),
        [VM, VM],
        [shape((cap, width), BF)] * experts,
        [],
        2 * rows * width * experts * cap,
        2 * (rows + experts * cap) * width,
        "spread",
    )(rows_in, place)


def places_of(routes, live, experts, capacity):
    tokens = routes.shape[0]
    ids = jnp.arange(experts, dtype=jnp.int32)
    match = [
        ((routes[:, k : k + 1] == ids[None, :]) & live[:, None]).astype(F32) for k in range(TOP)
    ]
    order = jnp.arange(tokens, dtype=jnp.int32)
    below = (order[:, None] > order[None, :]).astype(BF)
    before = jnp.zeros((1, experts), F32)
    out = []
    for k in range(TOP):
        counts = dot(below, match[k].astype(BF)) + before
        before = before + jnp.sum(match[k], axis=0, keepdims=True)
        within = jnp.sum(counts * match[k], axis=1).astype(jnp.int32)
        out.append(jnp.where(live, routes[:, k] * capacity + within, experts * capacity))
    return out

def local(
    tokens,
    image_ids,
    routes,
    norm1_gain,
    norm1_bias,
    qkv_weight,
    attn_out_weight,
    norm2_gain,
    norm2_bias,
    fc1_weight,
    fc2_weight,
    norm3_gain,
    norm3_bias,
    router_weight,
    expert_up,
    expert_down,
    cotangent,
):
    s = lax.axis_index("section")
    e = lax.axis_index("dp") // GROUP
    q = lax.axis_index("dp") % GROUP
    dp_count = lax.axis_size("dp")
    experts = dp_count // GROUP
    cap = GROUP * ((21 * SLOTS + 10 * experts * GROUP - 1) // (10 * experts * GROUP))
    cap = -(-cap // 16) * 16
    half = tokens.shape[1]
    width = 2 * half
    few = experts <= 8
    planes = [[p * GROUP + i for p in range(experts)] for i in range(GROUP)]
    here = jnp.reshape(s, (1,))

    def swap(v):
        return lax.ppermute(v, "section", [(0, 1), (1, 0)])

    def over_q(v, bit):
        return lax.ppermute(v, "dp", [(i, i ^ bit) for i in range(dp_count)])

    def over_e(v, r):
        return lax.ppermute(
            v,
            "dp",
            [(i, ((i // GROUP + r) % experts) * GROUP + i % GROUP) for i in range(dp_count)],
        )

    def part(v, index, size, axis=0):
        return lax.dynamic_slice_in_dim(v, index * size, size, axis)

    def join(own, other, axis):
        return jnp.where(
            s == 0,
            jnp.concatenate([own, other], axis=axis),
            jnp.concatenate([other, own], axis=axis),
        )

    def add(a, b):
        return (a.astype(F32) + b.astype(F32)).astype(BF)

    def out_chunks(chunks):
        if not few:
            return list(lax.all_to_all(jnp.stack(chunks), "dp", 0, 0, axis_index_groups=planes))
        return [chunks[0]] + [over_e(chunks[r], r) for r in range(1, experts)]

    def home_chunks(chunks):
        if not few:
            return list(lax.all_to_all(jnp.stack(chunks), "dp", 0, 0, axis_index_groups=planes))
        return [chunks[0]] + [over_e(chunks[r], experts - r) for r in range(1, experts)]

    small = jnp.stack([norm1_gain, norm1_bias, norm2_gain, norm2_bias, norm3_gain, norm3_bias])
    small = jnp.concatenate([small, jnp.transpose(router_weight)])
    small = join(small, swap(small), 1)
    x = join(part(tokens, s, SLOTS), swap(part(tokens, 1 - s, SLOTS)), 1)
    dy = join(part(cotangent, s, SLOTS), swap(part(cotangent, 1 - s, SLOTS)), 1)
    ids = part(image_ids, s, 1).reshape(-1)
    route = part(routes, s, SLOTS)
    live = ids >= 0
    gb = jnp.concatenate([small[:6], jnp.zeros((2, width), BF)]).astype(F32)
    router_rows = -(-experts // 16) * 16
    router = jnp.concatenate([small[6 : 6 + experts], jnp.zeros((router_rows - experts, width), BF)])
    qkv, wo = (qkv_weight, swap(qkv_weight)), (attn_out_weight, swap(attn_out_weight))

    pair = jnp.stack([expert_up, expert_down])

    def gather(v, tiled):
        return lax.all_gather(v, "section", axis=0, tiled=tiled)

    tie = lax.optimization_barrier
    x, dy, qkv, wo, fc1_weight, fc2_weight, pair = tie(
        (x, dy, qkv, wo, fc1_weight, fc2_weight, pair)
    )
    fc1, fc2 = gather(fc1_weight, True), gather(fc2_weight, True)
    from_x, from_y, other_pair = over_q(pair, 1), over_q(pair, 2), swap(pair)

    if few:
        distance = (route - e) % experts
    else:
        distance = route
    spots = places_of(distance, live, experts, cap)
    place = jnp.stack(spots + [jnp.full_like(spots[0], -1)] * 6)
    route_rows = jnp.concatenate([jnp.transpose(route), jnp.full((6, SLOTS), -1, jnp.int32)])
    live_row = live.astype(F32)[None, :]
    dy_sent = spread(dy, place, experts, cap)
    dy_out = out_chunks(dy_sent)

    normed1, packed, context, lse, hidden = front(here, x, ids, gb, qkv, wo, dy_sent[:1])
    hidden, from_x, from_y, other_pair, *dy_out[:-1] = tie(
        (hidden, from_x, from_y, other_pair, *dy_out[:-1])
    )
    other_x, other_y = swap(from_x), swap(from_y)
    far = [over_q(from_x[0], 2), over_q(from_y[1], 1)]
    normed2, act, slope, dense, normed3, soft, *sent = mlp(
        hidden, gb, router, place, route_rows, live_row, fc1, fc2, experts, cap, []
    )
    sent, far, other_x, other_y, dy_out[-1] = tie((sent, far, other_x, other_y, dy_out[-1]))
    far = jnp.stack(far)
    own, other = [pair, from_x, from_y, far], [other_pair, other_x, other_y, swap(far)]
    got = out_chunks(sent)

    step = max(1, experts // 4)
    results = [None] * experts
    previous, homes = None, [None] * experts
    for i in [0] + list(range(experts - step, 0, -step)):
        if i:
            got[i], results[previous] = tie((got[i], results[previous]))
        if few and 0 < i < experts - 2:
            got[i], homes[i + 2] = tie((got[i], homes[i + 2]))
        results[i : i + step] = expert(
            here, got[i : i + step], dy_out[i : i + step], own, other, cap
        )
        previous = i
        homes[i] = over_e(results[i][0], experts - i) if few and i else results[i][0]
    if not few:
        homes = home_chunks([r[0] for r in results])
    acts, dinners, scaled = ([r[i] for r in results] for i in (2, 3, 4))

    def grad_sum(*operands, weight=16):
        give, keep = weight_grad(here, *operands, weight=weight)
        return add(keep, swap(give))

    if few:
        dinners, homes[2 % experts] = tie((dinners, homes[2 % experts]))
    sum_up, sum_down = grad_sum(got, dinners, cap), grad_sum(scaled, acts)
    dmlp, dpre, dhidden, tiny23, drouter = back(
        dy, dense, hidden, gb, router, place, route_rows, live_row, soft, normed3, slope,
        fc1, fc2, homes, experts, cap, [],
    )
    outs = hold([r[1] for r in results], homes[2:3])
    dpre, dmlp, sum_up, sum_down = tie((dpre, dmlp, sum_up, sum_down))

    moved_up = over_q(jnp.stack([sum_up[1], sum_up[3]]), 1)
    moved_down = over_q(sum_down[2:], 2)
    grads1, grads2 = weight_grad(here, [normed2], [dpre]), weight_grad(here, [act], [dmlp])
    if few:
        outs = list(outs[:2]) + [over_e(outs[r], experts - r) for r in range(2, experts)]
    dhidden, grads1, grads2, moved_up, moved_down, outs = tie(
        (dhidden, grads1, grads2, moved_up, moved_down, outs)
    )
    near_up, far_up = add(sum_up[0], moved_up[0]), add(sum_up[2], moved_up[1])
    near_down, far_down = add(sum_down[0], moved_down[0]), add(sum_down[1], moved_down[1])
    far_up, far_down = over_q(far_up, 2), over_q(far_down, 1)

    def fold(v, bit):
        mine, rows = (q // bit) % 2, v.shape[0] // 2
        return part(v, mine, rows), over_q(part(v, 1 - mine, rows), bit)

    def unfold(v, got, bit):
        return jnp.where(
            (q // bit) % 2 == 0, jnp.concatenate([v, got]), jnp.concatenate([got, v])
        )

    def plane_out(a, b):
        ab = jnp.stack([a, b])
        rows = a.shape[0] // experts
        if not few:
            return [lax.psum(ab, "dp", axis_index_groups=planes)]
        return [part(ab, (e + r) % experts, rows, 1) for r in range(experts)]

    def plane_sum(pieces):
        if not few:
            return pieces
        total = sum(p.astype(F32) for p in pieces).astype(BF)
        return [total] * experts

    def plane_move(pieces):
        return pieces[:1] + [over_e(p, r) for r, p in enumerate(pieces) if r]

    def plane_join(pieces):
        if not few:
            return pieces[0][0], pieces[0][1]
        rows = pieces[0].shape[1]
        whole = jnp.zeros((2, experts * rows, width), BF)
        for r, piece in enumerate(pieces):
            whole = lax.dynamic_update_slice_in_dim(whole, piece, ((e - r) % experts) * rows, 1)
        return whole[0], whole[1]

    dattn, dpacked = attend_back(here, dhidden, ids, packed, lse, wo, [])
    away1, away2 = swap(grads1[0]), swap(grads2[0])
    out1 = over_e(outs[1], experts - 1) if few else outs[1]
    dpacked, dattn, away1, away2, far_up, far_down, out1 = tie(
        (dpacked, dattn, away1, away2, far_up, far_down, out1)
    )
    half_up = near_up.astype(F32) + far_up.astype(F32)
    half_down = near_down.astype(F32) + far_down.astype(F32)

    a, b = add(grads2[1], away2).reshape(-1, width), add(grads1[1], away1).reshape(-1, width)
    a, b = fold(a, 1), fold(b, 2)
    if few:
        home_outs = [outs[0], out1, *outs[2:]]
    else:
        home_outs = home_chunks([outs[0], out1, *outs[2:]])
    give, keep = attention_grad(here, normed1, context, dpacked, dattn)
    give, keep, a, b, home_outs, dpacked = tie((give, keep, a, b, home_outs, dpacked))
    grad_in, tiny1 = input_back(here, x, dhidden, gb, dpacked, qkv, [])
    tiny = jnp.concatenate([tiny1[:2], tiny23[2:6], drouter[:experts]])

    def swapped(v):
        return part(v, s, half, 1), swap(part(v, 1 - s, half, 1))

    away = swap(give)
    a, b = fold(add(*a), 2), fold(add(*b), 1)
    away, a, b, grad_in, tiny = tie((away, a, b, grad_in, tiny))
    grad_in, tiny = swapped(grad_in), swapped(tiny)
    tiny = tiny[0] + tiny[1]

    ab = plane_move(plane_out(add(*a), add(*b)))
    t = add(keep, away).reshape(-1, width)
    ta, tb = fold(t[:width], 1), fold(t[width:], 2)
    ab, ta, tb, home_outs, grad_in = tie((ab, ta, tb, home_outs, grad_in))
    block_out = merge(dense, place, home_outs, experts, cap)

    ab = plane_move(plane_sum(ab))
    ta, tb = fold(add(*ta), 2), fold(add(*tb), 1)
    ab, ta, tb, block_out = tie((ab, ta, tb, block_out))

    a, b = plane_join(ab)
    a_got, b_got = over_q(a, 2), over_q(b, 1)
    tab = plane_move(plane_out(add(*ta), add(*tb)))
    a_got, b_got, tab = tie((a_got, b_got, tab))
    a, b = unfold(a, a_got, 2), unfold(b, b_got, 1)
    a_got, b_got = over_q(a, 1), over_q(b, 2)
    tab = plane_move(plane_sum(tab))
    a_got, b_got, tab = tie((a_got, b_got, tab))

    side_x, side_y = jnp.reshape(q % 2, (1,)), jnp.reshape(q // 2, (1,))

    def blocks(v):
        return v.reshape(-1, half, width)

    ta, tb = plane_join(tab)
    ta_got, tb_got = over_q(ta, 2), over_q(tb, 1)
    block_out = swapped(block_out)
    tiny_q = [over_q(tiny, bit) for bit in (1, 2, 3)]
    sum_fc2 = finish(side_x, blocks(a), blocks(a_got), False)
    sum_fc1 = finish(side_y, blocks(b), blocks(b_got), True)
    ta_got, tb_got, block_out, tiny_q, sum_fc2, sum_fc1 = tie(
        (ta_got, tb_got, block_out, tiny_q, sum_fc2, sum_fc1)
    )
    ta, tb = unfold(ta, ta_got, 2), unfold(tb, tb_got, 1)
    ta_got, tb_got = over_q(ta, 1), over_q(tb, 2)
    tiny = tiny + tiny_q[0] + (tiny_q[1] + tiny_q[2])
    if few:
        total = sum(over_e(tiny, r) if r else tiny for r in range(experts))
    else:
        total = lax.psum(tiny, "dp", axis_index_groups=planes)
    q_and_k = finish(side_x, blocks(ta), blocks(ta_got), True)
    first = q // 2 == 0
    v_sum, sum_attn = (
        jnp.where(first, p, r).astype(F32) for p, r in ((tb, tb_got), (tb_got, tb))
    )
    sum_qkv = jnp.concatenate([q_and_k, v_sum], axis=1)
    return (
        join(*block_out, 0),
        join(*grad_in, 0),
        total[0],
        total[1],
        sum_qkv,
        sum_attn,
        total[2],
        total[3],
        sum_fc1,
        sum_fc2,
        total[4],
        total[5],
        jnp.transpose(total[6:]),
        half_up,
        half_down,
    )


def solution(mesh):
    placed = (
        P("dp", "section"),
        P("dp", None),
        P("dp", None),
        P("section"),
        P("section"),
        P("section", None),
        P("section", None),
        P("section"),
        P("section"),
        P("section", None),
        P("section", None),
        P("section"),
        P("section"),
        P("section", None),
        P("section", "dp"),
        P("section", "dp"),
        P("dp", "section"),
    )
    return jax.shard_map(
        local,
        mesh=mesh,
        in_specs=placed,
        out_specs=(
            P("dp", "section"),
            P("dp", "section"),
            P("section"),
            P("section"),
            P("section", None),
            P("section", None),
            P("section"),
            P("section"),
            P("section", None),
            P("section", None),
            P("section"),
            P("section"),
            P("section", None),
            P("section", "dp"),
            P("section", "dp"),
        ),
        check_vma=False,
    )
```

```python
import functools

import jax
import jax.numpy as jnp
from jax import lax
from jax.experimental import pallas as pl
from jax.experimental.pallas import tpu as pltpu
from jax.sharding import PartitionSpec as P

HEAD = 64
TOP = 2
GROUP = 4
SLOTS = 576
WIDE = 128

EPSILON = 1e-06
MASKED = -1e30
BF = jnp.bfloat16
F32 = jnp.float32
LIMIT = 24 * 1024 * 1024
LIMITS = dict(
    attention_forward=28,
    dense_forward=36,
    expert=28,
    dense_backward=40,
    attention_backward=28,
    input_backward=24,
    merge=20,
    hold=12,
    finish=24,
    spread=16,
)


def dot(a, b):
    return jnp.dot(a, b, preferred_element_type=F32)


def dot_nt(a, b):
    return lax.dot_general(a, b, (((1,), (1,)), ((), ())), preferred_element_type=F32)


def dot_tn(a, b):
    return lax.dot_general(a, b, (((0,), (0,)), ((), ())), preferred_element_type=F32)


def normalize(v):
    center = v - jnp.mean(v, axis=-1, keepdims=True)
    scale = lax.rsqrt(jnp.mean(center * center, axis=-1, keepdims=True) + EPSILON)
    return center * scale, scale


def gelu_pair(x):
    bell = jnp.exp(x * x * -0.5)
    t = 1.0 / (1.0 + jnp.abs(x) * (0.3275911 * 0.5**0.5))
    tail = (
        t
        * (
            0.127414796
            + t * (-0.142248368 + t * (0.7107068705 + t * (-0.7265760135 + t * 0.5307027145)))
        )
        * bell
    )
    cdf = jnp.where(x >= 0.0, 1.0 - tail, tail)
    return x * cdf, cdf + x * (bell * 0.3989422804014327)


def iota(shape, axis):
    return lax.broadcasted_iota(jnp.int32, shape, axis)


def halves_into(s, own, other, dest, sems, first):
    rows = own.shape[0]
    return [
        pltpu.make_async_copy(own, dest.at[pl.ds(pl.multiple_of(s * rows, rows), rows)], sems.at[first]),
        pltpu.make_async_copy(
            other, dest.at[pl.ds(pl.multiple_of((1 - s) * rows, rows), rows)], sems.at[first + 1]
        ),
    ]


def split3(v):
    hi = v.astype(BF)
    rest = v - hi.astype(F32)
    mid = rest.astype(BF)
    low = (rest - mid.astype(F32)).astype(BF)
    return hi, mid, low


VM = pl.BlockSpec(memory_space=pltpu.VMEM)
SM = pl.BlockSpec(memory_space=pltpu.SMEM)
HB = pl.BlockSpec(memory_space=pl.ANY)


def call(kernel, in_specs, out_shape, scratch, flops, moved, name, after=(), weight=16):
    limit = LIMITS[name] * 1024 * 1024
    count, extra = len(in_specs), len(after)

    def body(*refs):
        kernel(*refs[:count], *refs[count + extra :])

    made = pl.pallas_call(
        body,
        in_specs=in_specs + [HB] * extra,
        out_specs=jax.tree.map(lambda _: VM, out_shape),
        out_shape=out_shape,
        scratch_shapes=scratch,
        compiler_params=pltpu.CompilerParams(vmem_limit_bytes=limit),
        cost_estimate=pl.CostEstimate(
            flops=int(weight * flops), bytes_accessed=int(weight * moved), transcendentals=0
        ),
        name=name,
    )
    return lambda *operands: made(*operands, *after)


def shape(dims, kind):
    return jax.ShapeDtypeStruct(dims, kind)


def front_kernel(
    s_ref, x_ref, id_row, id_col, gb_ref, qkv_a, qkv_b, wo_a, wo_b,
    normed, packed, context, lse, hidden,
    wq, wo, bias, lse_col, sems,
):
    s = s_ref[0]
    rows, width = x_ref.shape
    copies = halves_into(s, qkv_a, qkv_b, wq, sems, 0) + halves_into(s, wo_a, wo_b, wo, sems, 2)
    for c in copies:
        c.start()
    tile = rows // 6

    @pl.loop(0, 6)
    def _(i):
        at = pl.ds(pl.multiple_of(i * tile, 16), tile)
        n, _ = normalize(x_ref[at, :].astype(F32))
        normed[at, :] = (n * gb_ref[0:1, :] + gb_ref[1:2, :]).astype(BF)
        bias[at, :] = jnp.where(id_col[at, :] == id_row[...], 0.0, MASKED)

    copies[0].wait()
    copies[1].wait()

    @pl.loop(0, wq.shape[1] // 256)
    def _(j):
        at = pl.ds(pl.multiple_of(j * 256, 256), 256)
        packed[:, at] = dot(normed[...], wq[:, at]).astype(BF)

    lane = iota((1, WIDE), 1)
    lse_col[...] = jnp.zeros_like(lse_col)
    third = rows // 3

    @pl.loop(0, width // WIDE)
    def _(pair):
        col = pl.multiple_of(pair * WIDE, WIDE)
        keys = packed[:, pl.ds(width + col, WIDE)]
        values = packed[:, pl.ds(2 * width + col, WIDE)]
        for r in range(3):
            at = slice(r * third, (r + 1) * third)
            q = packed[at, pl.ds(col, WIDE)] * jnp.asarray(HEAD**-0.5, BF)
            outs = []
            sums = lse_col[at, :]
            for h in range(2):
                mine = (lane >= h * HEAD) & (lane < (h + 1) * HEAD)
                scores = dot_nt(jnp.where(mine, q, jnp.zeros_like(q)), keys) + bias[at, :]
                top = jnp.max(scores, axis=1, keepdims=True)
                p = jnp.exp(scores - top)
                total = jnp.sum(p, axis=1, keepdims=True)
                outs.append(dot(p.astype(BF), values) * (1.0 / total))
                sums = jnp.where(lane == 2 * pair + h, top + jnp.log(total), sums)
            lse_col[at, :] = sums
            context[at, pl.ds(col, WIDE)] = jnp.where(lane < HEAD, outs[0], outs[1]).astype(BF)

    lse[...] = jnp.transpose(lse_col[...])[0 : lse.shape[0], :]
    copies[2].wait()
    copies[3].wait()

    @pl.loop(0, width // 256)
    def _(j):
        at = pl.ds(pl.multiple_of(j * 256, 256), 256)
        hidden[:, at] = x_ref[:, at].astype(F32) + dot(context[...], wo[:, at])


def front(s, x, ids, gb, qkv, wo, after):
    rows, width = x.shape
    n3 = qkv[0].shape[1]
    return call(
        front_kernel,
        [SM, VM, VM, VM, VM, HB, HB, HB, HB],
        [
            shape((rows, width), BF),
            shape((rows, n3), BF),
            shape((rows, width), BF),
            shape((16, rows), F32),
            shape((rows, width), F32),
        ],
        [
            pltpu.VMEM((width, n3), BF),
            pltpu.VMEM((width, width), BF),
            pltpu.VMEM((rows, rows), F32),
            pltpu.VMEM((rows, WIDE), F32),
            pltpu.SemaphoreType.DMA((4,)),
        ],
        2 * rows * width * (n3 + width) + 4 * rows * rows * width,
        2 * (width * (n3 + width) + rows * (3 * width + n3)) + 4 * rows * width,
        "attention_forward",
        after,
    )(s, x, ids[None, :], ids[:, None], gb, *qkv, *wo)


def mlp_kernel(experts, cap, hid, gb_ref, router, place, route, live, fc1, fc2, *refs):
    normed2, act, slope, dense, normed3, soft = refs[:6]
    chunks = refs[6 : 6 + experts]
    w1, w2, sems = refs[6 + experts :]
    rows, width = hid.shape
    copies = [
        pltpu.make_async_copy(fc1, w1, sems.at[0]),
        pltpu.make_async_copy(fc2, w2, sems.at[1]),
    ]
    for c in copies:
        c.start()
    tile = rows // 6

    @pl.loop(0, 6)
    def _(i):
        at = pl.ds(pl.multiple_of(i * tile, 16), tile)
        n, _ = normalize(hid[at, :])
        normed2[at, :] = (n * gb_ref[2:3, :] + gb_ref[3:4, :]).astype(BF)
        dense[at, :] = hid[at, :]

    for c in copies:
        c.wait()

    @pl.loop(0, w1.shape[1] // 512)
    def _(j):
        at = pl.ds(pl.multiple_of(j * 512, 512), 512)
        a, sl = gelu_pair(dot(normed2[...], w1[:, at]))
        act[:, at] = a.astype(BF)
        slope[:, at] = sl.astype(BF)
        dense[...] += dot(act[:, at], w2[at, :])

    @pl.loop(0, 6)
    def _(i):
        at = pl.ds(pl.multiple_of(i * tile, 16), tile)
        n, _ = normalize(dense[at, :])
        normed3[at, :] = (n * gb_ref[4:5, :] + gb_ref[5:6, :]).astype(BF)

    logits = dot_nt(router[...], normed3[...])
    expert = iota(logits.shape, 0)
    chosen = [
        jnp.sum(jnp.where(expert == route[k : k + 1, :], logits, 0.0), axis=0, keepdims=True)
        for k in range(TOP)
    ]
    top = jnp.maximum(chosen[0], chosen[1])
    raised = [jnp.exp(c - top) for c in chosen]
    total = raised[0] + raised[1]
    pieces = []
    for k in range(TOP):
        share = raised[k] / total
        soft[k : k + 1, :] = share
        three = split3(share * live[...])
        row = iota((16, rows), 0)
        pieces.append(
            jnp.where(row == 0, three[0].astype(F32), 0.0)
            + jnp.where(row == 1, three[1].astype(F32), 0.0)
            + jnp.where(row == 2, three[2].astype(F32), 0.0)
        )
    pieces = [p.astype(BF) for p in pieces]
    lanes = -(-cap // WIDE) * WIDE
    spot = iota((lanes, rows), 0)
    spot = jnp.where(spot < cap, spot, -2 * experts * cap)
    for r in range(experts):
        hot = [jnp.where(spot + r * cap == place[k : k + 1, :], 1.0, 0.0).astype(BF) for k in range(TOP)]
        both = (hot[0] + hot[1])[0:cap, :]
        chunks[r][0:cap, :] = dot(both, normed3[...]).astype(BF)
        chunks[r][cap : cap + 16, :] = jnp.zeros((16, width), BF)
        chunks[r][cap : cap + 16, 0:lanes] = (
            dot_nt(pieces[0], hot[0]) + dot_nt(pieces[1], hot[1])
        ).astype(BF)


def mlp(hid, gb, router, place, route, live, fc1, fc2, experts, cap, after):
    rows, width = hid.shape
    ff = fc1.shape[1]
    return call(
        functools.partial(mlp_kernel, experts, cap),
        [VM, VM, VM, VM, VM, VM, HB, HB],
        [
            shape((rows, width), BF),
            shape((rows, ff), BF),
            shape((rows, ff), BF),
            shape((rows, width), F32),
            shape((rows, width), BF),
            shape((8, rows), F32),
        ]
        + [shape((cap + 16, width), BF)] * experts,
        [
            pltpu.VMEM((width, ff), BF),
            pltpu.VMEM((ff, width), BF),
            pltpu.SemaphoreType.DMA((2,)),
        ],
        4 * rows * width * ff + 2 * rows * width * experts * cap,
        4 * width * ff + rows * (4 * ff + 12 * width),
        "dense_forward",
        after,
    )(hid, gb, router, place, route, live, fc1, fc2)


def expert_kernel(cap, n, s_ref, *refs):
    rows_in, dys = refs[:n], refs[n : 2 * n]
    own, other = refs[2 * n : 2 * n + 5], refs[2 * n + 5 : 2 * n + 10]
    outs = refs[2 * n + 10 : -3]
    wu, wd, sems = refs[-3:]
    s = s_ref[0]
    width = wu.shape[1]
    half = width // 2
    copies = [
        [
            pltpu.make_async_copy(
                src[b].at[u] if b < 3 else src[b + u],
                w.at[b, pl.ds(pl.multiple_of(side * half, half), half)],
                sems.at[4 * b + 2 * h + u],
            )
            for h, (side, src) in enumerate(((s, own), (1 - s, other)))
            for u, w in enumerate((wu, wd))
        ]
        for b in range(GROUP)
    ]
    for b in range(GROUP):
        for c in copies[b]:
            c.start()
    lanes = -(-cap // WIDE) * WIDE
    eye = iota((lanes, lanes), 0) == iota((lanes, lanes), 1)
    gates = []
    for i in range(n):
        back, out, act, dinner, gp = outs[5 * i : 5 * i + 5]
        g = jnp.sum(rows_in[i][cap : cap + 16, 0:lanes].astype(F32), axis=0, keepdims=True)
        gate = jnp.sum(jnp.where(eye, g, 0.0), axis=1, keepdims=True)[0:cap, :]
        gp[...] = (gate * dys[i][...].astype(F32)).astype(BF)
        gates.append(gate)
    sums = [None] * n
    backs = [None] * n
    for b in range(GROUP):
        for c in copies[b]:
            c.wait()
        at = slice(b * width, (b + 1) * width)
        for i in range(n):
            back, out, act, dinner, gp = outs[5 * i : 5 * i + 5]
            a, slope = gelu_pair(dot(rows_in[i][0:cap, :], wu[b]))
            act[:, at] = a.astype(BF)
            dinner[:, at] = (dot(gp[...], wd[b]) * slope).astype(BF)
            o = dot_nt(act[:, at], wd[b])
            d = dot_nt(dinner[:, at], wu[b])
            sums[i] = o if b == 0 else sums[i] + o
            backs[i] = d if b == 0 else backs[i] + d
    for i in range(n):
        back, out, act, dinner, gp = outs[5 * i : 5 * i + 5]
        out[...] = (gates[i] * sums[i]).astype(BF)
        back[0:cap, :] = backs[i].astype(BF)
        dg = jnp.sum(dys[i][...].astype(F32) * sums[i], axis=1, keepdims=True)
        pad = jnp.where(eye[0:cap, :], dg, 0.0)
        dg_row = jnp.sum(pad, axis=0, keepdims=True)
        three = split3(dg_row)
        row = iota((16, lanes), 0)
        back[cap : cap + 16, :] = jnp.zeros((16, width), BF)
        back[cap : cap + 16, 0:lanes] = (
            jnp.where(row == 0, three[0].astype(F32), 0.0)
            + jnp.where(row == 1, three[1].astype(F32), 0.0)
            + jnp.where(row == 2, three[2].astype(F32), 0.0)
        ).astype(BF)


def expert(s, rows_in, dys, own, other, cap):
    n = len(rows_in)
    width = rows_in[0].shape[1]
    ff = GROUP * width
    res = call(
        functools.partial(expert_kernel, cap, n),
        [SM] + [VM] * (2 * n) + [HB] * 10,
        [
            shape((cap + 16, width), BF),
            shape((cap, width), BF),
            shape((cap, ff), BF),
            shape((cap, ff), BF),
            shape((cap, width), BF),
        ]
        * n,
        [
            pltpu.VMEM((GROUP, width, width), BF),
            pltpu.VMEM((GROUP, width, width), BF),
            pltpu.SemaphoreType.DMA((16,)),
        ],
        8 * n * cap * width * ff,
        4 * width * ff + n * cap * (4 * ff + 10 * width),
        "expert",
    )(s, *rows_in, *dys, *own, *other)
    return [res[5 * i : 5 * i + 5] for i in range(n)]


def grad_kernel(n, skip, s_ref, *refs):
    lefts, rights, refs = refs[:n], refs[n : 2 * n], refs[2 * n + skip :]
    give, keep = refs[:2]
    if n == 1:
        left, right = lefts[0], rights[0]
    else:
        left, right = refs[2:]
        rows = lefts[0].shape[0]
        for i in range(n):
            left[i * rows : (i + 1) * rows, :] = lefts[i][...]
            right[i * rows : (i + 1) * rows, :] = rights[i][...]
    value = dot_tn(left[...], right[...]).astype(BF)

    @pl.when(pl.program_id(0) == 0)
    def _():
        give[0] = value

    @pl.when(pl.program_id(0) == 1)
    def _():
        keep[0] = value


def weight_grad(s, lefts, rights, rows=None, weight=16, stride=1, into=()):
    n = len(lefts)
    t = rows or lefts[0].shape[0]
    width = min(lefts[0].shape[1], rights[0].shape[1])
    high = width // 2
    m, nb = lefts[0].shape[1] // width, rights[0].shape[1] // width
    scratch = []
    if n > 1:
        scratch = [pltpu.VMEM((n * t, high), BF), pltpu.VMEM((n * t, width), BF)]
    left_at = lambda h, i, j, c: (0, jnp.where(h == 0, 1 - c[0], c[0]) * m + i)
    offset = 1 if into else 0

    def place_of(k, c):
        return ((k ^ c[1]) * stride + offset, 0, 0)

    give_at = lambda h, i, j, c: place_of(jnp.where(h == 0, i * nb + j, m * nb - 1), c)
    keep_at = lambda h, i, j, c: place_of(jnp.where(h == 0, 0, i * nb + j), c)
    return pl.pallas_call(
        functools.partial(grad_kernel, n, len(into)),
        grid_spec=pltpu.PrefetchScalarGridSpec(
            num_scalar_prefetch=1,
            grid=(2, m, nb),
            in_specs=[pl.BlockSpec((t, high), left_at)] * n
            + [pl.BlockSpec((t, width), lambda h, i, j, c: (0, j))] * n
            + [HB] * len(into),
            out_specs=[pl.BlockSpec((1, high, width), at) for at in (give_at, keep_at)],
            scratch_shapes=scratch,
        ),
        out_shape=[shape((m * nb * stride, high, width), BF)] * 2,
        input_output_aliases={1 + 2 * n + i: i for i in range(len(into))},
        compiler_params=pltpu.CompilerParams(vmem_limit_bytes=LIMIT),
        cost_estimate=pl.CostEstimate(
            flops=int(weight * 4) * n * t * m * high * width * nb,
            bytes_accessed=int(weight * 2) * (n * t * (2 * m * high + width * nb) + 2 * m * high * width * nb),
            transcendentals=0,
        ),
        name="weight_grad",
    )(s, *lefts, *rights, *into)


def attention_grad_kernel(s_ref, normed, context, dpacked, dattn, give, keep):
    j = pl.program_id(1)

    def write(value):
        @pl.when(pl.program_id(0) == 0)
        def _():
            give[0] = value

        @pl.when(pl.program_id(0) == 1)
        def _():
            keep[0] = value

    @pl.when(j < 3)
    def _():
        write(dot_tn(normed[...], dpacked[...]).astype(BF))

    @pl.when(j == 3)
    def _():
        write(dot_tn(context[...], dattn[...]).astype(BF))


def attention_grad(s, normed, context, dpacked, dattn):
    t, width = normed.shape
    high = width // 2
    half_at = lambda h, j, c: (0, jnp.where(h == 0, 1 - c[0], c[0]))
    return pl.pallas_call(
        attention_grad_kernel,
        grid_spec=pltpu.PrefetchScalarGridSpec(
            num_scalar_prefetch=1,
            grid=(2, 4),
            in_specs=[
                pl.BlockSpec((t, high), half_at),
                pl.BlockSpec((t, high), half_at),
                pl.BlockSpec((t, width), lambda h, j, c: (0, jnp.minimum(j, 2))),
                pl.BlockSpec((t, width), lambda h, j, c: (0, 0)),
            ],
            out_specs=[
                pl.BlockSpec((1, high, width), lambda h, j, c: (jnp.where(h == 0, j, 3), 0, 0)),
                pl.BlockSpec((1, high, width), lambda h, j, c: (jnp.where(h == 0, 0, j), 0, 0)),
            ],
        ),
        out_shape=[shape((4, high, width), BF)] * 2,
        compiler_params=pltpu.CompilerParams(vmem_limit_bytes=LIMIT),
        cost_estimate=pl.CostEstimate(
            flops=t * width * width, bytes_accessed=t * width, transcendentals=0
        ),
        name="attention_grad",
    )(s, normed, context, dpacked, dattn)


def back_kernel(
    experts, cap, dy, dense, hid, gb_ref, router, place, route, live, soft, normed3, slope, fc1, fc2, *refs
):
    homes = refs[:experts]
    dmlp, dpre, dhidden, tiny, drouter = refs[experts : experts + 5]
    w1, w2, ups, sems = refs[experts + 5 :]
    rows, width = hid.shape
    copies = [
        pltpu.make_async_copy(fc1, w1, sems.at[0]),
        pltpu.make_async_copy(fc2, w2, sems.at[1]),
    ]
    for c in copies:
        c.start()
    lanes = -(-cap // WIDE) * WIDE
    spot = iota((lanes, rows), 0)
    spot = jnp.where(spot < cap, spot, -2 * experts * cap)
    dgate = [jnp.zeros((16, rows), F32) for _ in range(TOP)]
    for r in range(experts):
        tail = homes[r][cap : cap + 16, 0:lanes]
        hot = [jnp.where(spot + r * cap == place[k : k + 1, :], 1.0, 0.0).astype(BF) for k in range(TOP)]
        for k in range(TOP):
            dgate[k] = dgate[k] + dot(tail, hot[k])
        term = dot_tn((hot[0] + hot[1])[0:cap, :], homes[r][0:cap, :])
        ups[...] = term if r == 0 else ups[...] + term
    dgate = [jnp.sum(d, axis=0, keepdims=True) * live[...] for d in dgate]
    mix = soft[0:1, :] * dgate[0] + soft[1:2, :] * dgate[1]
    dsoft = [soft[k : k + 1, :] * (dgate[k] - mix) for k in range(TOP)]
    index = iota((router.shape[0], rows), 0)
    dlogits = sum(jnp.where(index == route[k : k + 1, :], dsoft[k], 0.0) for k in range(TOP))
    dlogits = dlogits.astype(BF)
    drouter[...] = dot(dlogits, normed3[...])
    ups[...] += dot_tn(dlogits, router[...])
    tile = rows // 6
    tiny[...] = jnp.zeros_like(tiny)

    def norm_back(at, values, gain, bias_row, base):
        n, scale = normalize(values)
        u = ups[at, :]
        tiny[bias_row - 1 : bias_row, :] += jnp.sum(u * n, axis=0, keepdims=True)
        tiny[bias_row : bias_row + 1, :] += jnp.sum(u, axis=0, keepdims=True)
        ug = u * gain
        dv = scale * (
            ug
            - jnp.mean(ug, axis=-1, keepdims=True)
            - n * jnp.mean(ug * n, axis=-1, keepdims=True)
        )
        return base + dv

    @pl.loop(0, 6)
    def _(i):
        at = pl.ds(pl.multiple_of(i * tile, 16), tile)
        dd = norm_back(at, dense[at, :], gb_ref[4:5, :], 5, dy[at, :].astype(F32))
        dhidden[at, :] = dd
        dmlp[at, :] = dd.astype(BF)

    for c in copies:
        c.wait()
    ups[...] = jnp.zeros_like(ups)

    @pl.loop(0, w1.shape[1] // 512)
    def _(j):
        at = pl.ds(pl.multiple_of(j * 512, 512), 512)
        dpre[:, at] = (dot_nt(dmlp[...], w2[at, :]) * slope[:, at].astype(F32)).astype(BF)
        ups[...] += dot_nt(dpre[:, at], w1[:, at])

    @pl.loop(0, 6)
    def _(i):
        at = pl.ds(pl.multiple_of(i * tile, 16), tile)
        dhidden[at, :] = norm_back(at, hid[at, :], gb_ref[2:3, :], 3, dhidden[at, :])


def back(
    dy, dense, hid, gb, router, place, route, live, soft, normed3, slope, fc1, fc2, homes, experts, cap, after
):
    rows, width = hid.shape
    ff = fc1.shape[1]
    return call(
        functools.partial(back_kernel, experts, cap),
        [VM] * 11 + [HB] * 2 + [VM] * experts,
        [
            shape((rows, width), BF),
            shape((rows, ff), BF),
            shape((rows, width), F32),
            shape((8, width), F32),
            shape(router.shape, F32),
        ],
        [
            pltpu.VMEM((width, ff), BF),
            pltpu.VMEM((ff, width), BF),
            pltpu.VMEM((rows, width), F32),
            pltpu.SemaphoreType.DMA((2,)),
        ],
        4 * rows * width * ff + 2 * rows * width * experts * cap,
        4 * width * ff + rows * (4 * ff + 18 * width),
        "dense_backward",
        after,
    )(dy, dense, hid, gb, router, place, route, live, soft, normed3, slope, fc1, fc2, *homes)


def attend_back_kernel(
    s_ref, dhid, id_row, id_col, packed, lse, wo_a, wo_b, dattn, dpacked, wo, bias, dctx, sems
):
    s = s_ref[0]
    rows, width = dhid.shape
    copies = halves_into(s, wo_a, wo_b, wo, sems, 0)
    for c in copies:
        c.start()
    tile = rows // 6

    @pl.loop(0, 6)
    def _(i):
        at = pl.ds(pl.multiple_of(i * tile, 16), tile)
        dattn[at, :] = dhid[at, :].astype(BF)
        bias[at, :] = jnp.where(id_col[at, :] == id_row[...], 0.0, MASKED)

    copies[0].wait()
    copies[1].wait()

    @pl.loop(0, width // 256)
    def _(j):
        at = pl.ds(pl.multiple_of(j * 256, 256), 256)
        dctx[:, at] = dot_nt(dattn[...], wo[at, :]).astype(BF)

    lane = iota((1, WIDE), 1)

    @pl.loop(0, width // WIDE)
    def _(pair):
        col = pl.multiple_of(pair * WIDE, WIDE)
        q = packed[:, pl.ds(col, WIDE)] * jnp.asarray(HEAD**-0.5, BF)
        keys = packed[:, pl.ds(width + col, WIDE)]
        values = packed[:, pl.ds(2 * width + col, WIDE)]
        dc = dctx[:, pl.ds(col, WIDE)]
        dq, dk, dv = [], [], []
        for h in range(2):
            mine = (lane >= h * HEAD) & (lane < (h + 1) * HEAD)
            scores = dot_nt(jnp.where(mine, keys, jnp.zeros_like(keys)), q) + bias[...]
            p = jnp.exp(scores - lse[pl.ds(2 * pair + h, 1), :])
            dp = dot_nt(jnp.where(mine, values, jnp.zeros_like(values)), dc)
            inner = jnp.sum(p * dp, axis=0, keepdims=True)
            ds = (p * (dp - inner)).astype(BF)
            dv.append(dot(p.astype(BF), dc))
            dk.append(dot(ds, q))
            dq.append(dot_tn(ds, keys) * HEAD**-0.5)
        low = lane < HEAD
        dpacked[:, pl.ds(col, WIDE)] = jnp.where(low, dq[0], dq[1]).astype(BF)
        dpacked[:, pl.ds(width + col, WIDE)] = jnp.where(low, dk[0], dk[1]).astype(BF)
        dpacked[:, pl.ds(2 * width + col, WIDE)] = jnp.where(low, dv[0], dv[1]).astype(BF)


def input_kernel(s_ref, x_ref, dhid, gb_ref, dpacked, qkv_a, qkv_b, grad_in, tiny, wq, ups, sems):
    s = s_ref[0]
    rows, width = x_ref.shape
    tile = rows // 6
    copies = halves_into(s, qkv_a, qkv_b, wq, sems, 0)
    for c in copies:
        c.start()
    copies[0].wait()
    copies[1].wait()

    @pl.loop(0, width // 256)
    def _(j):
        at = pl.ds(pl.multiple_of(j * 256, 256), 256)
        ups[:, at] = dot_nt(dpacked[...], wq[at, :])

    tiny[...] = jnp.zeros_like(tiny)

    @pl.loop(0, 6)
    def _(i):
        at = pl.ds(pl.multiple_of(i * tile, 16), tile)
        n, scale = normalize(x_ref[at, :].astype(F32))
        u = ups[at, :]
        tiny[0:1, :] += jnp.sum(u * n, axis=0, keepdims=True)
        tiny[1:2, :] += jnp.sum(u, axis=0, keepdims=True)
        ug = u * gb_ref[0:1, :]
        grad_in[at, :] = dhid[at, :] + scale * (
            ug
            - jnp.mean(ug, axis=-1, keepdims=True)
            - n * jnp.mean(ug * n, axis=-1, keepdims=True)
        )


def attend_back(s, dhid, ids, packed, lse, wo, after):
    rows, width = dhid.shape
    n3 = packed.shape[1]
    return call(
        attend_back_kernel,
        [SM] + [VM] * 5 + [HB] * 2,
        [shape((rows, width), BF), shape((rows, n3), BF)],
        [
            pltpu.VMEM((width, width), BF),
            pltpu.VMEM((rows, rows), F32),
            pltpu.VMEM((rows, width), BF),
            pltpu.SemaphoreType.DMA((2,)),
        ],
        2 * rows * width * width + 20 * rows * rows * width,
        2 * (width * width + rows * (3 * width + 2 * n3)),
        "attention_backward",
        after,
    )(s, dhid, ids[None, :], ids[:, None], packed, lse, *wo)


def input_back(s, x, dhid, gb, dpacked, qkv, after):
    rows, width = x.shape
    n3 = dpacked.shape[1]
    return call(
        input_kernel,
        [SM] + [VM] * 4 + [HB] * 2,
        [shape((rows, width), F32), shape((8, width), F32)],
        [
            pltpu.VMEM((width, n3), BF),
            pltpu.VMEM((rows, width), F32),
            pltpu.SemaphoreType.DMA((2,)),
        ],
        2 * rows * width * n3,
        2 * (width * n3 + rows * n3) + 10 * rows * width,
        "input_backward",
        after,
    )(s, x, dhid, gb, dpacked, *qkv)


def merge_kernel(experts, cap, dense, place, *refs):
    outs, result = refs[:experts], refs[experts]
    rows = dense.shape[0]
    total = dense[...]
    spot = iota((cap, rows), 0)
    for r in range(experts):
        hot = sum(jnp.where(spot + r * cap == place[k : k + 1, :], 1.0, 0.0) for k in range(TOP))
        total = total + dot_tn(hot.astype(BF), outs[r][...])
    result[...] = total.astype(BF)


def merge(dense, place, outs, experts, cap):
    rows, width = dense.shape
    return call(
        functools.partial(merge_kernel, experts, cap),
        [VM] * (2 + experts),
        shape((rows, width), BF),
        [],
        2 * rows * width * experts * cap,
        rows * width * 6 + 2 * experts * cap * width,
        "merge",
        (),
        0.25,
    )(dense, place, *outs)


def hold_kernel(n, *refs):
    for i in range(n):
        refs[n + i][...] = refs[i][...]


def hold(chunks, after):
    n = len(chunks)
    dims = chunks[0].shape
    return call(
        functools.partial(hold_kernel, n),
        [VM] * n,
        [shape(dims, BF)] * n,
        [],
        0,
        4 * n * dims[0] * dims[1],
        "hold",
        after,
    )(*chunks)


def finish_kernel(columns, m_ref, mine, got, out):
    n, high, width = mine.shape
    for which, src in ((m_ref[0], mine), (1 - m_ref[0], got)):
        for i in range(n):
            value = src[i].astype(F32)
            if columns:
                out[:, pl.ds(pl.multiple_of((which * n + i) * width, width), width)] = value
            else:
                out[pl.ds(pl.multiple_of((which * n + i) * high, high), high), :] = value


def finish(m, mine, got, columns):
    n, high, width = mine.shape
    dims = (high, 2 * n * width) if columns else (2 * n * high, width)
    return call(
        functools.partial(finish_kernel, columns),
        [SM, VM, VM],
        shape(dims, F32),
        [],
        0,
        12 * n * high * width,
        "finish",
    )(m, mine, got)


def spread_kernel(experts, cap, rows_in, place, *chunks):
    spot = iota((cap, rows_in.shape[0]), 0)
    for r in range(experts):
        hot = sum(jnp.where(spot + r * cap == place[k : k + 1, :], 1.0, 0.0) for k in range(TOP))
        chunks[r][...] = dot(hot.astype(BF), rows_in[...]).astype(BF)


def spread(rows_in, place, experts, cap):
    rows, width = rows_in.shape
    return call(
        functools.partial(spread_kernel, experts, cap),
        [VM, VM],
        [shape((cap, width), BF)] * experts,
        [],
        2 * rows * width * experts * cap,
        2 * (rows + experts * cap) * width,
        "spread",
    )(rows_in, place)


def places_of(routes, live, experts, capacity):
    tokens = routes.shape[0]
    ids = jnp.arange(experts, dtype=jnp.int32)
    match = [
        ((routes[:, k : k + 1] == ids[None, :]) & live[:, None]).astype(F32) for k in range(TOP)
    ]
    order = jnp.arange(tokens, dtype=jnp.int32)
    below = (order[:, None] > order[None, :]).astype(BF)
    before = jnp.zeros((1, experts), F32)
    out = []
    for k in range(TOP):
        counts = dot(below, match[k].astype(BF)) + before
        before = before + jnp.sum(match[k], axis=0, keepdims=True)
        within = jnp.sum(counts * match[k], axis=1).astype(jnp.int32)
        out.append(jnp.where(live, routes[:, k] * capacity + within, experts * capacity))
    return out

def local(
    tokens,
    image_ids,
    routes,
    norm1_gain,
    norm1_bias,
    qkv_weight,
    attn_out_weight,
    norm2_gain,
    norm2_bias,
    fc1_weight,
    fc2_weight,
    norm3_gain,
    norm3_bias,
    router_weight,
    expert_up,
    expert_down,
    cotangent,
):
    s = lax.axis_index("section")
    e = lax.axis_index("dp") // GROUP
    q = lax.axis_index("dp") % GROUP
    dp_count = lax.axis_size("dp")
    experts = dp_count // GROUP
    cap = GROUP * ((21 * SLOTS + 10 * experts * GROUP - 1) // (10 * experts * GROUP))
    cap = -(-cap // 16) * 16
    half = tokens.shape[1]
    width = 2 * half
    few = experts <= 8
    planes = [[p * GROUP + i for p in range(experts)] for i in range(GROUP)]
    here, here_q = jnp.stack([s, 0 * s]), jnp.stack([s, q])
    quads = [[p * GROUP + i for i in range(GROUP)] for p in range(experts)]

    def swap(v):
        return lax.ppermute(v, "section", [(0, 1), (1, 0)])

    def over_q(v, bit):
        return lax.ppermute(v, "dp", [(i, i ^ bit) for i in range(dp_count)])

    def over_e(v, r):
        return lax.ppermute(
            v,
            "dp",
            [(i, ((i // GROUP + r) % experts) * GROUP + i % GROUP) for i in range(dp_count)],
        )

    def part(v, index, size, axis=0):
        return lax.dynamic_slice_in_dim(v, index * size, size, axis)

    def join(own, other, axis):
        return jnp.where(
            s == 0,
            jnp.concatenate([own, other], axis=axis),
            jnp.concatenate([other, own], axis=axis),
        )

    def add(a, b):
        return (a.astype(F32) + b.astype(F32)).astype(BF)

    def out_chunks(chunks):
        if not few:
            return list(lax.all_to_all(jnp.stack(chunks), "dp", 0, 0, axis_index_groups=planes))
        return [chunks[0]] + [over_e(chunks[r], r) for r in range(1, experts)]

    def home_chunks(chunks):
        if not few:
            return list(lax.all_to_all(jnp.stack(chunks), "dp", 0, 0, axis_index_groups=planes))
        return [chunks[0]] + [over_e(chunks[r], experts - r) for r in range(1, experts)]

    small = jnp.stack([norm1_gain, norm1_bias, norm2_gain, norm2_bias, norm3_gain, norm3_bias])
    small = jnp.concatenate([small, jnp.transpose(router_weight)])
    small = join(small, swap(small), 1)
    x = join(part(tokens, s, SLOTS), swap(part(tokens, 1 - s, SLOTS)), 1)
    dy = join(part(cotangent, s, SLOTS), swap(part(cotangent, 1 - s, SLOTS)), 1)
    ids = part(image_ids, s, 1).reshape(-1)
    route = part(routes, s, SLOTS)
    live = ids >= 0
    gb = jnp.concatenate([small[:6], jnp.zeros((2, width), BF)]).astype(F32)
    router_rows = -(-experts // 16) * 16
    router = jnp.concatenate([small[6 : 6 + experts], jnp.zeros((router_rows - experts, width), BF)])
    qkv, wo = (qkv_weight, swap(qkv_weight)), (attn_out_weight, swap(attn_out_weight))

    pair = jnp.stack([expert_up, expert_down])

    def gather(v, tiled):
        return lax.all_gather(v, "section", axis=0, tiled=tiled)

    tie = lax.optimization_barrier
    x, dy, qkv, wo, fc1_weight, fc2_weight, pair = tie(
        (x, dy, qkv, wo, fc1_weight, fc2_weight, pair)
    )
    fc1, fc2 = gather(fc1_weight, True), gather(fc2_weight, True)
    from_x, from_y, other_pair = over_q(pair, 1), over_q(pair, 2), swap(pair)

    if few:
        distance = (route - e) % experts
    else:
        distance = route
    spots = places_of(distance, live, experts, cap)
    place = jnp.stack(spots + [jnp.full_like(spots[0], -1)] * 6)
    route_rows = jnp.concatenate([jnp.transpose(route), jnp.full((6, SLOTS), -1, jnp.int32)])
    live_row = live.astype(F32)[None, :]
    dy_sent = spread(dy, place, experts, cap)
    dy_out = out_chunks(dy_sent)

    normed1, packed, context, lse, hidden = front(here, x, ids, gb, qkv, wo, dy_sent[:1])
    hidden, from_x, from_y, other_pair, *dy_out[:-1] = tie(
        (hidden, from_x, from_y, other_pair, *dy_out[:-1])
    )
    other_x, other_y = swap(from_x), swap(from_y)
    far = [over_q(from_x[0], 2), over_q(from_y[1], 1)]
    normed2, act, slope, dense, normed3, soft, *sent = mlp(
        hidden, gb, router, place, route_rows, live_row, fc1, fc2, experts, cap, []
    )
    sent, far, other_x, other_y, dy_out[-1] = tie((sent, far, other_x, other_y, dy_out[-1]))
    got = out_chunks(sent)
    own = [pair, from_x, from_y, *far]
    other = [other_pair, other_x, other_y, swap(far[0]), swap(far[1])]

    step = max(1, experts // 4)
    results = [None] * experts
    previous, homes = None, [None] * experts
    order = [0, 3, 1, 2] if experts == 4 else list(range(0, experts, step))
    for place_in_order, i in enumerate(order):
        if i:
            got[i], results[previous] = tie((got[i], results[previous]))
        if few and place_in_order == 3:
            got[i], homes[order[1]] = tie((got[i], homes[order[1]]))
        results[i : i + step] = expert(
            here, got[i : i + step], dy_out[i : i + step], own, other, cap
        )
        previous = i
        homes[i] = over_e(results[i][0], experts - i) if few and i else results[i][0]
    if not few:
        homes = home_chunks([r[0] for r in results])
    acts, dinners, scaled = ([r[i] for r in results] for i in (2, 3, 4))

    if experts == 4:
        dinners, homes[1] = tie((dinners, homes[1]))
        acts, homes[2] = tie((acts, homes[2]))
    give, keep = weight_grad(
        here_q, scaled, acts, stride=2,
        into=weight_grad(here_q, got, dinners, cap, stride=2),
    )
    sum_experts = add(keep, swap(give))
    dmlp, dpre, dhidden, tiny23, drouter = back(
        dy, dense, hidden, gb, router, place, route_rows, live_row, soft, normed3, slope,
        fc1, fc2, homes, experts, cap, [],
    )
    outs = hold([r[1] for r in results], homes)
    dpre, sum_experts = tie((dpre, sum_experts))
    half_experts = lax.psum_scatter(
        sum_experts.reshape(GROUP, 2, half, -1),
        "dp", scatter_dimension=0, axis_index_groups=quads, tiled=False,
    )
    grads1, grads2 = weight_grad(here, [normed2], [dpre]), weight_grad(here, [act], [dmlp])

    def fold(v, bit):
        mine, rows = (q // bit) % 2, v.shape[0] // 2
        return part(v, mine, rows), over_q(part(v, 1 - mine, rows), bit)

    def unfold(v, got, bit):
        return jnp.where(
            (q // bit) % 2 == 0, jnp.concatenate([v, got]), jnp.concatenate([got, v])
        )

    def plane_out(a, b):
        ab = jnp.stack([a, b])
        rows = a.shape[0] // experts
        if not few:
            return [lax.psum(ab, "dp", axis_index_groups=planes)]
        return [part(ab, (e + r) % experts, rows, 1) for r in range(experts)]

    def plane_sum(pieces):
        if not few:
            return pieces
        total = sum(p.astype(F32) for p in pieces).astype(BF)
        return [total] * experts

    def plane_move(pieces):
        return pieces[:1] + [over_e(p, r) for r, p in enumerate(pieces) if r]

    def plane_join(pieces):
        if not few:
            return pieces[0][0], pieces[0][1]
        rows = pieces[0].shape[1]
        whole = jnp.zeros((2, experts * rows, width), BF)
        for r, piece in enumerate(pieces):
            whole = lax.dynamic_update_slice_in_dim(whole, piece, ((e - r) % experts) * rows, 1)
        return whole[0], whole[1]

    away1, away2 = swap(grads1[0]), swap(grads2[0])
    dhidden, away1, away2, grads1, grads2 = tie((dhidden, away1, away2, grads1, grads2))
    a, b = add(grads2[1], away2).reshape(-1, width), add(grads1[1], away1).reshape(-1, width)
    a, b = fold(a, 1), fold(b, 2)
    dattn, dpacked = attend_back(here, dhidden, ids, packed, lse, wo, [])
    home_outs = home_chunks(outs)
    dpacked, dattn, home_outs = tie((dpacked, dattn, home_outs))
    give, keep = attention_grad(here, normed1, context, dpacked, dattn)
    give, keep, a, b, dpacked = tie((give, keep, a, b, dpacked))
    grad_in, tiny1 = input_back(here, x, dhidden, gb, dpacked, qkv, [])
    tiny = jnp.concatenate([tiny1[:2], tiny23[2:6], drouter[:experts]])

    def swapped(v):
        return part(v, s, half, 1), swap(part(v, 1 - s, half, 1))

    away = swap(give)
    a, b = fold(add(*a), 2), fold(add(*b), 1)
    away, a, b, grad_in, tiny = tie((away, a, b, grad_in, tiny))
    grad_in, tiny = swapped(grad_in), swapped(tiny)
    tiny = tiny[0] + tiny[1]

    ab = plane_move(plane_out(add(*a), add(*b)))
    t = add(keep, away).reshape(-1, width)
    ta, tb = fold(t[:width], 1), fold(t[width:], 2)
    ab, ta, tb, grad_in = tie((ab, ta, tb, grad_in))
    block_out = merge(dense, place, home_outs, experts, cap)

    ab = plane_move(plane_sum(ab))
    ta, tb = fold(add(*ta), 2), fold(add(*tb), 1)
    ab, ta, tb, block_out = tie((ab, ta, tb, block_out))

    a, b = plane_join(ab)
    a_got, b_got = over_q(a, 2), over_q(b, 1)
    tab = plane_move(plane_out(add(*ta), add(*tb)))
    a_got, b_got, tab, half_experts = tie((a_got, b_got, tab, half_experts))
    a, b = unfold(a, a_got, 2), unfold(b, b_got, 1)
    a_got, b_got = over_q(a, 1), over_q(b, 2)
    tab = plane_move(plane_sum(tab))
    a_got, b_got, tab = tie((a_got, b_got, tab))

    side_x, side_y = jnp.reshape(q % 2, (1,)), jnp.reshape(q // 2, (1,))

    def blocks(v):
        return v.reshape(-1, half, width)

    ta, tb = plane_join(tab)
    ta_got, tb_got = over_q(ta, 2), over_q(tb, 1)
    block_out = swapped(block_out)
    tiny_q = [over_q(tiny, bit) for bit in (1, 2, 3)]
    sum_fc2 = finish(side_x, blocks(a), blocks(a_got), False)
    sum_fc1 = finish(side_y, blocks(b), blocks(b_got), True)
    ta_got, tb_got, block_out, tiny_q, sum_fc2, sum_fc1 = tie(
        (ta_got, tb_got, block_out, tiny_q, sum_fc2, sum_fc1)
    )
    half_up, half_down = half_experts[0].astype(F32), half_experts[1].astype(F32)
    ta, tb = unfold(ta, ta_got, 2), unfold(tb, tb_got, 1)
    ta_got, tb_got = over_q(ta, 1), over_q(tb, 2)
    tiny = tiny + tiny_q[0] + (tiny_q[1] + tiny_q[2])
    if few:
        total = sum(over_e(tiny, r) if r else tiny for r in range(experts))
    else:
        total = lax.psum(tiny, "dp", axis_index_groups=planes)
    q_and_k = finish(side_x, blocks(ta), blocks(ta_got), True)
    first = q // 2 == 0
    v_sum, sum_attn = (
        jnp.where(first, p, r).astype(F32) for p, r in ((tb, tb_got), (tb_got, tb))
    )
    sum_qkv = jnp.concatenate([q_and_k, v_sum], axis=1)
    return (
        join(*block_out, 0),
        join(*grad_in, 0),
        total[0],
        total[1],
        sum_qkv,
        sum_attn,
        total[2],
        total[3],
        sum_fc1,
        sum_fc2,
        total[4],
        total[5],
        jnp.transpose(total[6:]),
        half_up,
        half_down,
    )


def solution(mesh):
    placed = (
        P("dp", "section"),
        P("dp", None),
        P("dp", None),
        P("section"),
        P("section"),
        P("section", None),
        P("section", None),
        P("section"),
        P("section"),
        P("section", None),
        P("section", None),
        P("section"),
        P("section"),
        P("section", None),
        P("section", "dp"),
        P("section", "dp"),
        P("dp", "section"),
    )
    return jax.shard_map(
        local,
        mesh=mesh,
        in_specs=placed,
        out_specs=(
            P("dp", "section"),
            P("dp", "section"),
            P("section"),
            P("section"),
            P("section", None),
            P("section", None),
            P("section"),
            P("section"),
            P("section", None),
            P("section", None),
            P("section"),
            P("section"),
            P("section", None),
            P("section", "dp"),
            P("section", "dp"),
        ),
        check_vma=False,
    )
```

```python
import functools

import jax
import jax.numpy as jnp
from jax import lax
from jax.experimental import pallas as pl
from jax.experimental.pallas import tpu as pltpu
from jax.sharding import PartitionSpec as P

HEAD = 64
TOP = 2
GROUP = 4
SLOTS = 576
WIDE = 128

EPSILON = 1e-06
MASKED = -1e30
BF = jnp.bfloat16
F32 = jnp.float32
LIMIT = 24 * 1024 * 1024
LIMITS = dict(
    attention_forward=28,
    dense_forward=36,
    expert=28,
    dense_backward=40,
    attention_backward=28,
    input_backward=24,
    merge=20,
    hold=12,
    finish=24,
    spread=16,
)


def dot(a, b):
    return jnp.dot(a, b, preferred_element_type=F32)


def dot_nt(a, b):
    return lax.dot_general(a, b, (((1,), (1,)), ((), ())), preferred_element_type=F32)


def dot_tn(a, b):
    return lax.dot_general(a, b, (((0,), (0,)), ((), ())), preferred_element_type=F32)


def normalize(v):
    center = v - jnp.mean(v, axis=-1, keepdims=True)
    scale = lax.rsqrt(jnp.mean(center * center, axis=-1, keepdims=True) + EPSILON)
    return center * scale, scale


def gelu_pair(x):
    bell = jnp.exp(x * x * -0.5)
    t = 1.0 / (1.0 + jnp.abs(x) * (0.3275911 * 0.5**0.5))
    tail = (
        t
        * (
            0.127414796
            + t * (-0.142248368 + t * (0.7107068705 + t * (-0.7265760135 + t * 0.5307027145)))
        )
        * bell
    )
    cdf = jnp.where(x >= 0.0, 1.0 - tail, tail)
    return x * cdf, cdf + x * (bell * 0.3989422804014327)


def iota(shape, axis):
    return lax.broadcasted_iota(jnp.int32, shape, axis)


def halves_into(s, own, other, dest, sems, first):
    rows = own.shape[0]
    return [
        pltpu.make_async_copy(own, dest.at[pl.ds(pl.multiple_of(s * rows, rows), rows)], sems.at[first]),
        pltpu.make_async_copy(
            other, dest.at[pl.ds(pl.multiple_of((1 - s) * rows, rows), rows)], sems.at[first + 1]
        ),
    ]


def split3(v):
    hi = v.astype(BF)
    rest = v - hi.astype(F32)
    mid = rest.astype(BF)
    low = (rest - mid.astype(F32)).astype(BF)
    return hi, mid, low


VM = pl.BlockSpec(memory_space=pltpu.VMEM)
SM = pl.BlockSpec(memory_space=pltpu.SMEM)
HB = pl.BlockSpec(memory_space=pl.ANY)


def call(kernel, in_specs, out_shape, scratch, flops, moved, name, after=(), weight=16):
    limit = LIMITS[name] * 1024 * 1024
    count, extra = len(in_specs), len(after)

    def body(*refs):
        kernel(*refs[:count], *refs[count + extra :])

    made = pl.pallas_call(
        body,
        in_specs=in_specs + [HB] * extra,
        out_specs=jax.tree.map(lambda _: VM, out_shape),
        out_shape=out_shape,
        scratch_shapes=scratch,
        compiler_params=pltpu.CompilerParams(vmem_limit_bytes=limit),
        cost_estimate=pl.CostEstimate(
            flops=int(weight * flops), bytes_accessed=int(weight * moved), transcendentals=0
        ),
        name=name,
    )
    return lambda *operands: made(*operands, *after)


def shape(dims, kind):
    return jax.ShapeDtypeStruct(dims, kind)


def front_kernel(
    s_ref, x_ref, id_row, id_col, gb_ref, qkv_a, qkv_b, wo_a, wo_b,
    normed, packed, context, lse, hidden,
    wq, wo, bias, lse_col, sems,
):
    s = s_ref[0]
    rows, width = x_ref.shape
    copies = halves_into(s, qkv_a, qkv_b, wq, sems, 0) + halves_into(s, wo_a, wo_b, wo, sems, 2)
    for c in copies:
        c.start()
    tile = rows // 6

    @pl.loop(0, 6)
    def _(i):
        at = pl.ds(pl.multiple_of(i * tile, 16), tile)
        n, _ = normalize(x_ref[at, :].astype(F32))
        normed[at, :] = (n * gb_ref[0:1, :] + gb_ref[1:2, :]).astype(BF)
        bias[at, :] = jnp.where(id_col[at, :] == id_row[...], 0.0, MASKED)

    copies[0].wait()
    copies[1].wait()

    @pl.loop(0, wq.shape[1] // 256)
    def _(j):
        at = pl.ds(pl.multiple_of(j * 256, 256), 256)
        packed[:, at] = dot(normed[...], wq[:, at]).astype(BF)

    lane = iota((1, WIDE), 1)
    lse_col[...] = jnp.zeros_like(lse_col)
    third = rows // 3

    @pl.loop(0, width // WIDE)
    def _(pair):
        col = pl.multiple_of(pair * WIDE, WIDE)
        keys = packed[:, pl.ds(width + col, WIDE)]
        values = packed[:, pl.ds(2 * width + col, WIDE)]
        for r in range(3):
            at = slice(r * third, (r + 1) * third)
            q = packed[at, pl.ds(col, WIDE)] * jnp.asarray(HEAD**-0.5, BF)
            outs = []
            sums = lse_col[at, :]
            for h in range(2):
                mine = (lane >= h * HEAD) & (lane < (h + 1) * HEAD)
                scores = dot_nt(jnp.where(mine, q, jnp.zeros_like(q)), keys) + bias[at, :]
                top = jnp.max(scores, axis=1, keepdims=True)
                p = jnp.exp(scores - top)
                total = jnp.sum(p, axis=1, keepdims=True)
                outs.append(dot(p.astype(BF), values) * (1.0 / total))
                sums = jnp.where(lane == 2 * pair + h, top + jnp.log(total), sums)
            lse_col[at, :] = sums
            context[at, pl.ds(col, WIDE)] = jnp.where(lane < HEAD, outs[0], outs[1]).astype(BF)

    lse[...] = jnp.transpose(lse_col[...])[0 : lse.shape[0], :]
    copies[2].wait()
    copies[3].wait()

    @pl.loop(0, width // 256)
    def _(j):
        at = pl.ds(pl.multiple_of(j * 256, 256), 256)
        hidden[:, at] = x_ref[:, at].astype(F32) + dot(context[...], wo[:, at])


def front(s, x, ids, gb, qkv, wo, after):
    rows, width = x.shape
    n3 = qkv[0].shape[1]
    return call(
        front_kernel,
        [SM, VM, VM, VM, VM, HB, HB, HB, HB],
        [
            shape((rows, width), BF),
            shape((rows, n3), BF),
            shape((rows, width), BF),
            shape((16, rows), F32),
            shape((rows, width), F32),
        ],
        [
            pltpu.VMEM((width, n3), BF),
            pltpu.VMEM((width, width), BF),
            pltpu.VMEM((rows, rows), F32),
            pltpu.VMEM((rows, WIDE), F32),
            pltpu.SemaphoreType.DMA((4,)),
        ],
        2 * rows * width * (n3 + width) + 4 * rows * rows * width,
        2 * (width * (n3 + width) + rows * (3 * width + n3)) + 4 * rows * width,
        "attention_forward",
        after,
    )(s, x, ids[None, :], ids[:, None], gb, *qkv, *wo)


def mlp_kernel(experts, cap, hid, gb_ref, router, place, route, live, fc1, fc2, *refs):
    normed2, act, slope, dense, normed3, soft = refs[:6]
    chunks = refs[6 : 6 + experts]
    w1, w2, sems = refs[6 + experts :]
    rows, width = hid.shape
    copies = [
        pltpu.make_async_copy(fc1, w1, sems.at[0]),
        pltpu.make_async_copy(fc2, w2, sems.at[1]),
    ]
    for c in copies:
        c.start()
    tile = rows // 6

    @pl.loop(0, 6)
    def _(i):
        at = pl.ds(pl.multiple_of(i * tile, 16), tile)
        n, _ = normalize(hid[at, :])
        normed2[at, :] = (n * gb_ref[2:3, :] + gb_ref[3:4, :]).astype(BF)
        dense[at, :] = hid[at, :]

    for c in copies:
        c.wait()

    @pl.loop(0, w1.shape[1] // 512)
    def _(j):
        at = pl.ds(pl.multiple_of(j * 512, 512), 512)
        a, sl = gelu_pair(dot(normed2[...], w1[:, at]))
        act[:, at] = a.astype(BF)
        slope[:, at] = sl.astype(BF)
        dense[...] += dot(act[:, at], w2[at, :])

    @pl.loop(0, 6)
    def _(i):
        at = pl.ds(pl.multiple_of(i * tile, 16), tile)
        n, _ = normalize(dense[at, :])
        normed3[at, :] = (n * gb_ref[4:5, :] + gb_ref[5:6, :]).astype(BF)

    logits = dot_nt(router[...], normed3[...])
    expert = iota(logits.shape, 0)
    chosen = [
        jnp.sum(jnp.where(expert == route[k : k + 1, :], logits, 0.0), axis=0, keepdims=True)
        for k in range(TOP)
    ]
    top = jnp.maximum(chosen[0], chosen[1])
    raised = [jnp.exp(c - top) for c in chosen]
    total = raised[0] + raised[1]
    pieces = []
    for k in range(TOP):
        share = raised[k] / total
        soft[k : k + 1, :] = share
        three = split3(share * live[...])
        row = iota((16, rows), 0)
        pieces.append(
            jnp.where(row == 0, three[0].astype(F32), 0.0)
            + jnp.where(row == 1, three[1].astype(F32), 0.0)
            + jnp.where(row == 2, three[2].astype(F32), 0.0)
        )
    pieces = [p.astype(BF) for p in pieces]
    lanes = -(-cap // WIDE) * WIDE
    spot = iota((lanes, rows), 0)
    spot = jnp.where(spot < cap, spot, -2 * experts * cap)
    for r in range(experts):
        hot = [jnp.where(spot + r * cap == place[k : k + 1, :], 1.0, 0.0).astype(BF) for k in range(TOP)]
        both = (hot[0] + hot[1])[0:cap, :]
        chunks[r][0:cap, :] = dot(both, normed3[...]).astype(BF)
        chunks[r][cap : cap + 16, :] = jnp.zeros((16, width), BF)
        chunks[r][cap : cap + 16, 0:lanes] = (
            dot_nt(pieces[0], hot[0]) + dot_nt(pieces[1], hot[1])
        ).astype(BF)


def mlp(hid, gb, router, place, route, live, fc1, fc2, experts, cap, after):
    rows, width = hid.shape
    ff = fc1.shape[1]
    return call(
        functools.partial(mlp_kernel, experts, cap),
        [VM, VM, VM, VM, VM, VM, HB, HB],
        [
            shape((rows, width), BF),
            shape((rows, ff), BF),
            shape((rows, ff), BF),
            shape((rows, width), F32),
            shape((rows, width), BF),
            shape((8, rows), F32),
        ]
        + [shape((cap + 16, width), BF)] * experts,
        [
            pltpu.VMEM((width, ff), BF),
            pltpu.VMEM((ff, width), BF),
            pltpu.SemaphoreType.DMA((2,)),
        ],
        4 * rows * width * ff + 2 * rows * width * experts * cap,
        4 * width * ff + rows * (4 * ff + 12 * width),
        "dense_forward",
        after,
    )(hid, gb, router, place, route, live, fc1, fc2)


def expert_kernel(cap, n, s_ref, *refs):
    rows_in, dys = refs[:n], refs[n : 2 * n]
    own, other = refs[2 * n : 2 * n + 5], refs[2 * n + 5 : 2 * n + 10]
    outs = refs[2 * n + 10 : -3]
    wu, wd, sems = refs[-3:]
    s = s_ref[0]
    width = wu.shape[1]
    half = width // 2
    copies = [
        [
            pltpu.make_async_copy(
                src[b].at[u] if b < 3 else src[b + u],
                w.at[b, pl.ds(pl.multiple_of(side * half, half), half)],
                sems.at[4 * b + 2 * h + u],
            )
            for h, (side, src) in enumerate(((s, own), (1 - s, other)))
            for u, w in enumerate((wu, wd))
        ]
        for b in range(GROUP)
    ]
    for b in range(GROUP):
        for c in copies[b]:
            c.start()
    lanes = -(-cap // WIDE) * WIDE
    eye = iota((lanes, lanes), 0) == iota((lanes, lanes), 1)
    gates = []
    for i in range(n):
        back, out, act, dinner, gp = outs[5 * i : 5 * i + 5]
        g = jnp.sum(rows_in[i][cap : cap + 16, 0:lanes].astype(F32), axis=0, keepdims=True)
        gate = jnp.sum(jnp.where(eye, g, 0.0), axis=1, keepdims=True)[0:cap, :]
        gp[...] = (gate * dys[i][...].astype(F32)).astype(BF)
        gates.append(gate)
    sums = [None] * n
    backs = [None] * n
    for b in range(GROUP):
        for c in copies[b]:
            c.wait()
        at = slice(b * width, (b + 1) * width)
        for i in range(n):
            back, out, act, dinner, gp = outs[5 * i : 5 * i + 5]
            a, slope = gelu_pair(dot(rows_in[i][0:cap, :], wu[b]))
            act[:, at] = a.astype(BF)
            dinner[:, at] = (dot(gp[...], wd[b]) * slope).astype(BF)
            o = dot_nt(act[:, at], wd[b])
            d = dot_nt(dinner[:, at], wu[b])
            sums[i] = o if b == 0 else sums[i] + o
            backs[i] = d if b == 0 else backs[i] + d
    for i in range(n):
        back, out, act, dinner, gp = outs[5 * i : 5 * i + 5]
        out[...] = (gates[i] * sums[i]).astype(BF)
        back[0:cap, :] = backs[i].astype(BF)
        dg = jnp.sum(dys[i][...].astype(F32) * sums[i], axis=1, keepdims=True)
        pad = jnp.where(eye[0:cap, :], dg, 0.0)
        dg_row = jnp.sum(pad, axis=0, keepdims=True)
        three = split3(dg_row)
        row = iota((16, lanes), 0)
        back[cap : cap + 16, :] = jnp.zeros((16, width), BF)
        back[cap : cap + 16, 0:lanes] = (
            jnp.where(row == 0, three[0].astype(F32), 0.0)
            + jnp.where(row == 1, three[1].astype(F32), 0.0)
            + jnp.where(row == 2, three[2].astype(F32), 0.0)
        ).astype(BF)


def expert(s, rows_in, dys, own, other, cap):
    n = len(rows_in)
    width = rows_in[0].shape[1]
    ff = GROUP * width
    res = call(
        functools.partial(expert_kernel, cap, n),
        [SM] + [VM] * (2 * n) + [HB] * 10,
        [
            shape((cap + 16, width), BF),
            shape((cap, width), BF),
            shape((cap, ff), BF),
            shape((cap, ff), BF),
            shape((cap, width), BF),
        ]
        * n,
        [
            pltpu.VMEM((GROUP, width, width), BF),
            pltpu.VMEM((GROUP, width, width), BF),
            pltpu.SemaphoreType.DMA((16,)),
        ],
        8 * n * cap * width * ff,
        4 * width * ff + n * cap * (4 * ff + 10 * width),
        "expert",
    )(s, *rows_in, *dys, *own, *other)
    return [res[5 * i : 5 * i + 5] for i in range(n)]


def grad_kernel(n, skip, s_ref, *refs):
    lefts, rights, refs = refs[:n], refs[n : 2 * n], refs[2 * n + skip :]
    give, keep = refs[:2]
    if n == 1:
        left, right = lefts[0], rights[0]
    else:
        left, right = refs[2:]
        rows = lefts[0].shape[0]
        for i in range(n):
            left[i * rows : (i + 1) * rows, :] = lefts[i][...]
            right[i * rows : (i + 1) * rows, :] = rights[i][...]
    value = dot_tn(left[...], right[...]).astype(BF)

    @pl.when(pl.program_id(0) == 0)
    def _():
        give[0] = value

    @pl.when(pl.program_id(0) == 1)
    def _():
        keep[0] = value


def weight_grad(s, lefts, rights, rows=None, weight=16, stride=1, into=()):
    n = len(lefts)
    t = rows or lefts[0].shape[0]
    width = min(lefts[0].shape[1], rights[0].shape[1])
    high = width // 2
    m, nb = lefts[0].shape[1] // width, rights[0].shape[1] // width
    scratch = []
    if n > 1:
        scratch = [pltpu.VMEM((n * t, high), BF), pltpu.VMEM((n * t, width), BF)]
    left_at = lambda h, i, j, c: (0, jnp.where(h == 0, 1 - c[0], c[0]) * m + i)
    offset = 1 if into else 0

    def place_of(k, c):
        return ((k ^ c[1]) * stride + offset, 0, 0)

    give_at = lambda h, i, j, c: place_of(jnp.where(h == 0, i * nb + j, m * nb - 1), c)
    keep_at = lambda h, i, j, c: place_of(jnp.where(h == 0, 0, i * nb + j), c)
    return pl.pallas_call(
        functools.partial(grad_kernel, n, len(into)),
        grid_spec=pltpu.PrefetchScalarGridSpec(
            num_scalar_prefetch=1,
            grid=(2, m, nb),
            in_specs=[pl.BlockSpec((t, high), left_at)] * n
            + [pl.BlockSpec((t, width), lambda h, i, j, c: (0, j))] * n
            + [HB] * len(into),
            out_specs=[pl.BlockSpec((1, high, width), at) for at in (give_at, keep_at)],
            scratch_shapes=scratch,
        ),
        out_shape=[shape((m * nb * stride, high, width), BF)] * 2,
        input_output_aliases={1 + 2 * n + i: i for i in range(len(into))},
        compiler_params=pltpu.CompilerParams(vmem_limit_bytes=LIMIT),
        cost_estimate=pl.CostEstimate(
            flops=int(weight * 4) * n * t * m * high * width * nb,
            bytes_accessed=int(weight * 2) * (n * t * (2 * m * high + width * nb) + 2 * m * high * width * nb),
            transcendentals=0,
        ),
        name="weight_grad",
    )(s, *lefts, *rights, *into)


def attention_grad_kernel(s_ref, normed, context, dpacked, dattn, give, keep):
    j = pl.program_id(1)

    def write(value):
        @pl.when(pl.program_id(0) == 0)
        def _():
            give[0] = value

        @pl.when(pl.program_id(0) == 1)
        def _():
            keep[0] = value

    @pl.when(j < 3)
    def _():
        write(dot_tn(normed[...], dpacked[...]).astype(BF))

    @pl.when(j == 3)
    def _():
        write(dot_tn(context[...], dattn[...]).astype(BF))


def attention_grad(s, normed, context, dpacked, dattn):
    t, width = normed.shape
    high = width // 2
    half_at = lambda h, j, c: (0, jnp.where(h == 0, 1 - c[0], c[0]))
    return pl.pallas_call(
        attention_grad_kernel,
        grid_spec=pltpu.PrefetchScalarGridSpec(
            num_scalar_prefetch=1,
            grid=(2, 4),
            in_specs=[
                pl.BlockSpec((t, high), half_at),
                pl.BlockSpec((t, high), half_at),
                pl.BlockSpec((t, width), lambda h, j, c: (0, jnp.minimum(j, 2))),
                pl.BlockSpec((t, width), lambda h, j, c: (0, 0)),
            ],
            out_specs=[
                pl.BlockSpec((1, high, width), lambda h, j, c: (jnp.where(h == 0, j, 3), 0, 0)),
                pl.BlockSpec((1, high, width), lambda h, j, c: (jnp.where(h == 0, 0, j), 0, 0)),
            ],
        ),
        out_shape=[shape((4, high, width), BF)] * 2,
        compiler_params=pltpu.CompilerParams(vmem_limit_bytes=LIMIT),
        cost_estimate=pl.CostEstimate(
            flops=t * width * width, bytes_accessed=t * width, transcendentals=0
        ),
        name="attention_grad",
    )(s, normed, context, dpacked, dattn)


def back_kernel(
    experts, cap, dy, dense, hid, gb_ref, router, place, route, live, soft, normed3, slope, fc1, fc2, *refs
):
    homes = refs[:experts]
    dmlp, dpre, dhidden, tiny, drouter = refs[experts : experts + 5]
    w1, w2, ups, sems = refs[experts + 5 :]
    rows, width = hid.shape
    copies = [
        pltpu.make_async_copy(fc1, w1, sems.at[0]),
        pltpu.make_async_copy(fc2, w2, sems.at[1]),
    ]
    for c in copies:
        c.start()
    lanes = -(-cap // WIDE) * WIDE
    spot = iota((lanes, rows), 0)
    spot = jnp.where(spot < cap, spot, -2 * experts * cap)
    dgate = [jnp.zeros((16, rows), F32) for _ in range(TOP)]
    for r in range(experts):
        tail = homes[r][cap : cap + 16, 0:lanes]
        hot = [jnp.where(spot + r * cap == place[k : k + 1, :], 1.0, 0.0).astype(BF) for k in range(TOP)]
        for k in range(TOP):
            dgate[k] = dgate[k] + dot(tail, hot[k])
        term = dot_tn((hot[0] + hot[1])[0:cap, :], homes[r][0:cap, :])
        ups[...] = term if r == 0 else ups[...] + term
    dgate = [jnp.sum(d, axis=0, keepdims=True) * live[...] for d in dgate]
    mix = soft[0:1, :] * dgate[0] + soft[1:2, :] * dgate[1]
    dsoft = [soft[k : k + 1, :] * (dgate[k] - mix) for k in range(TOP)]
    index = iota((router.shape[0], rows), 0)
    dlogits = sum(jnp.where(index == route[k : k + 1, :], dsoft[k], 0.0) for k in range(TOP))
    dlogits = dlogits.astype(BF)
    drouter[...] = dot(dlogits, normed3[...])
    ups[...] += dot_tn(dlogits, router[...])
    tile = rows // 6
    tiny[...] = jnp.zeros_like(tiny)

    def norm_back(at, values, gain, bias_row, base):
        n, scale = normalize(values)
        u = ups[at, :]
        tiny[bias_row - 1 : bias_row, :] += jnp.sum(u * n, axis=0, keepdims=True)
        tiny[bias_row : bias_row + 1, :] += jnp.sum(u, axis=0, keepdims=True)
        ug = u * gain
        dv = scale * (
            ug
            - jnp.mean(ug, axis=-1, keepdims=True)
            - n * jnp.mean(ug * n, axis=-1, keepdims=True)
        )
        return base + dv

    @pl.loop(0, 6)
    def _(i):
        at = pl.ds(pl.multiple_of(i * tile, 16), tile)
        dd = norm_back(at, dense[at, :], gb_ref[4:5, :], 5, dy[at, :].astype(F32))
        dhidden[at, :] = dd
        dmlp[at, :] = dd.astype(BF)

    for c in copies:
        c.wait()
    ups[...] = jnp.zeros_like(ups)

    @pl.loop(0, w1.shape[1] // 512)
    def _(j):
        at = pl.ds(pl.multiple_of(j * 512, 512), 512)
        dpre[:, at] = (dot_nt(dmlp[...], w2[at, :]) * slope[:, at].astype(F32)).astype(BF)
        ups[...] += dot_nt(dpre[:, at], w1[:, at])

    @pl.loop(0, 6)
    def _(i):
        at = pl.ds(pl.multiple_of(i * tile, 16), tile)
        dhidden[at, :] = norm_back(at, hid[at, :], gb_ref[2:3, :], 3, dhidden[at, :])


def back(
    dy, dense, hid, gb, router, place, route, live, soft, normed3, slope, fc1, fc2, homes, experts, cap, after
):
    rows, width = hid.shape
    ff = fc1.shape[1]
    return call(
        functools.partial(back_kernel, experts, cap),
        [VM] * 11 + [HB] * 2 + [VM] * experts,
        [
            shape((rows, width), BF),
            shape((rows, ff), BF),
            shape((rows, width), F32),
            shape((8, width), F32),
            shape(router.shape, F32),
        ],
        [
            pltpu.VMEM((width, ff), BF),
            pltpu.VMEM((ff, width), BF),
            pltpu.VMEM((rows, width), F32),
            pltpu.SemaphoreType.DMA((2,)),
        ],
        4 * rows * width * ff + 2 * rows * width * experts * cap,
        4 * width * ff + rows * (4 * ff + 18 * width),
        "dense_backward",
        after,
    )(dy, dense, hid, gb, router, place, route, live, soft, normed3, slope, fc1, fc2, *homes)


def attend_back_kernel(
    s_ref, dhid, id_row, id_col, packed, lse, wo_a, wo_b, dattn, dpacked, wo, bias, dctx, sems
):
    s = s_ref[0]
    rows, width = dhid.shape
    copies = halves_into(s, wo_a, wo_b, wo, sems, 0)
    for c in copies:
        c.start()
    tile = rows // 6

    @pl.loop(0, 6)
    def _(i):
        at = pl.ds(pl.multiple_of(i * tile, 16), tile)
        dattn[at, :] = dhid[at, :].astype(BF)
        bias[at, :] = jnp.where(id_col[at, :] == id_row[...], 0.0, MASKED)

    copies[0].wait()
    copies[1].wait()

    @pl.loop(0, width // 256)
    def _(j):
        at = pl.ds(pl.multiple_of(j * 256, 256), 256)
        dctx[:, at] = dot_nt(dattn[...], wo[at, :]).astype(BF)

    lane = iota((1, WIDE), 1)

    @pl.loop(0, width // WIDE)
    def _(pair):
        col = pl.multiple_of(pair * WIDE, WIDE)
        q = packed[:, pl.ds(col, WIDE)] * jnp.asarray(HEAD**-0.5, BF)
        keys = packed[:, pl.ds(width + col, WIDE)]
        values = packed[:, pl.ds(2 * width + col, WIDE)]
        dc = dctx[:, pl.ds(col, WIDE)]
        dq, dk, dv = [], [], []
        for h in range(2):
            mine = (lane >= h * HEAD) & (lane < (h + 1) * HEAD)
            scores = dot_nt(jnp.where(mine, keys, jnp.zeros_like(keys)), q) + bias[...]
            p = jnp.exp(scores - lse[pl.ds(2 * pair + h, 1), :])
            dp = dot_nt(jnp.where(mine, values, jnp.zeros_like(values)), dc)
            inner = jnp.sum(p * dp, axis=0, keepdims=True)
            ds = (p * (dp - inner)).astype(BF)
            dv.append(dot(p.astype(BF), dc))
            dk.append(dot(ds, q))
            dq.append(dot_tn(ds, keys) * HEAD**-0.5)
        low = lane < HEAD
        dpacked[:, pl.ds(col, WIDE)] = jnp.where(low, dq[0], dq[1]).astype(BF)
        dpacked[:, pl.ds(width + col, WIDE)] = jnp.where(low, dk[0], dk[1]).astype(BF)
        dpacked[:, pl.ds(2 * width + col, WIDE)] = jnp.where(low, dv[0], dv[1]).astype(BF)


def input_kernel(s_ref, x_ref, dhid, gb_ref, dpacked, qkv_a, qkv_b, grad_in, tiny, wq, ups, sems):
    s = s_ref[0]
    rows, width = x_ref.shape
    tile = rows // 6
    copies = halves_into(s, qkv_a, qkv_b, wq, sems, 0)
    for c in copies:
        c.start()
    copies[0].wait()
    copies[1].wait()

    @pl.loop(0, width // 256)
    def _(j):
        at = pl.ds(pl.multiple_of(j * 256, 256), 256)
        ups[:, at] = dot_nt(dpacked[...], wq[at, :])

    tiny[...] = jnp.zeros_like(tiny)

    @pl.loop(0, 6)
    def _(i):
        at = pl.ds(pl.multiple_of(i * tile, 16), tile)
        n, scale = normalize(x_ref[at, :].astype(F32))
        u = ups[at, :]
        tiny[0:1, :] += jnp.sum(u * n, axis=0, keepdims=True)
        tiny[1:2, :] += jnp.sum(u, axis=0, keepdims=True)
        ug = u * gb_ref[0:1, :]
        grad_in[at, :] = dhid[at, :] + scale * (
            ug
            - jnp.mean(ug, axis=-1, keepdims=True)
            - n * jnp.mean(ug * n, axis=-1, keepdims=True)
        )


def attend_back(s, dhid, ids, packed, lse, wo, after):
    rows, width = dhid.shape
    n3 = packed.shape[1]
    return call(
        attend_back_kernel,
        [SM] + [VM] * 5 + [HB] * 2,
        [shape((rows, width), BF), shape((rows, n3), BF)],
        [
            pltpu.VMEM((width, width), BF),
            pltpu.VMEM((rows, rows), F32),
            pltpu.VMEM((rows, width), BF),
            pltpu.SemaphoreType.DMA((2,)),
        ],
        2 * rows * width * width + 20 * rows * rows * width,
        2 * (width * width + rows * (3 * width + 2 * n3)),
        "attention_backward",
        after,
    )(s, dhid, ids[None, :], ids[:, None], packed, lse, *wo)


def input_back(s, x, dhid, gb, dpacked, qkv, after):
    rows, width = x.shape
    n3 = dpacked.shape[1]
    return call(
        input_kernel,
        [SM] + [VM] * 4 + [HB] * 2,
        [shape((rows, width), F32), shape((8, width), F32)],
        [
            pltpu.VMEM((width, n3), BF),
            pltpu.VMEM((rows, width), F32),
            pltpu.SemaphoreType.DMA((2,)),
        ],
        2 * rows * width * n3,
        2 * (width * n3 + rows * n3) + 10 * rows * width,
        "input_backward",
        after,
    )(s, x, dhid, gb, dpacked, *qkv)


def merge_kernel(experts, cap, dense, place, *refs):
    outs, result = refs[:experts], refs[experts]
    rows = dense.shape[0]
    total = dense[...]
    spot = iota((cap, rows), 0)
    for r in range(experts):
        hot = sum(jnp.where(spot + r * cap == place[k : k + 1, :], 1.0, 0.0) for k in range(TOP))
        total = total + dot_tn(hot.astype(BF), outs[r][...])
    result[...] = total.astype(BF)


def merge(dense, place, outs, experts, cap):
    rows, width = dense.shape
    return call(
        functools.partial(merge_kernel, experts, cap),
        [VM] * (2 + experts),
        shape((rows, width), BF),
        [],
        2 * rows * width * experts * cap,
        rows * width * 6 + 2 * experts * cap * width,
        "merge",
        (),
        0.25,
    )(dense, place, *outs)


def hold_kernel(n, *refs):
    for i in range(n):
        refs[n + i][...] = refs[i][...]


def hold(chunks, after):
    n = len(chunks)
    dims = chunks[0].shape
    return call(
        functools.partial(hold_kernel, n),
        [VM] * n,
        [shape(dims, BF)] * n,
        [],
        0,
        4 * n * dims[0] * dims[1],
        "hold",
        after,
    )(*chunks)


def finish_kernel(columns, m_ref, mine, got, out):
    n, high, width = mine.shape
    for which, src in ((m_ref[0], mine), (1 - m_ref[0], got)):
        for i in range(n):
            value = src[i].astype(F32)
            if columns:
                out[:, pl.ds(pl.multiple_of((which * n + i) * width, width), width)] = value
            else:
                out[pl.ds(pl.multiple_of((which * n + i) * high, high), high), :] = value


def finish(m, mine, got, columns):
    n, high, width = mine.shape
    dims = (high, 2 * n * width) if columns else (2 * n * high, width)
    return call(
        functools.partial(finish_kernel, columns),
        [SM, VM, VM],
        shape(dims, F32),
        [],
        0,
        12 * n * high * width,
        "finish",
    )(m, mine, got)


def spread_kernel(experts, cap, rows_in, place, *chunks):
    spot = iota((cap, rows_in.shape[0]), 0)
    for r in range(experts):
        hot = sum(jnp.where(spot + r * cap == place[k : k + 1, :], 1.0, 0.0) for k in range(TOP))
        chunks[r][...] = dot(hot.astype(BF), rows_in[...]).astype(BF)


def spread(rows_in, place, experts, cap):
    rows, width = rows_in.shape
    return call(
        functools.partial(spread_kernel, experts, cap),
        [VM, VM],
        [shape((cap, width), BF)] * experts,
        [],
        2 * rows * width * experts * cap,
        2 * (rows + experts * cap) * width,
        "spread",
    )(rows_in, place)


def places_of(routes, live, experts, capacity):
    tokens = routes.shape[0]
    ids = jnp.arange(experts, dtype=jnp.int32)
    match = [
        ((routes[:, k : k + 1] == ids[None, :]) & live[:, None]).astype(F32) for k in range(TOP)
    ]
    order = jnp.arange(tokens, dtype=jnp.int32)
    below = (order[:, None] > order[None, :]).astype(BF)
    before = jnp.zeros((1, experts), F32)
    out = []
    for k in range(TOP):
        counts = dot(below, match[k].astype(BF)) + before
        before = before + jnp.sum(match[k], axis=0, keepdims=True)
        within = jnp.sum(counts * match[k], axis=1).astype(jnp.int32)
        out.append(jnp.where(live, routes[:, k] * capacity + within, experts * capacity))
    return out

def local(
    tokens,
    image_ids,
    routes,
    norm1_gain,
    norm1_bias,
    qkv_weight,
    attn_out_weight,
    norm2_gain,
    norm2_bias,
    fc1_weight,
    fc2_weight,
    norm3_gain,
    norm3_bias,
    router_weight,
    expert_up,
    expert_down,
    cotangent,
):
    s = lax.axis_index("section")
    e = lax.axis_index("dp") // GROUP
    q = lax.axis_index("dp") % GROUP
    dp_count = lax.axis_size("dp")
    experts = dp_count // GROUP
    cap = GROUP * ((21 * SLOTS + 10 * experts * GROUP - 1) // (10 * experts * GROUP))
    cap = -(-cap // 16) * 16
    half = tokens.shape[1]
    width = 2 * half
    few = experts <= 8
    planes = [[p * GROUP + i for p in range(experts)] for i in range(GROUP)]
    here, here_q = jnp.stack([s, 0 * s]), jnp.stack([s, q])
    quads = [[p * GROUP + i for i in range(GROUP)] for p in range(experts)]

    def swap(v):
        return lax.ppermute(v, "section", [(0, 1), (1, 0)])

    def over_q(v, bit):
        return lax.ppermute(v, "dp", [(i, i ^ bit) for i in range(dp_count)])

    def over_e(v, r):
        return lax.ppermute(
            v,
            "dp",
            [(i, ((i // GROUP + r) % experts) * GROUP + i % GROUP) for i in range(dp_count)],
        )

    def part(v, index, size, axis=0):
        return lax.dynamic_slice_in_dim(v, index * size, size, axis)

    def join(own, other, axis):
        return jnp.where(
            s == 0,
            jnp.concatenate([own, other], axis=axis),
            jnp.concatenate([other, own], axis=axis),
        )

    def add(a, b):
        return (a.astype(F32) + b.astype(F32)).astype(BF)

    def out_chunks(chunks):
        if not few:
            return list(lax.all_to_all(jnp.stack(chunks), "dp", 0, 0, axis_index_groups=planes))
        return [chunks[0]] + [over_e(chunks[r], r) for r in range(1, experts)]

    def home_chunks(chunks):
        if not few:
            return list(lax.all_to_all(jnp.stack(chunks), "dp", 0, 0, axis_index_groups=planes))
        return [chunks[0]] + [over_e(chunks[r], experts - r) for r in range(1, experts)]

    small = jnp.stack([norm1_gain, norm1_bias, norm2_gain, norm2_bias, norm3_gain, norm3_bias])
    small = jnp.concatenate([small, jnp.transpose(router_weight)])
    small = join(small, swap(small), 1)
    x = join(part(tokens, s, SLOTS), swap(part(tokens, 1 - s, SLOTS)), 1)
    dy = join(part(cotangent, s, SLOTS), swap(part(cotangent, 1 - s, SLOTS)), 1)
    ids = part(image_ids, s, 1).reshape(-1)
    route = part(routes, s, SLOTS)
    live = ids >= 0
    gb = jnp.concatenate([small[:6], jnp.zeros((2, width), BF)]).astype(F32)
    router_rows = -(-experts // 16) * 16
    router = jnp.concatenate([small[6 : 6 + experts], jnp.zeros((router_rows - experts, width), BF)])
    qkv, wo = (qkv_weight, swap(qkv_weight)), (attn_out_weight, swap(attn_out_weight))

    pair = jnp.stack([expert_up, expert_down])

    def gather(v, tiled):
        return lax.all_gather(v, "section", axis=0, tiled=tiled)

    tie = lax.optimization_barrier
    x, dy, qkv, wo, fc1_weight, fc2_weight, pair = tie(
        (x, dy, qkv, wo, fc1_weight, fc2_weight, pair)
    )
    fc1, fc2 = gather(fc1_weight, True), gather(fc2_weight, True)
    from_x, from_y, other_pair = over_q(pair, 1), over_q(pair, 2), swap(pair)

    if few:
        distance = (route - e) % experts
    else:
        distance = route
    spots = places_of(distance, live, experts, cap)
    place = jnp.stack(spots + [jnp.full_like(spots[0], -1)] * 6)
    route_rows = jnp.concatenate([jnp.transpose(route), jnp.full((6, SLOTS), -1, jnp.int32)])
    live_row = live.astype(F32)[None, :]
    dy_sent = spread(dy, place, experts, cap)
    dy_out = out_chunks(dy_sent)

    normed1, packed, context, lse, hidden = front(here, x, ids, gb, qkv, wo, dy_sent[:1])
    hidden, from_x, from_y, other_pair, *dy_out[:-1] = tie(
        (hidden, from_x, from_y, other_pair, *dy_out[:-1])
    )
    other_x, other_y = swap(from_x), swap(from_y)
    far = [over_q(from_x[0], 2), over_q(from_y[1], 1)]
    normed2, act, slope, dense, normed3, soft, *sent = mlp(
        hidden, gb, router, place, route_rows, live_row, fc1, fc2, experts, cap, []
    )
    sent, far, other_x, other_y, dy_out[-1] = tie((sent, far, other_x, other_y, dy_out[-1]))
    got = out_chunks(sent)
    own = [pair, from_x, from_y, *far]
    other = [other_pair, other_x, other_y, swap(far[0]), swap(far[1])]

    step = max(1, experts // 4)
    results = [None] * experts
    previous, homes = None, [None] * experts
    order = [0, 3, 1, 2] if experts == 4 else list(range(0, experts, step))
    for place_in_order, i in enumerate(order):
        if i:
            got[i], results[previous] = tie((got[i], results[previous]))
        if few and place_in_order == 3:
            got[i], homes[order[1]] = tie((got[i], homes[order[1]]))
        results[i : i + step] = expert(
            here, got[i : i + step], dy_out[i : i + step], own, other, cap
        )
        previous = i
        homes[i] = over_e(results[i][0], experts - i) if few and i else results[i][0]
    if not few:
        homes = home_chunks([r[0] for r in results])
    acts, dinners, scaled = ([r[i] for r in results] for i in (2, 3, 4))

    if experts == 4:
        dinners, homes[1] = tie((dinners, homes[1]))
    up_grads = weight_grad(here_q, got, dinners, cap, stride=2)
    dmlp, dpre, dhidden, tiny23, drouter = back(
        dy, dense, hidden, gb, router, place, route_rows, live_row, soft, normed3, slope,
        fc1, fc2, homes, experts, cap, [],
    )
    outs = hold([r[1] for r in results], homes)
    grads1, grads2 = weight_grad(here, [normed2], [dpre]), weight_grad(here, [act], [dmlp])
    acts, grads1, grads2 = tie((acts, grads1, grads2))
    expert_grads = weight_grad(here_q, scaled, acts, stride=2, into=up_grads)

    def fold(v, bit):
        mine, rows = (q // bit) % 2, v.shape[0] // 2
        return part(v, mine, rows), over_q(part(v, 1 - mine, rows), bit)

    def unfold(v, got, bit):
        return jnp.where(
            (q // bit) % 2 == 0, jnp.concatenate([v, got]), jnp.concatenate([got, v])
        )

    def plane_out(a, b):
        ab = jnp.stack([a, b])
        rows = a.shape[0] // experts
        if not few:
            return [lax.psum(ab, "dp", axis_index_groups=planes)]
        return [part(ab, (e + r) % experts, rows, 1) for r in range(experts)]

    def plane_sum(pieces):
        if not few:
            return pieces
        total = sum(p.astype(F32) for p in pieces).astype(BF)
        return [total] * experts

    def plane_move(pieces):
        return pieces[:1] + [over_e(p, r) for r, p in enumerate(pieces) if r]

    def plane_join(pieces):
        if not few:
            return pieces[0][0], pieces[0][1]
        rows = pieces[0].shape[1]
        whole = jnp.zeros((2, experts * rows, width), BF)
        for r, piece in enumerate(pieces):
            whole = lax.dynamic_update_slice_in_dim(whole, piece, ((e - r) % experts) * rows, 1)
        return whole[0], whole[1]

    away1, away2 = swap(grads1[0]), swap(grads2[0])
    dhidden, away1, away2, grads1, grads2, expert_grads = tie(
        (dhidden, away1, away2, grads1, grads2, expert_grads)
    )
    a, b = add(grads2[1], away2).reshape(-1, width), add(grads1[1], away1).reshape(-1, width)
    a, b = fold(a, 1), fold(b, 2)
    dattn, dpacked = attend_back(here, dhidden, ids, packed, lse, wo, [])
    home_outs = home_chunks(outs)
    give, keep = attention_grad(here, normed1, context, dpacked, dattn)
    give, keep, a, b, dpacked, home_outs = tie((give, keep, a, b, dpacked, home_outs))
    grad_in, tiny1 = input_back(here, x, dhidden, gb, dpacked, qkv, [])
    tiny = jnp.concatenate([tiny1[:2], tiny23[2:6], drouter[:experts]])

    def swapped(v):
        return part(v, s, half, 1), swap(part(v, 1 - s, half, 1))

    away = swap(give)
    a, b = fold(add(*a), 2), fold(add(*b), 1)
    sum_experts = add(expert_grads[1], swap(expert_grads[0]))
    away, a, b, grad_in, tiny, sum_experts = tie((away, a, b, grad_in, tiny, sum_experts))
    half_experts = lax.psum_scatter(
        sum_experts.reshape(GROUP, 2, half, -1),
        "dp", scatter_dimension=0, axis_index_groups=quads, tiled=False,
    )
    grad_in, tiny = swapped(grad_in), swapped(tiny)
    tiny = tiny[0] + tiny[1]

    ab = plane_move(plane_out(add(*a), add(*b)))
    t = add(keep, away).reshape(-1, width)
    ta, tb = fold(t[:width], 1), fold(t[width:], 2)
    ab, ta, tb = tie((ab, ta, tb))
    block_out = merge(dense, place, home_outs, experts, cap)

    ab = plane_move(plane_sum(ab))
    ta, tb = fold(add(*ta), 2), fold(add(*tb), 1)
    ab, ta, tb, block_out = tie((ab, ta, tb, block_out))

    a, b = plane_join(ab)
    a_got, b_got = over_q(a, 2), over_q(b, 1)
    tab = plane_move(plane_out(add(*ta), add(*tb)))
    a_got, b_got, tab = tie((a_got, b_got, tab))
    a, b = unfold(a, a_got, 2), unfold(b, b_got, 1)
    a_got, b_got = over_q(a, 1), over_q(b, 2)
    tab = plane_move(plane_sum(tab))
    a_got, b_got, tab = tie((a_got, b_got, tab))

    side_x, side_y = jnp.reshape(q % 2, (1,)), jnp.reshape(q // 2, (1,))

    def blocks(v):
        return v.reshape(-1, half, width)

    ta, tb = plane_join(tab)
    ta_got, tb_got = over_q(ta, 2), over_q(tb, 1)
    block_out = swapped(block_out)
    tiny_q = [over_q(tiny, bit) for bit in (1, 2, 3)]
    sum_fc2 = finish(side_x, blocks(a), blocks(a_got), False)
    sum_fc1 = finish(side_y, blocks(b), blocks(b_got), True)
    ta_got, tb_got, block_out, grad_in, tiny_q, sum_fc2, sum_fc1, half_experts = tie(
        (ta_got, tb_got, block_out, grad_in, tiny_q, sum_fc2, sum_fc1, half_experts)
    )
    half_up, half_down = half_experts[0].astype(F32), half_experts[1].astype(F32)
    ta, tb = unfold(ta, ta_got, 2), unfold(tb, tb_got, 1)
    ta_got, tb_got = over_q(ta, 1), over_q(tb, 2)
    tiny = tiny + tiny_q[0] + (tiny_q[1] + tiny_q[2])
    if few:
        total = sum(over_e(tiny, r) if r else tiny for r in range(experts))
    else:
        total = lax.psum(tiny, "dp", axis_index_groups=planes)
    q_and_k = finish(side_x, blocks(ta), blocks(ta_got), True)
    first = q // 2 == 0
    v_sum, sum_attn = (
        jnp.where(first, p, r).astype(F32) for p, r in ((tb, tb_got), (tb_got, tb))
    )
    sum_qkv = jnp.concatenate([q_and_k, v_sum], axis=1)
    return (
        join(*block_out, 0),
        join(*grad_in, 0),
        total[0],
        total[1],
        sum_qkv,
        sum_attn,
        total[2],
        total[3],
        sum_fc1,
        sum_fc2,
        total[4],
        total[5],
        jnp.transpose(total[6:]),
        half_up,
        half_down,
    )


def solution(mesh):
    placed = (
        P("dp", "section"),
        P("dp", None),
        P("dp", None),
        P("section"),
        P("section"),
        P("section", None),
        P("section", None),
        P("section"),
        P("section"),
        P("section", None),
        P("section", None),
        P("section"),
        P("section"),
        P("section", None),
        P("section", "dp"),
        P("section", "dp"),
        P("dp", "section"),
    )
    return jax.shard_map(
        local,
        mesh=mesh,
        in_specs=placed,
        out_specs=(
            P("dp", "section"),
            P("dp", "section"),
            P("section"),
            P("section"),
            P("section", None),
            P("section", None),
            P("section"),
            P("section"),
            P("section", None),
            P("section", None),
            P("section"),
            P("section"),
            P("section", None),
            P("section", "dp"),
            P("section", "dp"),
        ),
        check_vma=False,
    )
```

```python
import functools

import jax
import jax.numpy as jnp
from jax import lax
from jax.experimental import pallas as pl
from jax.experimental.pallas import tpu as pltpu
from jax.sharding import PartitionSpec as P

HEAD = 64
TOP = 2
GROUP = 4
SLOTS = 576
WIDE = 128

EPSILON = 1e-06
MASKED = -1e30
BF = jnp.bfloat16
F32 = jnp.float32
LIMIT = 24 * 1024 * 1024
LIMITS = dict(
    attention_forward=28,
    dense_forward=36,
    expert=28,
    dense_backward=40,
    attention_backward=28,
    input_backward=24,
    merge=20,
    hold=12,
    finish=24,
    spread=16,
)


def dot(a, b):
    return jnp.dot(a, b, preferred_element_type=F32)


def dot_nt(a, b):
    return lax.dot_general(a, b, (((1,), (1,)), ((), ())), preferred_element_type=F32)


def dot_tn(a, b):
    return lax.dot_general(a, b, (((0,), (0,)), ((), ())), preferred_element_type=F32)


def normalize(v):
    center = v - jnp.mean(v, axis=-1, keepdims=True)
    scale = lax.rsqrt(jnp.mean(center * center, axis=-1, keepdims=True) + EPSILON)
    return center * scale, scale


def gelu_pair(x):
    bell = jnp.exp(x * x * -0.5)
    t = 1.0 / (1.0 + jnp.abs(x) * (0.3275911 * 0.5**0.5))
    tail = (
        t
        * (
            0.127414796
            + t * (-0.142248368 + t * (0.7107068705 + t * (-0.7265760135 + t * 0.5307027145)))
        )
        * bell
    )
    cdf = jnp.where(x >= 0.0, 1.0 - tail, tail)
    return x * cdf, cdf + x * (bell * 0.3989422804014327)


def iota(shape, axis):
    return lax.broadcasted_iota(jnp.int32, shape, axis)


def halves_into(s, own, other, dest, sems, first):
    rows = own.shape[0]
    return [
        pltpu.make_async_copy(own, dest.at[pl.ds(pl.multiple_of(s * rows, rows), rows)], sems.at[first]),
        pltpu.make_async_copy(
            other, dest.at[pl.ds(pl.multiple_of((1 - s) * rows, rows), rows)], sems.at[first + 1]
        ),
    ]


def split3(v):
    hi = v.astype(BF)
    rest = v - hi.astype(F32)
    mid = rest.astype(BF)
    low = (rest - mid.astype(F32)).astype(BF)
    return hi, mid, low


VM = pl.BlockSpec(memory_space=pltpu.VMEM)
SM = pl.BlockSpec(memory_space=pltpu.SMEM)
HB = pl.BlockSpec(memory_space=pl.ANY)


def call(kernel, in_specs, out_shape, scratch, flops, moved, name, after=(), weight=16, flushed=()):
    limit = LIMITS[name] * 1024 * 1024
    count, extra = len(in_specs), len(after)
    single = not isinstance(out_shape, list)
    shapes = [out_shape] if single else out_shape
    total, held = len(shapes), len(flushed)

    def body(*refs):
        inputs, outs = refs[:count], list(refs[count + extra : count + extra + total])
        rest = refs[count + extra + total :]
        if not held:
            kernel(*inputs, *outs, *rest)
            return
        own, (buffers, sems) = rest[: len(rest) - held - 1], (rest[len(rest) - held - 1 : -1], rest[-1])
        copies = {}
        for k, index in enumerate(flushed):
            copies[index] = pltpu.make_async_copy(buffers[k], outs[index], sems.at[k])
            outs[index] = buffers[k]
        kernel(*inputs, *outs, *own, flush=lambda index: copies[index].start())
        for index in flushed:
            copies[index].wait()

    made = pl.pallas_call(
        body,
        in_specs=in_specs + [HB] * extra,
        out_specs=VM
        if single
        else [pl.BlockSpec(memory_space=pltpu.HBM) if i in flushed else VM for i in range(total)],
        out_shape=out_shape
        if not held
        else [pltpu.HBM(v.shape, v.dtype) if i in flushed else v for i, v in enumerate(shapes)],
        scratch_shapes=scratch
        + [pltpu.VMEM(shapes[i].shape, shapes[i].dtype) for i in flushed]
        + ([pltpu.SemaphoreType.DMA((held,))] if held else []),
        compiler_params=pltpu.CompilerParams(vmem_limit_bytes=limit),
        cost_estimate=pl.CostEstimate(
            flops=int(weight * flops), bytes_accessed=int(weight * moved), transcendentals=0
        ),
        name=name,
    )
    return lambda *operands: made(*operands, *after)


def shape(dims, kind):
    return jax.ShapeDtypeStruct(dims, kind)


def front_kernel(
    s_ref, x_ref, id_row, id_col, gb_ref, qkv_a, qkv_b, wo_a, wo_b,
    normed, packed, context, lse, hidden,
    wq, wo, bias, lse_col, sems, flush,
):
    s = s_ref[0]
    rows, width = x_ref.shape
    copies = halves_into(s, qkv_a, qkv_b, wq, sems, 0) + halves_into(s, wo_a, wo_b, wo, sems, 2)
    for c in copies:
        c.start()
    tile = rows // 6

    @pl.loop(0, 6)
    def _(i):
        at = pl.ds(pl.multiple_of(i * tile, 16), tile)
        n, _ = normalize(x_ref[at, :].astype(F32))
        normed[at, :] = (n * gb_ref[0:1, :] + gb_ref[1:2, :]).astype(BF)
        bias[at, :] = jnp.where(id_col[at, :] == id_row[...], 0.0, MASKED)

    copies[0].wait()
    copies[1].wait()

    @pl.loop(0, wq.shape[1] // 256)
    def _(j):
        at = pl.ds(pl.multiple_of(j * 256, 256), 256)
        packed[:, at] = dot(normed[...], wq[:, at]).astype(BF)

    flush(0)
    flush(1)
    lane = iota((1, WIDE), 1)
    lse_col[...] = jnp.zeros_like(lse_col)
    third = rows // 3

    @pl.loop(0, width // WIDE)
    def _(pair):
        col = pl.multiple_of(pair * WIDE, WIDE)
        keys = packed[:, pl.ds(width + col, WIDE)]
        values = packed[:, pl.ds(2 * width + col, WIDE)]
        for r in range(3):
            at = slice(r * third, (r + 1) * third)
            q = packed[at, pl.ds(col, WIDE)] * jnp.asarray(HEAD**-0.5, BF)
            outs = []
            sums = lse_col[at, :]
            for h in range(2):
                mine = (lane >= h * HEAD) & (lane < (h + 1) * HEAD)
                scores = dot_nt(jnp.where(mine, q, jnp.zeros_like(q)), keys) + bias[at, :]
                top = jnp.max(scores, axis=1, keepdims=True)
                p = jnp.exp(scores - top)
                total = jnp.sum(p, axis=1, keepdims=True)
                outs.append(dot(p.astype(BF), values) * (1.0 / total))
                sums = jnp.where(lane == 2 * pair + h, top + jnp.log(total), sums)
            lse_col[at, :] = sums
            context[at, pl.ds(col, WIDE)] = jnp.where(lane < HEAD, outs[0], outs[1]).astype(BF)

    flush(2)
    lse[...] = jnp.transpose(lse_col[...])[0 : lse.shape[0], :]
    copies[2].wait()
    copies[3].wait()

    @pl.loop(0, width // 256)
    def _(j):
        at = pl.ds(pl.multiple_of(j * 256, 256), 256)
        hidden[:, at] = x_ref[:, at].astype(F32) + dot(context[...], wo[:, at])


def front(s, x, ids, gb, qkv, wo, after):
    rows, width = x.shape
    n3 = qkv[0].shape[1]
    return call(
        front_kernel,
        [SM, VM, VM, VM, VM, HB, HB, HB, HB],
        [
            shape((rows, width), BF),
            shape((rows, n3), BF),
            shape((rows, width), BF),
            shape((16, rows), F32),
            shape((rows, width), F32),
        ],
        [
            pltpu.VMEM((width, n3), BF),
            pltpu.VMEM((width, width), BF),
            pltpu.VMEM((rows, rows), F32),
            pltpu.VMEM((rows, WIDE), F32),
            pltpu.SemaphoreType.DMA((4,)),
        ],
        2 * rows * width * (n3 + width) + 4 * rows * rows * width,
        2 * (width * (n3 + width) + rows * (3 * width + n3)) + 4 * rows * width,
        "attention_forward",
        after,
        flushed=(0, 1, 2),
    )(s, x, ids[None, :], ids[:, None], gb, *qkv, *wo)


def mlp_kernel(experts, cap, hid, gb_ref, router, place, route, live, fc1, fc2, *refs, flush):
    normed2, act, slope, dense, normed3, soft = refs[:6]
    chunks = refs[6 : 6 + experts]
    w1, w2, sems = refs[6 + experts :]
    rows, width = hid.shape
    copies = [
        pltpu.make_async_copy(fc1, w1, sems.at[0]),
        pltpu.make_async_copy(fc2, w2, sems.at[1]),
    ]
    for c in copies:
        c.start()
    tile = rows // 6

    @pl.loop(0, 6)
    def _(i):
        at = pl.ds(pl.multiple_of(i * tile, 16), tile)
        n, _ = normalize(hid[at, :])
        normed2[at, :] = (n * gb_ref[2:3, :] + gb_ref[3:4, :]).astype(BF)
        dense[at, :] = hid[at, :]

    flush(0)
    for c in copies:
        c.wait()

    @pl.loop(0, w1.shape[1] // 512)
    def _(j):
        at = pl.ds(pl.multiple_of(j * 512, 512), 512)
        a, sl = gelu_pair(dot(normed2[...], w1[:, at]))
        act[:, at] = a.astype(BF)
        slope[:, at] = sl.astype(BF)
        dense[...] += dot(act[:, at], w2[at, :])

    flush(1)
    flush(2)
    flush(3)

    @pl.loop(0, 6)
    def _(i):
        at = pl.ds(pl.multiple_of(i * tile, 16), tile)
        n, _ = normalize(dense[at, :])
        normed3[at, :] = (n * gb_ref[4:5, :] + gb_ref[5:6, :]).astype(BF)

    flush(4)
    logits = dot_nt(router[...], normed3[...])
    expert = iota(logits.shape, 0)
    chosen = [
        jnp.sum(jnp.where(expert == route[k : k + 1, :], logits, 0.0), axis=0, keepdims=True)
        for k in range(TOP)
    ]
    top = jnp.maximum(chosen[0], chosen[1])
    raised = [jnp.exp(c - top) for c in chosen]
    total = raised[0] + raised[1]
    pieces = []
    for k in range(TOP):
        share = raised[k] / total
        soft[k : k + 1, :] = share
        three = split3(share * live[...])
        row = iota((16, rows), 0)
        pieces.append(
            jnp.where(row == 0, three[0].astype(F32), 0.0)
            + jnp.where(row == 1, three[1].astype(F32), 0.0)
            + jnp.where(row == 2, three[2].astype(F32), 0.0)
        )
    pieces = [p.astype(BF) for p in pieces]
    lanes = -(-cap // WIDE) * WIDE
    spot = iota((lanes, rows), 0)
    spot = jnp.where(spot < cap, spot, -2 * experts * cap)
    for r in range(experts):
        hot = [jnp.where(spot + r * cap == place[k : k + 1, :], 1.0, 0.0).astype(BF) for k in range(TOP)]
        both = (hot[0] + hot[1])[0:cap, :]
        chunks[r][0:cap, :] = dot(both, normed3[...]).astype(BF)
        chunks[r][cap : cap + 16, :] = jnp.zeros((16, width), BF)
        chunks[r][cap : cap + 16, 0:lanes] = (
            dot_nt(pieces[0], hot[0]) + dot_nt(pieces[1], hot[1])
        ).astype(BF)
        if r:
            flush(6 + r)


def mlp(hid, gb, router, place, route, live, fc1, fc2, experts, cap, after):
    rows, width = hid.shape
    ff = fc1.shape[1]
    return call(
        functools.partial(mlp_kernel, experts, cap),
        [VM, VM, VM, VM, VM, VM, HB, HB],
        [
            shape((rows, width), BF),
            shape((rows, ff), BF),
            shape((rows, ff), BF),
            shape((rows, width), F32),
            shape((rows, width), BF),
            shape((8, rows), F32),
        ]
        + [shape((cap + 16, width), BF)] * experts,
        [
            pltpu.VMEM((width, ff), BF),
            pltpu.VMEM((ff, width), BF),
            pltpu.SemaphoreType.DMA((2,)),
        ],
        4 * rows * width * ff + 2 * rows * width * experts * cap,
        4 * width * ff + rows * (4 * ff + 12 * width),
        "dense_forward",
        after,
        flushed=(0, 1, 2, 3, 4) + tuple(range(7, 6 + experts)),
    )(hid, gb, router, place, route, live, fc1, fc2)


def expert_kernel(cap, n, s_ref, *refs, flush):
    rows_in, dys = refs[:n], refs[n : 2 * n]
    own, other = refs[2 * n : 2 * n + GROUP], refs[2 * n + GROUP : 2 * n + 2 * GROUP]
    outs = refs[2 * n + 2 * GROUP : -3]
    wu, wd, sems = refs[-3:]
    s = s_ref[0]
    width = wu.shape[1]
    half = width // 2
    copies = [
        [
            pltpu.make_async_copy(
                src[b].at[u],
                w.at[b, pl.ds(pl.multiple_of(side * half, half), half)],
                sems.at[4 * b + 2 * h + u],
            )
            for h, (side, src) in enumerate(((s, own), (1 - s, other)))
            for u, w in enumerate((wu, wd))
        ]
        for b in range(GROUP)
    ]
    for b in range(GROUP):
        for c in copies[b]:
            c.start()
    lanes = -(-cap // WIDE) * WIDE
    eye = iota((lanes, lanes), 0) == iota((lanes, lanes), 1)
    gates = []
    for i in range(n):
        back, out, act, dinner, gp = outs[5 * i : 5 * i + 5]
        g = jnp.sum(rows_in[i][cap : cap + 16, 0:lanes].astype(F32), axis=0, keepdims=True)
        gate = jnp.sum(jnp.where(eye, g, 0.0), axis=1, keepdims=True)[0:cap, :]
        gp[...] = (gate * dys[i][...].astype(F32)).astype(BF)
        gates.append(gate)
    sums = [None] * n
    backs = [None] * n
    for b in range(GROUP):
        for c in copies[b]:
            c.wait()
        at = slice(b * width, (b + 1) * width)
        for i in range(n):
            back, out, act, dinner, gp = outs[5 * i : 5 * i + 5]
            a, slope = gelu_pair(dot(rows_in[i][0:cap, :], wu[b]))
            act[:, at] = a.astype(BF)
            dinner[:, at] = (dot(gp[...], wd[b]) * slope).astype(BF)
            o = dot_nt(act[:, at], wd[b])
            d = dot_nt(dinner[:, at], wu[b])
            sums[i] = o if b == 0 else sums[i] + o
            backs[i] = d if b == 0 else backs[i] + d
    for i in range(n):
        back, out, act, dinner, gp = outs[5 * i : 5 * i + 5]
        out[...] = (gates[i] * sums[i]).astype(BF)
        flush(5 * i + 1)
        back[0:cap, :] = backs[i].astype(BF)
        dg = jnp.sum(dys[i][...].astype(F32) * sums[i], axis=1, keepdims=True)
        pad = jnp.where(eye[0:cap, :], dg, 0.0)
        dg_row = jnp.sum(pad, axis=0, keepdims=True)
        three = split3(dg_row)
        row = iota((16, lanes), 0)
        back[cap : cap + 16, :] = jnp.zeros((16, width), BF)
        back[cap : cap + 16, 0:lanes] = (
            jnp.where(row == 0, three[0].astype(F32), 0.0)
            + jnp.where(row == 1, three[1].astype(F32), 0.0)
            + jnp.where(row == 2, three[2].astype(F32), 0.0)
        ).astype(BF)
        flush(5 * i)


def expert(s, rows_in, dys, own, other, cap):
    n = len(rows_in)
    width = rows_in[0].shape[1]
    ff = GROUP * width
    res = call(
        functools.partial(expert_kernel, cap, n),
        [SM] + [VM] * (2 * n) + [HB] * (2 * GROUP),
        [
            shape((cap + 16, width), BF),
            shape((cap, width), BF),
            shape((cap, ff), BF),
            shape((cap, ff), BF),
            shape((cap, width), BF),
        ]
        * n,
        [
            pltpu.VMEM((GROUP, width, width), BF),
            pltpu.VMEM((GROUP, width, width), BF),
            pltpu.SemaphoreType.DMA((16,)),
        ],
        8 * n * cap * width * ff,
        4 * width * ff + n * cap * (4 * ff + 10 * width),
        "expert",
        flushed=tuple(range(0, 5 * n, 5)) + tuple(range(1, 5 * n, 5)),
    )(s, *rows_in, *dys, *own, *other)
    return [res[5 * i : 5 * i + 5] for i in range(n)]


def grad_kernel(n, skip, s_ref, *refs):
    lefts, rights, refs = refs[:n], refs[n : 2 * n], refs[2 * n + skip :]
    give, keep = refs[:2]
    if n == 1:
        left, right = lefts[0], rights[0]
    else:
        left, right = refs[2:]
        rows = lefts[0].shape[0]
        for i in range(n):
            left[i * rows : (i + 1) * rows, :] = lefts[i][...]
            right[i * rows : (i + 1) * rows, :] = rights[i][...]
    value = dot_tn(left[...], right[...]).astype(BF)

    @pl.when(pl.program_id(0) == 0)
    def _():
        give[0] = value

    @pl.when(pl.program_id(0) == 1)
    def _():
        keep[0] = value


def weight_grad(s, lefts, rights, rows=None, weight=16, stride=1, into=()):
    n = len(lefts)
    t = rows or lefts[0].shape[0]
    width = min(lefts[0].shape[1], rights[0].shape[1])
    high = width // 2
    m, nb = lefts[0].shape[1] // width, rights[0].shape[1] // width
    scratch = []
    if n > 1:
        scratch = [pltpu.VMEM((n * t, high), BF), pltpu.VMEM((n * t, width), BF)]
    left_at = lambda h, i, j, c: (0, jnp.where(h == 0, 1 - c[0], c[0]) * m + i)
    offset = 1 if into else 0

    def place_of(k, c):
        return ((k ^ c[1]) * stride + offset, 0, 0)

    give_at = lambda h, i, j, c: place_of(jnp.where(h == 0, i * nb + j, m * nb - 1), c)
    keep_at = lambda h, i, j, c: place_of(jnp.where(h == 0, 0, i * nb + j), c)
    return pl.pallas_call(
        functools.partial(grad_kernel, n, len(into)),
        grid_spec=pltpu.PrefetchScalarGridSpec(
            num_scalar_prefetch=1,
            grid=(2, m, nb),
            in_specs=[pl.BlockSpec((t, high), left_at)] * n
            + [pl.BlockSpec((t, width), lambda h, i, j, c: (0, j))] * n
            + [HB] * len(into),
            out_specs=[pl.BlockSpec((1, high, width), at) for at in (give_at, keep_at)],
            scratch_shapes=scratch,
        ),
        out_shape=[shape((m * nb * stride, high, width), BF)] * 2,
        input_output_aliases={1 + 2 * n + i: i for i in range(len(into))},
        compiler_params=pltpu.CompilerParams(vmem_limit_bytes=LIMIT),
        cost_estimate=pl.CostEstimate(
            flops=int(weight * 4) * n * t * m * high * width * nb,
            bytes_accessed=int(weight * 2) * (n * t * (2 * m * high + width * nb) + 2 * m * high * width * nb),
            transcendentals=0,
        ),
        name="weight_grad",
    )(s, *lefts, *rights, *into)


def attention_grad_kernel(s_ref, normed, context, dpacked, dattn, give, keep):
    j = pl.program_id(1)

    def write(value):
        @pl.when(pl.program_id(0) == 0)
        def _():
            give[0] = value

        @pl.when(pl.program_id(0) == 1)
        def _():
            keep[0] = value

    @pl.when(j < 3)
    def _():
        write(dot_tn(normed[...], dpacked[...]).astype(BF))

    @pl.when(j == 3)
    def _():
        write(dot_tn(context[...], dattn[...]).astype(BF))


def attention_grad(s, normed, context, dpacked, dattn):
    t, width = normed.shape
    high = width // 2
    half_at = lambda h, j, c: (0, jnp.where(h == 0, 1 - c[0], c[0]))
    return pl.pallas_call(
        attention_grad_kernel,
        grid_spec=pltpu.PrefetchScalarGridSpec(
            num_scalar_prefetch=1,
            grid=(2, 4),
            in_specs=[
                pl.BlockSpec((t, high), half_at),
                pl.BlockSpec((t, high), half_at),
                pl.BlockSpec((t, width), lambda h, j, c: (0, jnp.minimum(j, 2))),
                pl.BlockSpec((t, width), lambda h, j, c: (0, 0)),
            ],
            out_specs=[
                pl.BlockSpec((1, high, width), lambda h, j, c: (jnp.where(h == 0, j, 3), 0, 0)),
                pl.BlockSpec((1, high, width), lambda h, j, c: (jnp.where(h == 0, 0, j), 0, 0)),
            ],
        ),
        out_shape=[shape((4, high, width), BF)] * 2,
        compiler_params=pltpu.CompilerParams(vmem_limit_bytes=LIMIT),
        cost_estimate=pl.CostEstimate(
            flops=t * width * width, bytes_accessed=t * width, transcendentals=0
        ),
        name="attention_grad",
    )(s, normed, context, dpacked, dattn)


def back_kernel(
    experts, cap, dy, dense, hid, gb_ref, router, place, route, live, soft, normed3, slope, fc1, fc2, *refs
):
    homes = refs[:experts]
    dmlp, dpre, dhidden, tiny, drouter = refs[experts : experts + 5]
    w1, w2, ups, sems = refs[experts + 5 :]
    rows, width = hid.shape
    copies = [
        pltpu.make_async_copy(fc1, w1, sems.at[0]),
        pltpu.make_async_copy(fc2, w2, sems.at[1]),
    ]
    for c in copies:
        c.start()
    lanes = -(-cap // WIDE) * WIDE
    spot = iota((lanes, rows), 0)
    spot = jnp.where(spot < cap, spot, -2 * experts * cap)
    dgate = [jnp.zeros((16, rows), F32) for _ in range(TOP)]
    for r in range(experts):
        tail = homes[r][cap : cap + 16, 0:lanes]
        hot = [jnp.where(spot + r * cap == place[k : k + 1, :], 1.0, 0.0).astype(BF) for k in range(TOP)]
        for k in range(TOP):
            dgate[k] = dgate[k] + dot(tail, hot[k])
        term = dot_tn((hot[0] + hot[1])[0:cap, :], homes[r][0:cap, :])
        ups[...] = term if r == 0 else ups[...] + term
    dgate = [jnp.sum(d, axis=0, keepdims=True) * live[...] for d in dgate]
    mix = soft[0:1, :] * dgate[0] + soft[1:2, :] * dgate[1]
    dsoft = [soft[k : k + 1, :] * (dgate[k] - mix) for k in range(TOP)]
    index = iota((router.shape[0], rows), 0)
    dlogits = sum(jnp.where(index == route[k : k + 1, :], dsoft[k], 0.0) for k in range(TOP))
    dlogits = dlogits.astype(BF)
    drouter[...] = dot(dlogits, normed3[...])
    ups[...] += dot_tn(dlogits, router[...])
    tile = rows // 6
    tiny[...] = jnp.zeros_like(tiny)

    def norm_back(at, values, gain, bias_row, base):
        n, scale = normalize(values)
        u = ups[at, :]
        tiny[bias_row - 1 : bias_row, :] += jnp.sum(u * n, axis=0, keepdims=True)
        tiny[bias_row : bias_row + 1, :] += jnp.sum(u, axis=0, keepdims=True)
        ug = u * gain
        dv = scale * (
            ug
            - jnp.mean(ug, axis=-1, keepdims=True)
            - n * jnp.mean(ug * n, axis=-1, keepdims=True)
        )
        return base + dv

    @pl.loop(0, 6)
    def _(i):
        at = pl.ds(pl.multiple_of(i * tile, 16), tile)
        dd = norm_back(at, dense[at, :], gb_ref[4:5, :], 5, dy[at, :].astype(F32))
        dhidden[at, :] = dd
        dmlp[at, :] = dd.astype(BF)

    for c in copies:
        c.wait()
    ups[...] = jnp.zeros_like(ups)

    @pl.loop(0, w1.shape[1] // 512)
    def _(j):
        at = pl.ds(pl.multiple_of(j * 512, 512), 512)
        dpre[:, at] = (dot_nt(dmlp[...], w2[at, :]) * slope[:, at].astype(F32)).astype(BF)
        ups[...] += dot_nt(dpre[:, at], w1[:, at])

    @pl.loop(0, 6)
    def _(i):
        at = pl.ds(pl.multiple_of(i * tile, 16), tile)
        dhidden[at, :] = norm_back(at, hid[at, :], gb_ref[2:3, :], 3, dhidden[at, :])


def back(
    dy, dense, hid, gb, router, place, route, live, soft, normed3, slope, fc1, fc2, homes, experts, cap, after
):
    rows, width = hid.shape
    ff = fc1.shape[1]
    return call(
        functools.partial(back_kernel, experts, cap),
        [VM] * 11 + [HB] * 2 + [VM] * experts,
        [
            shape((rows, width), BF),
            shape((rows, ff), BF),
            shape((rows, width), F32),
            shape((8, width), F32),
            shape(router.shape, F32),
        ],
        [
            pltpu.VMEM((width, ff), BF),
            pltpu.VMEM((ff, width), BF),
            pltpu.VMEM((rows, width), F32),
            pltpu.SemaphoreType.DMA((2,)),
        ],
        4 * rows * width * ff + 2 * rows * width * experts * cap,
        4 * width * ff + rows * (4 * ff + 18 * width),
        "dense_backward",
        after,
    )(dy, dense, hid, gb, router, place, route, live, soft, normed3, slope, fc1, fc2, *homes)


def attend_back_kernel(
    s_ref, dhid, id_row, id_col, packed, lse, wo_a, wo_b, dattn, dpacked, wo, bias, dctx, sems
):
    s = s_ref[0]
    rows, width = dhid.shape
    copies = halves_into(s, wo_a, wo_b, wo, sems, 0)
    for c in copies:
        c.start()
    tile = rows // 6

    @pl.loop(0, 6)
    def _(i):
        at = pl.ds(pl.multiple_of(i * tile, 16), tile)
        dattn[at, :] = dhid[at, :].astype(BF)
        bias[at, :] = jnp.where(id_col[at, :] == id_row[...], 0.0, MASKED)

    copies[0].wait()
    copies[1].wait()

    @pl.loop(0, width // 256)
    def _(j):
        at = pl.ds(pl.multiple_of(j * 256, 256), 256)
        dctx[:, at] = dot_nt(dattn[...], wo[at, :]).astype(BF)

    lane = iota((1, WIDE), 1)

    @pl.loop(0, width // WIDE)
    def _(pair):
        col = pl.multiple_of(pair * WIDE, WIDE)
        q = packed[:, pl.ds(col, WIDE)] * jnp.asarray(HEAD**-0.5, BF)
        keys = packed[:, pl.ds(width + col, WIDE)]
        values = packed[:, pl.ds(2 * width + col, WIDE)]
        dc = dctx[:, pl.ds(col, WIDE)]
        dq, dk, dv = [], [], []
        for h in range(2):
            mine = (lane >= h * HEAD) & (lane < (h + 1) * HEAD)
            scores = dot_nt(jnp.where(mine, keys, jnp.zeros_like(keys)), q) + bias[...]
            p = jnp.exp(scores - lse[pl.ds(2 * pair + h, 1), :])
            dp = dot_nt(jnp.where(mine, values, jnp.zeros_like(values)), dc)
            inner = jnp.sum(p * dp, axis=0, keepdims=True)
            ds = (p * (dp - inner)).astype(BF)
            dv.append(dot(p.astype(BF), dc))
            dk.append(dot(ds, q))
            dq.append(dot_tn(ds, keys) * HEAD**-0.5)
        low = lane < HEAD
        dpacked[:, pl.ds(col, WIDE)] = jnp.where(low, dq[0], dq[1]).astype(BF)
        dpacked[:, pl.ds(width + col, WIDE)] = jnp.where(low, dk[0], dk[1]).astype(BF)
        dpacked[:, pl.ds(2 * width + col, WIDE)] = jnp.where(low, dv[0], dv[1]).astype(BF)


def input_kernel(s_ref, x_ref, dhid, gb_ref, dpacked, qkv_a, qkv_b, grad_in, tiny, wq, ups, sems):
    s = s_ref[0]
    rows, width = x_ref.shape
    tile = rows // 6
    copies = halves_into(s, qkv_a, qkv_b, wq, sems, 0)
    for c in copies:
        c.start()
    copies[0].wait()
    copies[1].wait()

    @pl.loop(0, width // 256)
    def _(j):
        at = pl.ds(pl.multiple_of(j * 256, 256), 256)
        ups[:, at] = dot_nt(dpacked[...], wq[at, :])

    tiny[...] = jnp.zeros_like(tiny)

    @pl.loop(0, 6)
    def _(i):
        at = pl.ds(pl.multiple_of(i * tile, 16), tile)
        n, scale = normalize(x_ref[at, :].astype(F32))
        u = ups[at, :]
        tiny[0:1, :] += jnp.sum(u * n, axis=0, keepdims=True)
        tiny[1:2, :] += jnp.sum(u, axis=0, keepdims=True)
        ug = u * gb_ref[0:1, :]
        grad_in[at, :] = dhid[at, :] + scale * (
            ug
            - jnp.mean(ug, axis=-1, keepdims=True)
            - n * jnp.mean(ug * n, axis=-1, keepdims=True)
        )


def attend_back(s, dhid, ids, packed, lse, wo, after):
    rows, width = dhid.shape
    n3 = packed.shape[1]
    return call(
        attend_back_kernel,
        [SM] + [VM] * 5 + [HB] * 2,
        [shape((rows, width), BF), shape((rows, n3), BF)],
        [
            pltpu.VMEM((width, width), BF),
            pltpu.VMEM((rows, rows), F32),
            pltpu.VMEM((rows, width), BF),
            pltpu.SemaphoreType.DMA((2,)),
        ],
        2 * rows * width * width + 20 * rows * rows * width,
        2 * (width * width + rows * (3 * width + 2 * n3)),
        "attention_backward",
        after,
    )(s, dhid, ids[None, :], ids[:, None], packed, lse, *wo)


def input_back(s, x, dhid, gb, dpacked, qkv, after):
    rows, width = x.shape
    n3 = dpacked.shape[1]
    return call(
        input_kernel,
        [SM] + [VM] * 4 + [HB] * 2,
        [shape((rows, width), F32), shape((8, width), F32)],
        [
            pltpu.VMEM((width, n3), BF),
            pltpu.VMEM((rows, width), F32),
            pltpu.SemaphoreType.DMA((2,)),
        ],
        2 * rows * width * n3,
        2 * (width * n3 + rows * n3) + 10 * rows * width,
        "input_backward",
        after,
    )(s, x, dhid, gb, dpacked, *qkv)


def merge_kernel(experts, cap, dense, place, *refs):
    outs, result = refs[:experts], refs[experts]
    rows = dense.shape[0]
    total = dense[...]
    spot = iota((cap, rows), 0)
    for r in range(experts):
        hot = sum(jnp.where(spot + r * cap == place[k : k + 1, :], 1.0, 0.0) for k in range(TOP))
        total = total + dot_tn(hot.astype(BF), outs[r][...])
    result[...] = total.astype(BF)


def merge(dense, place, outs, experts, cap):
    rows, width = dense.shape
    return call(
        functools.partial(merge_kernel, experts, cap),
        [VM] * (2 + experts),
        shape((rows, width), BF),
        [],
        2 * rows * width * experts * cap,
        rows * width * 6 + 2 * experts * cap * width,
        "merge",
        (),
        0.25,
    )(dense, place, *outs)


def hold_kernel(n, *refs):
    for i in range(n):
        refs[n + i][...] = refs[i][...]


def hold(chunks, after):
    n = len(chunks)
    dims = chunks[0].shape
    return call(
        functools.partial(hold_kernel, n),
        [VM] * n,
        [shape(dims, BF)] * n,
        [],
        0,
        4 * n * dims[0] * dims[1],
        "hold",
        after,
    )(*chunks)


def finish_kernel(columns, m_ref, mine, got, out):
    n, high, width = mine.shape
    for which, src in ((m_ref[0], mine), (1 - m_ref[0], got)):
        for i in range(n):
            value = src[i].astype(F32)
            if columns:
                out[:, pl.ds(pl.multiple_of((which * n + i) * width, width), width)] = value
            else:
                out[pl.ds(pl.multiple_of((which * n + i) * high, high), high), :] = value


def finish(m, mine, got, columns):
    n, high, width = mine.shape
    dims = (high, 2 * n * width) if columns else (2 * n * high, width)
    return call(
        functools.partial(finish_kernel, columns),
        [SM, VM, VM],
        shape(dims, F32),
        [],
        0,
        12 * n * high * width,
        "finish",
    )(m, mine, got)


def spread_kernel(experts, cap, rows_in, place, *chunks):
    spot = iota((cap, rows_in.shape[0]), 0)
    for r in range(experts):
        hot = sum(jnp.where(spot + r * cap == place[k : k + 1, :], 1.0, 0.0) for k in range(TOP))
        chunks[r][...] = dot(hot.astype(BF), rows_in[...]).astype(BF)


def spread(rows_in, place, experts, cap):
    rows, width = rows_in.shape
    return call(
        functools.partial(spread_kernel, experts, cap),
        [VM, VM],
        [shape((cap, width), BF)] * experts,
        [],
        2 * rows * width * experts * cap,
        2 * (rows + experts * cap) * width,
        "spread",
    )(rows_in, place)


def places_of(routes, live, experts, capacity):
    tokens = routes.shape[0]
    ids = jnp.arange(experts, dtype=jnp.int32)
    match = [
        ((routes[:, k : k + 1] == ids[None, :]) & live[:, None]).astype(F32) for k in range(TOP)
    ]
    order = jnp.arange(tokens, dtype=jnp.int32)
    below = (order[:, None] > order[None, :]).astype(BF)
    before = jnp.zeros((1, experts), F32)
    out = []
    for k in range(TOP):
        counts = dot(below, match[k].astype(BF)) + before
        before = before + jnp.sum(match[k], axis=0, keepdims=True)
        within = jnp.sum(counts * match[k], axis=1).astype(jnp.int32)
        out.append(jnp.where(live, routes[:, k] * capacity + within, experts * capacity))
    return out

def local(
    tokens,
    image_ids,
    routes,
    norm1_gain,
    norm1_bias,
    qkv_weight,
    attn_out_weight,
    norm2_gain,
    norm2_bias,
    fc1_weight,
    fc2_weight,
    norm3_gain,
    norm3_bias,
    router_weight,
    expert_up,
    expert_down,
    cotangent,
):
    s = lax.axis_index("section")
    e = lax.axis_index("dp") // GROUP
    q = lax.axis_index("dp") % GROUP
    dp_count = lax.axis_size("dp")
    experts = dp_count // GROUP
    cap = GROUP * ((21 * SLOTS + 10 * experts * GROUP - 1) // (10 * experts * GROUP))
    cap = -(-cap // 16) * 16
    half = tokens.shape[1]
    width = 2 * half
    few = experts <= 8
    planes = [[p * GROUP + i for p in range(experts)] for i in range(GROUP)]
    here, here_q = jnp.stack([s, 0 * s]), jnp.stack([s, q])
    quads = [[p * GROUP + i for i in range(GROUP)] for p in range(experts)]

    def swap(v):
        return lax.ppermute(v, "section", [(0, 1), (1, 0)])

    def over_q(v, bit):
        return lax.ppermute(v, "dp", [(i, i ^ bit) for i in range(dp_count)])

    def over_e(v, r):
        return lax.ppermute(
            v,
            "dp",
            [(i, ((i // GROUP + r) % experts) * GROUP + i % GROUP) for i in range(dp_count)],
        )

    def part(v, index, size, axis=0):
        return lax.dynamic_slice_in_dim(v, index * size, size, axis)

    def join(own, other, axis):
        return jnp.where(
            s == 0,
            jnp.concatenate([own, other], axis=axis),
            jnp.concatenate([other, own], axis=axis),
        )

    def add(a, b):
        return (a.astype(F32) + b.astype(F32)).astype(BF)

    def out_chunks(chunks):
        if not few:
            return list(lax.all_to_all(jnp.stack(chunks), "dp", 0, 0, axis_index_groups=planes))
        return [chunks[0]] + [over_e(chunks[r], r) for r in range(1, experts)]

    def home_chunks(chunks):
        if not few:
            return list(lax.all_to_all(jnp.stack(chunks), "dp", 0, 0, axis_index_groups=planes))
        return [chunks[0]] + [over_e(chunks[r], experts - r) for r in range(1, experts)]

    small = jnp.stack([norm1_gain, norm1_bias, norm2_gain, norm2_bias, norm3_gain, norm3_bias])
    small = jnp.concatenate([small, jnp.transpose(router_weight)])
    small = join(small, swap(small), 1)
    x = join(part(tokens, s, SLOTS), swap(part(tokens, 1 - s, SLOTS)), 1)
    dy = join(part(cotangent, s, SLOTS), swap(part(cotangent, 1 - s, SLOTS)), 1)
    ids = part(image_ids, s, 1).reshape(-1)
    route = part(routes, s, SLOTS)
    live = ids >= 0
    gb = jnp.concatenate([small[:6], jnp.zeros((2, width), BF)]).astype(F32)
    router_rows = -(-experts // 16) * 16
    router = jnp.concatenate([small[6 : 6 + experts], jnp.zeros((router_rows - experts, width), BF)])
    qkv, wo = (qkv_weight, swap(qkv_weight)), (attn_out_weight, swap(attn_out_weight))

    pair = jnp.stack([expert_up, expert_down])

    def gather(v, tiled):
        return lax.all_gather(v, "section", axis=0, tiled=tiled)

    tie = lax.optimization_barrier
    x, dy, qkv, wo, fc1_weight, fc2_weight, pair = tie(
        (x, dy, qkv, wo, fc1_weight, fc2_weight, pair)
    )
    fc1, fc2 = gather(fc1_weight, True), gather(fc2_weight, True)
    from_x, from_y, other_pair = over_q(pair, 1), over_q(pair, 2), swap(pair)

    if few:
        distance = (route - e) % experts
    else:
        distance = route
    spots = places_of(distance, live, experts, cap)
    place = jnp.stack(spots + [jnp.full_like(spots[0], -1)] * 6)
    route_rows = jnp.concatenate([jnp.transpose(route), jnp.full((6, SLOTS), -1, jnp.int32)])
    live_row = live.astype(F32)[None, :]
    dy_sent = spread(dy, place, experts, cap)
    dy_out = out_chunks(dy_sent)

    normed1, packed, context, lse, hidden = front(here, x, ids, gb, qkv, wo, dy_sent[:1])
    hidden, from_x, from_y, other_pair, *dy_out[:-1] = tie(
        (hidden, from_x, from_y, other_pair, *dy_out[:-1])
    )
    other_x, other_y = swap(from_x), swap(from_y)
    far = over_q(from_x, 2)
    normed2, act, slope, dense, normed3, soft, *sent = mlp(
        hidden, gb, router, place, route_rows, live_row, fc1, fc2, experts, cap, []
    )
    sent, other_x, other_y, dy_out[-1] = tie((sent, other_x, other_y, dy_out[-1]))
    got = out_chunks(sent)
    got[0], far = tie((got[0], far))
    own, other = [pair, from_x, from_y, far], [other_pair, other_x, other_y, swap(far)]

    step = max(1, experts // 4)
    results = [None] * experts
    previous, homes = None, [None] * experts
    order = [0, 3, 1, 2] if experts == 4 else list(range(0, experts, step))
    for place_in_order, i in enumerate(order):
        if i:
            got[i], results[previous] = tie((got[i], results[previous]))
        if few and place_in_order == 3:
            got[i], homes[order[1]] = tie((got[i], homes[order[1]]))
        results[i : i + step] = expert(
            here, got[i : i + step], dy_out[i : i + step], own, other, cap
        )
        previous = i
        homes[i] = over_e(results[i][0], experts - i) if few and i else results[i][0]
    if not few:
        homes = home_chunks([r[0] for r in results])
    acts, dinners, scaled = ([r[i] for r in results] for i in (2, 3, 4))

    if experts == 4:
        dinners, homes[1] = tie((dinners, homes[1]))
    up_grads = weight_grad(here_q, got, dinners, cap, stride=2)
    dmlp, dpre, dhidden, tiny23, drouter = back(
        dy, dense, hidden, gb, router, place, route_rows, live_row, soft, normed3, slope,
        fc1, fc2, homes, experts, cap, [],
    )
    outs = hold([r[1] for r in results], [dmlp])
    grads1, grads2 = weight_grad(here, [normed2], [dpre]), weight_grad(here, [act], [dmlp])
    acts, grads1, grads2 = tie((acts, grads1, grads2))
    expert_grads = weight_grad(here_q, scaled, acts, stride=2, into=up_grads)

    def fold(v, bit):
        mine, rows = (q // bit) % 2, v.shape[0] // 2
        return part(v, mine, rows), over_q(part(v, 1 - mine, rows), bit)

    def unfold(v, got, bit):
        return jnp.where(
            (q // bit) % 2 == 0, jnp.concatenate([v, got]), jnp.concatenate([got, v])
        )

    def plane_out(a, b):
        ab = jnp.stack([a, b])
        rows = a.shape[0] // experts
        if not few:
            return [lax.psum(ab, "dp", axis_index_groups=planes)]
        return [part(ab, (e + r) % experts, rows, 1) for r in range(experts)]

    def plane_sum(pieces):
        if not few:
            return pieces
        total = sum(p.astype(F32) for p in pieces).astype(BF)
        return [total] * experts

    def plane_move(pieces):
        return pieces[:1] + [over_e(p, r) for r, p in enumerate(pieces) if r]

    def plane_join(pieces):
        if not few:
            return pieces[0][0], pieces[0][1]
        rows = pieces[0].shape[1]
        whole = jnp.zeros((2, experts * rows, width), BF)
        for r, piece in enumerate(pieces):
            whole = lax.dynamic_update_slice_in_dim(whole, piece, ((e - r) % experts) * rows, 1)
        return whole[0], whole[1]

    away1, away2 = swap(grads1[0]), swap(grads2[0])
    dhidden, away1, away2, grads1, grads2, expert_grads = tie(
        (dhidden, away1, away2, grads1, grads2, expert_grads)
    )
    a, b = add(grads2[1], away2).reshape(-1, width), add(grads1[1], away1).reshape(-1, width)
    a, b = fold(a, 1), fold(b, 2)
    dattn, dpacked = attend_back(here, dhidden, ids, packed, lse, wo, [])
    home_outs = home_chunks(outs)
    give, keep = attention_grad(here, normed1, context, dpacked, dattn)
    give, keep, a, b, dpacked, home_outs = tie((give, keep, a, b, dpacked, home_outs))
    grad_in, tiny1 = input_back(here, x, dhidden, gb, dpacked, qkv, [])
    tiny = jnp.concatenate([tiny1[:2], tiny23[2:6], drouter[:experts]])

    def swapped(v):
        return part(v, s, half, 1), swap(part(v, 1 - s, half, 1))

    away = swap(give)
    a, b = fold(add(*a), 2), fold(add(*b), 1)
    sum_experts = add(expert_grads[1], swap(expert_grads[0]))
    tiny = swapped(tiny)
    away, a, b, grad_in, tiny, sum_experts = tie((away, a, b, grad_in, tiny, sum_experts))
    half_experts = lax.psum_scatter(
        sum_experts.reshape(GROUP, 2, half, -1),
        "dp", scatter_dimension=0, axis_index_groups=quads, tiled=False,
    )
    grad_in = swapped(grad_in)
    tiny = tiny[0] + tiny[1]

    ab = plane_move(plane_out(add(*a), add(*b)))
    t = add(keep, away).reshape(-1, width)
    ta, tb = fold(t[:width], 1), fold(t[width:], 2)
    ab, ta, tb = tie((ab, ta, tb))
    block_out = merge(dense, place, home_outs, experts, cap)

    ab = plane_move(plane_sum(ab))
    ta, tb = fold(add(*ta), 2), fold(add(*tb), 1)
    ab, ta, tb, block_out = tie((ab, ta, tb, block_out))

    a, b = plane_join(ab)
    a_got, b_got = over_q(a, 2), over_q(b, 1)
    tab = plane_move(plane_out(add(*ta), add(*tb)))
    a_got, b_got, tab = tie((a_got, b_got, tab))
    a, b = unfold(a, a_got, 2), unfold(b, b_got, 1)
    a_got, b_got = over_q(a, 1), over_q(b, 2)
    tab = plane_move(plane_sum(tab))
    a_got, b_got, tab = tie((a_got, b_got, tab))

    side_x, side_y = jnp.reshape(q % 2, (1,)), jnp.reshape(q // 2, (1,))

    def blocks(v):
        return v.reshape(-1, half, width)

    ta, tb = plane_join(tab)
    ta_got, tb_got = over_q(ta, 2), over_q(tb, 1)
    block_out = swapped(block_out)
    tiny_q = [over_q(tiny, bit) for bit in (1, 2, 3)]
    sum_fc2 = finish(side_x, blocks(a), blocks(a_got), False)
    sum_fc1 = finish(side_y, blocks(b), blocks(b_got), True)
    ta_got, tb_got, block_out, grad_in, tiny_q, sum_fc2, sum_fc1, half_experts = tie(
        (ta_got, tb_got, block_out, grad_in, tiny_q, sum_fc2, sum_fc1, half_experts)
    )
    half_up, half_down = half_experts[0].astype(F32), half_experts[1].astype(F32)
    ta, tb = unfold(ta, ta_got, 2), unfold(tb, tb_got, 1)
    ta_got, tb_got = over_q(ta, 1), over_q(tb, 2)
    tiny = tiny + tiny_q[0] + (tiny_q[1] + tiny_q[2])
    if few:
        total = sum(over_e(tiny, r) if r else tiny for r in range(experts))
    else:
        total = lax.psum(tiny, "dp", axis_index_groups=planes)
    q_and_k = finish(side_x, blocks(ta), blocks(ta_got), True)
    first = q // 2 == 0
    v_sum, sum_attn = (
        jnp.where(first, p, r).astype(F32) for p, r in ((tb, tb_got), (tb_got, tb))
    )
    sum_qkv = jnp.concatenate([q_and_k, v_sum], axis=1)
    return (
        join(*block_out, 0),
        join(*grad_in, 0),
        total[0],
        total[1],
        sum_qkv,
        sum_attn,
        total[2],
        total[3],
        sum_fc1,
        sum_fc2,
        total[4],
        total[5],
        jnp.transpose(total[6:]),
        half_up,
        half_down,
    )


def solution(mesh):
    placed = (
        P("dp", "section"),
        P("dp", None),
        P("dp", None),
        P("section"),
        P("section"),
        P("section", None),
        P("section", None),
        P("section"),
        P("section"),
        P("section", None),
        P("section", None),
        P("section"),
        P("section"),
        P("section", None),
        P("section", "dp"),
        P("section", "dp"),
        P("dp", "section"),
    )
    return jax.shard_map(
        local,
        mesh=mesh,
        in_specs=placed,
        out_specs=(
            P("dp", "section"),
            P("dp", "section"),
            P("section"),
            P("section"),
            P("section", None),
            P("section", None),
            P("section"),
            P("section"),
            P("section", None),
            P("section", None),
            P("section"),
            P("section"),
            P("section", None),
            P("section", "dp"),
            P("section", "dp"),
        ),
        check_vma=False,
    )
```

```python
import functools

import jax
import jax.numpy as jnp
from jax import lax
from jax.experimental import pallas as pl
from jax.experimental.pallas import tpu as pltpu
from jax.sharding import PartitionSpec as P

HEAD = 64
TOP = 2
GROUP = 4
SLOTS = 576
WIDE = 128

EPSILON = 1e-06
MASKED = -1e30
BF = jnp.bfloat16
F32 = jnp.float32
LIMIT = 24 * 1024 * 1024
LIMITS = dict(
    attention_forward=28,
    dense_forward=36,
    expert=28,
    dense_backward=40,
    attention_backward=28,
    input_backward=24,
    merge=20,
    hold=12,
    finish=24,
    spread=16,
)


def dot(a, b):
    return jnp.dot(a, b, preferred_element_type=F32)


def dot_nt(a, b):
    return lax.dot_general(a, b, (((1,), (1,)), ((), ())), preferred_element_type=F32)


def dot_tn(a, b):
    return lax.dot_general(a, b, (((0,), (0,)), ((), ())), preferred_element_type=F32)


def normalize(v):
    center = v - jnp.mean(v, axis=-1, keepdims=True)
    scale = lax.rsqrt(jnp.mean(center * center, axis=-1, keepdims=True) + EPSILON)
    return center * scale, scale


def gelu_pair(x):
    bell = jnp.exp(x * x * -0.5)
    t = 1.0 / (1.0 + jnp.abs(x) * (0.3275911 * 0.5**0.5))
    tail = (
        t
        * (
            0.127414796
            + t * (-0.142248368 + t * (0.7107068705 + t * (-0.7265760135 + t * 0.5307027145)))
        )
        * bell
    )
    cdf = jnp.where(x >= 0.0, 1.0 - tail, tail)
    return x * cdf, cdf + x * (bell * 0.3989422804014327)


def iota(shape, axis):
    return lax.broadcasted_iota(jnp.int32, shape, axis)


def halves_into(s, own, other, dest, sems, first):
    rows = own.shape[0]
    return [
        pltpu.make_async_copy(own, dest.at[pl.ds(pl.multiple_of(s * rows, rows), rows)], sems.at[first]),
        pltpu.make_async_copy(
            other, dest.at[pl.ds(pl.multiple_of((1 - s) * rows, rows), rows)], sems.at[first + 1]
        ),
    ]


def split3(v):
    hi = v.astype(BF)
    rest = v - hi.astype(F32)
    mid = rest.astype(BF)
    low = (rest - mid.astype(F32)).astype(BF)
    return hi, mid, low


VM = pl.BlockSpec(memory_space=pltpu.VMEM)
SM = pl.BlockSpec(memory_space=pltpu.SMEM)
HB = pl.BlockSpec(memory_space=pl.ANY)


def call(kernel, in_specs, out_shape, scratch, flops, moved, name, after=(), weight=16, flushed=()):
    limit = LIMITS[name] * 1024 * 1024
    count, extra = len(in_specs), len(after)
    single = not isinstance(out_shape, list)
    shapes = [out_shape] if single else out_shape
    total, held = len(shapes), len(flushed)

    def body(*refs):
        inputs, outs = refs[:count], list(refs[count + extra : count + extra + total])
        rest = refs[count + extra + total :]
        if not held:
            kernel(*inputs, *outs, *rest)
            return
        own, (buffers, sems) = rest[: len(rest) - held - 1], (rest[len(rest) - held - 1 : -1], rest[-1])
        copies = {}
        for k, index in enumerate(flushed):
            copies[index] = pltpu.make_async_copy(buffers[k], outs[index], sems.at[k])
            outs[index] = buffers[k]
        kernel(*inputs, *outs, *own, flush=lambda index: copies[index].start())
        for index in flushed:
            copies[index].wait()

    made = pl.pallas_call(
        body,
        in_specs=in_specs + [HB] * extra,
        out_specs=VM
        if single
        else [pl.BlockSpec(memory_space=pltpu.HBM) if i in flushed else VM for i in range(total)],
        out_shape=out_shape
        if not held
        else [pltpu.HBM(v.shape, v.dtype) if i in flushed else v for i, v in enumerate(shapes)],
        scratch_shapes=scratch
        + [pltpu.VMEM(shapes[i].shape, shapes[i].dtype) for i in flushed]
        + ([pltpu.SemaphoreType.DMA((held,))] if held else []),
        compiler_params=pltpu.CompilerParams(vmem_limit_bytes=limit),
        cost_estimate=pl.CostEstimate(
            flops=int(weight * flops), bytes_accessed=int(weight * moved), transcendentals=0
        ),
        name=name,
    )
    return lambda *operands: made(*operands, *after)


def shape(dims, kind):
    return jax.ShapeDtypeStruct(dims, kind)


def front_kernel(
    s_ref, x_ref, id_row, id_col, gb_ref, qkv_a, qkv_b, wo_a, wo_b,
    normed, packed, context, lse, hidden,
    wq, wo, bias, lse_col, sems, flush,
):
    s = s_ref[0]
    rows, width = x_ref.shape
    copies = halves_into(s, qkv_a, qkv_b, wq, sems, 0) + halves_into(s, wo_a, wo_b, wo, sems, 2)
    for c in copies:
        c.start()
    tile = rows // 6

    @pl.loop(0, 6)
    def _(i):
        at = pl.ds(pl.multiple_of(i * tile, 16), tile)
        n, _ = normalize(x_ref[at, :].astype(F32))
        normed[at, :] = (n * gb_ref[0:1, :] + gb_ref[1:2, :]).astype(BF)
        bias[at, :] = jnp.where(id_col[at, :] == id_row[...], 0.0, MASKED)

    copies[0].wait()
    copies[1].wait()

    @pl.loop(0, wq.shape[1] // 256)
    def _(j):
        at = pl.ds(pl.multiple_of(j * 256, 256), 256)
        packed[:, at] = dot(normed[...], wq[:, at]).astype(BF)

    flush(0)
    flush(1)
    lane = iota((1, WIDE), 1)
    lse_col[...] = jnp.zeros_like(lse_col)
    third = rows // 3

    @pl.loop(0, width // WIDE)
    def _(pair):
        col = pl.multiple_of(pair * WIDE, WIDE)
        keys = packed[:, pl.ds(width + col, WIDE)]
        values = packed[:, pl.ds(2 * width + col, WIDE)]
        for r in range(3):
            at = slice(r * third, (r + 1) * third)
            q = packed[at, pl.ds(col, WIDE)] * jnp.asarray(HEAD**-0.5, BF)
            outs = []
            sums = lse_col[at, :]
            for h in range(2):
                mine = (lane >= h * HEAD) & (lane < (h + 1) * HEAD)
                scores = dot_nt(jnp.where(mine, q, jnp.zeros_like(q)), keys) + bias[at, :]
                top = jnp.max(scores, axis=1, keepdims=True)
                p = jnp.exp(scores - top)
                total = jnp.sum(p, axis=1, keepdims=True)
                outs.append(dot(p.astype(BF), values) * (1.0 / total))
                sums = jnp.where(lane == 2 * pair + h, top + jnp.log(total), sums)
            lse_col[at, :] = sums
            context[at, pl.ds(col, WIDE)] = jnp.where(lane < HEAD, outs[0], outs[1]).astype(BF)

    flush(2)
    lse[...] = jnp.transpose(lse_col[...])[0 : lse.shape[0], :]
    copies[2].wait()
    copies[3].wait()

    @pl.loop(0, width // 256)
    def _(j):
        at = pl.ds(pl.multiple_of(j * 256, 256), 256)
        hidden[:, at] = x_ref[:, at].astype(F32) + dot(context[...], wo[:, at])


def front(s, x, ids, gb, qkv, wo, after):
    rows, width = x.shape
    n3 = qkv[0].shape[1]
    return call(
        front_kernel,
        [SM, VM, VM, VM, VM, HB, HB, HB, HB],
        [
            shape((rows, width), BF),
            shape((rows, n3), BF),
            shape((rows, width), BF),
            shape((16, rows), F32),
            shape((rows, width), F32),
        ],
        [
            pltpu.VMEM((width, n3), BF),
            pltpu.VMEM((width, width), BF),
            pltpu.VMEM((rows, rows), F32),
            pltpu.VMEM((rows, WIDE), F32),
            pltpu.SemaphoreType.DMA((4,)),
        ],
        2 * rows * width * (n3 + width) + 4 * rows * rows * width,
        2 * (width * (n3 + width) + rows * (3 * width + n3)) + 4 * rows * width,
        "attention_forward",
        after,
        flushed=(0, 1, 2),
    )(s, x, ids[None, :], ids[:, None], gb, *qkv, *wo)


def mlp_kernel(experts, cap, hid, gb_ref, router, place, route, live, fc1, fc2, *refs, flush):
    normed2, act, slope, dense, normed3, soft = refs[:6]
    chunks = refs[6 : 6 + experts]
    w1, w2, sems = refs[6 + experts :]
    rows, width = hid.shape
    copies = [
        pltpu.make_async_copy(fc1, w1, sems.at[0]),
        pltpu.make_async_copy(fc2, w2, sems.at[1]),
    ]
    for c in copies:
        c.start()
    tile = rows // 6

    @pl.loop(0, 6)
    def _(i):
        at = pl.ds(pl.multiple_of(i * tile, 16), tile)
        n, _ = normalize(hid[at, :])
        normed2[at, :] = (n * gb_ref[2:3, :] + gb_ref[3:4, :]).astype(BF)
        dense[at, :] = hid[at, :]

    flush(0)
    for c in copies:
        c.wait()

    @pl.loop(0, w1.shape[1] // 512)
    def _(j):
        at = pl.ds(pl.multiple_of(j * 512, 512), 512)
        a, sl = gelu_pair(dot(normed2[...], w1[:, at]))
        act[:, at] = a.astype(BF)
        slope[:, at] = sl.astype(BF)
        dense[...] += dot(act[:, at], w2[at, :])

    flush(1)
    flush(2)
    flush(3)

    @pl.loop(0, 6)
    def _(i):
        at = pl.ds(pl.multiple_of(i * tile, 16), tile)
        n, _ = normalize(dense[at, :])
        normed3[at, :] = (n * gb_ref[4:5, :] + gb_ref[5:6, :]).astype(BF)

    flush(4)
    logits = dot_nt(router[...], normed3[...])
    expert = iota(logits.shape, 0)
    chosen = [
        jnp.sum(jnp.where(expert == route[k : k + 1, :], logits, 0.0), axis=0, keepdims=True)
        for k in range(TOP)
    ]
    top = jnp.maximum(chosen[0], chosen[1])
    raised = [jnp.exp(c - top) for c in chosen]
    total = raised[0] + raised[1]
    pieces = []
    for k in range(TOP):
        share = raised[k] / total
        soft[k : k + 1, :] = share
        three = split3(share * live[...])
        row = iota((16, rows), 0)
        pieces.append(
            jnp.where(row == 0, three[0].astype(F32), 0.0)
            + jnp.where(row == 1, three[1].astype(F32), 0.0)
            + jnp.where(row == 2, three[2].astype(F32), 0.0)
        )
    pieces = [p.astype(BF) for p in pieces]
    lanes = -(-cap // WIDE) * WIDE
    spot = iota((lanes, rows), 0)
    spot = jnp.where(spot < cap, spot, -2 * experts * cap)
    for r in range(experts):
        hot = [jnp.where(spot + r * cap == place[k : k + 1, :], 1.0, 0.0).astype(BF) for k in range(TOP)]
        both = (hot[0] + hot[1])[0:cap, :]
        chunks[r][0:cap, :] = dot(both, normed3[...]).astype(BF)
        chunks[r][cap : cap + 16, :] = jnp.zeros((16, width), BF)
        chunks[r][cap : cap + 16, 0:lanes] = (
            dot_nt(pieces[0], hot[0]) + dot_nt(pieces[1], hot[1])
        ).astype(BF)
        if r:
            flush(6 + r)


def mlp(hid, gb, router, place, route, live, fc1, fc2, experts, cap, after):
    rows, width = hid.shape
    ff = fc1.shape[1]
    return call(
        functools.partial(mlp_kernel, experts, cap),
        [VM, VM, VM, VM, VM, VM, HB, HB],
        [
            shape((rows, width), BF),
            shape((rows, ff), BF),
            shape((rows, ff), BF),
            shape((rows, width), F32),
            shape((rows, width), BF),
            shape((8, rows), F32),
        ]
        + [shape((cap + 16, width), BF)] * experts,
        [
            pltpu.VMEM((width, ff), BF),
            pltpu.VMEM((ff, width), BF),
            pltpu.SemaphoreType.DMA((2,)),
        ],
        4 * rows * width * ff + 2 * rows * width * experts * cap,
        4 * width * ff + rows * (4 * ff + 12 * width),
        "dense_forward",
        after,
        flushed=(0, 1, 2, 3, 4) + tuple(range(7, 6 + experts)),
    )(hid, gb, router, place, route, live, fc1, fc2)


def expert_kernel(cap, n, s_ref, *refs, flush):
    rows_in, dys = refs[:n], refs[n : 2 * n]
    own, other = refs[2 * n : 2 * n + GROUP], refs[2 * n + GROUP : 2 * n + 2 * GROUP]
    outs = refs[2 * n + 2 * GROUP : -3]
    wu, wd, sems = refs[-3:]
    s = s_ref[0]
    width = wu.shape[1]
    half = width // 2
    copies = [
        [
            pltpu.make_async_copy(
                src[b].at[u],
                w.at[b, pl.ds(pl.multiple_of(side * half, half), half)],
                sems.at[4 * b + 2 * h + u],
            )
            for h, (side, src) in enumerate(((s, own), (1 - s, other)))
            for u, w in enumerate((wu, wd))
        ]
        for b in range(GROUP)
    ]
    for b in range(GROUP):
        for c in copies[b]:
            c.start()
    lanes = -(-cap // WIDE) * WIDE
    eye = iota((lanes, lanes), 0) == iota((lanes, lanes), 1)
    gates = []
    for i in range(n):
        back, out, act, dinner, gp = outs[5 * i : 5 * i + 5]
        g = jnp.sum(rows_in[i][cap : cap + 16, 0:lanes].astype(F32), axis=0, keepdims=True)
        gate = jnp.sum(jnp.where(eye, g, 0.0), axis=1, keepdims=True)[0:cap, :]
        gp[...] = (gate * dys[i][...].astype(F32)).astype(BF)
        gates.append(gate)
    sums = [None] * n
    backs = [None] * n
    for b in range(GROUP):
        for c in copies[b]:
            c.wait()
        at = slice(b * width, (b + 1) * width)
        for i in range(n):
            back, out, act, dinner, gp = outs[5 * i : 5 * i + 5]
            a, slope = gelu_pair(dot(rows_in[i][0:cap, :], wu[b]))
            act[:, at] = a.astype(BF)
            dinner[:, at] = (dot(gp[...], wd[b]) * slope).astype(BF)
            o = dot_nt(act[:, at], wd[b])
            d = dot_nt(dinner[:, at], wu[b])
            sums[i] = o if b == 0 else sums[i] + o
            backs[i] = d if b == 0 else backs[i] + d
    for i in range(n):
        back, out, act, dinner, gp = outs[5 * i : 5 * i + 5]
        out[...] = (gates[i] * sums[i]).astype(BF)
        flush(5 * i + 1)
        back[0:cap, :] = backs[i].astype(BF)
        dg = jnp.sum(dys[i][...].astype(F32) * sums[i], axis=1, keepdims=True)
        pad = jnp.where(eye[0:cap, :], dg, 0.0)
        dg_row = jnp.sum(pad, axis=0, keepdims=True)
        three = split3(dg_row)
        row = iota((16, lanes), 0)
        back[cap : cap + 16, :] = jnp.zeros((16, width), BF)
        back[cap : cap + 16, 0:lanes] = (
            jnp.where(row == 0, three[0].astype(F32), 0.0)
            + jnp.where(row == 1, three[1].astype(F32), 0.0)
            + jnp.where(row == 2, three[2].astype(F32), 0.0)
        ).astype(BF)
        flush(5 * i)


def expert(s, rows_in, dys, own, other, cap):
    n = len(rows_in)
    width = rows_in[0].shape[1]
    ff = GROUP * width
    res = call(
        functools.partial(expert_kernel, cap, n),
        [SM] + [VM] * (2 * n) + [HB] * (2 * GROUP),
        [
            shape((cap + 16, width), BF),
            shape((cap, width), BF),
            shape((cap, ff), BF),
            shape((cap, ff), BF),
            shape((cap, width), BF),
        ]
        * n,
        [
            pltpu.VMEM((GROUP, width, width), BF),
            pltpu.VMEM((GROUP, width, width), BF),
            pltpu.SemaphoreType.DMA((16,)),
        ],
        8 * n * cap * width * ff,
        4 * width * ff + n * cap * (4 * ff + 10 * width),
        "expert",
        flushed=tuple(range(0, 5 * n, 5)) + tuple(range(1, 5 * n, 5)),
    )(s, *rows_in, *dys, *own, *other)
    return [res[5 * i : 5 * i + 5] for i in range(n)]


def grad_kernel(n, skip, s_ref, *refs):
    lefts, rights, refs = refs[:n], refs[n : 2 * n], refs[2 * n + skip :]
    give, keep = refs[:2]
    if n == 1:
        left, right = lefts[0], rights[0]
    else:
        left, right = refs[2:]
        rows = lefts[0].shape[0]
        for i in range(n):
            left[i * rows : (i + 1) * rows, :] = lefts[i][...]
            right[i * rows : (i + 1) * rows, :] = rights[i][...]
    value = dot_tn(left[...], right[...]).astype(BF)

    @pl.when(pl.program_id(0) == 0)
    def _():
        give[0] = value

    @pl.when(pl.program_id(0) == 1)
    def _():
        keep[0] = value


def weight_grad(s, lefts, rights, rows=None, weight=16, stride=1, into=()):
    n = len(lefts)
    t = rows or lefts[0].shape[0]
    width = min(lefts[0].shape[1], rights[0].shape[1])
    high = width // 2
    m, nb = lefts[0].shape[1] // width, rights[0].shape[1] // width
    scratch = []
    if n > 1:
        scratch = [pltpu.VMEM((n * t, high), BF), pltpu.VMEM((n * t, width), BF)]
    left_at = lambda h, i, j, c: (0, jnp.where(h == 0, 1 - c[0], c[0]) * m + i)
    offset = 1 if into else 0

    def place_of(k, c):
        return ((k ^ c[1]) * stride + offset, 0, 0)

    give_at = lambda h, i, j, c: place_of(jnp.where(h == 0, i * nb + j, m * nb - 1), c)
    keep_at = lambda h, i, j, c: place_of(jnp.where(h == 0, 0, i * nb + j), c)
    return pl.pallas_call(
        functools.partial(grad_kernel, n, len(into)),
        grid_spec=pltpu.PrefetchScalarGridSpec(
            num_scalar_prefetch=1,
            grid=(2, m, nb),
            in_specs=[pl.BlockSpec((t, high), left_at)] * n
            + [pl.BlockSpec((t, width), lambda h, i, j, c: (0, j))] * n
            + [HB] * len(into),
            out_specs=[pl.BlockSpec((1, high, width), at) for at in (give_at, keep_at)],
            scratch_shapes=scratch,
        ),
        out_shape=[shape((m * nb * stride, high, width), BF)] * 2,
        input_output_aliases={1 + 2 * n + i: i for i in range(len(into))},
        compiler_params=pltpu.CompilerParams(vmem_limit_bytes=LIMIT),
        cost_estimate=pl.CostEstimate(
            flops=int(weight * 4) * n * t * m * high * width * nb,
            bytes_accessed=int(weight * 2) * (n * t * (2 * m * high + width * nb) + 2 * m * high * width * nb),
            transcendentals=0,
        ),
        name="weight_grad",
    )(s, *lefts, *rights, *into)


def attention_grad_kernel(s_ref, normed, context, dpacked, dattn, give, keep):
    j = pl.program_id(1)

    def write(value):
        @pl.when(pl.program_id(0) == 0)
        def _():
            give[0] = value

        @pl.when(pl.program_id(0) == 1)
        def _():
            keep[0] = value

    @pl.when(j < 3)
    def _():
        write(dot_tn(normed[...], dpacked[...]).astype(BF))

    @pl.when(j == 3)
    def _():
        write(dot_tn(context[...], dattn[...]).astype(BF))


def attention_grad(s, normed, context, dpacked, dattn):
    t, width = normed.shape
    high = width // 2
    half_at = lambda h, j, c: (0, jnp.where(h == 0, 1 - c[0], c[0]))
    return pl.pallas_call(
        attention_grad_kernel,
        grid_spec=pltpu.PrefetchScalarGridSpec(
            num_scalar_prefetch=1,
            grid=(2, 4),
            in_specs=[
                pl.BlockSpec((t, high), half_at),
                pl.BlockSpec((t, high), half_at),
                pl.BlockSpec((t, width), lambda h, j, c: (0, jnp.minimum(j, 2))),
                pl.BlockSpec((t, width), lambda h, j, c: (0, 0)),
            ],
            out_specs=[
                pl.BlockSpec((1, high, width), lambda h, j, c: (jnp.where(h == 0, j, 3), 0, 0)),
                pl.BlockSpec((1, high, width), lambda h, j, c: (jnp.where(h == 0, 0, j), 0, 0)),
            ],
        ),
        out_shape=[shape((4, high, width), BF)] * 2,
        compiler_params=pltpu.CompilerParams(vmem_limit_bytes=LIMIT),
        cost_estimate=pl.CostEstimate(
            flops=t * width * width, bytes_accessed=t * width, transcendentals=0
        ),
        name="attention_grad",
    )(s, normed, context, dpacked, dattn)


def back_kernel(
    experts, cap, dy, dense, hid, gb_ref, router, place, route, live, soft, normed3, slope, fc1, fc2, *refs
):
    homes = refs[:experts]
    dmlp, dpre, dhidden, tiny, drouter = refs[experts : experts + 5]
    w1, w2, ups, sems = refs[experts + 5 :]
    rows, width = hid.shape
    copies = [
        pltpu.make_async_copy(fc1, w1, sems.at[0]),
        pltpu.make_async_copy(fc2, w2, sems.at[1]),
    ]
    for c in copies:
        c.start()
    lanes = -(-cap // WIDE) * WIDE
    spot = iota((lanes, rows), 0)
    spot = jnp.where(spot < cap, spot, -2 * experts * cap)
    dgate = [jnp.zeros((16, rows), F32) for _ in range(TOP)]
    for r in range(experts):
        tail = homes[r][cap : cap + 16, 0:lanes]
        hot = [jnp.where(spot + r * cap == place[k : k + 1, :], 1.0, 0.0).astype(BF) for k in range(TOP)]
        for k in range(TOP):
            dgate[k] = dgate[k] + dot(tail, hot[k])
        term = dot_tn((hot[0] + hot[1])[0:cap, :], homes[r][0:cap, :])
        ups[...] = term if r == 0 else ups[...] + term
    dgate = [jnp.sum(d, axis=0, keepdims=True) * live[...] for d in dgate]
    mix = soft[0:1, :] * dgate[0] + soft[1:2, :] * dgate[1]
    dsoft = [soft[k : k + 1, :] * (dgate[k] - mix) for k in range(TOP)]
    index = iota((router.shape[0], rows), 0)
    dlogits = sum(jnp.where(index == route[k : k + 1, :], dsoft[k], 0.0) for k in range(TOP))
    dlogits = dlogits.astype(BF)
    drouter[...] = dot(dlogits, normed3[...])
    ups[...] += dot_tn(dlogits, router[...])
    tile = rows // 6
    tiny[...] = jnp.zeros_like(tiny)

    def norm_back(at, values, gain, bias_row, base):
        n, scale = normalize(values)
        u = ups[at, :]
        tiny[bias_row - 1 : bias_row, :] += jnp.sum(u * n, axis=0, keepdims=True)
        tiny[bias_row : bias_row + 1, :] += jnp.sum(u, axis=0, keepdims=True)
        ug = u * gain
        dv = scale * (
            ug
            - jnp.mean(ug, axis=-1, keepdims=True)
            - n * jnp.mean(ug * n, axis=-1, keepdims=True)
        )
        return base + dv

    @pl.loop(0, 6)
    def _(i):
        at = pl.ds(pl.multiple_of(i * tile, 16), tile)
        dd = norm_back(at, dense[at, :], gb_ref[4:5, :], 5, dy[at, :].astype(F32))
        dhidden[at, :] = dd
        dmlp[at, :] = dd.astype(BF)

    for c in copies:
        c.wait()
    ups[...] = jnp.zeros_like(ups)

    @pl.loop(0, w1.shape[1] // 512)
    def _(j):
        at = pl.ds(pl.multiple_of(j * 512, 512), 512)
        dpre[:, at] = (dot_nt(dmlp[...], w2[at, :]) * slope[:, at].astype(F32)).astype(BF)
        ups[...] += dot_nt(dpre[:, at], w1[:, at])

    @pl.loop(0, 6)
    def _(i):
        at = pl.ds(pl.multiple_of(i * tile, 16), tile)
        dhidden[at, :] = norm_back(at, hid[at, :], gb_ref[2:3, :], 3, dhidden[at, :])


def back(
    dy, dense, hid, gb, router, place, route, live, soft, normed3, slope, fc1, fc2, homes, experts, cap, after
):
    rows, width = hid.shape
    ff = fc1.shape[1]
    return call(
        functools.partial(back_kernel, experts, cap),
        [VM] * 11 + [HB] * 2 + [VM] * experts,
        [
            shape((rows, width), BF),
            shape((rows, ff), BF),
            shape((rows, width), F32),
            shape((8, width), F32),
            shape(router.shape, F32),
        ],
        [
            pltpu.VMEM((width, ff), BF),
            pltpu.VMEM((ff, width), BF),
            pltpu.VMEM((rows, width), F32),
            pltpu.SemaphoreType.DMA((2,)),
        ],
        4 * rows * width * ff + 2 * rows * width * experts * cap,
        4 * width * ff + rows * (4 * ff + 18 * width),
        "dense_backward",
        after,
    )(dy, dense, hid, gb, router, place, route, live, soft, normed3, slope, fc1, fc2, *homes)


def attend_back_kernel(
    s_ref, dhid, id_row, id_col, packed, lse, wo_a, wo_b, dattn, dpacked, wo, bias, dctx, sems
):
    s = s_ref[0]
    rows, width = dhid.shape
    copies = halves_into(s, wo_a, wo_b, wo, sems, 0)
    for c in copies:
        c.start()
    tile = rows // 6

    @pl.loop(0, 6)
    def _(i):
        at = pl.ds(pl.multiple_of(i * tile, 16), tile)
        dattn[at, :] = dhid[at, :].astype(BF)
        bias[at, :] = jnp.where(id_col[at, :] == id_row[...], 0.0, MASKED)

    copies[0].wait()
    copies[1].wait()

    @pl.loop(0, width // 256)
    def _(j):
        at = pl.ds(pl.multiple_of(j * 256, 256), 256)
        dctx[:, at] = dot_nt(dattn[...], wo[at, :]).astype(BF)

    lane = iota((1, WIDE), 1)

    @pl.loop(0, width // WIDE)
    def _(pair):
        col = pl.multiple_of(pair * WIDE, WIDE)
        q = packed[:, pl.ds(col, WIDE)] * jnp.asarray(HEAD**-0.5, BF)
        keys = packed[:, pl.ds(width + col, WIDE)]
        values = packed[:, pl.ds(2 * width + col, WIDE)]
        dc = dctx[:, pl.ds(col, WIDE)]
        dq, dk, dv = [], [], []
        for h in range(2):
            mine = (lane >= h * HEAD) & (lane < (h + 1) * HEAD)
            scores = dot_nt(jnp.where(mine, keys, jnp.zeros_like(keys)), q) + bias[...]
            p = jnp.exp(scores - lse[pl.ds(2 * pair + h, 1), :])
            dp = dot_nt(jnp.where(mine, values, jnp.zeros_like(values)), dc)
            inner = jnp.sum(p * dp, axis=0, keepdims=True)
            ds = (p * (dp - inner)).astype(BF)
            dv.append(dot(p.astype(BF), dc))
            dk.append(dot(ds, q))
            dq.append(dot_tn(ds, keys) * HEAD**-0.5)
        low = lane < HEAD
        dpacked[:, pl.ds(col, WIDE)] = jnp.where(low, dq[0], dq[1]).astype(BF)
        dpacked[:, pl.ds(width + col, WIDE)] = jnp.where(low, dk[0], dk[1]).astype(BF)
        dpacked[:, pl.ds(2 * width + col, WIDE)] = jnp.where(low, dv[0], dv[1]).astype(BF)


def input_kernel(s_ref, x_ref, dhid, gb_ref, dpacked, qkv_a, qkv_b, grad_in, tiny, wq, ups, sems):
    s = s_ref[0]
    rows, width = x_ref.shape
    tile = rows // 6
    copies = halves_into(s, qkv_a, qkv_b, wq, sems, 0)
    for c in copies:
        c.start()
    copies[0].wait()
    copies[1].wait()

    @pl.loop(0, width // 256)
    def _(j):
        at = pl.ds(pl.multiple_of(j * 256, 256), 256)
        ups[:, at] = dot_nt(dpacked[...], wq[at, :])

    tiny[...] = jnp.zeros_like(tiny)

    @pl.loop(0, 6)
    def _(i):
        at = pl.ds(pl.multiple_of(i * tile, 16), tile)
        n, scale = normalize(x_ref[at, :].astype(F32))
        u = ups[at, :]
        tiny[0:1, :] += jnp.sum(u * n, axis=0, keepdims=True)
        tiny[1:2, :] += jnp.sum(u, axis=0, keepdims=True)
        ug = u * gb_ref[0:1, :]
        grad_in[at, :] = dhid[at, :] + scale * (
            ug
            - jnp.mean(ug, axis=-1, keepdims=True)
            - n * jnp.mean(ug * n, axis=-1, keepdims=True)
        )


def attend_back(s, dhid, ids, packed, lse, wo, after):
    rows, width = dhid.shape
    n3 = packed.shape[1]
    return call(
        attend_back_kernel,
        [SM] + [VM] * 5 + [HB] * 2,
        [shape((rows, width), BF), shape((rows, n3), BF)],
        [
            pltpu.VMEM((width, width), BF),
            pltpu.VMEM((rows, rows), F32),
            pltpu.VMEM((rows, width), BF),
            pltpu.SemaphoreType.DMA((2,)),
        ],
        2 * rows * width * width + 20 * rows * rows * width,
        2 * (width * width + rows * (3 * width + 2 * n3)),
        "attention_backward",
        after,
    )(s, dhid, ids[None, :], ids[:, None], packed, lse, *wo)


def input_back(s, x, dhid, gb, dpacked, qkv, after):
    rows, width = x.shape
    n3 = dpacked.shape[1]
    return call(
        input_kernel,
        [SM] + [VM] * 4 + [HB] * 2,
        [shape((rows, width), F32), shape((8, width), F32)],
        [
            pltpu.VMEM((width, n3), BF),
            pltpu.VMEM((rows, width), F32),
            pltpu.SemaphoreType.DMA((2,)),
        ],
        2 * rows * width * n3,
        2 * (width * n3 + rows * n3) + 10 * rows * width,
        "input_backward",
        after,
    )(s, x, dhid, gb, dpacked, *qkv)


def merge_kernel(experts, cap, dense, place, *refs):
    outs, result = refs[:experts], refs[experts]
    rows = dense.shape[0]
    total = dense[...]
    spot = iota((cap, rows), 0)
    for r in range(experts):
        hot = sum(jnp.where(spot + r * cap == place[k : k + 1, :], 1.0, 0.0) for k in range(TOP))
        total = total + dot_tn(hot.astype(BF), outs[r][...])
    result[...] = total.astype(BF)


def merge(dense, place, outs, experts, cap):
    rows, width = dense.shape
    return call(
        functools.partial(merge_kernel, experts, cap),
        [VM] * (2 + experts),
        shape((rows, width), BF),
        [],
        2 * rows * width * experts * cap,
        rows * width * 6 + 2 * experts * cap * width,
        "merge",
        (),
        0.25,
    )(dense, place, *outs)


def hold_kernel(n, *refs):
    for i in range(n):
        refs[n + i][...] = refs[i][...]


def hold(chunks, after):
    n = len(chunks)
    dims = chunks[0].shape
    return call(
        functools.partial(hold_kernel, n),
        [VM] * n,
        [shape(dims, BF)] * n,
        [],
        0,
        4 * n * dims[0] * dims[1],
        "hold",
        after,
    )(*chunks)


def finish_kernel(columns, m_ref, mine, got, out):
    n, high, width = mine.shape
    for which, src in ((m_ref[0], mine), (1 - m_ref[0], got)):
        for i in range(n):
            value = src[i].astype(F32)
            if columns:
                out[:, pl.ds(pl.multiple_of((which * n + i) * width, width), width)] = value
            else:
                out[pl.ds(pl.multiple_of((which * n + i) * high, high), high), :] = value


def finish(m, mine, got, columns):
    n, high, width = mine.shape
    dims = (high, 2 * n * width) if columns else (2 * n * high, width)
    return call(
        functools.partial(finish_kernel, columns),
        [SM, VM, VM],
        shape(dims, F32),
        [],
        0,
        12 * n * high * width,
        "finish",
    )(m, mine, got)


def spread_kernel(experts, cap, rows_in, place, *chunks):
    spot = iota((cap, rows_in.shape[0]), 0)
    for r in range(experts):
        hot = sum(jnp.where(spot + r * cap == place[k : k + 1, :], 1.0, 0.0) for k in range(TOP))
        chunks[r][...] = dot(hot.astype(BF), rows_in[...]).astype(BF)


def spread(rows_in, place, experts, cap):
    rows, width = rows_in.shape
    return call(
        functools.partial(spread_kernel, experts, cap),
        [VM, VM],
        [shape((cap, width), BF)] * experts,
        [],
        2 * rows * width * experts * cap,
        2 * (rows + experts * cap) * width,
        "spread",
    )(rows_in, place)


def places_of(routes, live, experts, capacity):
    tokens = routes.shape[0]
    ids = jnp.arange(experts, dtype=jnp.int32)
    match = [
        ((routes[:, k : k + 1] == ids[None, :]) & live[:, None]).astype(F32) for k in range(TOP)
    ]
    order = jnp.arange(tokens, dtype=jnp.int32)
    below = (order[:, None] > order[None, :]).astype(BF)
    before = jnp.zeros((1, experts), F32)
    out = []
    for k in range(TOP):
        counts = dot(below, match[k].astype(BF)) + before
        before = before + jnp.sum(match[k], axis=0, keepdims=True)
        within = jnp.sum(counts * match[k], axis=1).astype(jnp.int32)
        out.append(jnp.where(live, routes[:, k] * capacity + within, experts * capacity))
    return out

def local(
    tokens,
    image_ids,
    routes,
    norm1_gain,
    norm1_bias,
    qkv_weight,
    attn_out_weight,
    norm2_gain,
    norm2_bias,
    fc1_weight,
    fc2_weight,
    norm3_gain,
    norm3_bias,
    router_weight,
    expert_up,
    expert_down,
    cotangent,
):
    s = lax.axis_index("section")
    e = lax.axis_index("dp") // GROUP
    q = lax.axis_index("dp") % GROUP
    dp_count = lax.axis_size("dp")
    experts = dp_count // GROUP
    cap = GROUP * ((21 * SLOTS + 10 * experts * GROUP - 1) // (10 * experts * GROUP))
    cap = -(-cap // 16) * 16
    half = tokens.shape[1]
    width = 2 * half
    few = experts <= 8
    planes = [[p * GROUP + i for p in range(experts)] for i in range(GROUP)]
    here, here_q = jnp.stack([s, 0 * s]), jnp.stack([s, q])
    quads = [[p * GROUP + i for i in range(GROUP)] for p in range(experts)]

    def swap(v):
        return lax.ppermute(v, "section", [(0, 1), (1, 0)])

    def over_q(v, bit):
        return lax.ppermute(v, "dp", [(i, i ^ bit) for i in range(dp_count)])

    def over_e(v, r):
        return lax.ppermute(
            v,
            "dp",
            [(i, ((i // GROUP + r) % experts) * GROUP + i % GROUP) for i in range(dp_count)],
        )

    def part(v, index, size, axis=0):
        return lax.dynamic_slice_in_dim(v, index * size, size, axis)

    def join(own, other, axis):
        return jnp.where(
            s == 0,
            jnp.concatenate([own, other], axis=axis),
            jnp.concatenate([other, own], axis=axis),
        )

    def add(a, b):
        return (a.astype(F32) + b.astype(F32)).astype(BF)

    def out_chunks(chunks):
        if not few:
            return list(lax.all_to_all(jnp.stack(chunks), "dp", 0, 0, axis_index_groups=planes))
        return [chunks[0]] + [over_e(chunks[r], r) for r in range(1, experts)]

    def home_chunks(chunks):
        if not few:
            return list(lax.all_to_all(jnp.stack(chunks), "dp", 0, 0, axis_index_groups=planes))
        return [chunks[0]] + [over_e(chunks[r], experts - r) for r in range(1, experts)]

    small = jnp.stack([norm1_gain, norm1_bias, norm2_gain, norm2_bias, norm3_gain, norm3_bias])
    small = jnp.concatenate([small, jnp.transpose(router_weight)])
    small = join(small, swap(small), 1)
    x = join(part(tokens, s, SLOTS), swap(part(tokens, 1 - s, SLOTS)), 1)
    dy = join(part(cotangent, s, SLOTS), swap(part(cotangent, 1 - s, SLOTS)), 1)
    ids = part(image_ids, s, 1).reshape(-1)
    route = part(routes, s, SLOTS)
    live = ids >= 0
    gb = jnp.concatenate([small[:6], jnp.zeros((2, width), BF)]).astype(F32)
    router_rows = -(-experts // 16) * 16
    router = jnp.concatenate([small[6 : 6 + experts], jnp.zeros((router_rows - experts, width), BF)])
    qkv, wo = (qkv_weight, swap(qkv_weight)), (attn_out_weight, swap(attn_out_weight))

    pair = jnp.stack([expert_up, expert_down])

    def gather(v, tiled):
        return lax.all_gather(v, "section", axis=0, tiled=tiled)

    tie = lax.optimization_barrier
    x, dy, qkv, wo, fc1_weight, fc2_weight, pair = tie(
        (x, dy, qkv, wo, fc1_weight, fc2_weight, pair)
    )
    fc1, fc2 = gather(fc1_weight, True), gather(fc2_weight, True)
    from_x, from_y, other_pair = over_q(pair, 1), over_q(pair, 2), swap(pair)

    if few:
        distance = (route - e) % experts
    else:
        distance = route
    spots = places_of(distance, live, experts, cap)
    place = jnp.stack(spots + [jnp.full_like(spots[0], -1)] * 6)
    route_rows = jnp.concatenate([jnp.transpose(route), jnp.full((6, SLOTS), -1, jnp.int32)])
    live_row = live.astype(F32)[None, :]
    dy_sent = spread(dy, place, experts, cap)
    dy_out = out_chunks(dy_sent)

    normed1, packed, context, lse, hidden = front(here, x, ids, gb, qkv, wo, dy_sent[:1])
    hidden, from_x, from_y, other_pair, *dy_out[:-1] = tie(
        (hidden, from_x, from_y, other_pair, *dy_out[:-1])
    )
    other_x, other_y = swap(from_x), swap(from_y)
    far = over_q(from_x, 2)
    normed2, act, slope, dense, normed3, soft, *sent = mlp(
        hidden, gb, router, place, route_rows, live_row, fc1, fc2, experts, cap, []
    )
    sent, other_x, other_y, dy_out[-1] = tie((sent, other_x, other_y, dy_out[-1]))
    got = out_chunks(sent)
    got[0], far = tie((got[0], far))
    own, other = [pair, from_x, from_y, far], [other_pair, other_x, other_y, swap(far)]

    step = max(1, experts // 4)
    results = [None] * experts
    previous, homes = None, [None] * experts
    order = [0, 3, 1, 2] if experts == 4 else list(range(0, experts, step))
    for place_in_order, i in enumerate(order):
        if i:
            got[i], results[previous] = tie((got[i], results[previous]))
        if few and place_in_order == 3:
            got[i], homes[order[1]] = tie((got[i], homes[order[1]]))
        results[i : i + step] = expert(
            here, got[i : i + step], dy_out[i : i + step], own, other, cap
        )
        previous = i
        homes[i] = over_e(results[i][0], experts - i) if few and i else results[i][0]
    if not few:
        homes = home_chunks([r[0] for r in results])
    acts, dinners, scaled = ([r[i] for r in results] for i in (2, 3, 4))

    if experts == 4:
        dinners, homes[1] = tie((dinners, homes[1]))
    up_grads = weight_grad(here_q, got, dinners, cap, stride=2)
    dmlp, dpre, dhidden, tiny23, drouter = back(
        dy, dense, hidden, gb, router, place, route_rows, live_row, soft, normed3, slope,
        fc1, fc2, homes, experts, cap, [],
    )
    outs = hold([r[1] for r in results], [dmlp])
    grads1, grads2 = weight_grad(here, [normed2], [dpre]), weight_grad(here, [act], [dmlp])
    acts, grads1, grads2 = tie((acts, grads1, grads2))
    expert_grads = weight_grad(here_q, scaled, acts, stride=2, into=up_grads)

    def fold(v, bit):
        mine, rows = (q // bit) % 2, v.shape[0] // 2
        return part(v, mine, rows), over_q(part(v, 1 - mine, rows), bit)

    def unfold(v, got, bit):
        return jnp.where(
            (q // bit) % 2 == 0, jnp.concatenate([v, got]), jnp.concatenate([got, v])
        )

    def plane_out(a, b):
        ab = jnp.stack([a, b])
        rows = a.shape[0] // experts
        if not few:
            return [lax.psum(ab, "dp", axis_index_groups=planes)]
        return [part(ab, (e + r) % experts, rows, 1) for r in range(experts)]

    def plane_sum(pieces):
        if not few:
            return pieces
        total = sum(p.astype(F32) for p in pieces).astype(BF)
        return [total] * experts

    def plane_move(pieces):
        return pieces[:1] + [over_e(p, r) for r, p in enumerate(pieces) if r]

    def plane_join(pieces):
        if not few:
            return pieces[0][0], pieces[0][1]
        rows = pieces[0].shape[1]
        whole = jnp.zeros((2, experts * rows, width), BF)
        for r, piece in enumerate(pieces):
            whole = lax.dynamic_update_slice_in_dim(whole, piece, ((e - r) % experts) * rows, 1)
        return whole[0], whole[1]

    away1, away2 = swap(grads1[0]), swap(grads2[0])
    dhidden, away1, away2, grads1, grads2, expert_grads = tie(
        (dhidden, away1, away2, grads1, grads2, expert_grads)
    )
    a, b = add(grads2[1], away2).reshape(-1, width), add(grads1[1], away1).reshape(-1, width)
    a, b = fold(a, 1), fold(b, 2)
    dattn, dpacked = attend_back(here, dhidden, ids, packed, lse, wo, [])
    home_outs = home_chunks(outs)
    give, keep = attention_grad(here, normed1, context, dpacked, dattn)
    give, keep, a, b, dpacked, home_outs = tie((give, keep, a, b, dpacked, home_outs))
    grad_in, tiny1 = input_back(here, x, dhidden, gb, dpacked, qkv, [])
    tiny = jnp.concatenate([tiny1[:2], tiny23[2:6], drouter[:experts]])

    def swapped(v):
        return part(v, s, half, 1), swap(part(v, 1 - s, half, 1))

    away = swap(give)
    a, b = fold(add(*a), 2), fold(add(*b), 1)
    sum_experts = add(expert_grads[1], swap(expert_grads[0]))
    tiny = swapped(tiny)
    away, a, b, grad_in, tiny, sum_experts = tie((away, a, b, grad_in, tiny, sum_experts))
    half_experts = lax.psum_scatter(
        sum_experts.reshape(GROUP, 2, half, -1),
        "dp", scatter_dimension=0, axis_index_groups=quads, tiled=False,
    )
    grad_in = swapped(grad_in)
    tiny = tiny[0] + tiny[1]

    ab = plane_out(add(*a), add(*b))
    keep, away, ab = tie((keep, away, ab))
    ab = plane_move(ab)
    t = add(keep, away).reshape(-1, width)
    ta, tb = fold(t[:width], 1), fold(t[width:], 2)
    ab, ta, tb = tie((ab, ta, tb))
    block_out = merge(dense, place, home_outs, experts, cap)

    ab = plane_sum(ab)
    ta, tb, ab = tie((ta, tb, ab))
    ab = plane_move(ab)
    ta, tb = fold(add(*ta), 2), fold(add(*tb), 1)
    ab, ta, tb, block_out = tie((ab, ta, tb, block_out))

    a, b = plane_join(ab)
    a_got, b_got = over_q(a, 2), over_q(b, 1)
    tab = plane_move(plane_out(add(*ta), add(*tb)))
    a_got, b_got, tab = tie((a_got, b_got, tab))
    a, b = unfold(a, a_got, 2), unfold(b, b_got, 1)
    a_got, b_got = over_q(a, 1), over_q(b, 2)
    tab = plane_move(plane_sum(tab))
    tiny_q = [over_q(tiny, bit) for bit in (1, 2, 3)]
    a_got, b_got, tab, tiny_q = tie((a_got, b_got, tab, tiny_q))

    side_x, side_y = jnp.reshape(q % 2, (1,)), jnp.reshape(q // 2, (1,))

    def blocks(v):
        return v.reshape(-1, half, width)

    ta, tb = plane_join(tab)
    ta_got, tb_got = over_q(ta, 2), over_q(tb, 1)
    block_out = swapped(block_out)
    tiny = tiny + tiny_q[0] + (tiny_q[1] + tiny_q[2])
    if few:
        tiny = [over_e(tiny, r) if r else tiny for r in range(experts)]
    else:
        tiny = [lax.psum(tiny, "dp", axis_index_groups=planes)]
    sum_fc2 = finish(side_x, blocks(a), blocks(a_got), False)
    sum_fc1 = finish(side_y, blocks(b), blocks(b_got), True)
    ta_got, tb_got, tiny, sum_fc2, sum_fc1, half_experts = tie(
        (ta_got, tb_got, tiny, sum_fc2, sum_fc1, half_experts)
    )
    half_up, half_down = half_experts[0].astype(F32), half_experts[1].astype(F32)
    ta, tb = unfold(ta, ta_got, 2), unfold(tb, tb_got, 1)
    ta_got, tb_got = over_q(ta, 1), over_q(tb, 2)
    total = sum(tiny)
    q_and_k = finish(side_x, blocks(ta), blocks(ta_got), True)
    first = q // 2 == 0
    v_sum, sum_attn = (
        jnp.where(first, p, r).astype(F32) for p, r in ((tb, tb_got), (tb_got, tb))
    )
    sum_qkv = jnp.concatenate([q_and_k, v_sum], axis=1)
    return (
        join(*block_out, 0),
        join(*grad_in, 0),
        total[0],
        total[1],
        sum_qkv,
        sum_attn,
        total[2],
        total[3],
        sum_fc1,
        sum_fc2,
        total[4],
        total[5],
        jnp.transpose(total[6:]),
        half_up,
        half_down,
    )


def solution(mesh):
    placed = (
        P("dp", "section"),
        P("dp", None),
        P("dp", None),
        P("section"),
        P("section"),
        P("section", None),
        P("section", None),
        P("section"),
        P("section"),
        P("section", None),
        P("section", None),
        P("section"),
        P("section"),
        P("section", None),
        P("section", "dp"),
        P("section", "dp"),
        P("dp", "section"),
    )
    return jax.shard_map(
        local,
        mesh=mesh,
        in_specs=placed,
        out_specs=(
            P("dp", "section"),
            P("dp", "section"),
            P("section"),
            P("section"),
            P("section", None),
            P("section", None),
            P("section"),
            P("section"),
            P("section", None),
            P("section", None),
            P("section"),
            P("section"),
            P("section", None),
            P("section", "dp"),
            P("section", "dp"),
        ),
        check_vma=False,
    )
```

```python
import functools

import jax
import jax.numpy as jnp
from jax import lax
from jax.experimental import pallas as pl
from jax.experimental.pallas import tpu as pltpu
from jax.sharding import PartitionSpec as P

HEAD = 64
TOP = 2
GROUP = 4
SLOTS = 576
WIDE = 128

EPSILON = 1e-06
MASKED = -1e30
BF = jnp.bfloat16
F32 = jnp.float32
LIMIT = 24 * 1024 * 1024
LIMITS = dict(
    attention_forward=28,
    dense_forward=36,
    expert=28,
    dense_backward=40,
    attention_backward=28,
    input_backward=24,
    merge=20,
    hold=12,
    finish=24,
    spread=16,
)


def dot(a, b):
    return jnp.dot(a, b, preferred_element_type=F32)


def dot_nt(a, b):
    return lax.dot_general(a, b, (((1,), (1,)), ((), ())), preferred_element_type=F32)


def dot_tn(a, b):
    return lax.dot_general(a, b, (((0,), (0,)), ((), ())), preferred_element_type=F32)


def normalize(v):
    center = v - jnp.mean(v, axis=-1, keepdims=True)
    scale = lax.rsqrt(jnp.mean(center * center, axis=-1, keepdims=True) + EPSILON)
    return center * scale, scale


def gelu_pair(x):
    bell = jnp.exp(x * x * -0.5)
    t = 1.0 / (1.0 + jnp.abs(x) * (0.3275911 * 0.5**0.5))
    tail = (
        t
        * (
            0.127414796
            + t * (-0.142248368 + t * (0.7107068705 + t * (-0.7265760135 + t * 0.5307027145)))
        )
        * bell
    )
    cdf = jnp.where(x >= 0.0, 1.0 - tail, tail)
    return x * cdf, cdf + x * (bell * 0.3989422804014327)


def iota(shape, axis):
    return lax.broadcasted_iota(jnp.int32, shape, axis)


def halves_into(s, own, other, dest, sems, first):
    rows = own.shape[0]
    return [
        pltpu.make_async_copy(own, dest.at[pl.ds(pl.multiple_of(s * rows, rows), rows)], sems.at[first]),
        pltpu.make_async_copy(
            other, dest.at[pl.ds(pl.multiple_of((1 - s) * rows, rows), rows)], sems.at[first + 1]
        ),
    ]


def split3(v):
    hi = v.astype(BF)
    rest = v - hi.astype(F32)
    mid = rest.astype(BF)
    low = (rest - mid.astype(F32)).astype(BF)
    return hi, mid, low


VM = pl.BlockSpec(memory_space=pltpu.VMEM)
SM = pl.BlockSpec(memory_space=pltpu.SMEM)
HB = pl.BlockSpec(memory_space=pl.ANY)


def call(kernel, in_specs, out_shape, scratch, flops, moved, name, after=(), weight=16, flushed=()):
    limit = LIMITS[name] * 1024 * 1024
    count, extra = len(in_specs), len(after)
    single = not isinstance(out_shape, list)
    shapes = [out_shape] if single else out_shape
    total, held = len(shapes), len(flushed)

    def body(*refs):
        inputs, outs = refs[:count], list(refs[count + extra : count + extra + total])
        rest = refs[count + extra + total :]
        if not held:
            kernel(*inputs, *outs, *rest)
            return
        own, (buffers, sems) = rest[: len(rest) - held - 1], (rest[len(rest) - held - 1 : -1], rest[-1])
        copies = {}
        for k, index in enumerate(flushed):
            copies[index] = pltpu.make_async_copy(buffers[k], outs[index], sems.at[k])
            outs[index] = buffers[k]
        kernel(*inputs, *outs, *own, flush=lambda index: copies[index].start())
        for index in flushed:
            copies[index].wait()

    made = pl.pallas_call(
        body,
        in_specs=in_specs + [HB] * extra,
        out_specs=VM
        if single
        else [pl.BlockSpec(memory_space=pltpu.HBM) if i in flushed else VM for i in range(total)],
        out_shape=out_shape
        if not held
        else [pltpu.HBM(v.shape, v.dtype) if i in flushed else v for i, v in enumerate(shapes)],
        scratch_shapes=scratch
        + [pltpu.VMEM(shapes[i].shape, shapes[i].dtype) for i in flushed]
        + ([pltpu.SemaphoreType.DMA((held,))] if held else []),
        compiler_params=pltpu.CompilerParams(vmem_limit_bytes=limit),
        cost_estimate=pl.CostEstimate(
            flops=int(weight * flops), bytes_accessed=int(weight * moved), transcendentals=0
        ),
        name=name,
    )
    return lambda *operands: made(*operands, *after)


def shape(dims, kind):
    return jax.ShapeDtypeStruct(dims, kind)


def front_kernel(
    s_ref, x_ref, id_row, id_col, gb_ref, qkv_a, qkv_b, wo_a, wo_b,
    normed, packed, context, lse, hidden,
    wq, wo, bias, lse_col, sems, flush,
):
    s = s_ref[0]
    rows, width = x_ref.shape
    copies = halves_into(s, qkv_a, qkv_b, wq, sems, 0) + halves_into(s, wo_a, wo_b, wo, sems, 2)
    for c in copies:
        c.start()
    tile = rows // 6

    @pl.loop(0, 6)
    def _(i):
        at = pl.ds(pl.multiple_of(i * tile, 16), tile)
        n, _ = normalize(x_ref[at, :].astype(F32))
        normed[at, :] = (n * gb_ref[0:1, :] + gb_ref[1:2, :]).astype(BF)
        bias[at, :] = jnp.where(id_col[at, :] == id_row[...], 0.0, MASKED)

    copies[0].wait()
    copies[1].wait()

    @pl.loop(0, wq.shape[1] // 256)
    def _(j):
        at = pl.ds(pl.multiple_of(j * 256, 256), 256)
        packed[:, at] = dot(normed[...], wq[:, at]).astype(BF)

    flush(0)
    flush(1)
    lane = iota((1, WIDE), 1)
    lse_col[...] = jnp.zeros_like(lse_col)
    third = rows // 3

    @pl.loop(0, width // WIDE)
    def _(pair):
        col = pl.multiple_of(pair * WIDE, WIDE)
        keys = packed[:, pl.ds(width + col, WIDE)]
        values = packed[:, pl.ds(2 * width + col, WIDE)]
        for r in range(3):
            at = slice(r * third, (r + 1) * third)
            q = packed[at, pl.ds(col, WIDE)] * jnp.asarray(HEAD**-0.5, BF)
            outs = []
            sums = lse_col[at, :]
            for h in range(2):
                mine = (lane >= h * HEAD) & (lane < (h + 1) * HEAD)
                scores = dot_nt(jnp.where(mine, q, jnp.zeros_like(q)), keys) + bias[at, :]
                top = jnp.max(scores, axis=1, keepdims=True)
                p = jnp.exp(scores - top)
                total = jnp.sum(p, axis=1, keepdims=True)
                outs.append(dot(p.astype(BF), values) * (1.0 / total))
                sums = jnp.where(lane == 2 * pair + h, top + jnp.log(total), sums)
            lse_col[at, :] = sums
            context[at, pl.ds(col, WIDE)] = jnp.where(lane < HEAD, outs[0], outs[1]).astype(BF)

    flush(2)
    lse[...] = jnp.transpose(lse_col[...])[0 : lse.shape[0], :]
    copies[2].wait()
    copies[3].wait()

    @pl.loop(0, width // 256)
    def _(j):
        at = pl.ds(pl.multiple_of(j * 256, 256), 256)
        hidden[:, at] = x_ref[:, at].astype(F32) + dot(context[...], wo[:, at])


def front(s, x, ids, gb, qkv, wo, after):
    rows, width = x.shape
    n3 = qkv[0].shape[1]
    return call(
        front_kernel,
        [SM, VM, VM, VM, VM, HB, HB, HB, HB],
        [
            shape((rows, width), BF),
            shape((rows, n3), BF),
            shape((rows, width), BF),
            shape((16, rows), F32),
            shape((rows, width), F32),
        ],
        [
            pltpu.VMEM((width, n3), BF),
            pltpu.VMEM((width, width), BF),
            pltpu.VMEM((rows, rows), F32),
            pltpu.VMEM((rows, WIDE), F32),
            pltpu.SemaphoreType.DMA((4,)),
        ],
        2 * rows * width * (n3 + width) + 4 * rows * rows * width,
        2 * (width * (n3 + width) + rows * (3 * width + n3)) + 4 * rows * width,
        "attention_forward",
        after,
        flushed=(0, 1, 2),
    )(s, x, ids[None, :], ids[:, None], gb, *qkv, *wo)


def mlp_kernel(experts, cap, hid, gb_ref, router, place, route, live, fc1, fc2, *refs, flush):
    normed2, act, slope, dense, normed3, soft = refs[:6]
    chunks = refs[6 : 6 + experts]
    w1, w2, sems = refs[6 + experts :]
    rows, width = hid.shape
    copies = [
        pltpu.make_async_copy(fc1, w1, sems.at[0]),
        pltpu.make_async_copy(fc2, w2, sems.at[1]),
    ]
    for c in copies:
        c.start()
    tile = rows // 6

    @pl.loop(0, 6)
    def _(i):
        at = pl.ds(pl.multiple_of(i * tile, 16), tile)
        n, _ = normalize(hid[at, :])
        normed2[at, :] = (n * gb_ref[2:3, :] + gb_ref[3:4, :]).astype(BF)
        dense[at, :] = hid[at, :]

    flush(0)
    for c in copies:
        c.wait()

    @pl.loop(0, w1.shape[1] // 512)
    def _(j):
        at = pl.ds(pl.multiple_of(j * 512, 512), 512)
        a, sl = gelu_pair(dot(normed2[...], w1[:, at]))
        act[:, at] = a.astype(BF)
        slope[:, at] = sl.astype(BF)
        dense[...] += dot(act[:, at], w2[at, :])

    flush(1)
    flush(2)
    flush(3)

    @pl.loop(0, 6)
    def _(i):
        at = pl.ds(pl.multiple_of(i * tile, 16), tile)
        n, _ = normalize(dense[at, :])
        normed3[at, :] = (n * gb_ref[4:5, :] + gb_ref[5:6, :]).astype(BF)

    flush(4)
    logits = dot_nt(router[...], normed3[...])
    expert = iota(logits.shape, 0)
    chosen = [
        jnp.sum(jnp.where(expert == route[k : k + 1, :], logits, 0.0), axis=0, keepdims=True)
        for k in range(TOP)
    ]
    top = jnp.maximum(chosen[0], chosen[1])
    raised = [jnp.exp(c - top) for c in chosen]
    total = raised[0] + raised[1]
    pieces = []
    for k in range(TOP):
        share = raised[k] / total
        soft[k : k + 1, :] = share
        three = split3(share * live[...])
        row = iota((16, rows), 0)
        pieces.append(
            jnp.where(row == 0, three[0].astype(F32), 0.0)
            + jnp.where(row == 1, three[1].astype(F32), 0.0)
            + jnp.where(row == 2, three[2].astype(F32), 0.0)
        )
    pieces = [p.astype(BF) for p in pieces]
    lanes = -(-cap // WIDE) * WIDE
    spot = iota((lanes, rows), 0)
    spot = jnp.where(spot < cap, spot, -2 * experts * cap)
    for r in range(experts):
        hot = [jnp.where(spot + r * cap == place[k : k + 1, :], 1.0, 0.0).astype(BF) for k in range(TOP)]
        both = (hot[0] + hot[1])[0:cap, :]
        chunks[r][0:cap, :] = dot(both, normed3[...]).astype(BF)
        chunks[r][cap : cap + 16, :] = jnp.zeros((16, width), BF)
        chunks[r][cap : cap + 16, 0:lanes] = (
            dot_nt(pieces[0], hot[0]) + dot_nt(pieces[1], hot[1])
        ).astype(BF)
        if r:
            flush(6 + r)


def mlp(hid, gb, router, place, route, live, fc1, fc2, experts, cap, after):
    rows, width = hid.shape
    ff = fc1.shape[1]
    return call(
        functools.partial(mlp_kernel, experts, cap),
        [VM, VM, VM, VM, VM, VM, HB, HB],
        [
            shape((rows, width), BF),
            shape((rows, ff), BF),
            shape((rows, ff), BF),
            shape((rows, width), F32),
            shape((rows, width), BF),
            shape((8, rows), F32),
        ]
        + [shape((cap + 16, width), BF)] * experts,
        [
            pltpu.VMEM((width, ff), BF),
            pltpu.VMEM((ff, width), BF),
            pltpu.SemaphoreType.DMA((2,)),
        ],
        4 * rows * width * ff + 2 * rows * width * experts * cap,
        4 * width * ff + rows * (4 * ff + 12 * width),
        "dense_forward",
        after,
        flushed=(0, 1, 2, 3, 4) + tuple(range(7, 6 + experts)),
    )(hid, gb, router, place, route, live, fc1, fc2)


def expert_kernel(cap, n, s_ref, *refs, flush):
    rows_in, dys = refs[:n], refs[n : 2 * n]
    own, other = refs[2 * n : 2 * n + GROUP], refs[2 * n + GROUP : 2 * n + 2 * GROUP]
    outs = refs[2 * n + 2 * GROUP : -3]
    wu, wd, sems = refs[-3:]
    s = s_ref[0]
    width = wu.shape[1]
    half = width // 2
    copies = [
        [
            pltpu.make_async_copy(
                src[b].at[u],
                w.at[b, pl.ds(pl.multiple_of(side * half, half), half)],
                sems.at[4 * b + 2 * h + u],
            )
            for h, (side, src) in enumerate(((s, own), (1 - s, other)))
            for u, w in enumerate((wu, wd))
        ]
        for b in range(GROUP)
    ]
    for b in range(GROUP):
        for c in copies[b]:
            c.start()
    lanes = -(-cap // WIDE) * WIDE
    eye = iota((lanes, lanes), 0) == iota((lanes, lanes), 1)
    gates = []
    for i in range(n):
        back, out, act, dinner, gp = outs[5 * i : 5 * i + 5]
        g = jnp.sum(rows_in[i][cap : cap + 16, 0:lanes].astype(F32), axis=0, keepdims=True)
        gate = jnp.sum(jnp.where(eye, g, 0.0), axis=1, keepdims=True)[0:cap, :]
        gp[...] = (gate * dys[i][...].astype(F32)).astype(BF)
        gates.append(gate)
    sums = [None] * n
    backs = [None] * n
    for b in range(GROUP):
        for c in copies[b]:
            c.wait()
        at = slice(b * width, (b + 1) * width)
        for i in range(n):
            back, out, act, dinner, gp = outs[5 * i : 5 * i + 5]
            a, slope = gelu_pair(dot(rows_in[i][0:cap, :], wu[b]))
            act[:, at] = a.astype(BF)
            dinner[:, at] = (dot(gp[...], wd[b]) * slope).astype(BF)
            o = dot_nt(act[:, at], wd[b])
            d = dot_nt(dinner[:, at], wu[b])
            sums[i] = o if b == 0 else sums[i] + o
            backs[i] = d if b == 0 else backs[i] + d
    for i in range(n):
        back, out, act, dinner, gp = outs[5 * i : 5 * i + 5]
        out[...] = (gates[i] * sums[i]).astype(BF)
        flush(5 * i + 1)
        back[0:cap, :] = backs[i].astype(BF)
        dg = jnp.sum(dys[i][...].astype(F32) * sums[i], axis=1, keepdims=True)
        pad = jnp.where(eye[0:cap, :], dg, 0.0)
        dg_row = jnp.sum(pad, axis=0, keepdims=True)
        three = split3(dg_row)
        row = iota((16, lanes), 0)
        back[cap : cap + 16, :] = jnp.zeros((16, width), BF)
        back[cap : cap + 16, 0:lanes] = (
            jnp.where(row == 0, three[0].astype(F32), 0.0)
            + jnp.where(row == 1, three[1].astype(F32), 0.0)
            + jnp.where(row == 2, three[2].astype(F32), 0.0)
        ).astype(BF)
        flush(5 * i)


def expert(s, rows_in, dys, own, other, cap):
    n = len(rows_in)
    width = rows_in[0].shape[1]
    ff = GROUP * width
    res = call(
        functools.partial(expert_kernel, cap, n),
        [SM] + [VM] * (2 * n) + [HB] * (2 * GROUP),
        [
            shape((cap + 16, width), BF),
            shape((cap, width), BF),
            shape((cap, ff), BF),
            shape((cap, ff), BF),
            shape((cap, width), BF),
        ]
        * n,
        [
            pltpu.VMEM((GROUP, width, width), BF),
            pltpu.VMEM((GROUP, width, width), BF),
            pltpu.SemaphoreType.DMA((16,)),
        ],
        8 * n * cap * width * ff,
        4 * width * ff + n * cap * (4 * ff + 10 * width),
        "expert",
        flushed=tuple(range(0, 5 * n, 5)) + tuple(range(1, 5 * n, 5)),
    )(s, *rows_in, *dys, *own, *other)
    return [res[5 * i : 5 * i + 5] for i in range(n)]


def grad_kernel(n, skip, s_ref, *refs):
    lefts, rights, refs = refs[:n], refs[n : 2 * n], refs[2 * n + skip :]
    give, keep = refs[:2]
    if n == 1:
        left, right = lefts[0], rights[0]
    else:
        left, right = refs[2:]
        rows = lefts[0].shape[0]
        for i in range(n):
            left[i * rows : (i + 1) * rows, :] = lefts[i][...]
            right[i * rows : (i + 1) * rows, :] = rights[i][...]
    value = dot_tn(left[...], right[...]).astype(BF)

    @pl.when(pl.program_id(0) == 0)
    def _():
        give[0] = value

    @pl.when(pl.program_id(0) == 1)
    def _():
        keep[0] = value


def weight_grad(s, lefts, rights, rows=None, weight=16, stride=1, into=()):
    n = len(lefts)
    t = rows or lefts[0].shape[0]
    width = min(lefts[0].shape[1], rights[0].shape[1])
    high = width // 2
    m, nb = lefts[0].shape[1] // width, rights[0].shape[1] // width
    scratch = []
    if n > 1:
        scratch = [pltpu.VMEM((n * t, high), BF), pltpu.VMEM((n * t, width), BF)]
    left_at = lambda h, i, j, c: (0, jnp.where(h == 0, 1 - c[0], c[0]) * m + i)
    offset = 1 if into else 0

    def place_of(k, c):
        return ((k ^ c[1]) * stride + offset, 0, 0)

    give_at = lambda h, i, j, c: place_of(jnp.where(h == 0, i * nb + j, m * nb - 1), c)
    keep_at = lambda h, i, j, c: place_of(jnp.where(h == 0, 0, i * nb + j), c)
    return pl.pallas_call(
        functools.partial(grad_kernel, n, len(into)),
        grid_spec=pltpu.PrefetchScalarGridSpec(
            num_scalar_prefetch=1,
            grid=(2, m, nb),
            in_specs=[pl.BlockSpec((t, high), left_at)] * n
            + [pl.BlockSpec((t, width), lambda h, i, j, c: (0, j))] * n
            + [HB] * len(into),
            out_specs=[pl.BlockSpec((1, high, width), at) for at in (give_at, keep_at)],
            scratch_shapes=scratch,
        ),
        out_shape=[shape((m * nb * stride, high, width), BF)] * 2,
        input_output_aliases={1 + 2 * n + i: i for i in range(len(into))},
        compiler_params=pltpu.CompilerParams(vmem_limit_bytes=LIMIT),
        cost_estimate=pl.CostEstimate(
            flops=int(weight * 4) * n * t * m * high * width * nb,
            bytes_accessed=int(weight * 2) * (n * t * (2 * m * high + width * nb) + 2 * m * high * width * nb),
            transcendentals=0,
        ),
        name="weight_grad",
    )(s, *lefts, *rights, *into)


def attention_grad_kernel(s_ref, normed, context, dpacked, dattn, give, keep):
    j = pl.program_id(1)

    def write(value):
        @pl.when(pl.program_id(0) == 0)
        def _():
            give[0] = value

        @pl.when(pl.program_id(0) == 1)
        def _():
            keep[0] = value

    @pl.when(j < 3)
    def _():
        write(dot_tn(normed[...], dpacked[...]).astype(BF))

    @pl.when(j == 3)
    def _():
        write(dot_tn(context[...], dattn[...]).astype(BF))


def attention_grad(s, normed, context, dpacked, dattn):
    t, width = normed.shape
    high = width // 2
    half_at = lambda h, j, c: (0, jnp.where(h == 0, 1 - c[0], c[0]))
    return pl.pallas_call(
        attention_grad_kernel,
        grid_spec=pltpu.PrefetchScalarGridSpec(
            num_scalar_prefetch=1,
            grid=(2, 4),
            in_specs=[
                pl.BlockSpec((t, high), half_at),
                pl.BlockSpec((t, high), half_at),
                pl.BlockSpec((t, width), lambda h, j, c: (0, jnp.minimum(j, 2))),
                pl.BlockSpec((t, width), lambda h, j, c: (0, 0)),
            ],
            out_specs=[
                pl.BlockSpec((1, high, width), lambda h, j, c: (jnp.where(h == 0, j, 3), 0, 0)),
                pl.BlockSpec((1, high, width), lambda h, j, c: (jnp.where(h == 0, 0, j), 0, 0)),
            ],
        ),
        out_shape=[shape((4, high, width), BF)] * 2,
        compiler_params=pltpu.CompilerParams(vmem_limit_bytes=LIMIT),
        cost_estimate=pl.CostEstimate(
            flops=t * width * width, bytes_accessed=t * width, transcendentals=0
        ),
        name="attention_grad",
    )(s, normed, context, dpacked, dattn)


def back_kernel(
    experts, cap, dy, dense, hid, gb_ref, router, place, route, live, soft, normed3, slope, fc1, fc2, *refs
):
    homes = refs[:experts]
    dmlp, dpre, dhidden, tiny, drouter = refs[experts : experts + 5]
    w1, w2, ups, sems = refs[experts + 5 :]
    rows, width = hid.shape
    copies = [
        pltpu.make_async_copy(fc1, w1, sems.at[0]),
        pltpu.make_async_copy(fc2, w2, sems.at[1]),
    ]
    for c in copies:
        c.start()
    lanes = -(-cap // WIDE) * WIDE
    spot = iota((lanes, rows), 0)
    spot = jnp.where(spot < cap, spot, -2 * experts * cap)
    dgate = [jnp.zeros((16, rows), F32) for _ in range(TOP)]
    for r in range(experts):
        tail = homes[r][cap : cap + 16, 0:lanes]
        hot = [jnp.where(spot + r * cap == place[k : k + 1, :], 1.0, 0.0).astype(BF) for k in range(TOP)]
        for k in range(TOP):
            dgate[k] = dgate[k] + dot(tail, hot[k])
        term = dot_tn((hot[0] + hot[1])[0:cap, :], homes[r][0:cap, :])
        ups[...] = term if r == 0 else ups[...] + term
    dgate = [jnp.sum(d, axis=0, keepdims=True) * live[...] for d in dgate]
    mix = soft[0:1, :] * dgate[0] + soft[1:2, :] * dgate[1]
    dsoft = [soft[k : k + 1, :] * (dgate[k] - mix) for k in range(TOP)]
    index = iota((router.shape[0], rows), 0)
    dlogits = sum(jnp.where(index == route[k : k + 1, :], dsoft[k], 0.0) for k in range(TOP))
    dlogits = dlogits.astype(BF)
    drouter[...] = dot(dlogits, normed3[...])
    ups[...] += dot_tn(dlogits, router[...])
    tile = rows // 6
    tiny[...] = jnp.zeros_like(tiny)

    def norm_back(at, values, gain, bias_row, base):
        n, scale = normalize(values)
        u = ups[at, :]
        tiny[bias_row - 1 : bias_row, :] += jnp.sum(u * n, axis=0, keepdims=True)
        tiny[bias_row : bias_row + 1, :] += jnp.sum(u, axis=0, keepdims=True)
        ug = u * gain
        dv = scale * (
            ug
            - jnp.mean(ug, axis=-1, keepdims=True)
            - n * jnp.mean(ug * n, axis=-1, keepdims=True)
        )
        return base + dv

    @pl.loop(0, 6)
    def _(i):
        at = pl.ds(pl.multiple_of(i * tile, 16), tile)
        dd = norm_back(at, dense[at, :], gb_ref[4:5, :], 5, dy[at, :].astype(F32))
        dhidden[at, :] = dd
        dmlp[at, :] = dd.astype(BF)

    for c in copies:
        c.wait()
    ups[...] = jnp.zeros_like(ups)

    @pl.loop(0, w1.shape[1] // 512)
    def _(j):
        at = pl.ds(pl.multiple_of(j * 512, 512), 512)
        dpre[:, at] = (dot_nt(dmlp[...], w2[at, :]) * slope[:, at].astype(F32)).astype(BF)
        ups[...] += dot_nt(dpre[:, at], w1[:, at])

    @pl.loop(0, 6)
    def _(i):
        at = pl.ds(pl.multiple_of(i * tile, 16), tile)
        dhidden[at, :] = norm_back(at, hid[at, :], gb_ref[2:3, :], 3, dhidden[at, :])


def back(
    dy, dense, hid, gb, router, place, route, live, soft, normed3, slope, fc1, fc2, homes, experts, cap, after
):
    rows, width = hid.shape
    ff = fc1.shape[1]
    return call(
        functools.partial(back_kernel, experts, cap),
        [VM] * 11 + [HB] * 2 + [VM] * experts,
        [
            shape((rows, width), BF),
            shape((rows, ff), BF),
            shape((rows, width), F32),
            shape((8, width), F32),
            shape(router.shape, F32),
        ],
        [
            pltpu.VMEM((width, ff), BF),
            pltpu.VMEM((ff, width), BF),
            pltpu.VMEM((rows, width), F32),
            pltpu.SemaphoreType.DMA((2,)),
        ],
        4 * rows * width * ff + 2 * rows * width * experts * cap,
        4 * width * ff + rows * (4 * ff + 18 * width),
        "dense_backward",
        after,
    )(dy, dense, hid, gb, router, place, route, live, soft, normed3, slope, fc1, fc2, *homes)


def attend_back_kernel(
    s_ref, dhid, id_row, id_col, packed, lse, wo_a, wo_b, dattn, dpacked, wo, bias, dctx, sems
):
    s = s_ref[0]
    rows, width = dhid.shape
    copies = halves_into(s, wo_a, wo_b, wo, sems, 0)
    for c in copies:
        c.start()
    tile = rows // 6

    @pl.loop(0, 6)
    def _(i):
        at = pl.ds(pl.multiple_of(i * tile, 16), tile)
        dattn[at, :] = dhid[at, :].astype(BF)
        bias[at, :] = jnp.where(id_col[at, :] == id_row[...], 0.0, MASKED)

    copies[0].wait()
    copies[1].wait()

    @pl.loop(0, width // 256)
    def _(j):
        at = pl.ds(pl.multiple_of(j * 256, 256), 256)
        dctx[:, at] = dot_nt(dattn[...], wo[at, :]).astype(BF)

    lane = iota((1, WIDE), 1)

    @pl.loop(0, width // WIDE)
    def _(pair):
        col = pl.multiple_of(pair * WIDE, WIDE)
        q = packed[:, pl.ds(col, WIDE)] * jnp.asarray(HEAD**-0.5, BF)
        keys = packed[:, pl.ds(width + col, WIDE)]
        values = packed[:, pl.ds(2 * width + col, WIDE)]
        dc = dctx[:, pl.ds(col, WIDE)]
        dq, dk, dv = [], [], []
        for h in range(2):
            mine = (lane >= h * HEAD) & (lane < (h + 1) * HEAD)
            scores = dot_nt(jnp.where(mine, keys, jnp.zeros_like(keys)), q) + bias[...]
            p = jnp.exp(scores - lse[pl.ds(2 * pair + h, 1), :])
            dp = dot_nt(jnp.where(mine, values, jnp.zeros_like(values)), dc)
            inner = jnp.sum(p * dp, axis=0, keepdims=True)
            ds = (p * (dp - inner)).astype(BF)
            dv.append(dot(p.astype(BF), dc))
            dk.append(dot(ds, q))
            dq.append(dot_tn(ds, keys) * HEAD**-0.5)
        low = lane < HEAD
        dpacked[:, pl.ds(col, WIDE)] = jnp.where(low, dq[0], dq[1]).astype(BF)
        dpacked[:, pl.ds(width + col, WIDE)] = jnp.where(low, dk[0], dk[1]).astype(BF)
        dpacked[:, pl.ds(2 * width + col, WIDE)] = jnp.where(low, dv[0], dv[1]).astype(BF)


def input_kernel(s_ref, x_ref, dhid, gb_ref, dpacked, qkv_a, qkv_b, grad_in, tiny, wq, ups, sems):
    s = s_ref[0]
    rows, width = x_ref.shape
    tile = rows // 6
    copies = halves_into(s, qkv_a, qkv_b, wq, sems, 0)
    for c in copies:
        c.start()
    copies[0].wait()
    copies[1].wait()

    @pl.loop(0, width // 256)
    def _(j):
        at = pl.ds(pl.multiple_of(j * 256, 256), 256)
        ups[:, at] = dot_nt(dpacked[...], wq[at, :])

    tiny[...] = jnp.zeros_like(tiny)

    @pl.loop(0, 6)
    def _(i):
        at = pl.ds(pl.multiple_of(i * tile, 16), tile)
        n, scale = normalize(x_ref[at, :].astype(F32))
        u = ups[at, :]
        tiny[0:1, :] += jnp.sum(u * n, axis=0, keepdims=True)
        tiny[1:2, :] += jnp.sum(u, axis=0, keepdims=True)
        ug = u * gb_ref[0:1, :]
        grad_in[at, :] = dhid[at, :] + scale * (
            ug
            - jnp.mean(ug, axis=-1, keepdims=True)
            - n * jnp.mean(ug * n, axis=-1, keepdims=True)
        )


def attend_back(s, dhid, ids, packed, lse, wo, after):
    rows, width = dhid.shape
    n3 = packed.shape[1]
    return call(
        attend_back_kernel,
        [SM] + [VM] * 5 + [HB] * 2,
        [shape((rows, width), BF), shape((rows, n3), BF)],
        [
            pltpu.VMEM((width, width), BF),
            pltpu.VMEM((rows, rows), F32),
            pltpu.VMEM((rows, width), BF),
            pltpu.SemaphoreType.DMA((2,)),
        ],
        2 * rows * width * width + 20 * rows * rows * width,
        2 * (width * width + rows * (3 * width + 2 * n3)),
        "attention_backward",
        after,
    )(s, dhid, ids[None, :], ids[:, None], packed, lse, *wo)


def input_back(s, x, dhid, gb, dpacked, qkv, after):
    rows, width = x.shape
    n3 = dpacked.shape[1]
    return call(
        input_kernel,
        [SM] + [VM] * 4 + [HB] * 2,
        [shape((rows, width), F32), shape((8, width), F32)],
        [
            pltpu.VMEM((width, n3), BF),
            pltpu.VMEM((rows, width), F32),
            pltpu.SemaphoreType.DMA((2,)),
        ],
        2 * rows * width * n3,
        2 * (width * n3 + rows * n3) + 10 * rows * width,
        "input_backward",
        after,
    )(s, x, dhid, gb, dpacked, *qkv)


def merge_kernel(experts, cap, dense, place, *refs):
    outs, result = refs[:experts], refs[experts]
    rows = dense.shape[0]
    total = dense[...]
    spot = iota((cap, rows), 0)
    for r in range(experts):
        hot = sum(jnp.where(spot + r * cap == place[k : k + 1, :], 1.0, 0.0) for k in range(TOP))
        total = total + dot_tn(hot.astype(BF), outs[r][...])
    result[...] = total.astype(BF)


def merge(dense, place, outs, experts, cap):
    rows, width = dense.shape
    return call(
        functools.partial(merge_kernel, experts, cap),
        [VM] * (2 + experts),
        shape((rows, width), BF),
        [],
        2 * rows * width * experts * cap,
        rows * width * 6 + 2 * experts * cap * width,
        "merge",
        (),
        0.25,
    )(dense, place, *outs)


def hold_kernel(n, *refs):
    for i in range(n):
        refs[n + i][...] = refs[i][...]


def hold(chunks, after):
    n = len(chunks)
    dims = chunks[0].shape
    return call(
        functools.partial(hold_kernel, n),
        [VM] * n,
        [shape(dims, BF)] * n,
        [],
        0,
        4 * n * dims[0] * dims[1],
        "hold",
        after,
    )(*chunks)


def finish_kernel(columns, m_ref, mine, got, out):
    n, high, width = mine.shape
    for which, src in ((m_ref[0], mine), (1 - m_ref[0], got)):
        for i in range(n):
            value = src[i].astype(F32)
            if columns:
                out[:, pl.ds(pl.multiple_of((which * n + i) * width, width), width)] = value
            else:
                out[pl.ds(pl.multiple_of((which * n + i) * high, high), high), :] = value


def finish(m, mine, got, columns):
    n, high, width = mine.shape
    dims = (high, 2 * n * width) if columns else (2 * n * high, width)
    return call(
        functools.partial(finish_kernel, columns),
        [SM, VM, VM],
        shape(dims, F32),
        [],
        0,
        12 * n * high * width,
        "finish",
    )(m, mine, got)


def spread_kernel(experts, cap, rows_in, place, *chunks):
    spot = iota((cap, rows_in.shape[0]), 0)
    for r in range(experts):
        hot = sum(jnp.where(spot + r * cap == place[k : k + 1, :], 1.0, 0.0) for k in range(TOP))
        chunks[r][...] = dot(hot.astype(BF), rows_in[...]).astype(BF)


def spread(rows_in, place, experts, cap):
    rows, width = rows_in.shape
    return call(
        functools.partial(spread_kernel, experts, cap),
        [VM, VM],
        [shape((cap, width), BF)] * experts,
        [],
        2 * rows * width * experts * cap,
        2 * (rows + experts * cap) * width,
        "spread",
    )(rows_in, place)


def places_of(routes, live, experts, capacity):
    tokens = routes.shape[0]
    ids = jnp.arange(experts, dtype=jnp.int32)
    match = [
        ((routes[:, k : k + 1] == ids[None, :]) & live[:, None]).astype(F32) for k in range(TOP)
    ]
    order = jnp.arange(tokens, dtype=jnp.int32)
    below = (order[:, None] > order[None, :]).astype(BF)
    before = jnp.zeros((1, experts), F32)
    out = []
    for k in range(TOP):
        counts = dot(below, match[k].astype(BF)) + before
        before = before + jnp.sum(match[k], axis=0, keepdims=True)
        within = jnp.sum(counts * match[k], axis=1).astype(jnp.int32)
        out.append(jnp.where(live, routes[:, k] * capacity + within, experts * capacity))
    return out

def local(
    tokens,
    image_ids,
    routes,
    norm1_gain,
    norm1_bias,
    qkv_weight,
    attn_out_weight,
    norm2_gain,
    norm2_bias,
    fc1_weight,
    fc2_weight,
    norm3_gain,
    norm3_bias,
    router_weight,
    expert_up,
    expert_down,
    cotangent,
):
    s = lax.axis_index("section")
    e = lax.axis_index("dp") // GROUP
    q = lax.axis_index("dp") % GROUP
    dp_count = lax.axis_size("dp")
    experts = dp_count // GROUP
    cap = GROUP * ((21 * SLOTS + 10 * experts * GROUP - 1) // (10 * experts * GROUP))
    cap = -(-cap // 16) * 16
    half = tokens.shape[1]
    width = 2 * half
    few = experts <= 8
    planes = [[p * GROUP + i for p in range(experts)] for i in range(GROUP)]
    here, here_q = jnp.stack([s, 0 * s]), jnp.stack([s, q])
    quads = [[p * GROUP + i for i in range(GROUP)] for p in range(experts)]

    def swap(v):
        return lax.ppermute(v, "section", [(0, 1), (1, 0)])

    def over_q(v, bit):
        return lax.ppermute(v, "dp", [(i, i ^ bit) for i in range(dp_count)])

    def over_e(v, r):
        return lax.ppermute(
            v,
            "dp",
            [(i, ((i // GROUP + r) % experts) * GROUP + i % GROUP) for i in range(dp_count)],
        )

    def part(v, index, size, axis=0):
        return lax.dynamic_slice_in_dim(v, index * size, size, axis)

    def join(own, other, axis):
        return jnp.where(
            s == 0,
            jnp.concatenate([own, other], axis=axis),
            jnp.concatenate([other, own], axis=axis),
        )

    def add(a, b):
        return (a.astype(F32) + b.astype(F32)).astype(BF)

    def out_chunks(chunks):
        if not few:
            return list(lax.all_to_all(jnp.stack(chunks), "dp", 0, 0, axis_index_groups=planes))
        return [chunks[0]] + [over_e(chunks[r], r) for r in range(1, experts)]

    def home_chunks(chunks):
        if not few:
            return list(lax.all_to_all(jnp.stack(chunks), "dp", 0, 0, axis_index_groups=planes))
        return [chunks[0]] + [over_e(chunks[r], experts - r) for r in range(1, experts)]

    small = jnp.stack([norm1_gain, norm1_bias, norm2_gain, norm2_bias, norm3_gain, norm3_bias])
    small = jnp.concatenate([small, jnp.transpose(router_weight)])
    small = join(small, swap(small), 1)
    x = join(part(tokens, s, SLOTS), swap(part(tokens, 1 - s, SLOTS)), 1)
    dy = join(part(cotangent, s, SLOTS), swap(part(cotangent, 1 - s, SLOTS)), 1)
    ids = part(image_ids, s, 1).reshape(-1)
    route = part(routes, s, SLOTS)
    live = ids >= 0
    gb = jnp.concatenate([small[:6], jnp.zeros((2, width), BF)]).astype(F32)
    router_rows = -(-experts // 16) * 16
    router = jnp.concatenate([small[6 : 6 + experts], jnp.zeros((router_rows - experts, width), BF)])
    qkv, wo = (qkv_weight, swap(qkv_weight)), (attn_out_weight, swap(attn_out_weight))

    pair = jnp.stack([expert_up, expert_down])

    def gather(v, tiled):
        return lax.all_gather(v, "section", axis=0, tiled=tiled)

    tie = lax.optimization_barrier
    x, dy, qkv, wo, fc1_weight, fc2_weight, pair = tie(
        (x, dy, qkv, wo, fc1_weight, fc2_weight, pair)
    )
    fc1, fc2 = gather(fc1_weight, True), gather(fc2_weight, True)
    from_x, from_y, other_pair = over_q(pair, 1), over_q(pair, 2), swap(pair)

    if few:
        distance = (route - e) % experts
    else:
        distance = route
    spots = places_of(distance, live, experts, cap)
    place = jnp.stack(spots + [jnp.full_like(spots[0], -1)] * 6)
    route_rows = jnp.concatenate([jnp.transpose(route), jnp.full((6, SLOTS), -1, jnp.int32)])
    live_row = live.astype(F32)[None, :]
    dy_sent = spread(dy, place, experts, cap)
    dy_out = out_chunks(dy_sent)

    normed1, packed, context, lse, hidden = front(here, x, ids, gb, qkv, wo, dy_sent[:1])
    hidden, from_x, from_y, other_pair, *dy_out[:-1] = tie(
        (hidden, from_x, from_y, other_pair, *dy_out[:-1])
    )
    other_x, other_y = swap(from_x), swap(from_y)
    far = over_q(from_x, 2)
    normed2, act, slope, dense, normed3, soft, *sent = mlp(
        hidden, gb, router, place, route_rows, live_row, fc1, fc2, experts, cap, []
    )
    sent, other_x, other_y, dy_out[-1] = tie((sent, other_x, other_y, dy_out[-1]))
    got = out_chunks(sent)
    got[0], far = tie((got[0], far))
    own, other = [pair, from_x, from_y, far], [other_pair, other_x, other_y, swap(far)]

    step = max(1, experts // 4)
    results = [None] * experts
    previous, homes = None, [None] * experts
    order = [0, 3, 1, 2] if experts == 4 else list(range(0, experts, step))
    for place_in_order, i in enumerate(order):
        if i:
            got[i], results[previous] = tie((got[i], results[previous]))
        if few and place_in_order == 3:
            got[i], homes[order[1]] = tie((got[i], homes[order[1]]))
        results[i : i + step] = expert(
            here, got[i : i + step], dy_out[i : i + step], own, other, cap
        )
        previous = i
        homes[i] = over_e(results[i][0], experts - i) if few and i else results[i][0]
    if not few:
        homes = home_chunks([r[0] for r in results])
    acts, dinners, scaled = ([r[i] for r in results] for i in (2, 3, 4))

    if experts == 4:
        dinners, homes[1] = tie((dinners, homes[1]))
    up_grads = weight_grad(here_q, got, dinners, cap, stride=2)
    dmlp, dpre, dhidden, tiny23, drouter = back(
        dy, dense, hidden, gb, router, place, route_rows, live_row, soft, normed3, slope,
        fc1, fc2, homes, experts, cap, [],
    )
    outs = hold([r[1] for r in results], [dmlp])
    grads1, grads2 = weight_grad(here, [normed2], [dpre]), weight_grad(here, [act], [dmlp])
    acts, grads1, grads2 = tie((acts, grads1, grads2))
    expert_grads = weight_grad(here_q, scaled, acts, stride=2, into=up_grads)

    def fold(v, bit):
        mine, rows = (q // bit) % 2, v.shape[0] // 2
        return part(v, mine, rows), over_q(part(v, 1 - mine, rows), bit)

    def unfold(v, got, bit):
        return jnp.where(
            (q // bit) % 2 == 0, jnp.concatenate([v, got]), jnp.concatenate([got, v])
        )

    def plane_out(a, b):
        ab = jnp.stack([a, b])
        rows = a.shape[0] // experts
        if not few:
            return [lax.psum(ab, "dp", axis_index_groups=planes)]
        return [part(ab, (e + r) % experts, rows, 1) for r in range(experts)]

    def plane_sum(pieces):
        if not few:
            return pieces
        total = sum(p.astype(F32) for p in pieces).astype(BF)
        return [total] * experts

    def plane_move(pieces):
        return pieces[:1] + [over_e(p, r) for r, p in enumerate(pieces) if r]

    def plane_join(pieces):
        if not few:
            return pieces[0][0], pieces[0][1]
        rows = pieces[0].shape[1]
        whole = jnp.zeros((2, experts * rows, width), BF)
        for r, piece in enumerate(pieces):
            whole = lax.dynamic_update_slice_in_dim(whole, piece, ((e - r) % experts) * rows, 1)
        return whole[0], whole[1]

    away1, away2 = swap(grads1[0]), swap(grads2[0])
    dhidden, away1, away2, grads1, grads2, expert_grads = tie(
        (dhidden, away1, away2, grads1, grads2, expert_grads)
    )
    a, b = add(grads2[1], away2).reshape(-1, width), add(grads1[1], away1).reshape(-1, width)
    a, b = fold(a, 1), fold(b, 2)
    dattn, dpacked = attend_back(here, dhidden, ids, packed, lse, wo, [])
    home_outs = home_chunks(outs)
    give, keep = attention_grad(here, normed1, context, dpacked, dattn)
    give, keep, a, b, dpacked, home_outs = tie((give, keep, a, b, dpacked, home_outs))
    grad_in, tiny1 = input_back(here, x, dhidden, gb, dpacked, qkv, [])
    tiny = jnp.concatenate([tiny1[:2], tiny23[2:6], drouter[:experts]])

    def swapped(v):
        return part(v, s, half, 1), swap(part(v, 1 - s, half, 1))

    away = swap(give)
    a, b = fold(add(*a), 2), fold(add(*b), 1)
    sum_experts = add(expert_grads[1], swap(expert_grads[0]))
    tiny = swapped(tiny)
    away, a, b, grad_in, tiny, sum_experts = tie((away, a, b, grad_in, tiny, sum_experts))
    half_experts = lax.psum_scatter(
        sum_experts.reshape(GROUP, 2, half, -1),
        "dp", scatter_dimension=0, axis_index_groups=quads, tiled=False,
    )
    grad_in = swapped(grad_in)
    tiny = tiny[0] + tiny[1]

    ab = plane_out(add(*a), add(*b))
    keep, away, ab = tie((keep, away, ab))
    ab = plane_move(ab)
    t = add(keep, away).reshape(-1, width)
    ta, tb = fold(t[:width], 1), fold(t[width:], 2)
    ab, ta, tb = tie((ab, ta, tb))
    block_out = merge(dense, place, home_outs, experts, cap)

    ab = plane_sum(ab)
    ta, tb, ab = tie((ta, tb, ab))
    ab = plane_move(ab)
    ta, tb = fold(add(*ta), 2), fold(add(*tb), 1)
    tiny_x = over_q(tiny, 1)
    ab, ta, tb, block_out, tiny_x = tie((ab, ta, tb, block_out, tiny_x))
    tiny = tiny + tiny_x
    tiny_y = over_q(tiny, 2)

    a, b = plane_join(ab)
    a_got, b_got = over_q(a, 2), over_q(b, 1)
    tab = plane_move(plane_out(add(*ta), add(*tb)))
    a_got, b_got, tab, tiny_y = tie((a_got, b_got, tab, tiny_y))
    a, b = unfold(a, a_got, 2), unfold(b, b_got, 1)
    a_got, b_got = over_q(a, 1), over_q(b, 2)
    tab = plane_move(plane_sum(tab))
    a_got, b_got, tab = tie((a_got, b_got, tab))

    side_x, side_y = jnp.reshape(q % 2, (1,)), jnp.reshape(q // 2, (1,))

    def blocks(v):
        return v.reshape(-1, half, width)

    ta, tb = plane_join(tab)
    ta_got, tb_got = over_q(ta, 2), over_q(tb, 1)
    block_out = swapped(block_out)
    tiny = tiny + tiny_y
    if few:
        tiny = [over_e(tiny, r) if r else tiny for r in range(experts)]
    else:
        tiny = [lax.psum(tiny, "dp", axis_index_groups=planes)]
    sum_fc2 = finish(side_x, blocks(a), blocks(a_got), False)
    sum_fc1 = finish(side_y, blocks(b), blocks(b_got), True)
    ta_got, tb_got, tiny, sum_fc2, sum_fc1, half_experts = tie(
        (ta_got, tb_got, tiny, sum_fc2, sum_fc1, half_experts)
    )
    half_up, half_down = half_experts[0].astype(F32), half_experts[1].astype(F32)
    ta, tb = unfold(ta, ta_got, 2), unfold(tb, tb_got, 1)
    ta_got, tb_got = over_q(ta, 1), over_q(tb, 2)
    total = sum(tiny)
    q_and_k = finish(side_x, blocks(ta), blocks(ta_got), True)
    first = q // 2 == 0
    v_sum, sum_attn = (
        jnp.where(first, p, r).astype(F32) for p, r in ((tb, tb_got), (tb_got, tb))
    )
    sum_qkv = jnp.concatenate([q_and_k, v_sum], axis=1)
    return (
        join(*block_out, 0),
        join(*grad_in, 0),
        total[0],
        total[1],
        sum_qkv,
        sum_attn,
        total[2],
        total[3],
        sum_fc1,
        sum_fc2,
        total[4],
        total[5],
        jnp.transpose(total[6:]),
        half_up,
        half_down,
    )


def solution(mesh):
    placed = (
        P("dp", "section"),
        P("dp", None),
        P("dp", None),
        P("section"),
        P("section"),
        P("section", None),
        P("section", None),
        P("section"),
        P("section"),
        P("section", None),
        P("section", None),
        P("section"),
        P("section"),
        P("section", None),
        P("section", "dp"),
        P("section", "dp"),
        P("dp", "section"),
    )
    return jax.shard_map(
        local,
        mesh=mesh,
        in_specs=placed,
        out_specs=(
            P("dp", "section"),
            P("dp", "section"),
            P("section"),
            P("section"),
            P("section", None),
            P("section", None),
            P("section"),
            P("section"),
            P("section", None),
            P("section", None),
            P("section"),
            P("section"),
            P("section", None),
            P("section", "dp"),
            P("section", "dp"),
        ),
        check_vma=False,
    )
```

```python
import functools

import jax
import jax.numpy as jnp
from jax import lax
from jax.experimental import pallas as pl
from jax.experimental.pallas import tpu as pltpu
from jax.sharding import PartitionSpec as P

HEAD = 64
TOP = 2
GROUP = 4
SLOTS = 576
WIDE = 128

EPSILON = 1e-06
MASKED = -1e30
BF = jnp.bfloat16
F32 = jnp.float32
LIMIT = 24 * 1024 * 1024
LIMITS = dict(
    attention_forward=28,
    dense_forward=36,
    expert=28,
    dense_backward=40,
    attention_backward=28,
    input_backward=24,
    merge=20,
    hold=12,
    finish=24,
    spread=16,
)


def dot(a, b):
    return jnp.dot(a, b, preferred_element_type=F32)


def dot_nt(a, b):
    return lax.dot_general(a, b, (((1,), (1,)), ((), ())), preferred_element_type=F32)


def dot_tn(a, b):
    return lax.dot_general(a, b, (((0,), (0,)), ((), ())), preferred_element_type=F32)


def normalize(v):
    center = v - jnp.mean(v, axis=-1, keepdims=True)
    scale = lax.rsqrt(jnp.mean(center * center, axis=-1, keepdims=True) + EPSILON)
    return center * scale, scale


def gelu_pair(x):
    bell = jnp.exp(x * x * -0.5)
    t = 1.0 / (1.0 + jnp.abs(x) * (0.3275911 * 0.5**0.5))
    tail = (
        t
        * (
            0.127414796
            + t * (-0.142248368 + t * (0.7107068705 + t * (-0.7265760135 + t * 0.5307027145)))
        )
        * bell
    )
    cdf = jnp.where(x >= 0.0, 1.0 - tail, tail)
    return x * cdf, cdf + x * (bell * 0.3989422804014327)


def iota(shape, axis):
    return lax.broadcasted_iota(jnp.int32, shape, axis)


def halves_into(s, own, other, dest, sems, first):
    rows = own.shape[0]
    return [
        pltpu.make_async_copy(own, dest.at[pl.ds(pl.multiple_of(s * rows, rows), rows)], sems.at[first]),
        pltpu.make_async_copy(
            other, dest.at[pl.ds(pl.multiple_of((1 - s) * rows, rows), rows)], sems.at[first + 1]
        ),
    ]


def split3(v):
    hi = v.astype(BF)
    rest = v - hi.astype(F32)
    mid = rest.astype(BF)
    low = (rest - mid.astype(F32)).astype(BF)
    return hi, mid, low


VM = pl.BlockSpec(memory_space=pltpu.VMEM)
SM = pl.BlockSpec(memory_space=pltpu.SMEM)
HB = pl.BlockSpec(memory_space=pl.ANY)


def call(kernel, in_specs, out_shape, scratch, flops, moved, name, after=(), weight=16, flushed=()):
    limit = LIMITS[name] * 1024 * 1024
    count, extra = len(in_specs), len(after)
    single = not isinstance(out_shape, list)
    shapes = [out_shape] if single else out_shape
    total, held = len(shapes), len(flushed)

    def body(*refs):
        inputs, outs = refs[:count], list(refs[count + extra : count + extra + total])
        rest = refs[count + extra + total :]
        if not held:
            kernel(*inputs, *outs, *rest)
            return
        own, (buffers, sems) = rest[: len(rest) - held - 1], (rest[len(rest) - held - 1 : -1], rest[-1])
        copies = {}
        for k, index in enumerate(flushed):
            copies[index] = pltpu.make_async_copy(buffers[k], outs[index], sems.at[k])
            outs[index] = buffers[k]
        kernel(*inputs, *outs, *own, flush=lambda index: copies[index].start())
        for index in flushed:
            copies[index].wait()

    made = pl.pallas_call(
        body,
        in_specs=in_specs + [HB] * extra,
        out_specs=VM
        if single
        else [pl.BlockSpec(memory_space=pltpu.HBM) if i in flushed else VM for i in range(total)],
        out_shape=out_shape
        if not held
        else [pltpu.HBM(v.shape, v.dtype) if i in flushed else v for i, v in enumerate(shapes)],
        scratch_shapes=scratch
        + [pltpu.VMEM(shapes[i].shape, shapes[i].dtype) for i in flushed]
        + ([pltpu.SemaphoreType.DMA((held,))] if held else []),
        compiler_params=pltpu.CompilerParams(vmem_limit_bytes=limit),
        cost_estimate=pl.CostEstimate(
            flops=int(weight * flops), bytes_accessed=int(weight * moved), transcendentals=0
        ),
        name=name,
    )
    return lambda *operands: made(*operands, *after)


def shape(dims, kind):
    return jax.ShapeDtypeStruct(dims, kind)


def front_kernel(
    s_ref, x_ref, id_row, id_col, gb_ref, qkv_a, qkv_b, wo_a, wo_b,
    normed, packed, context, lse, hidden,
    wq, wo, bias, lse_col, sems, flush,
):
    s = s_ref[0]
    rows, width = x_ref.shape
    copies = halves_into(s, qkv_a, qkv_b, wq, sems, 0) + halves_into(s, wo_a, wo_b, wo, sems, 2)
    for c in copies:
        c.start()
    tile = rows // 6

    @pl.loop(0, 6)
    def _(i):
        at = pl.ds(pl.multiple_of(i * tile, 16), tile)
        n, _ = normalize(x_ref[at, :].astype(F32))
        normed[at, :] = (n * gb_ref[0:1, :] + gb_ref[1:2, :]).astype(BF)
        bias[at, :] = jnp.where(id_col[at, :] == id_row[...], 0.0, MASKED)

    copies[0].wait()
    copies[1].wait()

    @pl.loop(0, wq.shape[1] // 256)
    def _(j):
        at = pl.ds(pl.multiple_of(j * 256, 256), 256)
        packed[:, at] = dot(normed[...], wq[:, at]).astype(BF)

    flush(0)
    flush(1)
    lane = iota((1, WIDE), 1)
    lse_col[...] = jnp.zeros_like(lse_col)
    third = rows // 3

    @pl.loop(0, width // WIDE)
    def _(pair):
        col = pl.multiple_of(pair * WIDE, WIDE)
        keys = packed[:, pl.ds(width + col, WIDE)]
        values = packed[:, pl.ds(2 * width + col, WIDE)]
        for r in range(3):
            at = slice(r * third, (r + 1) * third)
            q = packed[at, pl.ds(col, WIDE)] * jnp.asarray(HEAD**-0.5, BF)
            outs = []
            sums = lse_col[at, :]
            for h in range(2):
                mine = (lane >= h * HEAD) & (lane < (h + 1) * HEAD)
                scores = dot_nt(jnp.where(mine, q, jnp.zeros_like(q)), keys) + bias[at, :]
                top = jnp.max(scores, axis=1, keepdims=True)
                p = jnp.exp(scores - top)
                total = jnp.sum(p, axis=1, keepdims=True)
                outs.append(dot(p.astype(BF), values) * (1.0 / total))
                sums = jnp.where(lane == 2 * pair + h, top + jnp.log(total), sums)
            lse_col[at, :] = sums
            context[at, pl.ds(col, WIDE)] = jnp.where(lane < HEAD, outs[0], outs[1]).astype(BF)

    flush(2)
    lse[...] = jnp.transpose(lse_col[...])[0 : lse.shape[0], :]
    copies[2].wait()
    copies[3].wait()

    @pl.loop(0, width // 256)
    def _(j):
        at = pl.ds(pl.multiple_of(j * 256, 256), 256)
        hidden[:, at] = x_ref[:, at].astype(F32) + dot(context[...], wo[:, at])


def front(s, x, ids, gb, qkv, wo, after):
    rows, width = x.shape
    n3 = qkv[0].shape[1]
    return call(
        front_kernel,
        [SM, VM, VM, VM, VM, HB, HB, HB, HB],
        [
            shape((rows, width), BF),
            shape((rows, n3), BF),
            shape((rows, width), BF),
            shape((16, rows), F32),
            shape((rows, width), F32),
        ],
        [
            pltpu.VMEM((width, n3), BF),
            pltpu.VMEM((width, width), BF),
            pltpu.VMEM((rows, rows), F32),
            pltpu.VMEM((rows, WIDE), F32),
            pltpu.SemaphoreType.DMA((4,)),
        ],
        2 * rows * width * (n3 + width) + 4 * rows * rows * width,
        2 * (width * (n3 + width) + rows * (3 * width + n3)) + 4 * rows * width,
        "attention_forward",
        after,
        flushed=(0, 1, 2),
    )(s, x, ids[None, :], ids[:, None], gb, *qkv, *wo)


def mlp_kernel(experts, cap, hid, gb_ref, router, place, route, live, fc1, fc2, *refs, flush):
    normed2, act, slope, dense, normed3, soft = refs[:6]
    chunks = refs[6 : 6 + experts]
    w1, w2, sems = refs[6 + experts :]
    rows, width = hid.shape
    copies = [
        pltpu.make_async_copy(fc1, w1, sems.at[0]),
        pltpu.make_async_copy(fc2, w2, sems.at[1]),
    ]
    for c in copies:
        c.start()
    tile = rows // 6

    @pl.loop(0, 6)
    def _(i):
        at = pl.ds(pl.multiple_of(i * tile, 16), tile)
        n, _ = normalize(hid[at, :])
        normed2[at, :] = (n * gb_ref[2:3, :] + gb_ref[3:4, :]).astype(BF)
        dense[at, :] = hid[at, :]

    flush(0)
    for c in copies:
        c.wait()

    @pl.loop(0, w1.shape[1] // 512)
    def _(j):
        at = pl.ds(pl.multiple_of(j * 512, 512), 512)
        a, sl = gelu_pair(dot(normed2[...], w1[:, at]))
        act[:, at] = a.astype(BF)
        slope[:, at] = sl.astype(BF)
        dense[...] += dot(act[:, at], w2[at, :])

    flush(1)
    flush(2)
    flush(3)

    @pl.loop(0, 6)
    def _(i):
        at = pl.ds(pl.multiple_of(i * tile, 16), tile)
        n, _ = normalize(dense[at, :])
        normed3[at, :] = (n * gb_ref[4:5, :] + gb_ref[5:6, :]).astype(BF)

    flush(4)
    logits = dot_nt(router[...], normed3[...])
    expert = iota(logits.shape, 0)
    chosen = [
        jnp.sum(jnp.where(expert == route[k : k + 1, :], logits, 0.0), axis=0, keepdims=True)
        for k in range(TOP)
    ]
    top = jnp.maximum(chosen[0], chosen[1])
    raised = [jnp.exp(c - top) for c in chosen]
    total = raised[0] + raised[1]
    pieces = []
    for k in range(TOP):
        share = raised[k] / total
        soft[k : k + 1, :] = share
        three = split3(share * live[...])
        row = iota((16, rows), 0)
        pieces.append(
            jnp.where(row == 0, three[0].astype(F32), 0.0)
            + jnp.where(row == 1, three[1].astype(F32), 0.0)
            + jnp.where(row == 2, three[2].astype(F32), 0.0)
        )
    pieces = [p.astype(BF) for p in pieces]
    lanes = -(-cap // WIDE) * WIDE
    spot = iota((lanes, rows), 0)
    spot = jnp.where(spot < cap, spot, -2 * experts * cap)
    for r in range(experts):
        hot = [jnp.where(spot + r * cap == place[k : k + 1, :], 1.0, 0.0).astype(BF) for k in range(TOP)]
        both = (hot[0] + hot[1])[0:cap, :]
        chunks[r][0:cap, :] = dot(both, normed3[...]).astype(BF)
        chunks[r][cap : cap + 16, :] = jnp.zeros((16, width), BF)
        chunks[r][cap : cap + 16, 0:lanes] = (
            dot_nt(pieces[0], hot[0]) + dot_nt(pieces[1], hot[1])
        ).astype(BF)
        if r:
            flush(6 + r)


def mlp(hid, gb, router, place, route, live, fc1, fc2, experts, cap, after):
    rows, width = hid.shape
    ff = fc1.shape[1]
    return call(
        functools.partial(mlp_kernel, experts, cap),
        [VM, VM, VM, VM, VM, VM, HB, HB],
        [
            shape((rows, width), BF),
            shape((rows, ff), BF),
            shape((rows, ff), BF),
            shape((rows, width), F32),
            shape((rows, width), BF),
            shape((8, rows), F32),
        ]
        + [shape((cap + 16, width), BF)] * experts,
        [
            pltpu.VMEM((width, ff), BF),
            pltpu.VMEM((ff, width), BF),
            pltpu.SemaphoreType.DMA((2,)),
        ],
        4 * rows * width * ff + 2 * rows * width * experts * cap,
        4 * width * ff + rows * (4 * ff + 12 * width),
        "dense_forward",
        after,
        flushed=(0, 1, 2, 3, 4) + tuple(range(7, 6 + experts)),
    )(hid, gb, router, place, route, live, fc1, fc2)


def expert_kernel(cap, n, s_ref, *refs, flush):
    rows_in, dys = refs[:n], refs[n : 2 * n]
    own, other = refs[2 * n : 2 * n + GROUP], refs[2 * n + GROUP : 2 * n + 2 * GROUP]
    outs = refs[2 * n + 2 * GROUP : -3]
    wu, wd, sems = refs[-3:]
    s = s_ref[0]
    width = wu.shape[1]
    half = width // 2
    copies = [
        [
            pltpu.make_async_copy(
                src[b].at[u],
                w.at[b, pl.ds(pl.multiple_of(side * half, half), half)],
                sems.at[4 * b + 2 * h + u],
            )
            for h, (side, src) in enumerate(((s, own), (1 - s, other)))
            for u, w in enumerate((wu, wd))
        ]
        for b in range(GROUP)
    ]
    for b in range(GROUP):
        for c in copies[b]:
            c.start()
    lanes = -(-cap // WIDE) * WIDE
    eye = iota((lanes, lanes), 0) == iota((lanes, lanes), 1)
    gates = []
    for i in range(n):
        back, out, act, dinner, gp = outs[5 * i : 5 * i + 5]
        g = jnp.sum(rows_in[i][cap : cap + 16, 0:lanes].astype(F32), axis=0, keepdims=True)
        gate = jnp.sum(jnp.where(eye, g, 0.0), axis=1, keepdims=True)[0:cap, :]
        gp[...] = (gate * dys[i][...].astype(F32)).astype(BF)
        gates.append(gate)
    sums = [None] * n
    backs = [None] * n
    for b in range(GROUP):
        for c in copies[b]:
            c.wait()
        at = slice(b * width, (b + 1) * width)
        for i in range(n):
            back, out, act, dinner, gp = outs[5 * i : 5 * i + 5]
            a, slope = gelu_pair(dot(rows_in[i][0:cap, :], wu[b]))
            act[:, at] = a.astype(BF)
            dinner[:, at] = (dot(gp[...], wd[b]) * slope).astype(BF)
            o = dot_nt(act[:, at], wd[b])
            d = dot_nt(dinner[:, at], wu[b])
            sums[i] = o if b == 0 else sums[i] + o
            backs[i] = d if b == 0 else backs[i] + d
    for i in range(n):
        back, out, act, dinner, gp = outs[5 * i : 5 * i + 5]
        out[...] = (gates[i] * sums[i]).astype(BF)
        flush(5 * i + 1)
        back[0:cap, :] = backs[i].astype(BF)
        dg = jnp.sum(dys[i][...].astype(F32) * sums[i], axis=1, keepdims=True)
        pad = jnp.where(eye[0:cap, :], dg, 0.0)
        dg_row = jnp.sum(pad, axis=0, keepdims=True)
        three = split3(dg_row)
        row = iota((16, lanes), 0)
        back[cap : cap + 16, :] = jnp.zeros((16, width), BF)
        back[cap : cap + 16, 0:lanes] = (
            jnp.where(row == 0, three[0].astype(F32), 0.0)
            + jnp.where(row == 1, three[1].astype(F32), 0.0)
            + jnp.where(row == 2, three[2].astype(F32), 0.0)
        ).astype(BF)
        flush(5 * i)


def expert(s, rows_in, dys, own, other, cap):
    n = len(rows_in)
    width = rows_in[0].shape[1]
    ff = GROUP * width
    res = call(
        functools.partial(expert_kernel, cap, n),
        [SM] + [VM] * (2 * n) + [HB] * (2 * GROUP),
        [
            shape((cap + 16, width), BF),
            shape((cap, width), BF),
            shape((cap, ff), BF),
            shape((cap, ff), BF),
            shape((cap, width), BF),
        ]
        * n,
        [
            pltpu.VMEM((GROUP, width, width), BF),
            pltpu.VMEM((GROUP, width, width), BF),
            pltpu.SemaphoreType.DMA((16,)),
        ],
        8 * n * cap * width * ff,
        4 * width * ff + n * cap * (4 * ff + 10 * width),
        "expert",
        flushed=tuple(range(0, 5 * n, 5)) + tuple(range(1, 5 * n, 5)),
    )(s, *rows_in, *dys, *own, *other)
    return [res[5 * i : 5 * i + 5] for i in range(n)]


def grad_kernel(n, skip, s_ref, *refs):
    lefts, rights, refs = refs[:n], refs[n : 2 * n], refs[2 * n + skip :]
    give, keep = refs[:2]
    if n == 1:
        left, right = lefts[0], rights[0]
    else:
        left, right = refs[2:]
        rows = lefts[0].shape[0]
        for i in range(n):
            left[i * rows : (i + 1) * rows, :] = lefts[i][...]
            right[i * rows : (i + 1) * rows, :] = rights[i][...]
    value = dot_tn(left[...], right[...]).astype(BF)

    @pl.when(pl.program_id(0) == 0)
    def _():
        give[0] = value

    @pl.when(pl.program_id(0) == 1)
    def _():
        keep[0] = value


def weight_grad(s, lefts, rights, rows=None, weight=16, stride=1, into=()):
    n = len(lefts)
    t = rows or lefts[0].shape[0]
    width = min(lefts[0].shape[1], rights[0].shape[1])
    high = width // 2
    m, nb = lefts[0].shape[1] // width, rights[0].shape[1] // width
    scratch = []
    if n > 1:
        scratch = [pltpu.VMEM((n * t, high), BF), pltpu.VMEM((n * t, width), BF)]
    left_at = lambda h, i, j, c: (0, jnp.where(h == 0, 1 - c[0], c[0]) * m + i)
    offset = 1 if into else 0

    def place_of(k, c):
        return ((k ^ c[1]) * stride + offset, 0, 0)

    give_at = lambda h, i, j, c: place_of(jnp.where(h == 0, i * nb + j, m * nb - 1), c)
    keep_at = lambda h, i, j, c: place_of(jnp.where(h == 0, 0, i * nb + j), c)
    return pl.pallas_call(
        functools.partial(grad_kernel, n, len(into)),
        grid_spec=pltpu.PrefetchScalarGridSpec(
            num_scalar_prefetch=1,
            grid=(2, m, nb),
            in_specs=[pl.BlockSpec((t, high), left_at)] * n
            + [pl.BlockSpec((t, width), lambda h, i, j, c: (0, j))] * n
            + [HB] * len(into),
            out_specs=[pl.BlockSpec((1, high, width), at) for at in (give_at, keep_at)],
            scratch_shapes=scratch,
        ),
        out_shape=[shape((m * nb * stride, high, width), BF)] * 2,
        input_output_aliases={1 + 2 * n + i: i for i in range(len(into))},
        compiler_params=pltpu.CompilerParams(vmem_limit_bytes=LIMIT),
        cost_estimate=pl.CostEstimate(
            flops=int(weight * 4) * n * t * m * high * width * nb,
            bytes_accessed=int(weight * 2) * (n * t * (2 * m * high + width * nb) + 2 * m * high * width * nb),
            transcendentals=0,
        ),
        name="weight_grad",
    )(s, *lefts, *rights, *into)


def attention_grad_kernel(s_ref, normed, context, dpacked, dattn, give, keep):
    j = pl.program_id(1)

    def write(value):
        @pl.when(pl.program_id(0) == 0)
        def _():
            give[0] = value

        @pl.when(pl.program_id(0) == 1)
        def _():
            keep[0] = value

    @pl.when(j < 3)
    def _():
        write(dot_tn(normed[...], dpacked[...]).astype(BF))

    @pl.when(j == 3)
    def _():
        write(dot_tn(context[...], dattn[...]).astype(BF))


def attention_grad(s, normed, context, dpacked, dattn):
    t, width = normed.shape
    high = width // 2
    half_at = lambda h, j, c: (0, jnp.where(h == 0, 1 - c[0], c[0]))
    return pl.pallas_call(
        attention_grad_kernel,
        grid_spec=pltpu.PrefetchScalarGridSpec(
            num_scalar_prefetch=1,
            grid=(2, 4),
            in_specs=[
                pl.BlockSpec((t, high), half_at),
                pl.BlockSpec((t, high), half_at),
                pl.BlockSpec((t, width), lambda h, j, c: (0, jnp.minimum(j, 2))),
                pl.BlockSpec((t, width), lambda h, j, c: (0, 0)),
            ],
            out_specs=[
                pl.BlockSpec((1, high, width), lambda h, j, c: (jnp.where(h == 0, j, 3), 0, 0)),
                pl.BlockSpec((1, high, width), lambda h, j, c: (jnp.where(h == 0, 0, j), 0, 0)),
            ],
        ),
        out_shape=[shape((4, high, width), BF)] * 2,
        compiler_params=pltpu.CompilerParams(vmem_limit_bytes=LIMIT),
        cost_estimate=pl.CostEstimate(
            flops=t * width * width, bytes_accessed=t * width, transcendentals=0
        ),
        name="attention_grad",
    )(s, normed, context, dpacked, dattn)


def back_kernel(
    experts, cap, dy, dense, hid, gb_ref, router, place, route, live, soft, normed3, slope, fc1, fc2, *refs
):
    homes = refs[:experts]
    dmlp, dpre, dhidden, tiny, drouter = refs[experts : experts + 5]
    w1, w2, ups, sems = refs[experts + 5 :]
    rows, width = hid.shape
    copies = [
        pltpu.make_async_copy(fc1, w1, sems.at[0]),
        pltpu.make_async_copy(fc2, w2, sems.at[1]),
    ]
    for c in copies:
        c.start()
    lanes = -(-cap // WIDE) * WIDE
    spot = iota((lanes, rows), 0)
    spot = jnp.where(spot < cap, spot, -2 * experts * cap)
    dgate = [jnp.zeros((16, rows), F32) for _ in range(TOP)]
    for r in range(experts):
        tail = homes[r][cap : cap + 16, 0:lanes]
        hot = [jnp.where(spot + r * cap == place[k : k + 1, :], 1.0, 0.0).astype(BF) for k in range(TOP)]
        for k in range(TOP):
            dgate[k] = dgate[k] + dot(tail, hot[k])
        term = dot_tn((hot[0] + hot[1])[0:cap, :], homes[r][0:cap, :])
        ups[...] = term if r == 0 else ups[...] + term
    dgate = [jnp.sum(d, axis=0, keepdims=True) * live[...] for d in dgate]
    mix = soft[0:1, :] * dgate[0] + soft[1:2, :] * dgate[1]
    dsoft = [soft[k : k + 1, :] * (dgate[k] - mix) for k in range(TOP)]
    index = iota((router.shape[0], rows), 0)
    dlogits = sum(jnp.where(index == route[k : k + 1, :], dsoft[k], 0.0) for k in range(TOP))
    dlogits = dlogits.astype(BF)
    drouter[...] = dot(dlogits, normed3[...])
    ups[...] += dot_tn(dlogits, router[...])
    tile = rows // 6
    tiny[...] = jnp.zeros_like(tiny)

    def norm_back(at, values, gain, bias_row, base):
        n, scale = normalize(values)
        u = ups[at, :]
        tiny[bias_row - 1 : bias_row, :] += jnp.sum(u * n, axis=0, keepdims=True)
        tiny[bias_row : bias_row + 1, :] += jnp.sum(u, axis=0, keepdims=True)
        ug = u * gain
        dv = scale * (
            ug
            - jnp.mean(ug, axis=-1, keepdims=True)
            - n * jnp.mean(ug * n, axis=-1, keepdims=True)
        )
        return base + dv

    @pl.loop(0, 6)
    def _(i):
        at = pl.ds(pl.multiple_of(i * tile, 16), tile)
        dd = norm_back(at, dense[at, :], gb_ref[4:5, :], 5, dy[at, :].astype(F32))
        dhidden[at, :] = dd
        dmlp[at, :] = dd.astype(BF)

    for c in copies:
        c.wait()
    ups[...] = jnp.zeros_like(ups)

    @pl.loop(0, w1.shape[1] // 512)
    def _(j):
        at = pl.ds(pl.multiple_of(j * 512, 512), 512)
        dpre[:, at] = (dot_nt(dmlp[...], w2[at, :]) * slope[:, at].astype(F32)).astype(BF)
        ups[...] += dot_nt(dpre[:, at], w1[:, at])

    @pl.loop(0, 6)
    def _(i):
        at = pl.ds(pl.multiple_of(i * tile, 16), tile)
        dhidden[at, :] = norm_back(at, hid[at, :], gb_ref[2:3, :], 3, dhidden[at, :])


def back(
    dy, dense, hid, gb, router, place, route, live, soft, normed3, slope, fc1, fc2, homes, experts, cap, after
):
    rows, width = hid.shape
    ff = fc1.shape[1]
    return call(
        functools.partial(back_kernel, experts, cap),
        [VM] * 11 + [HB] * 2 + [VM] * experts,
        [
            shape((rows, width), BF),
            shape((rows, ff), BF),
            shape((rows, width), F32),
            shape((8, width), F32),
            shape(router.shape, F32),
        ],
        [
            pltpu.VMEM((width, ff), BF),
            pltpu.VMEM((ff, width), BF),
            pltpu.VMEM((rows, width), F32),
            pltpu.SemaphoreType.DMA((2,)),
        ],
        4 * rows * width * ff + 2 * rows * width * experts * cap,
        4 * width * ff + rows * (4 * ff + 18 * width),
        "dense_backward",
        after,
    )(dy, dense, hid, gb, router, place, route, live, soft, normed3, slope, fc1, fc2, *homes)


def attend_back_kernel(
    s_ref, dhid, id_row, id_col, packed, lse, wo_a, wo_b, dattn, dpacked, wo, bias, dctx, sems
):
    s = s_ref[0]
    rows, width = dhid.shape
    copies = halves_into(s, wo_a, wo_b, wo, sems, 0)
    for c in copies:
        c.start()
    tile = rows // 6

    @pl.loop(0, 6)
    def _(i):
        at = pl.ds(pl.multiple_of(i * tile, 16), tile)
        dattn[at, :] = dhid[at, :].astype(BF)
        bias[at, :] = jnp.where(id_col[at, :] == id_row[...], 0.0, MASKED)

    copies[0].wait()
    copies[1].wait()

    @pl.loop(0, width // 256)
    def _(j):
        at = pl.ds(pl.multiple_of(j * 256, 256), 256)
        dctx[:, at] = dot_nt(dattn[...], wo[at, :]).astype(BF)

    lane = iota((1, WIDE), 1)

    @pl.loop(0, width // WIDE)
    def _(pair):
        col = pl.multiple_of(pair * WIDE, WIDE)
        q = packed[:, pl.ds(col, WIDE)] * jnp.asarray(HEAD**-0.5, BF)
        keys = packed[:, pl.ds(width + col, WIDE)]
        values = packed[:, pl.ds(2 * width + col, WIDE)]
        dc = dctx[:, pl.ds(col, WIDE)]
        dq, dk, dv = [], [], []
        for h in range(2):
            mine = (lane >= h * HEAD) & (lane < (h + 1) * HEAD)
            scores = dot_nt(jnp.where(mine, keys, jnp.zeros_like(keys)), q) + bias[...]
            p = jnp.exp(scores - lse[pl.ds(2 * pair + h, 1), :])
            dp = dot_nt(jnp.where(mine, values, jnp.zeros_like(values)), dc)
            inner = jnp.sum(p * dp, axis=0, keepdims=True)
            ds = (p * (dp - inner)).astype(BF)
            dv.append(dot(p.astype(BF), dc))
            dk.append(dot(ds, q))
            dq.append(dot_tn(ds, keys) * HEAD**-0.5)
        low = lane < HEAD
        dpacked[:, pl.ds(col, WIDE)] = jnp.where(low, dq[0], dq[1]).astype(BF)
        dpacked[:, pl.ds(width + col, WIDE)] = jnp.where(low, dk[0], dk[1]).astype(BF)
        dpacked[:, pl.ds(2 * width + col, WIDE)] = jnp.where(low, dv[0], dv[1]).astype(BF)


def input_kernel(s_ref, x_ref, dhid, gb_ref, dpacked, qkv_a, qkv_b, grad_in, tiny, wq, ups, sems):
    s = s_ref[0]
    rows, width = x_ref.shape
    tile = rows // 6
    copies = halves_into(s, qkv_a, qkv_b, wq, sems, 0)
    for c in copies:
        c.start()
    copies[0].wait()
    copies[1].wait()

    @pl.loop(0, width // 256)
    def _(j):
        at = pl.ds(pl.multiple_of(j * 256, 256), 256)
        ups[:, at] = dot_nt(dpacked[...], wq[at, :])

    tiny[...] = jnp.zeros_like(tiny)

    @pl.loop(0, 6)
    def _(i):
        at = pl.ds(pl.multiple_of(i * tile, 16), tile)
        n, scale = normalize(x_ref[at, :].astype(F32))
        u = ups[at, :]
        tiny[0:1, :] += jnp.sum(u * n, axis=0, keepdims=True)
        tiny[1:2, :] += jnp.sum(u, axis=0, keepdims=True)
        ug = u * gb_ref[0:1, :]
        grad_in[at, :] = dhid[at, :] + scale * (
            ug
            - jnp.mean(ug, axis=-1, keepdims=True)
            - n * jnp.mean(ug * n, axis=-1, keepdims=True)
        )


def attend_back(s, dhid, ids, packed, lse, wo, after):
    rows, width = dhid.shape
    n3 = packed.shape[1]
    return call(
        attend_back_kernel,
        [SM] + [VM] * 5 + [HB] * 2,
        [shape((rows, width), BF), shape((rows, n3), BF)],
        [
            pltpu.VMEM((width, width), BF),
            pltpu.VMEM((rows, rows), F32),
            pltpu.VMEM((rows, width), BF),
            pltpu.SemaphoreType.DMA((2,)),
        ],
        2 * rows * width * width + 20 * rows * rows * width,
        2 * (width * width + rows * (3 * width + 2 * n3)),
        "attention_backward",
        after,
    )(s, dhid, ids[None, :], ids[:, None], packed, lse, *wo)


def input_back(s, x, dhid, gb, dpacked, qkv, after):
    rows, width = x.shape
    n3 = dpacked.shape[1]
    return call(
        input_kernel,
        [SM] + [VM] * 4 + [HB] * 2,
        [shape((rows, width), F32), shape((8, width), F32)],
        [
            pltpu.VMEM((width, n3), BF),
            pltpu.VMEM((rows, width), F32),
            pltpu.SemaphoreType.DMA((2,)),
        ],
        2 * rows * width * n3,
        2 * (width * n3 + rows * n3) + 10 * rows * width,
        "input_backward",
        after,
    )(s, x, dhid, gb, dpacked, *qkv)


def merge_kernel(experts, cap, dense, place, *refs):
    outs, result = refs[:experts], refs[experts]
    rows = dense.shape[0]
    total = dense[...]
    spot = iota((cap, rows), 0)
    for r in range(experts):
        hot = sum(jnp.where(spot + r * cap == place[k : k + 1, :], 1.0, 0.0) for k in range(TOP))
        total = total + dot_tn(hot.astype(BF), outs[r][...])
    result[...] = total.astype(BF)


def merge(dense, place, outs, experts, cap):
    rows, width = dense.shape
    return call(
        functools.partial(merge_kernel, experts, cap),
        [VM] * (2 + experts),
        shape((rows, width), BF),
        [],
        2 * rows * width * experts * cap,
        rows * width * 6 + 2 * experts * cap * width,
        "merge",
        (),
        0.25,
    )(dense, place, *outs)


def hold_kernel(n, *refs):
    for i in range(n):
        refs[n + i][...] = refs[i][...]


def hold(chunks, after):
    n = len(chunks)
    dims = chunks[0].shape
    return call(
        functools.partial(hold_kernel, n),
        [VM] * n,
        [shape(dims, BF)] * n,
        [],
        0,
        4 * n * dims[0] * dims[1],
        "hold",
        after,
    )(*chunks)


def finish_kernel(columns, m_ref, mine, got, out):
    n, high, width = mine.shape
    for which, src in ((m_ref[0], mine), (1 - m_ref[0], got)):
        for i in range(n):
            value = src[i].astype(F32)
            if columns:
                out[:, pl.ds(pl.multiple_of((which * n + i) * width, width), width)] = value
            else:
                out[pl.ds(pl.multiple_of((which * n + i) * high, high), high), :] = value


def finish(m, mine, got, columns):
    n, high, width = mine.shape
    dims = (high, 2 * n * width) if columns else (2 * n * high, width)
    return call(
        functools.partial(finish_kernel, columns),
        [SM, VM, VM],
        shape(dims, F32),
        [],
        0,
        12 * n * high * width,
        "finish",
    )(m, mine, got)


def spread_kernel(experts, cap, rows_in, place, *chunks):
    spot = iota((cap, rows_in.shape[0]), 0)
    for r in range(experts):
        hot = sum(jnp.where(spot + r * cap == place[k : k + 1, :], 1.0, 0.0) for k in range(TOP))
        chunks[r][...] = dot(hot.astype(BF), rows_in[...]).astype(BF)


def spread(rows_in, place, experts, cap):
    rows, width = rows_in.shape
    return call(
        functools.partial(spread_kernel, experts, cap),
        [VM, VM],
        [shape((cap, width), BF)] * experts,
        [],
        2 * rows * width * experts * cap,
        2 * (rows + experts * cap) * width,
        "spread",
    )(rows_in, place)


def places_of(routes, live, experts, capacity):
    tokens = routes.shape[0]
    ids = jnp.arange(experts, dtype=jnp.int32)
    match = [
        ((routes[:, k : k + 1] == ids[None, :]) & live[:, None]).astype(F32) for k in range(TOP)
    ]
    order = jnp.arange(tokens, dtype=jnp.int32)
    below = (order[:, None] > order[None, :]).astype(BF)
    before = jnp.zeros((1, experts), F32)
    out = []
    for k in range(TOP):
        counts = dot(below, match[k].astype(BF)) + before
        before = before + jnp.sum(match[k], axis=0, keepdims=True)
        within = jnp.sum(counts * match[k], axis=1).astype(jnp.int32)
        out.append(jnp.where(live, routes[:, k] * capacity + within, experts * capacity))
    return out

def local(
    tokens,
    image_ids,
    routes,
    norm1_gain,
    norm1_bias,
    qkv_weight,
    attn_out_weight,
    norm2_gain,
    norm2_bias,
    fc1_weight,
    fc2_weight,
    norm3_gain,
    norm3_bias,
    router_weight,
    expert_up,
    expert_down,
    cotangent,
):
    s = lax.axis_index("section")
    e = lax.axis_index("dp") // GROUP
    q = lax.axis_index("dp") % GROUP
    dp_count = lax.axis_size("dp")
    experts = dp_count // GROUP
    cap = GROUP * ((21 * SLOTS + 10 * experts * GROUP - 1) // (10 * experts * GROUP))
    cap = -(-cap // 16) * 16
    half = tokens.shape[1]
    width = 2 * half
    few = experts <= 8
    planes = [[p * GROUP + i for p in range(experts)] for i in range(GROUP)]
    here, here_q = jnp.stack([s, 0 * s]), jnp.stack([s, q])
    quads = [[p * GROUP + i for i in range(GROUP)] for p in range(experts)]

    def swap(v):
        return lax.ppermute(v, "section", [(0, 1), (1, 0)])

    def over_q(v, bit):
        return lax.ppermute(v, "dp", [(i, i ^ bit) for i in range(dp_count)])

    def over_e(v, r):
        return lax.ppermute(
            v,
            "dp",
            [(i, ((i // GROUP + r) % experts) * GROUP + i % GROUP) for i in range(dp_count)],
        )

    def part(v, index, size, axis=0):
        return lax.dynamic_slice_in_dim(v, index * size, size, axis)

    def join(own, other, axis):
        return jnp.where(
            s == 0,
            jnp.concatenate([own, other], axis=axis),
            jnp.concatenate([other, own], axis=axis),
        )

    def add(a, b):
        return (a.astype(F32) + b.astype(F32)).astype(BF)

    def out_chunks(chunks):
        if not few:
            return list(lax.all_to_all(jnp.stack(chunks), "dp", 0, 0, axis_index_groups=planes))
        return [chunks[0]] + [over_e(chunks[r], r) for r in range(1, experts)]

    def home_chunks(chunks):
        if not few:
            return list(lax.all_to_all(jnp.stack(chunks), "dp", 0, 0, axis_index_groups=planes))
        return [chunks[0]] + [over_e(chunks[r], experts - r) for r in range(1, experts)]

    small = jnp.stack([norm1_gain, norm1_bias, norm2_gain, norm2_bias, norm3_gain, norm3_bias])
    small = jnp.concatenate([small, jnp.transpose(router_weight)])
    small = join(small, swap(small), 1)
    x = join(part(tokens, s, SLOTS), swap(part(tokens, 1 - s, SLOTS)), 1)
    dy = join(part(cotangent, s, SLOTS), swap(part(cotangent, 1 - s, SLOTS)), 1)
    ids = part(image_ids, s, 1).reshape(-1)
    route = part(routes, s, SLOTS)
    live = ids >= 0
    gb = jnp.concatenate([small[:6], jnp.zeros((2, width), BF)]).astype(F32)
    router_rows = -(-experts // 16) * 16
    router = jnp.concatenate([small[6 : 6 + experts], jnp.zeros((router_rows - experts, width), BF)])
    qkv, wo = (qkv_weight, swap(qkv_weight)), (attn_out_weight, swap(attn_out_weight))

    pair = jnp.stack([expert_up, expert_down])

    def gather(v, tiled):
        return lax.all_gather(v, "section", axis=0, tiled=tiled)

    tie = lax.optimization_barrier
    x, dy, qkv, wo, fc1_weight, fc2_weight, pair = tie(
        (x, dy, qkv, wo, fc1_weight, fc2_weight, pair)
    )
    fc1, fc2 = gather(fc1_weight, True), gather(fc2_weight, True)
    from_x, from_y, other_pair = over_q(pair, 1), over_q(pair, 2), swap(pair)

    if few:
        distance = (route - e) % experts
    else:
        distance = route
    spots = places_of(distance, live, experts, cap)
    place = jnp.stack(spots + [jnp.full_like(spots[0], -1)] * 6)
    route_rows = jnp.concatenate([jnp.transpose(route), jnp.full((6, SLOTS), -1, jnp.int32)])
    live_row = live.astype(F32)[None, :]
    dy_sent = spread(dy, place, experts, cap)
    dy_out = out_chunks(dy_sent)

    normed1, packed, context, lse, hidden = front(here, x, ids, gb, qkv, wo, dy_sent[:1])
    hidden, from_x, from_y, other_pair, *dy_out[:-1] = tie(
        (hidden, from_x, from_y, other_pair, *dy_out[:-1])
    )
    other_x, other_y = swap(from_x), swap(from_y)
    far = over_q(from_x, 2)
    normed2, act, slope, dense, normed3, soft, *sent = mlp(
        hidden, gb, router, place, route_rows, live_row, fc1, fc2, experts, cap, []
    )
    sent, other_x, other_y, dy_out[-1] = tie((sent, other_x, other_y, dy_out[-1]))
    got = out_chunks(sent)
    got[0], far = tie((got[0], far))
    own, other = [pair, from_x, from_y, far], [other_pair, other_x, other_y, swap(far)]

    step = max(1, experts // 4)
    results = [None] * experts
    previous, homes = None, [None] * experts
    order = [0, 3, 1, 2] if experts == 4 else list(range(0, experts, step))
    for place_in_order, i in enumerate(order):
        if i:
            got[i], results[previous] = tie((got[i], results[previous]))
        if few and place_in_order == 3:
            got[i], homes[order[1]] = tie((got[i], homes[order[1]]))
        results[i : i + step] = expert(
            here, got[i : i + step], dy_out[i : i + step], own, other, cap
        )
        previous = i
        homes[i] = over_e(results[i][0], experts - i) if few and i else results[i][0]
    if not few:
        homes = home_chunks([r[0] for r in results])
    acts, dinners, scaled = ([r[i] for r in results] for i in (2, 3, 4))

    if experts == 4:
        dinners, homes[1] = tie((dinners, homes[1]))
    up_grads = weight_grad(here_q, got, dinners, cap, stride=2)
    dmlp, dpre, dhidden, tiny23, drouter = back(
        dy, dense, hidden, gb, router, place, route_rows, live_row, soft, normed3, slope,
        fc1, fc2, homes, experts, cap, [],
    )
    outs = hold([r[1] for r in results], [dmlp])
    grads1, grads2 = weight_grad(here, [normed2], [dpre]), weight_grad(here, [act], [dmlp])
    acts, grads1, grads2 = tie((acts, grads1, grads2))
    expert_grads = weight_grad(here_q, scaled, acts, stride=2, into=up_grads)

    def fold(v, bit):
        mine, rows = (q // bit) % 2, v.shape[0] // 2
        return part(v, mine, rows), over_q(part(v, 1 - mine, rows), bit)

    def unfold(v, got, bit):
        return jnp.where(
            (q // bit) % 2 == 0, jnp.concatenate([v, got]), jnp.concatenate([got, v])
        )

    def plane_out(a, b):
        ab = jnp.stack([a, b])
        rows = a.shape[0] // experts
        if not few:
            return [lax.psum(ab, "dp", axis_index_groups=planes)]
        return [part(ab, (e + r) % experts, rows, 1) for r in range(experts)]

    def plane_sum(pieces):
        if not few:
            return pieces
        total = sum(p.astype(F32) for p in pieces).astype(BF)
        return [total] * experts

    def plane_move(pieces):
        return pieces[:1] + [over_e(p, r) for r, p in enumerate(pieces) if r]

    def plane_join(pieces):
        if not few:
            return pieces[0][0], pieces[0][1]
        rows = pieces[0].shape[1]
        whole = jnp.zeros((2, experts * rows, width), BF)
        for r, piece in enumerate(pieces):
            whole = lax.dynamic_update_slice_in_dim(whole, piece, ((e - r) % experts) * rows, 1)
        return whole[0], whole[1]

    away1, away2 = swap(grads1[0]), swap(grads2[0])
    dhidden, away1, away2, grads1, grads2, expert_grads = tie(
        (dhidden, away1, away2, grads1, grads2, expert_grads)
    )
    a, b = add(grads2[1], away2).reshape(-1, width), add(grads1[1], away1).reshape(-1, width)
    a, b = fold(a, 1), fold(b, 2)
    dattn, dpacked = attend_back(here, dhidden, ids, packed, lse, wo, [])
    home_outs = home_chunks(outs)
    give, keep = attention_grad(here, normed1, context, dpacked, dattn)
    give, keep, a, b, dpacked, home_outs = tie((give, keep, a, b, dpacked, home_outs))
    grad_in, tiny1 = input_back(here, x, dhidden, gb, dpacked, qkv, [])
    tiny = jnp.concatenate([tiny1[:2], tiny23[2:6], drouter[:experts]])

    def swapped(v):
        return part(v, s, half, 1), swap(part(v, 1 - s, half, 1))

    away = swap(give)
    a, b = fold(add(*a), 2), fold(add(*b), 1)
    sum_experts = add(expert_grads[1], swap(expert_grads[0]))
    tiny = swapped(tiny)
    away, a, b, grad_in, tiny, sum_experts = tie((away, a, b, grad_in, tiny, sum_experts))
    half_experts = lax.psum_scatter(
        sum_experts.reshape(GROUP, 2, half, -1),
        "dp", scatter_dimension=0, axis_index_groups=quads, tiled=False,
    )
    grad_in = swapped(grad_in)
    tiny = tiny[0] + tiny[1]

    ab = plane_out(add(*a), add(*b))
    keep, away, ab = tie((keep, away, ab))
    ab = plane_move(ab)
    t = add(keep, away).reshape(-1, width)
    ta, tb = fold(t[:width], 1), fold(t[width:], 2)
    ab, ta, tb = tie((ab, ta, tb))
    block_out = merge(dense, place, home_outs, experts, cap)

    ab = plane_sum(ab)
    ta, tb, ab = tie((ta, tb, ab))
    ab = plane_move(ab)
    ta, tb = fold(add(*ta), 2), fold(add(*tb), 1)
    tiny_x = over_q(tiny, 1)
    ab, ta, tb, block_out, tiny_x = tie((ab, ta, tb, block_out, tiny_x))
    tiny = tiny + tiny_x
    tiny_y = over_q(tiny, 2)

    a, b = plane_join(ab)
    a_got, b_got = over_q(a, 2), over_q(b, 1)
    tab = plane_move(plane_out(add(*ta), add(*tb)))
    a_got, b_got, tab, tiny_y = tie((a_got, b_got, tab, tiny_y))
    a, b = unfold(a, a_got, 2), unfold(b, b_got, 1)
    a_got, b_got = over_q(a, 1), over_q(b, 2)
    tab = plane_move(plane_sum(tab))
    a_got, b_got, tab = tie((a_got, b_got, tab))

    side_x, side_y = jnp.reshape(q % 2, (1,)), jnp.reshape(q // 2, (1,))

    def blocks(v):
        return v.reshape(-1, half, width)

    ta, tb = plane_join(tab)
    ta_got, tb_got = over_q(ta, 2), over_q(tb, 1)
    block_out = swapped(block_out)
    tiny = tiny + tiny_y
    if few:
        tiny = [over_e(tiny, r) if r else tiny for r in range(experts)]
    else:
        tiny = [lax.psum(tiny, "dp", axis_index_groups=planes)]
    ta_got, tb_got, tiny, a, a_got, b, b_got, grad_in, block_out, half_experts = tie(
        (ta_got, tb_got, tiny, a, a_got, b, b_got, grad_in, block_out, half_experts)
    )
    half_up, half_down = half_experts[0].astype(F32), half_experts[1].astype(F32)
    ta, tb = unfold(ta, ta_got, 2), unfold(tb, tb_got, 1)
    ta_got, tb_got = over_q(ta, 1), over_q(tb, 2)
    total = sum(tiny)
    sum_fc2 = finish(side_x, blocks(a), blocks(a_got), False)
    sum_fc1 = finish(side_y, blocks(b), blocks(b_got), True)
    q_and_k = finish(side_x, blocks(ta), blocks(ta_got), True)
    first = q // 2 == 0
    v_sum, sum_attn = (
        jnp.where(first, p, r).astype(F32) for p, r in ((tb, tb_got), (tb_got, tb))
    )
    sum_qkv = jnp.concatenate([q_and_k, v_sum], axis=1)
    return (
        join(*block_out, 0),
        join(*grad_in, 0),
        total[0],
        total[1],
        sum_qkv,
        sum_attn,
        total[2],
        total[3],
        sum_fc1,
        sum_fc2,
        total[4],
        total[5],
        jnp.transpose(total[6:]),
        half_up,
        half_down,
    )


def solution(mesh):
    placed = (
        P("dp", "section"),
        P("dp", None),
        P("dp", None),
        P("section"),
        P("section"),
        P("section", None),
        P("section", None),
        P("section"),
        P("section"),
        P("section", None),
        P("section", None),
        P("section"),
        P("section"),
        P("section", None),
        P("section", "dp"),
        P("section", "dp"),
        P("dp", "section"),
    )
    return jax.shard_map(
        local,
        mesh=mesh,
        in_specs=placed,
        out_specs=(
            P("dp", "section"),
            P("dp", "section"),
            P("section"),
            P("section"),
            P("section", None),
            P("section", None),
            P("section"),
            P("section"),
            P("section", None),
            P("section", None),
            P("section"),
            P("section"),
            P("section", None),
            P("section", "dp"),
            P("section", "dp"),
        ),
        check_vma=False,
    )
```

```python
import functools

import jax
import jax.numpy as jnp
from jax import lax
from jax.experimental import pallas as pl
from jax.experimental.pallas import tpu as pltpu
from jax.sharding import PartitionSpec as P

HEAD = 64
TOP = 2
GROUP = 4
SLOTS = 576
WIDE = 128

EPSILON = 1e-06
MASKED = -1e30
BF = jnp.bfloat16
F32 = jnp.float32
LIMIT = 24 * 1024 * 1024
LIMITS = dict(
    attention_forward=28,
    dense_forward=36,
    expert=28,
    dense_backward=40,
    attention_backward=28,
    input_backward=24,
    merge=20,
    hold=12,
    finish=24,
    spread=16,
)


def dot(a, b):
    return jnp.dot(a, b, preferred_element_type=F32)


def dot_nt(a, b):
    return lax.dot_general(a, b, (((1,), (1,)), ((), ())), preferred_element_type=F32)


def dot_tn(a, b):
    return lax.dot_general(a, b, (((0,), (0,)), ((), ())), preferred_element_type=F32)


def normalize(v):
    center = v - jnp.mean(v, axis=-1, keepdims=True)
    scale = lax.rsqrt(jnp.mean(center * center, axis=-1, keepdims=True) + EPSILON)
    return center * scale, scale


def gelu_pair(x):
    bell = jnp.exp(x * x * -0.5)
    t = 1.0 / (1.0 + jnp.abs(x) * (0.3275911 * 0.5**0.5))
    tail = (
        t
        * (
            0.127414796
            + t * (-0.142248368 + t * (0.7107068705 + t * (-0.7265760135 + t * 0.5307027145)))
        )
        * bell
    )
    cdf = jnp.where(x >= 0.0, 1.0 - tail, tail)
    return x * cdf, cdf + x * (bell * 0.3989422804014327)


def iota(shape, axis):
    return lax.broadcasted_iota(jnp.int32, shape, axis)


def halves_into(s, own, other, dest, sems, first):
    rows = own.shape[0]
    return [
        pltpu.make_async_copy(own, dest.at[pl.ds(pl.multiple_of(s * rows, rows), rows)], sems.at[first]),
        pltpu.make_async_copy(
            other, dest.at[pl.ds(pl.multiple_of((1 - s) * rows, rows), rows)], sems.at[first + 1]
        ),
    ]


def split3(v):
    hi = v.astype(BF)
    rest = v - hi.astype(F32)
    mid = rest.astype(BF)
    low = (rest - mid.astype(F32)).astype(BF)
    return hi, mid, low


VM = pl.BlockSpec(memory_space=pltpu.VMEM)
SM = pl.BlockSpec(memory_space=pltpu.SMEM)
HB = pl.BlockSpec(memory_space=pl.ANY)


def call(kernel, in_specs, out_shape, scratch, flops, moved, name, after=(), weight=16, flushed=()):
    limit = LIMITS[name] * 1024 * 1024
    count, extra = len(in_specs), len(after)
    single = not isinstance(out_shape, list)
    shapes = [out_shape] if single else out_shape
    total, held = len(shapes), len(flushed)

    def body(*refs):
        inputs, outs = refs[:count], list(refs[count + extra : count + extra + total])
        rest = refs[count + extra + total :]
        if not held:
            kernel(*inputs, *outs, *rest)
            return
        own, (buffers, sems) = rest[: len(rest) - held - 1], (rest[len(rest) - held - 1 : -1], rest[-1])
        copies = {}
        for k, index in enumerate(flushed):
            copies[index] = pltpu.make_async_copy(buffers[k], outs[index], sems.at[k])
            outs[index] = buffers[k]
        kernel(*inputs, *outs, *own, flush=lambda index: copies[index].start())
        for index in flushed:
            copies[index].wait()

    made = pl.pallas_call(
        body,
        in_specs=in_specs + [HB] * extra,
        out_specs=VM
        if single
        else [pl.BlockSpec(memory_space=pltpu.HBM) if i in flushed else VM for i in range(total)],
        out_shape=out_shape
        if not held
        else [pltpu.HBM(v.shape, v.dtype) if i in flushed else v for i, v in enumerate(shapes)],
        scratch_shapes=scratch
        + [pltpu.VMEM(shapes[i].shape, shapes[i].dtype) for i in flushed]
        + ([pltpu.SemaphoreType.DMA((held,))] if held else []),
        compiler_params=pltpu.CompilerParams(vmem_limit_bytes=limit),
        cost_estimate=pl.CostEstimate(
            flops=int(weight * flops), bytes_accessed=int(weight * moved), transcendentals=0
        ),
        name=name,
    )
    return lambda *operands: made(*operands, *after)


def shape(dims, kind):
    return jax.ShapeDtypeStruct(dims, kind)


def front_kernel(
    s_ref, x_ref, id_row, id_col, gb_ref, qkv_a, qkv_b, wo_a, wo_b,
    normed, packed, context, lse, hidden,
    wq, wo, bias, lse_col, sems, flush,
):
    s = s_ref[0]
    rows, width = x_ref.shape
    copies = halves_into(s, qkv_a, qkv_b, wq, sems, 0) + halves_into(s, wo_a, wo_b, wo, sems, 2)
    for c in copies:
        c.start()
    tile = rows // 6

    @pl.loop(0, 6)
    def _(i):
        at = pl.ds(pl.multiple_of(i * tile, 16), tile)
        n, _ = normalize(x_ref[at, :].astype(F32))
        normed[at, :] = (n * gb_ref[0:1, :] + gb_ref[1:2, :]).astype(BF)
        bias[at, :] = jnp.where(id_col[at, :] == id_row[...], 0.0, MASKED)

    copies[0].wait()
    copies[1].wait()

    @pl.loop(0, wq.shape[1] // 256)
    def _(j):
        at = pl.ds(pl.multiple_of(j * 256, 256), 256)
        packed[:, at] = dot(normed[...], wq[:, at]).astype(BF)

    flush(0)
    flush(1)
    lane = iota((1, WIDE), 1)
    lse_col[...] = jnp.zeros_like(lse_col)
    third = rows // 3

    @pl.loop(0, width // WIDE)
    def _(pair):
        col = pl.multiple_of(pair * WIDE, WIDE)
        keys = packed[:, pl.ds(width + col, WIDE)]
        values = packed[:, pl.ds(2 * width + col, WIDE)]
        for r in range(3):
            at = slice(r * third, (r + 1) * third)
            q = packed[at, pl.ds(col, WIDE)] * jnp.asarray(HEAD**-0.5, BF)
            outs = []
            sums = lse_col[at, :]
            for h in range(2):
                mine = (lane >= h * HEAD) & (lane < (h + 1) * HEAD)
                scores = dot_nt(jnp.where(mine, q, jnp.zeros_like(q)), keys) + bias[at, :]
                top = jnp.max(scores, axis=1, keepdims=True)
                p = jnp.exp(scores - top)
                total = jnp.sum(p, axis=1, keepdims=True)
                outs.append(dot(p.astype(BF), values) * (1.0 / total))
                sums = jnp.where(lane == 2 * pair + h, top + jnp.log(total), sums)
            lse_col[at, :] = sums
            context[at, pl.ds(col, WIDE)] = jnp.where(lane < HEAD, outs[0], outs[1]).astype(BF)

    flush(2)
    lse[...] = jnp.transpose(lse_col[...])[0 : lse.shape[0], :]
    copies[2].wait()
    copies[3].wait()

    @pl.loop(0, width // 256)
    def _(j):
        at = pl.ds(pl.multiple_of(j * 256, 256), 256)
        hidden[:, at] = x_ref[:, at].astype(F32) + dot(context[...], wo[:, at])


def front(s, x, ids, gb, qkv, wo, after):
    rows, width = x.shape
    n3 = qkv[0].shape[1]
    return call(
        front_kernel,
        [SM, VM, VM, VM, VM, HB, HB, HB, HB],
        [
            shape((rows, width), BF),
            shape((rows, n3), BF),
            shape((rows, width), BF),
            shape((16, rows), F32),
            shape((rows, width), F32),
        ],
        [
            pltpu.VMEM((width, n3), BF),
            pltpu.VMEM((width, width), BF),
            pltpu.VMEM((rows, rows), F32),
            pltpu.VMEM((rows, WIDE), F32),
            pltpu.SemaphoreType.DMA((4,)),
        ],
        2 * rows * width * (n3 + width) + 4 * rows * rows * width,
        2 * (width * (n3 + width) + rows * (3 * width + n3)) + 4 * rows * width,
        "attention_forward",
        after,
        flushed=(0, 1, 2),
    )(s, x, ids[None, :], ids[:, None], gb, *qkv, *wo)


def mlp_kernel(experts, cap, hid, gb_ref, router, place, route, live, fc1, fc2, *refs, flush):
    normed2, act, slope, dense, normed3, soft = refs[:6]
    chunks = refs[6 : 6 + experts]
    w1, w2, sems = refs[6 + experts :]
    rows, width = hid.shape
    copies = [
        pltpu.make_async_copy(fc1, w1, sems.at[0]),
        pltpu.make_async_copy(fc2, w2, sems.at[1]),
    ]
    for c in copies:
        c.start()
    tile = rows // 6

    @pl.loop(0, 6)
    def _(i):
        at = pl.ds(pl.multiple_of(i * tile, 16), tile)
        n, _ = normalize(hid[at, :])
        normed2[at, :] = (n * gb_ref[2:3, :] + gb_ref[3:4, :]).astype(BF)
        dense[at, :] = hid[at, :]

    flush(0)
    for c in copies:
        c.wait()

    @pl.loop(0, w1.shape[1] // 512)
    def _(j):
        at = pl.ds(pl.multiple_of(j * 512, 512), 512)
        a, sl = gelu_pair(dot(normed2[...], w1[:, at]))
        act[:, at] = a.astype(BF)
        slope[:, at] = sl.astype(BF)
        dense[...] += dot(act[:, at], w2[at, :])

    flush(1)
    flush(2)
    flush(3)

    @pl.loop(0, 6)
    def _(i):
        at = pl.ds(pl.multiple_of(i * tile, 16), tile)
        n, _ = normalize(dense[at, :])
        normed3[at, :] = (n * gb_ref[4:5, :] + gb_ref[5:6, :]).astype(BF)

    flush(4)
    logits = dot_nt(router[...], normed3[...])
    expert = iota(logits.shape, 0)
    chosen = [
        jnp.sum(jnp.where(expert == route[k : k + 1, :], logits, 0.0), axis=0, keepdims=True)
        for k in range(TOP)
    ]
    top = jnp.maximum(chosen[0], chosen[1])
    raised = [jnp.exp(c - top) for c in chosen]
    total = raised[0] + raised[1]
    pieces = []
    for k in range(TOP):
        share = raised[k] / total
        soft[k : k + 1, :] = share
        three = split3(share * live[...])
        row = iota((16, rows), 0)
        pieces.append(
            jnp.where(row == 0, three[0].astype(F32), 0.0)
            + jnp.where(row == 1, three[1].astype(F32), 0.0)
            + jnp.where(row == 2, three[2].astype(F32), 0.0)
        )
    pieces = [p.astype(BF) for p in pieces]
    lanes = -(-cap // WIDE) * WIDE
    spot = iota((lanes, rows), 0)
    spot = jnp.where(spot < cap, spot, -2 * experts * cap)
    for r in range(experts):
        hot = [jnp.where(spot + r * cap == place[k : k + 1, :], 1.0, 0.0).astype(BF) for k in range(TOP)]
        both = (hot[0] + hot[1])[0:cap, :]
        chunks[r][0:cap, :] = dot(both, normed3[...]).astype(BF)
        chunks[r][cap : cap + 16, :] = jnp.zeros((16, width), BF)
        chunks[r][cap : cap + 16, 0:lanes] = (
            dot_nt(pieces[0], hot[0]) + dot_nt(pieces[1], hot[1])
        ).astype(BF)
        if r:
            flush(6 + r)


def mlp(hid, gb, router, place, route, live, fc1, fc2, experts, cap, after):
    rows, width = hid.shape
    ff = fc1.shape[1]
    return call(
        functools.partial(mlp_kernel, experts, cap),
        [VM, VM, VM, VM, VM, VM, HB, HB],
        [
            shape((rows, width), BF),
            shape((rows, ff), BF),
            shape((rows, ff), BF),
            shape((rows, width), F32),
            shape((rows, width), BF),
            shape((8, rows), F32),
        ]
        + [shape((cap + 16, width), BF)] * experts,
        [
            pltpu.VMEM((width, ff), BF),
            pltpu.VMEM((ff, width), BF),
            pltpu.SemaphoreType.DMA((2,)),
        ],
        4 * rows * width * ff + 2 * rows * width * experts * cap,
        4 * width * ff + rows * (4 * ff + 12 * width),
        "dense_forward",
        after,
        flushed=(0, 1, 2, 3, 4) + tuple(range(7, 6 + experts)),
    )(hid, gb, router, place, route, live, fc1, fc2)


def expert_kernel(cap, n, s_ref, *refs, flush):
    rows_in, dys = refs[:n], refs[n : 2 * n]
    own, other = refs[2 * n : 2 * n + GROUP], refs[2 * n + GROUP : 2 * n + 2 * GROUP]
    outs = refs[2 * n + 2 * GROUP : -3]
    wu, wd, sems = refs[-3:]
    s = s_ref[0]
    width = wu.shape[1]
    half = width // 2
    copies = [
        [
            pltpu.make_async_copy(
                src[b].at[u],
                w.at[b, pl.ds(pl.multiple_of(side * half, half), half)],
                sems.at[4 * b + 2 * h + u],
            )
            for h, (side, src) in enumerate(((s, own), (1 - s, other)))
            for u, w in enumerate((wu, wd))
        ]
        for b in range(GROUP)
    ]
    for b in range(GROUP):
        for c in copies[b]:
            c.start()
    lanes = -(-cap // WIDE) * WIDE
    eye = iota((lanes, lanes), 0) == iota((lanes, lanes), 1)
    gates = []
    for i in range(n):
        back, out, act, dinner, gp = outs[5 * i : 5 * i + 5]
        g = jnp.sum(rows_in[i][cap : cap + 16, 0:lanes].astype(F32), axis=0, keepdims=True)
        gate = jnp.sum(jnp.where(eye, g, 0.0), axis=1, keepdims=True)[0:cap, :]
        gp[...] = (gate * dys[i][...].astype(F32)).astype(BF)
        gates.append(gate)
    sums = [None] * n
    backs = [None] * n
    for b in range(GROUP):
        for c in copies[b]:
            c.wait()
        at = slice(b * width, (b + 1) * width)
        for i in range(n):
            back, out, act, dinner, gp = outs[5 * i : 5 * i + 5]
            a, slope = gelu_pair(dot(rows_in[i][0:cap, :], wu[b]))
            act[:, at] = a.astype(BF)
            dinner[:, at] = (dot(gp[...], wd[b]) * slope).astype(BF)
            o = dot_nt(act[:, at], wd[b])
            d = dot_nt(dinner[:, at], wu[b])
            sums[i] = o if b == 0 else sums[i] + o
            backs[i] = d if b == 0 else backs[i] + d
    for i in range(n):
        back, out, act, dinner, gp = outs[5 * i : 5 * i + 5]
        out[...] = (gates[i] * sums[i]).astype(BF)
        flush(5 * i + 1)
        back[0:cap, :] = backs[i].astype(BF)
        dg = jnp.sum(dys[i][...].astype(F32) * sums[i], axis=1, keepdims=True)
        pad = jnp.where(eye[0:cap, :], dg, 0.0)
        dg_row = jnp.sum(pad, axis=0, keepdims=True)
        three = split3(dg_row)
        row = iota((16, lanes), 0)
        back[cap : cap + 16, :] = jnp.zeros((16, width), BF)
        back[cap : cap + 16, 0:lanes] = (
            jnp.where(row == 0, three[0].astype(F32), 0.0)
            + jnp.where(row == 1, three[1].astype(F32), 0.0)
            + jnp.where(row == 2, three[2].astype(F32), 0.0)
        ).astype(BF)
        flush(5 * i)


def expert(s, rows_in, dys, own, other, cap):
    n = len(rows_in)
    width = rows_in[0].shape[1]
    ff = GROUP * width
    res = call(
        functools.partial(expert_kernel, cap, n),
        [SM] + [VM] * (2 * n) + [HB] * (2 * GROUP),
        [
            shape((cap + 16, width), BF),
            shape((cap, width), BF),
            shape((cap, ff), BF),
            shape((cap, ff), BF),
            shape((cap, width), BF),
        ]
        * n,
        [
            pltpu.VMEM((GROUP, width, width), BF),
            pltpu.VMEM((GROUP, width, width), BF),
            pltpu.SemaphoreType.DMA((16,)),
        ],
        8 * n * cap * width * ff,
        4 * width * ff + n * cap * (4 * ff + 10 * width),
        "expert",
        flushed=tuple(range(0, 5 * n, 5)) + tuple(range(1, 5 * n, 5)),
    )(s, *rows_in, *dys, *own, *other)
    return [res[5 * i : 5 * i + 5] for i in range(n)]


def grad_kernel(n, skip, s_ref, *refs):
    lefts, rights, refs = refs[:n], refs[n : 2 * n], refs[2 * n + skip :]
    give, keep = refs[:2]
    if n == 1:
        left, right = lefts[0], rights[0]
    else:
        left, right = refs[2:]
        rows = lefts[0].shape[0]
        for i in range(n):
            left[i * rows : (i + 1) * rows, :] = lefts[i][...]
            right[i * rows : (i + 1) * rows, :] = rights[i][...]
    value = dot_tn(left[...], right[...]).astype(BF)

    @pl.when(pl.program_id(0) == 0)
    def _():
        give[0] = value

    @pl.when(pl.program_id(0) == 1)
    def _():
        keep[0] = value


def weight_grad(s, lefts, rights, rows=None, weight=16, stride=1, into=()):
    n = len(lefts)
    t = rows or lefts[0].shape[0]
    width = min(lefts[0].shape[1], rights[0].shape[1])
    high = width // 2
    m, nb = lefts[0].shape[1] // width, rights[0].shape[1] // width
    scratch = []
    if n > 1:
        scratch = [pltpu.VMEM((n * t, high), BF), pltpu.VMEM((n * t, width), BF)]
    left_at = lambda h, i, j, c: (0, jnp.where(h == 0, 1 - c[0], c[0]) * m + i)
    offset = 1 if into else 0

    def place_of(k, c):
        return ((k ^ c[1]) * stride + offset, 0, 0)

    give_at = lambda h, i, j, c: place_of(jnp.where(h == 0, i * nb + j, m * nb - 1), c)
    keep_at = lambda h, i, j, c: place_of(jnp.where(h == 0, 0, i * nb + j), c)
    return pl.pallas_call(
        functools.partial(grad_kernel, n, len(into)),
        grid_spec=pltpu.PrefetchScalarGridSpec(
            num_scalar_prefetch=1,
            grid=(2, m, nb),
            in_specs=[pl.BlockSpec((t, high), left_at)] * n
            + [pl.BlockSpec((t, width), lambda h, i, j, c: (0, j))] * n
            + [HB] * len(into),
            out_specs=[pl.BlockSpec((1, high, width), at) for at in (give_at, keep_at)],
            scratch_shapes=scratch,
        ),
        out_shape=[shape((m * nb * stride, high, width), BF)] * 2,
        input_output_aliases={1 + 2 * n + i: i for i in range(len(into))},
        compiler_params=pltpu.CompilerParams(vmem_limit_bytes=LIMIT),
        cost_estimate=pl.CostEstimate(
            flops=int(weight * 4) * n * t * m * high * width * nb,
            bytes_accessed=int(weight * 2) * (n * t * (2 * m * high + width * nb) + 2 * m * high * width * nb),
            transcendentals=0,
        ),
        name="weight_grad",
    )(s, *lefts, *rights, *into)


def attention_grad_kernel(s_ref, normed, context, dpacked, dattn, give, keep):
    j = pl.program_id(1)

    def write(value):
        @pl.when(pl.program_id(0) == 0)
        def _():
            give[0] = value

        @pl.when(pl.program_id(0) == 1)
        def _():
            keep[0] = value

    @pl.when(j < 3)
    def _():
        write(dot_tn(normed[...], dpacked[...]).astype(BF))

    @pl.when(j == 3)
    def _():
        write(dot_tn(context[...], dattn[...]).astype(BF))


def attention_grad(s, normed, context, dpacked, dattn):
    t, width = normed.shape
    high = width // 2
    half_at = lambda h, j, c: (0, jnp.where(h == 0, 1 - c[0], c[0]))
    return pl.pallas_call(
        attention_grad_kernel,
        grid_spec=pltpu.PrefetchScalarGridSpec(
            num_scalar_prefetch=1,
            grid=(2, 4),
            in_specs=[
                pl.BlockSpec((t, high), half_at),
                pl.BlockSpec((t, high), half_at),
                pl.BlockSpec((t, width), lambda h, j, c: (0, jnp.minimum(j, 2))),
                pl.BlockSpec((t, width), lambda h, j, c: (0, 0)),
            ],
            out_specs=[
                pl.BlockSpec((1, high, width), lambda h, j, c: (jnp.where(h == 0, j, 3), 0, 0)),
                pl.BlockSpec((1, high, width), lambda h, j, c: (jnp.where(h == 0, 0, j), 0, 0)),
            ],
        ),
        out_shape=[shape((4, high, width), BF)] * 2,
        compiler_params=pltpu.CompilerParams(vmem_limit_bytes=LIMIT),
        cost_estimate=pl.CostEstimate(
            flops=t * width * width, bytes_accessed=t * width, transcendentals=0
        ),
        name="attention_grad",
    )(s, normed, context, dpacked, dattn)


def back_kernel(
    experts, cap, dy, dense, hid, gb_ref, router, place, route, live, soft, normed3, slope, fc1, fc2, *refs
):
    homes = refs[:experts]
    dmlp, dpre, dhidden, tiny, drouter = refs[experts : experts + 5]
    w1, w2, ups, sems = refs[experts + 5 :]
    rows, width = hid.shape
    copies = [
        pltpu.make_async_copy(fc1, w1, sems.at[0]),
        pltpu.make_async_copy(fc2, w2, sems.at[1]),
    ]
    for c in copies:
        c.start()
    lanes = -(-cap // WIDE) * WIDE
    spot = iota((lanes, rows), 0)
    spot = jnp.where(spot < cap, spot, -2 * experts * cap)
    dgate = [jnp.zeros((16, rows), F32) for _ in range(TOP)]
    for r in range(experts):
        tail = homes[r][cap : cap + 16, 0:lanes]
        hot = [jnp.where(spot + r * cap == place[k : k + 1, :], 1.0, 0.0).astype(BF) for k in range(TOP)]
        for k in range(TOP):
            dgate[k] = dgate[k] + dot(tail, hot[k])
        term = dot_tn((hot[0] + hot[1])[0:cap, :], homes[r][0:cap, :])
        ups[...] = term if r == 0 else ups[...] + term
    dgate = [jnp.sum(d, axis=0, keepdims=True) * live[...] for d in dgate]
    mix = soft[0:1, :] * dgate[0] + soft[1:2, :] * dgate[1]
    dsoft = [soft[k : k + 1, :] * (dgate[k] - mix) for k in range(TOP)]
    index = iota((router.shape[0], rows), 0)
    dlogits = sum(jnp.where(index == route[k : k + 1, :], dsoft[k], 0.0) for k in range(TOP))
    dlogits = dlogits.astype(BF)
    drouter[...] = dot(dlogits, normed3[...])
    ups[...] += dot_tn(dlogits, router[...])
    tile = rows // 6
    tiny[...] = jnp.zeros_like(tiny)

    def norm_back(at, values, gain, bias_row, base):
        n, scale = normalize(values)
        u = ups[at, :]
        tiny[bias_row - 1 : bias_row, :] += jnp.sum(u * n, axis=0, keepdims=True)
        tiny[bias_row : bias_row + 1, :] += jnp.sum(u, axis=0, keepdims=True)
        ug = u * gain
        dv = scale * (
            ug
            - jnp.mean(ug, axis=-1, keepdims=True)
            - n * jnp.mean(ug * n, axis=-1, keepdims=True)
        )
        return base + dv

    @pl.loop(0, 6)
    def _(i):
        at = pl.ds(pl.multiple_of(i * tile, 16), tile)
        dd = norm_back(at, dense[at, :], gb_ref[4:5, :], 5, dy[at, :].astype(F32))
        dhidden[at, :] = dd
        dmlp[at, :] = dd.astype(BF)

    for c in copies:
        c.wait()
    ups[...] = jnp.zeros_like(ups)

    @pl.loop(0, w1.shape[1] // 512)
    def _(j):
        at = pl.ds(pl.multiple_of(j * 512, 512), 512)
        dpre[:, at] = (dot_nt(dmlp[...], w2[at, :]) * slope[:, at].astype(F32)).astype(BF)
        ups[...] += dot_nt(dpre[:, at], w1[:, at])

    @pl.loop(0, 6)
    def _(i):
        at = pl.ds(pl.multiple_of(i * tile, 16), tile)
        dhidden[at, :] = norm_back(at, hid[at, :], gb_ref[2:3, :], 3, dhidden[at, :])


def back(
    dy, dense, hid, gb, router, place, route, live, soft, normed3, slope, fc1, fc2, homes, experts, cap, after
):
    rows, width = hid.shape
    ff = fc1.shape[1]
    return call(
        functools.partial(back_kernel, experts, cap),
        [VM] * 11 + [HB] * 2 + [VM] * experts,
        [
            shape((rows, width), BF),
            shape((rows, ff), BF),
            shape((rows, width), F32),
            shape((8, width), F32),
            shape(router.shape, F32),
        ],
        [
            pltpu.VMEM((width, ff), BF),
            pltpu.VMEM((ff, width), BF),
            pltpu.VMEM((rows, width), F32),
            pltpu.SemaphoreType.DMA((2,)),
        ],
        4 * rows * width * ff + 2 * rows * width * experts * cap,
        4 * width * ff + rows * (4 * ff + 18 * width),
        "dense_backward",
        after,
    )(dy, dense, hid, gb, router, place, route, live, soft, normed3, slope, fc1, fc2, *homes)


def attend_back_kernel(
    s_ref, dhid, id_row, id_col, packed, lse, wo_a, wo_b, dattn, dpacked, wo, bias, dctx, sems
):
    s = s_ref[0]
    rows, width = dhid.shape
    copies = halves_into(s, wo_a, wo_b, wo, sems, 0)
    for c in copies:
        c.start()
    tile = rows // 6

    @pl.loop(0, 6)
    def _(i):
        at = pl.ds(pl.multiple_of(i * tile, 16), tile)
        dattn[at, :] = dhid[at, :].astype(BF)
        bias[at, :] = jnp.where(id_col[at, :] == id_row[...], 0.0, MASKED)

    copies[0].wait()
    copies[1].wait()

    @pl.loop(0, width // 256)
    def _(j):
        at = pl.ds(pl.multiple_of(j * 256, 256), 256)
        dctx[:, at] = dot_nt(dattn[...], wo[at, :]).astype(BF)

    lane = iota((1, WIDE), 1)

    @pl.loop(0, width // WIDE)
    def _(pair):
        col = pl.multiple_of(pair * WIDE, WIDE)
        q = packed[:, pl.ds(col, WIDE)] * jnp.asarray(HEAD**-0.5, BF)
        keys = packed[:, pl.ds(width + col, WIDE)]
        values = packed[:, pl.ds(2 * width + col, WIDE)]
        dc = dctx[:, pl.ds(col, WIDE)]
        dq, dk, dv = [], [], []
        for h in range(2):
            mine = (lane >= h * HEAD) & (lane < (h + 1) * HEAD)
            scores = dot_nt(jnp.where(mine, keys, jnp.zeros_like(keys)), q) + bias[...]
            p = jnp.exp(scores - lse[pl.ds(2 * pair + h, 1), :])
            dp = dot_nt(jnp.where(mine, values, jnp.zeros_like(values)), dc)
            inner = jnp.sum(p * dp, axis=0, keepdims=True)
            ds = (p * (dp - inner)).astype(BF)
            dv.append(dot(p.astype(BF), dc))
            dk.append(dot(ds, q))
            dq.append(dot_tn(ds, keys) * HEAD**-0.5)
        low = lane < HEAD
        dpacked[:, pl.ds(col, WIDE)] = jnp.where(low, dq[0], dq[1]).astype(BF)
        dpacked[:, pl.ds(width + col, WIDE)] = jnp.where(low, dk[0], dk[1]).astype(BF)
        dpacked[:, pl.ds(2 * width + col, WIDE)] = jnp.where(low, dv[0], dv[1]).astype(BF)


def input_kernel(s_ref, x_ref, dhid, gb_ref, dpacked, qkv_a, qkv_b, grad_in, tiny, wq, ups, sems):
    s = s_ref[0]
    rows, width = x_ref.shape
    tile = rows // 6
    copies = halves_into(s, qkv_a, qkv_b, wq, sems, 0)
    for c in copies:
        c.start()
    copies[0].wait()
    copies[1].wait()

    @pl.loop(0, width // 256)
    def _(j):
        at = pl.ds(pl.multiple_of(j * 256, 256), 256)
        ups[:, at] = dot_nt(dpacked[...], wq[at, :])

    tiny[...] = jnp.zeros_like(tiny)

    @pl.loop(0, 6)
    def _(i):
        at = pl.ds(pl.multiple_of(i * tile, 16), tile)
        n, scale = normalize(x_ref[at, :].astype(F32))
        u = ups[at, :]
        tiny[0:1, :] += jnp.sum(u * n, axis=0, keepdims=True)
        tiny[1:2, :] += jnp.sum(u, axis=0, keepdims=True)
        ug = u * gb_ref[0:1, :]
        grad_in[at, :] = dhid[at, :] + scale * (
            ug
            - jnp.mean(ug, axis=-1, keepdims=True)
            - n * jnp.mean(ug * n, axis=-1, keepdims=True)
        )


def attend_back(s, dhid, ids, packed, lse, wo, after):
    rows, width = dhid.shape
    n3 = packed.shape[1]
    return call(
        attend_back_kernel,
        [SM] + [VM] * 5 + [HB] * 2,
        [shape((rows, width), BF), shape((rows, n3), BF)],
        [
            pltpu.VMEM((width, width), BF),
            pltpu.VMEM((rows, rows), F32),
            pltpu.VMEM((rows, width), BF),
            pltpu.SemaphoreType.DMA((2,)),
        ],
        2 * rows * width * width + 20 * rows * rows * width,
        2 * (width * width + rows * (3 * width + 2 * n3)),
        "attention_backward",
        after,
    )(s, dhid, ids[None, :], ids[:, None], packed, lse, *wo)


def input_back(s, x, dhid, gb, dpacked, qkv, after):
    rows, width = x.shape
    n3 = dpacked.shape[1]
    return call(
        input_kernel,
        [SM] + [VM] * 4 + [HB] * 2,
        [shape((rows, width), F32), shape((8, width), F32)],
        [
            pltpu.VMEM((width, n3), BF),
            pltpu.VMEM((rows, width), F32),
            pltpu.SemaphoreType.DMA((2,)),
        ],
        2 * rows * width * n3,
        2 * (width * n3 + rows * n3) + 10 * rows * width,
        "input_backward",
        after,
    )(s, x, dhid, gb, dpacked, *qkv)


def merge_kernel(experts, cap, dense, place, *refs):
    outs, result = refs[:experts], refs[experts]
    rows = dense.shape[0]
    total = dense[...]
    spot = iota((cap, rows), 0)
    for r in range(experts):
        hot = sum(jnp.where(spot + r * cap == place[k : k + 1, :], 1.0, 0.0) for k in range(TOP))
        total = total + dot_tn(hot.astype(BF), outs[r][...])
    result[...] = total.astype(BF)


def merge(dense, place, outs, experts, cap):
    rows, width = dense.shape
    return call(
        functools.partial(merge_kernel, experts, cap),
        [VM] * (2 + experts),
        shape((rows, width), BF),
        [],
        2 * rows * width * experts * cap,
        rows * width * 6 + 2 * experts * cap * width,
        "merge",
        (),
        0.25,
    )(dense, place, *outs)


def hold_kernel(n, *refs):
    for i in range(n):
        refs[n + i][...] = refs[i][...]


def hold(chunks, after):
    n = len(chunks)
    dims = chunks[0].shape
    return call(
        functools.partial(hold_kernel, n),
        [VM] * n,
        [shape(dims, BF)] * n,
        [],
        0,
        4 * n * dims[0] * dims[1],
        "hold",
        after,
    )(*chunks)


def finish_kernel(columns, m_ref, mine, got, out):
    n, high, width = mine.shape
    for which, src in ((m_ref[0], mine), (1 - m_ref[0], got)):
        for i in range(n):
            value = src[i].astype(F32)
            if columns:
                out[:, pl.ds(pl.multiple_of((which * n + i) * width, width), width)] = value
            else:
                out[pl.ds(pl.multiple_of((which * n + i) * high, high), high), :] = value


def finish(m, mine, got, columns):
    n, high, width = mine.shape
    dims = (high, 2 * n * width) if columns else (2 * n * high, width)
    return call(
        functools.partial(finish_kernel, columns),
        [SM, VM, VM],
        shape(dims, F32),
        [],
        0,
        12 * n * high * width,
        "finish",
    )(m, mine, got)


def spread_kernel(experts, cap, rows_in, place, *chunks):
    spot = iota((cap, rows_in.shape[0]), 0)
    for r in range(experts):
        hot = sum(jnp.where(spot + r * cap == place[k : k + 1, :], 1.0, 0.0) for k in range(TOP))
        chunks[r][...] = dot(hot.astype(BF), rows_in[...]).astype(BF)


def spread(rows_in, place, experts, cap):
    rows, width = rows_in.shape
    return call(
        functools.partial(spread_kernel, experts, cap),
        [VM, VM],
        [shape((cap, width), BF)] * experts,
        [],
        2 * rows * width * experts * cap,
        2 * (rows + experts * cap) * width,
        "spread",
    )(rows_in, place)


def places_of(routes, live, experts, capacity):
    tokens = routes.shape[0]
    ids = jnp.arange(experts, dtype=jnp.int32)
    match = [
        ((routes[:, k : k + 1] == ids[None, :]) & live[:, None]).astype(F32) for k in range(TOP)
    ]
    order = jnp.arange(tokens, dtype=jnp.int32)
    below = (order[:, None] > order[None, :]).astype(BF)
    before = jnp.zeros((1, experts), F32)
    out = []
    for k in range(TOP):
        counts = dot(below, match[k].astype(BF)) + before
        before = before + jnp.sum(match[k], axis=0, keepdims=True)
        within = jnp.sum(counts * match[k], axis=1).astype(jnp.int32)
        out.append(jnp.where(live, routes[:, k] * capacity + within, experts * capacity))
    return out

def local(
    tokens,
    image_ids,
    routes,
    norm1_gain,
    norm1_bias,
    qkv_weight,
    attn_out_weight,
    norm2_gain,
    norm2_bias,
    fc1_weight,
    fc2_weight,
    norm3_gain,
    norm3_bias,
    router_weight,
    expert_up,
    expert_down,
    cotangent,
):
    s = lax.axis_index("section")
    e = lax.axis_index("dp") // GROUP
    q = lax.axis_index("dp") % GROUP
    dp_count = lax.axis_size("dp")
    experts = dp_count // GROUP
    cap = GROUP * ((21 * SLOTS + 10 * experts * GROUP - 1) // (10 * experts * GROUP))
    cap = -(-cap // 16) * 16
    half = tokens.shape[1]
    width = 2 * half
    few = experts <= 8
    planes = [[p * GROUP + i for p in range(experts)] for i in range(GROUP)]
    here, here_q = jnp.stack([s, 0 * s]), jnp.stack([s, q])
    quads = [[p * GROUP + i for i in range(GROUP)] for p in range(experts)]

    def swap(v):
        return lax.ppermute(v, "section", [(0, 1), (1, 0)])

    def over_q(v, bit):
        return lax.ppermute(v, "dp", [(i, i ^ bit) for i in range(dp_count)])

    def over_e(v, r):
        return lax.ppermute(
            v,
            "dp",
            [(i, ((i // GROUP + r) % experts) * GROUP + i % GROUP) for i in range(dp_count)],
        )

    def part(v, index, size, axis=0):
        return lax.dynamic_slice_in_dim(v, index * size, size, axis)

    def join(own, other, axis):
        return jnp.where(
            s == 0,
            jnp.concatenate([own, other], axis=axis),
            jnp.concatenate([other, own], axis=axis),
        )

    def add(a, b):
        return (a.astype(F32) + b.astype(F32)).astype(BF)

    def out_chunks(chunks):
        if not few:
            return list(lax.all_to_all(jnp.stack(chunks), "dp", 0, 0, axis_index_groups=planes))
        return [chunks[0]] + [over_e(chunks[r], r) for r in range(1, experts)]

    def home_chunks(chunks):
        if not few:
            return list(lax.all_to_all(jnp.stack(chunks), "dp", 0, 0, axis_index_groups=planes))
        return [chunks[0]] + [over_e(chunks[r], experts - r) for r in range(1, experts)]

    small = jnp.stack([norm1_gain, norm1_bias, norm2_gain, norm2_bias, norm3_gain, norm3_bias])
    small = jnp.concatenate([small, jnp.transpose(router_weight)])
    small = join(small, swap(small), 1)
    x = join(part(tokens, s, SLOTS), swap(part(tokens, 1 - s, SLOTS)), 1)
    dy = join(part(cotangent, s, SLOTS), swap(part(cotangent, 1 - s, SLOTS)), 1)
    ids = part(image_ids, s, 1).reshape(-1)
    route = part(routes, s, SLOTS)
    live = ids >= 0
    gb = jnp.concatenate([small[:6], jnp.zeros((2, width), BF)]).astype(F32)
    router_rows = -(-experts // 16) * 16
    router = jnp.concatenate([small[6 : 6 + experts], jnp.zeros((router_rows - experts, width), BF)])
    qkv, wo = (qkv_weight, swap(qkv_weight)), (attn_out_weight, swap(attn_out_weight))

    pair = jnp.stack([expert_up, expert_down])

    def gather(v, tiled):
        return lax.all_gather(v, "section", axis=0, tiled=tiled)

    tie = lax.optimization_barrier
    x, dy, qkv, wo, fc1_weight, fc2_weight, pair = tie(
        (x, dy, qkv, wo, fc1_weight, fc2_weight, pair)
    )
    fc1, fc2 = gather(fc1_weight, True), gather(fc2_weight, True)
    from_x, from_y, other_pair = over_q(pair, 1), over_q(pair, 2), swap(pair)

    if few:
        distance = (route - e) % experts
    else:
        distance = route
    spots = places_of(distance, live, experts, cap)
    place = jnp.stack(spots + [jnp.full_like(spots[0], -1)] * 6)
    route_rows = jnp.concatenate([jnp.transpose(route), jnp.full((6, SLOTS), -1, jnp.int32)])
    live_row = live.astype(F32)[None, :]
    dy_sent = spread(dy, place, experts, cap)
    dy_out = out_chunks(dy_sent)

    normed1, packed, context, lse, hidden = front(here, x, ids, gb, qkv, wo, dy_sent[:1])
    hidden, from_x, from_y, other_pair, *dy_out[:-1] = tie(
        (hidden, from_x, from_y, other_pair, *dy_out[:-1])
    )
    other_x, other_y = swap(from_x), swap(from_y)
    far = over_q(from_x, 2)
    normed2, act, slope, dense, normed3, soft, *sent = mlp(
        hidden, gb, router, place, route_rows, live_row, fc1, fc2, experts, cap, []
    )
    sent, other_x, other_y, dy_out[-1] = tie((sent, other_x, other_y, dy_out[-1]))
    got = out_chunks(sent)
    got[0], far = tie((got[0], far))
    own, other = [pair, from_x, from_y, far], [other_pair, other_x, other_y, swap(far)]

    step = max(1, experts // 4)
    results = [None] * experts
    previous, homes = None, [None] * experts
    order = [0, 3, 1, 2] if experts == 4 else list(range(0, experts, step))
    for place_in_order, i in enumerate(order):
        if i:
            got[i], results[previous] = tie((got[i], results[previous]))
        if few and place_in_order == 3:
            got[i], homes[order[1]] = tie((got[i], homes[order[1]]))
        results[i : i + step] = expert(
            here, got[i : i + step], dy_out[i : i + step], own, other, cap
        )
        previous = i
        homes[i] = over_e(results[i][0], experts - i) if few and i else results[i][0]
    if not few:
        homes = home_chunks([r[0] for r in results])
    acts, dinners, scaled = ([r[i] for r in results] for i in (2, 3, 4))

    if experts == 4:
        dinners, homes[1] = tie((dinners, homes[1]))
    up_grads = weight_grad(here_q, got, dinners, cap, stride=2)
    dmlp, dpre, dhidden, tiny23, drouter = back(
        dy, dense, hidden, gb, router, place, route_rows, live_row, soft, normed3, slope,
        fc1, fc2, homes, experts, cap, [],
    )
    outs = hold([r[1] for r in results], [dmlp])
    grads1, grads2 = weight_grad(here, [normed2], [dpre]), weight_grad(here, [act], [dmlp])
    acts, grads1, grads2 = tie((acts, grads1, grads2))
    expert_grads = weight_grad(here_q, scaled, acts, stride=2, into=up_grads)

    def fold(v, bit):
        mine, rows = (q // bit) % 2, v.shape[0] // 2
        return part(v, mine, rows), over_q(part(v, 1 - mine, rows), bit)

    def unfold(v, got, bit):
        return jnp.where(
            (q // bit) % 2 == 0, jnp.concatenate([v, got]), jnp.concatenate([got, v])
        )

    def plane_out(a, b):
        ab = jnp.stack([a, b])
        rows = a.shape[0] // experts
        if not few:
            return [lax.psum(ab, "dp", axis_index_groups=planes)]
        return [part(ab, (e + r) % experts, rows, 1) for r in range(experts)]

    def plane_sum(pieces):
        if not few:
            return pieces
        total = sum(p.astype(F32) for p in pieces).astype(BF)
        return [total] * experts

    def plane_move(pieces):
        return pieces[:1] + [over_e(p, r) for r, p in enumerate(pieces) if r]

    def plane_join(pieces):
        if not few:
            return pieces[0][0], pieces[0][1]
        rows = pieces[0].shape[1]
        whole = jnp.zeros((2, experts * rows, width), BF)
        for r, piece in enumerate(pieces):
            whole = lax.dynamic_update_slice_in_dim(whole, piece, ((e - r) % experts) * rows, 1)
        return whole[0], whole[1]

    away1, away2 = swap(grads1[0]), swap(grads2[0])
    dhidden, away1, away2, grads1, grads2, expert_grads = tie(
        (dhidden, away1, away2, grads1, grads2, expert_grads)
    )
    a, b = add(grads2[1], away2).reshape(-1, width), add(grads1[1], away1).reshape(-1, width)
    a, b = fold(a, 1), fold(b, 2)
    dattn, dpacked = attend_back(here, dhidden, ids, packed, lse, wo, [])
    home_outs = home_chunks(outs)
    give, keep = attention_grad(here, normed1, context, dpacked, dattn)
    give, keep, a, b, dpacked, home_outs = tie((give, keep, a, b, dpacked, home_outs))
    grad_in, tiny1 = input_back(here, x, dhidden, gb, dpacked, qkv, [])
    tiny = jnp.concatenate([tiny1[:2], tiny23[2:6], drouter[:experts]])

    def swapped(v):
        return part(v, s, half, 1), swap(part(v, 1 - s, half, 1))

    away = swap(give)
    a, b = fold(add(*a), 2), fold(add(*b), 1)
    sum_experts = add(expert_grads[1], swap(expert_grads[0]))
    tiny = swapped(tiny)
    away, a, b, grad_in, tiny, sum_experts = tie((away, a, b, grad_in, tiny, sum_experts))
    half_experts = lax.psum_scatter(
        sum_experts.reshape(GROUP, 2, half, -1),
        "dp", scatter_dimension=0, axis_index_groups=quads, tiled=False,
    )
    grad_in = swapped(grad_in)
    tiny = tiny[0] + tiny[1]

    ab = plane_out(add(*a), add(*b))
    keep, away, ab = tie((keep, away, ab))
    ab = plane_move(ab)
    t = add(keep, away).reshape(-1, width)
    ta, tb = fold(t[:width], 1), fold(t[width:], 2)
    ab, ta, tb = tie((ab, ta, tb))
    block_out = merge(dense, place, home_outs, experts, cap)

    ab = plane_sum(ab)
    ta, tb, ab = tie((ta, tb, ab))
    ab = plane_move(ab)
    ta, tb = fold(add(*ta), 2), fold(add(*tb), 1)
    tiny_x = over_q(tiny, 1)
    ab, ta, tb, block_out, tiny_x = tie((ab, ta, tb, block_out, tiny_x))
    tiny = tiny + tiny_x
    tiny_y = over_q(tiny, 2)

    a, b = plane_join(ab)
    a_got, b_got = over_q(a, 2), over_q(b, 1)
    tab = plane_move(plane_out(add(*ta), add(*tb)))
    a_got, b_got, tab, tiny_y = tie((a_got, b_got, tab, tiny_y))
    a, b = unfold(a, a_got, 2), unfold(b, b_got, 1)
    a_got, b_got = over_q(a, 1), over_q(b, 2)
    tab = plane_move(plane_sum(tab))
    grad_in, block_out = join(*grad_in, 0), join(*swapped(block_out), 0)
    a_got, b_got, tab, grad_in, block_out = tie((a_got, b_got, tab, grad_in, block_out))

    side_x, side_y = jnp.reshape(q % 2, (1,)), jnp.reshape(q // 2, (1,))

    def blocks(v):
        return v.reshape(-1, half, width)

    ta, tb = plane_join(tab)
    ta_got, tb_got = over_q(ta, 2), over_q(tb, 1)
    tiny = tiny + tiny_y
    if few:
        tiny = [over_e(tiny, r) if r else tiny for r in range(experts)]
    else:
        tiny = [lax.psum(tiny, "dp", axis_index_groups=planes)]
    ta_got, tb_got, tiny, a, a_got, b, b_got, half_experts = tie(
        (ta_got, tb_got, tiny, a, a_got, b, b_got, half_experts)
    )
    half_up, half_down = half_experts[0].astype(F32), half_experts[1].astype(F32)
    ta, tb = unfold(ta, ta_got, 2), unfold(tb, tb_got, 1)
    ta_got, tb_got = over_q(ta, 1), over_q(tb, 2)
    total = sum(tiny)
    sum_fc2 = finish(side_x, blocks(a), blocks(a_got), False)
    sum_fc1 = finish(side_y, blocks(b), blocks(b_got), True)
    q_and_k = finish(side_x, blocks(ta), blocks(ta_got), True)
    first = q // 2 == 0
    v_sum, sum_attn = (
        jnp.where(first, p, r).astype(F32) for p, r in ((tb, tb_got), (tb_got, tb))
    )
    sum_qkv = jnp.concatenate([q_and_k, v_sum], axis=1)
    return (
        block_out,
        grad_in,
        total[0],
        total[1],
        sum_qkv,
        sum_attn,
        total[2],
        total[3],
        sum_fc1,
        sum_fc2,
        total[4],
        total[5],
        jnp.transpose(total[6:]),
        half_up,
        half_down,
    )


def solution(mesh):
    placed = (
        P("dp", "section"),
        P("dp", None),
        P("dp", None),
        P("section"),
        P("section"),
        P("section", None),
        P("section", None),
        P("section"),
        P("section"),
        P("section", None),
        P("section", None),
        P("section"),
        P("section"),
        P("section", None),
        P("section", "dp"),
        P("section", "dp"),
        P("dp", "section"),
    )
    return jax.shard_map(
        local,
        mesh=mesh,
        in_specs=placed,
        out_specs=(
            P("dp", "section"),
            P("dp", "section"),
            P("section"),
            P("section"),
            P("section", None),
            P("section", None),
            P("section"),
            P("section"),
            P("section", None),
            P("section", None),
            P("section"),
            P("section"),
            P("section", None),
            P("section", "dp"),
            P("section", "dp"),
        ),
        check_vma=False,
    )
```
